32 devices in a mesh: dp: 4 (over x, core), expert: 2 (over y), tensor: 4 (over z).
Axes of the slice: x: 2, y: 2, z: 4, core: 2. Of those that a mesh axis runs over, the one named last changes fastest.
Arguments:
- block_input: bfloat16 [4096, 1024], P(('dp', 'expert')), may hold values from -6 to 6
- first_gain: float32 [1024], replicated, may hold values from 0.5 to 1.5
- w_query: bfloat16 [1024, 1024], P(None, 'tensor'), may hold values from -0.1875 to 0.1875
- key_weight: bfloat16 [1024, 512], P(None, 'tensor'), may hold values from -0.1875 to 0.1875
- value_weight: bfloat16 [1024, 512], P(None, 'tensor'), may hold values from -0.1875 to 0.1875
- w_output: bfloat16 [1024, 1024], P('tensor'), may hold values from -1 to 1
- second_gain: float32 [1024], replicated, may hold values from 0.5 to 1.5
- w_router: bfloat16 [1024, 32], replicated, may hold values from -0.09375 to 0.09375
- w_gate: bfloat16 [32, 1024, 512], P('expert', None, 'tensor'), may hold values from -0.1875 to 0.1875
- w_up: bfloat16 [32, 1024, 512], P('expert', None, 'tensor'), may hold values from -0.1875 to 0.1875
- w_down: bfloat16 [32, 512, 1024], P('expert', 'tensor'), may hold values from -1 to 1
- expert_ids: int32 [4096, 8], P(('dp', 'expert')), may hold values from 0 to 31, as said below
- slot_index: int32 [4096, 8], P(('dp', 'expert')), may hold values from -1 to 127, as said below
- piece_start_offsets: int32 [4, 2], P('dp'), may hold values from 0 to 256
- upstream: bfloat16 [4096, 1024], P(('dp', 'expert')), may hold values from -6 to 6
Outputs:
- block_output: bfloat16 [4096, 1024], P(('dp', 'expert'), 'tensor')
- grad_input: bfloat16 [4096, 1024], P(('dp', 'expert'))
- grad_first: float32 [1024], replicated
- grad_query: float32 [1024, 1024], P(None, 'tensor')
- grad_key: float32 [1024, 512], P(None, 'tensor')
- grad_value: float32 [1024, 512], P(None, 'tensor')
- grad_output: float32 [1024, 1024], P('tensor')
- grad_second: float32 [1024], replicated
- grad_router: float32 [1024, 32], replicated
- grad_gate: float32 [32, 1024, 512], P('expert', None, 'tensor')
- grad_up: float32 [32, 1024, 512], P('expert', None, 'tensor')
- grad_down: float32 [32, 512, 1024], P('expert', 'tensor')
The draws below stay inside these ranges and needn't reach their ends.
Inputs may be any that keep to these rules, and one draw needn't show every extreme that they name: `expert_ids`: each row names 8 different experts. `slot_index`: among the rows of one device, a pair (row, k) routed to expert e holds the number of earlier pairs of that device routed to e, rows in order and k in order within a row; a pair with 128 or more earlier ones holds -1. On every device some expert receives 128 pairs or more.
All inputs are finite; a program needn't handle non-finite values.
Results may differ from the reference program's by a relative error of at most 0.02.
Values may be sent and summed in bfloat16 or wider, within the bound.
A program may use at most 192 MiB of HBM per device.

```python
import math
import jax
import jax.numpy as jnp
from jax import lax

MODEL_WIDTH = 1024
QUERY_HEAD_COUNT = 16
KEY_VALUE_HEADS = 8
HEAD_SIZE = 64
EXPERTS = 32
TOPK = 8
FF = 512
PIC = 256
SEQUENCE_LENGTH = 1024
ROWS = 512
SEQUENCE_COUNT = 4
TOKEN_TOTAL = 4096
CAP = 128
NPIC = 2
N_EXPERT = 2


def route_table(key):
    base = jax.random.fold_in(key, 41)
    favour = jax.random.randint(jax.random.fold_in(base, 1), (EXPERTS,), 0, 16384, dtype=jnp.int32)
    noise = jax.random.randint(jax.random.fold_in(base, 2), (TOKEN_TOTAL, EXPERTS), 0, 65536, dtype=jnp.int32)
    score = (noise + favour[None, :]) * EXPERTS + jnp.arange(EXPERTS, dtype=jnp.int32)[None, :]
    chosen = lax.top_k(score, TOPK)[1].astype(jnp.int32)
    marks = (chosen[:, :, None] == jnp.arange(EXPERTS, dtype=jnp.int32)[None, None, :]).astype(jnp.int32)
    grouped_heads = marks.reshape(TOKEN_TOTAL // ROWS, ROWS * TOPK, EXPERTS)
    earlier = jnp.cumsum(grouped_heads, axis=1, dtype=jnp.int32) - grouped_heads
    place = jnp.sum(earlier * grouped_heads, axis=2, dtype=jnp.int32).reshape(TOKEN_TOTAL, TOPK)
    slots = jnp.where(place < CAP, place, -1).astype(jnp.int32)
    return (chosen, slots)


def draw_expert_ids(key, part):
    return route_table(key)[0]


def draw_slot_index(key, part):
    return route_table(key)[1]


def plant(array, key, low, largest):
    spot = [jax.random.randint(jax.random.fold_in(key, axis), (), 0, length) for axis, length in enumerate(array.shape)]
    longest = array.shape.index(max(array.shape))
    beside = spot[:longest] + [(spot[longest] + 1) % array.shape[longest]] + spot[longest + 1:]
    return array.at[tuple(spot)].set(low).at[tuple(beside)].set(largest)


def level_of(own_key, extent, cuts, low, top_value):
    level = 1.0
    for axis_at, blocks in cuts:
        heights = jax.random.uniform(jax.random.fold_in(jax.random.fold_in(own_key, 6), axis_at), (blocks,), jnp.float32, low / len(cuts), top_value / len(cuts))
        level = level * jnp.repeat(jnp.exp(heights), extent[axis_at] // blocks).reshape((-1,) + (1,) * (len(extent) - 1 - axis_at))
    return level


def bell_draw(key, dims, spread, bound, split=(), kind=jnp.bfloat16):
    loudness = level_of(key, dims, split, -0.22, 0.18) if split else 1.0
    drawn = jax.random.normal(key, dims, jnp.float32) * spread * loudness
    return jnp.minimum(jnp.maximum(drawn, -bound), bound).astype(kind)


def setup_inputs(seed: int = 0) -> dict:
    splits = jax.random.split(jax.random.key(seed), 16)
    return {
        "block_input": bell_draw(splits[0], (TOKEN_TOTAL, MODEL_WIDTH), 1.0, 6.0, ((0, 8),)),
        "first_gain": jnp.clip(1.0 + 0.1 * jax.random.normal(splits[1], (MODEL_WIDTH,), jnp.float32), 0.5, 1.5),
        "w_query": bell_draw(splits[2], (MODEL_WIDTH, QUERY_HEAD_COUNT * HEAD_SIZE), MODEL_WIDTH ** -0.5, 0.1875, ((1, 4),)),
        "key_weight": bell_draw(splits[3], (MODEL_WIDTH, KEY_VALUE_HEADS * HEAD_SIZE), MODEL_WIDTH ** -0.5, 0.1875, ((1, 4),)),
        "value_weight": bell_draw(splits[4], (MODEL_WIDTH, KEY_VALUE_HEADS * HEAD_SIZE), MODEL_WIDTH ** -0.5, 0.1875, ((1, 4),)),
        "w_output": bell_draw(splits[5], (QUERY_HEAD_COUNT * HEAD_SIZE, MODEL_WIDTH), (HEAD_SIZE // 2) ** -0.5, 1.0, ((0, 4),)),
        "second_gain": jnp.clip(1.0 + 0.1 * jax.random.normal(splits[6], (MODEL_WIDTH,), jnp.float32), 0.5, 1.5),
        "w_router": bell_draw(splits[7], (MODEL_WIDTH, EXPERTS), (4 * MODEL_WIDTH) ** -0.5, 0.09375),
        "w_gate": bell_draw(splits[8], (EXPERTS, MODEL_WIDTH, FF), MODEL_WIDTH ** -0.5, 0.1875, ((0, 2), (2, 4))),
        "w_up": bell_draw(splits[9], (EXPERTS, MODEL_WIDTH, FF), MODEL_WIDTH ** -0.5, 0.1875, ((0, 2), (2, 4))),
        "w_down": bell_draw(splits[10], (EXPERTS, FF, MODEL_WIDTH), (FF // 16) ** -0.5, 1.0, ((0, 2), (1, 4))),
        "expert_ids": draw_expert_ids(jax.random.fold_in(splits[15], 71), 0),
        "slot_index": draw_slot_index(jax.random.fold_in(splits[15], 71), 0),
        "piece_start_offsets": plant(jax.random.randint(splits[13], (SEQUENCE_COUNT, NPIC), 0, PIC + 1), jax.random.fold_in(splits[13], 1), 0, PIC).astype(jnp.int32),
        "upstream": bell_draw(splits[14], (TOKEN_TOTAL, MODEL_WIDTH), 1.0, 6.0, ((0, 8),)),
    }


epsilon = 1e-06
rope_base = 10000.0
highest = lax.Precision.HIGHEST

@jax.custom_vjp
def lower_precision(v):
    return lax.optimization_barrier(v.astype(jnp.bfloat16)).astype(jnp.float32)

@jax.custom_vjp
def low_back(v):
    return v

def low_keep(v):
    return (lower_precision(v), None)

def low_pass(kept, grad):
    return (grad,)

def back_keep(v):
    return (v, None)

def back_low(kept, grad):
    return (lower_precision(grad),)
lower_precision.defvjp(low_keep, low_pass)
low_back.defvjp(back_keep, back_low)

def rope_tables(positions):
    steps = jnp.arange(HEAD_SIZE // 2, dtype=jnp.float32)
    inverse = jnp.exp(steps * (-2.0 * math.log(rope_base) / HEAD_SIZE))
    angle = positions.astype(jnp.float32)[:, None] * inverse[None, :]
    return (jnp.cos(angle), jnp.sin(angle))

def apply_rotary(values, cosine_table, sine_table):
    half = values.shape[-1] // 2
    first = values[..., :half]
    second = values[..., half:]
    cosine_table = cosine_table[:, None, :]
    sine_table = sine_table[:, None, :]
    return jnp.concatenate([first * cosine_table - second * sine_table, second * cosine_table + first * sine_table], axis=-1)

def piece_ids(positions, offsets):
    span = 2 * PIC
    window = positions // span
    within = positions - window * span
    count = offsets.shape[0]
    match = window[:, None] == jnp.arange(count, dtype=jnp.int32)[None, :]
    start = lax.optimization_barrier(jnp.sum(jnp.where(match, offsets[None, :], 0), axis=1)).astype(jnp.int32)
    inside = (window < count) & (within >= start) & (within < start + PIC)
    return jnp.where(inside, window, -1).astype(jnp.int32)

def rms_norm(values, gain):
    scale = lax.rsqrt(lax.optimization_barrier(jnp.mean(values * values, axis=-1, keepdims=True)) + epsilon)
    return values * scale * gain

def sequence_attend(operands):
    query_rows, key, value_rows, offsets = operands
    positions = jnp.arange(SEQUENCE_LENGTH, dtype=jnp.int32)
    pieces = piece_ids(positions, offsets)
    allowed = (positions[None, :] <= positions[:, None]) | (pieces[:, None] == pieces[None, :]) & (pieces[:, None] >= 0)

    def attend_head(head_operands):
        head_query, head_key, head_value = head_operands
        scores = low_back(jnp.einsum('gqd,kd->gqk', head_query, head_key, precision=highest) * HEAD_SIZE ** (-0.5))
        scores = jnp.where(allowed[None], scores, -1e+30)
        probs = jax.nn.softmax(scores, axis=-1)
        return jnp.einsum('gqk,kd->gqd', lower_precision(probs), head_value, precision=highest)
    grouped_heads = query_rows.reshape(SEQUENCE_LENGTH, KEY_VALUE_HEADS, QUERY_HEAD_COUNT // KEY_VALUE_HEADS, HEAD_SIZE).transpose(1, 2, 0, 3)
    heads = lax.map(jax.checkpoint(attend_head), (grouped_heads, key.transpose(1, 0, 2), value_rows.transpose(1, 0, 2)))
    return heads.transpose(2, 0, 1, 3).reshape(SEQUENCE_LENGTH, QUERY_HEAD_COUNT * HEAD_SIZE)

def slot_tables(expert_ids, slot_index):
    token = jnp.arange(TOKEN_TOTAL, dtype=jnp.int32)
    sequence = token // SEQUENCE_LENGTH
    source = token % SEQUENCE_LENGTH // ROWS
    buffer = SEQUENCE_COUNT * N_EXPERT * CAP
    place = ((sequence * N_EXPERT + source) * CAP)[:, None] + slot_index
    flat = jnp.where(slot_index >= 0, expert_ids * buffer + place, EXPERTS * buffer).astype(jnp.int32)
    owner = jnp.full((EXPERTS * buffer + 1,), TOKEN_TOTAL, jnp.int32).at[flat.reshape(-1)].set(jnp.repeat(token, TOPK))
    return (flat, owner[:-1].astype(jnp.int32))

def forward(values, gain_one, query_w, key_w, value_w, output_w, gain_two, router_w, gate_w, up_w, down_w, flat, owner, expert_ids, piece_start_offsets):
    buffer = SEQUENCE_COUNT * N_EXPERT * CAP
    normed = lower_precision(rms_norm(values, gain_one))
    query_rows = low_back(jnp.dot(normed, query_w, precision=highest))
    key = low_back(jnp.dot(normed, key_w, precision=highest))
    value_rows = lower_precision(low_back(jnp.dot(normed, value_w, precision=highest)))
    positions = jnp.tile(jnp.arange(SEQUENCE_LENGTH, dtype=jnp.int32), SEQUENCE_COUNT)
    cosine_table, sine_table = rope_tables(positions)
    query_rows = lower_precision(apply_rotary(query_rows.reshape(TOKEN_TOTAL, QUERY_HEAD_COUNT, HEAD_SIZE), cosine_table, sine_table))
    key = lower_precision(apply_rotary(key.reshape(TOKEN_TOTAL, KEY_VALUE_HEADS, HEAD_SIZE), cosine_table, sine_table))
    value_rows = value_rows.reshape(TOKEN_TOTAL, KEY_VALUE_HEADS, HEAD_SIZE)
    mixed_output = lax.map(sequence_attend, (query_rows.reshape(SEQUENCE_COUNT, SEQUENCE_LENGTH, QUERY_HEAD_COUNT, HEAD_SIZE), key.reshape(SEQUENCE_COUNT, SEQUENCE_LENGTH, KEY_VALUE_HEADS, HEAD_SIZE), value_rows.reshape(SEQUENCE_COUNT, SEQUENCE_LENGTH, KEY_VALUE_HEADS, HEAD_SIZE), piece_start_offsets))
    attended = lower_precision(low_back(mixed_output.reshape(TOKEN_TOTAL, QUERY_HEAD_COUNT * HEAD_SIZE)))
    residual = values + low_back(jnp.dot(attended, output_w, precision=highest))
    second = lower_precision(rms_norm(residual, gain_two))
    logits = low_back(jnp.dot(second, router_w, precision=highest))
    chosen = jnp.take_along_axis(logits, expert_ids, axis=1)
    gates = jax.nn.softmax(chosen, axis=-1)
    padded = jnp.concatenate([second, jnp.zeros((1, MODEL_WIDTH), jnp.float32)], axis=0)
    rows = padded[owner].reshape(EXPERTS, buffer, MODEL_WIDTH)
    gate_in = low_back(jnp.einsum('ebd,edf->ebf', rows, gate_w, precision=highest))
    up_in = low_back(jnp.einsum('ebd,edf->ebf', rows, up_w, precision=highest))
    hidden = lower_precision(jax.nn.silu(gate_in) * up_in)
    expert_out = lower_precision(low_back(jnp.einsum('ebf,efd->ebd', hidden, down_w, precision=highest)))
    padded_out = jnp.concatenate([expert_out.reshape(EXPERTS * buffer, MODEL_WIDTH), jnp.zeros((1, MODEL_WIDTH), jnp.float32)], axis=0)
    mixture = jnp.zeros((TOKEN_TOTAL, MODEL_WIDTH), jnp.float32)
    for pick in range(TOPK):
        mixture = mixture + gates[:, pick:pick + 1] * padded_out[flat[:, pick]]
    return residual + mixture

def reference(block_input, first_gain, w_query, key_weight, value_weight, w_output, second_gain, w_router, w_gate, w_up, w_down, expert_ids, slot_index, piece_start_offsets, upstream):
    floats = tuple((item.astype(jnp.float32) for item in (block_input, first_gain, w_query, key_weight, value_weight, w_output, second_gain, w_router, w_gate, w_up, w_down)))
    flat, owner = slot_tables(expert_ids, slot_index)

    def run(*weights):
        return forward(*weights, flat, owner, expert_ids, piece_start_offsets)
    output, pullback = jax.vjp(run, *floats)
    grads = pullback(upstream.astype(jnp.float32))
    return (output.astype(jnp.bfloat16), grads[0].astype(jnp.bfloat16), grads[1], grads[2], grads[3], grads[4], grads[5], grads[6], grads[7], grads[8], grads[9], grads[10])
```

```python
import functools
import math

import jax
import jax.numpy as jnp
from jax import lax
from jax.experimental import pallas as pl
from jax.experimental.pallas import tpu as pltpu
from jax.sharding import PartitionSpec as P

HEAD_SIZE = 64
TOPK = 8
PIC = 256


epsilon = 1e-06
rope_base = 10000.0
masked_score = -1e30


def rope_tables(positions):
    steps = jnp.arange(HEAD_SIZE // 2, dtype=jnp.float32)
    inverse = jnp.exp(steps * (-2.0 * math.log(rope_base) / HEAD_SIZE))
    angle = positions.astype(jnp.float32)[:, None] * inverse[None, :]
    return (jnp.cos(angle), jnp.sin(angle))


def apply_rotary(values, cosine_table, sine_table):
    half = values.shape[-1] // 2
    first = values[..., :half]
    second = values[..., half:]
    cosine_table = cosine_table[:, None, :]
    sine_table = sine_table[:, None, :]
    return jnp.concatenate(
        [first * cosine_table - second * sine_table, second * cosine_table + first * sine_table],
        axis=-1,
    )


def unrotate(values, cosine_table, sine_table):
    half = values.shape[-1] // 2
    first = values[..., :half]
    second = values[..., half:]
    cosine_table = cosine_table[:, None, :]
    sine_table = sine_table[:, None, :]
    return jnp.concatenate(
        [first * cosine_table + second * sine_table, second * cosine_table - first * sine_table],
        axis=-1,
    )


def piece_ids(positions, offsets):
    span = 2 * PIC
    window = positions // span
    within = positions - window * span
    count = offsets.shape[0]
    match = window[:, None] == jnp.arange(count, dtype=jnp.int32)[None, :]
    start = jnp.sum(jnp.where(match, offsets[None, :], 0), axis=1)
    inside = (window < count) & (within >= start) & (within < start + PIC)
    return jnp.where(inside, window, -1)


def matmul(left, right):
    return jnp.dot(left, right, preferred_element_type=jnp.float32)


def matmul_nt(left, right):
    return lax.dot_general(
        left, right, (((1,), (1,)), ((), ())), preferred_element_type=jnp.float32
    )


def matmul_tn(left, right):
    return lax.dot_general(
        left, right, (((0,), (0,)), ((), ())), preferred_element_type=jnp.float32
    )


def norm_scale(values):
    return lax.rsqrt(jnp.mean(values * values, axis=-1, keepdims=True) + epsilon)


def norm_back(grad, unit, scale, gain):
    weighted = grad * gain
    return scale * (weighted - unit * jnp.mean(weighted * unit, axis=-1, keepdims=True))


def general_device(
    block_input,
    first_gain,
    w_query,
    key_weight,
    value_weight,
    w_output,
    second_gain,
    w_router,
    w_gate,
    w_up,
    w_down,
    expert_ids,
    slot_index,
    piece_start_offsets,
    upstream,
):
    rows_here = block_input.shape[0]
    width = block_input.shape[1]
    groups = lax.axis_size("expert")
    length = rows_here * groups
    local_heads = w_query.shape[1] // HEAD_SIZE
    local_kv = key_weight.shape[1] // HEAD_SIZE
    sharing = local_heads // local_kv
    head_rows = sharing * rows_here
    experts_all = w_router.shape[1]
    capacity = TOPK * rows_here // experts_all
    slots_all = experts_all * capacity
    score_scale = HEAD_SIZE ** (-0.5)
    positions = lax.axis_index("expert") * rows_here + jnp.arange(rows_here, dtype=jnp.int32)
    cosine_table, sine_table = rope_tables(positions)
    inputs = block_input.astype(jnp.float32)
    first_scale = norm_scale(inputs)
    first_unit = inputs * first_scale
    first_normed = (first_unit * first_gain).astype(jnp.bfloat16)
    query_rot = apply_rotary(
        matmul(first_normed, w_query).reshape(rows_here, local_heads, HEAD_SIZE),
        cosine_table,
        sine_table,
    ).astype(jnp.bfloat16)
    key_rot = (
        apply_rotary(
            matmul(first_normed, key_weight).reshape(rows_here, local_kv, HEAD_SIZE),
            cosine_table,
            sine_table,
        )
        .astype(jnp.bfloat16)
        .reshape(rows_here, local_kv * HEAD_SIZE)
    )
    value_low = matmul(first_normed, value_weight).astype(jnp.bfloat16)
    keys_all, values_all = (
        lax.all_gather(key_rot, "expert", axis=0, tiled=True),
        lax.all_gather(value_low, "expert", axis=0, tiled=True),
    )
    block = min(512, length)
    blocks = length // block

    def by_block(array):
        return array.reshape(blocks, block, local_kv, HEAD_SIZE).transpose(0, 2, 1, 3)

    def by_rows(stacked):
        return stacked.transpose(0, 2, 1, 3).reshape(length, local_kv * HEAD_SIZE)

    def head_major(array):
        return (
            array.reshape(rows_here, local_kv, sharing, HEAD_SIZE)
            .transpose(1, 2, 0, 3)
            .reshape(local_kv, head_rows, HEAD_SIZE)
        )

    def row_major(array):
        return (
            array.reshape(local_kv, sharing, rows_here, HEAD_SIZE)
            .transpose(2, 0, 1, 3)
            .reshape(rows_here, local_heads * HEAD_SIZE)
        )

    key_blocks = by_block(keys_all)
    value_blocks = by_block(values_all)
    block_starts = jnp.arange(blocks, dtype=jnp.int32) * block
    query_heads = head_major(query_rot.reshape(rows_here, local_heads * HEAD_SIZE))
    offsets = piece_start_offsets[0]
    key_pieces = piece_ids(jnp.arange(length, dtype=jnp.int32), offsets)
    query_pieces = jnp.tile(piece_ids(positions, offsets), sharing)
    query_places = jnp.tile(positions, sharing)

    def block_scores(key_block, start):
        places = start + jnp.arange(block, dtype=jnp.int32)
        pieces = lax.dynamic_slice_in_dim(key_pieces, start, block)
        causal = places[None, :] <= query_places[:, None]
        same = (pieces[None, :] == query_pieces[:, None]) & (query_pieces[:, None] >= 0)
        scores = (
            jnp.einsum("hqd,hkd->hqk", query_heads, key_block, preferred_element_type=jnp.float32)
            * score_scale
        )
        return (scores, (causal | same)[None])

    def max_step(carry, operands):
        running_max, running_sum = carry
        key_block, start = operands
        scores, allowed = block_scores(key_block, start)
        scores = jnp.where(allowed, scores, masked_score)
        new_max = jnp.maximum(running_max, jnp.max(scores, axis=-1))
        weights = jnp.where(allowed, jnp.exp(scores - new_max[..., None]), 0.0)
        new_sum = running_sum * jnp.exp(running_max - new_max) + jnp.sum(weights, axis=-1)
        return ((new_max, new_sum), None)

    start_max = jnp.full((local_kv, head_rows), masked_score, jnp.float32)
    start_sum = jnp.zeros((local_kv, head_rows), jnp.float32)
    (row_max, row_sum), _ = lax.scan(max_step, (start_max, start_sum), (key_blocks, block_starts))
    log_total = row_max + jnp.log(row_sum)

    def block_probs(key_block, start):
        scores, allowed = block_scores(key_block, start)
        return jnp.where(allowed, jnp.exp(scores - log_total[..., None]), 0.0)

    def value_step(total, operands):
        key_block, value_block, start = operands
        probs = block_probs(key_block, start).astype(jnp.bfloat16)
        return (
            total
            + jnp.einsum("hqk,hkd->hqd", probs, value_block, preferred_element_type=jnp.float32),
            None,
        )

    mixed_output, _ = lax.scan(
        value_step,
        jnp.zeros((local_kv, head_rows, HEAD_SIZE), jnp.float32),
        (key_blocks, value_blocks, block_starts),
    )
    attended = row_major(mixed_output).astype(jnp.bfloat16)
    attention = lax.psum(matmul(attended, w_output), "tensor")
    residual = inputs + attention
    second_scale = norm_scale(residual)
    second_unit = residual * second_scale
    second_normed = (second_unit * second_gain).astype(jnp.bfloat16)
    logits = matmul(second_normed, w_router)
    chosen = jnp.take_along_axis(logits, expert_ids, axis=1)
    gates = jax.nn.softmax(chosen, axis=-1)
    row_ids = jnp.arange(rows_here, dtype=jnp.int32)
    flat = jnp.where(slot_index >= 0, expert_ids * capacity + slot_index, slots_all)
    selector = (
        jnp.zeros((slots_all, rows_here), jnp.bfloat16)
        .at[flat.reshape(-1), jnp.repeat(row_ids, TOPK)]
        .set(1.0, mode="drop")
    )
    dispatched = (
        matmul(selector, second_normed).astype(jnp.bfloat16).reshape(experts_all, capacity, width)
    )
    expert_rows = lax.all_to_all(dispatched, "expert", split_axis=0, concat_axis=1, tiled=True)
    gate_in = jnp.einsum("ebd,edf->ebf", expert_rows, w_gate, preferred_element_type=jnp.float32)
    up_in = jnp.einsum("ebd,edf->ebf", expert_rows, w_up, preferred_element_type=jnp.float32)
    sigmoid_gate = jax.nn.sigmoid(gate_in)
    silu_gate = gate_in * sigmoid_gate
    hidden = (silu_gate * up_in).astype(jnp.bfloat16)
    partial_out = jnp.einsum("ebf,efd->ebd", hidden, w_down, preferred_element_type=jnp.float32)
    expert_part = lax.psum_scatter(
        partial_out.astype(jnp.bfloat16), "tensor", scatter_dimension=2, tiled=True
    )
    returned = lax.all_to_all(expert_part, "expert", split_axis=1, concat_axis=0, tiled=True)
    quarter = returned.shape[2]
    padded_out = jnp.concatenate(
        [returned.reshape(slots_all, quarter), jnp.zeros((1, quarter), jnp.bfloat16)], axis=0
    )
    feature_start = lax.axis_index("tensor") * quarter
    grad_full = upstream.astype(jnp.float32)
    grad_part = lax.dynamic_slice_in_dim(grad_full, feature_start, quarter, 1)
    mixture = jnp.zeros((rows_here, quarter), jnp.float32)
    gate_terms = []
    for pick in range(TOPK):
        picked = padded_out[flat[:, pick]].astype(jnp.float32)
        mixture = mixture + gates[:, pick : pick + 1] * picked
        gate_terms.append(jnp.sum(grad_part * picked, axis=1))
    gate_part = jnp.stack(gate_terms, axis=1)
    block_output = (lax.dynamic_slice_in_dim(residual, feature_start, quarter, 1) + mixture).astype(
        jnp.bfloat16
    )
    slot_gates = (
        jnp.zeros((slots_all + 1,), jnp.float32)
        .at[flat.reshape(-1)]
        .set(gates.reshape(-1))[:slots_all]
    )
    grad_slots = (
        (matmul(selector, upstream) * slot_gates[:, None])
        .astype(jnp.bfloat16)
        .reshape(experts_all, capacity, width)
    )
    grad_rows_in = lax.all_to_all(grad_slots, "expert", split_axis=0, concat_axis=1, tiled=True)
    hidden_grad = jnp.einsum(
        "ebd,efd->ebf", grad_rows_in, w_down, preferred_element_type=jnp.float32
    )
    grad_down = jnp.einsum("ebf,ebd->efd", hidden, grad_rows_in, preferred_element_type=jnp.float32)
    gate_in_grad = (
        hidden_grad * up_in * (sigmoid_gate * (1.0 + gate_in * (1.0 - sigmoid_gate)))
    ).astype(jnp.bfloat16)
    up_in_grad = (hidden_grad * silu_gate).astype(jnp.bfloat16)
    grad_gate = jnp.einsum(
        "ebd,ebf->edf", expert_rows, gate_in_grad, preferred_element_type=jnp.float32
    )
    grad_up = jnp.einsum(
        "ebd,ebf->edf", expert_rows, up_in_grad, preferred_element_type=jnp.float32
    )
    rows_part = jnp.einsum("ebf,edf->ebd", gate_in_grad, w_gate, preferred_element_type=jnp.float32)
    rows_part = rows_part + jnp.einsum(
        "ebf,edf->ebd", up_in_grad, w_up, preferred_element_type=jnp.float32
    )
    rows_back = lax.all_to_all(
        rows_part.astype(jnp.bfloat16), "expert", split_axis=1, concat_axis=0, tiled=True
    ).astype(rows_part.dtype)
    padded_back = jnp.concatenate(
        [rows_back.reshape(slots_all, width), jnp.zeros((1, width), jnp.float32)], axis=0
    )
    second_part = jnp.zeros((rows_here, width), jnp.float32)
    for pick in range(TOPK):
        second_part = second_part + padded_back[flat[:, pick]]
    second_sum, gate_grads = (
        lax.psum(second_part.astype(jnp.bfloat16), "tensor").astype(jnp.float32),
        lax.psum(gate_part.astype(jnp.bfloat16), "tensor").astype(jnp.float32),
    )
    chosen_grad = gates * (gate_grads - jnp.sum(gates * gate_grads, axis=1, keepdims=True))
    expert_axis = jnp.arange(experts_all, dtype=jnp.int32)
    logit_grad = jnp.zeros((rows_here, experts_all), jnp.float32)
    for pick in range(TOPK):
        logit_grad = logit_grad + jnp.where(
            expert_ids[:, pick : pick + 1] == expert_axis[None, :],
            chosen_grad[:, pick : pick + 1],
            0.0,
        )
    logit_low = logit_grad.astype(jnp.bfloat16)
    grad_router = matmul_tn(second_normed, logit_low)
    second_grad = second_sum + matmul_nt(logit_low, w_router)
    grad_second = jnp.sum(second_grad * second_unit, axis=0)
    residual_grad = grad_full + norm_back(second_grad, second_unit, second_scale, second_gain)
    residual_low = residual_grad.astype(jnp.bfloat16)
    grad_output = matmul_tn(attended, residual_low)
    attended_grad = head_major(matmul_nt(residual_low, w_output).astype(jnp.bfloat16))

    def delta_step(total, operands):
        key_block, value_block, start = operands
        probs = block_probs(key_block, start)
        prob_grad = jnp.einsum(
            "hqd,hkd->hqk", attended_grad, value_block, preferred_element_type=jnp.float32
        )
        return (total + jnp.sum(probs * prob_grad, axis=-1), None)

    delta, _ = lax.scan(
        delta_step,
        jnp.zeros((local_kv, head_rows), jnp.float32),
        (key_blocks, value_blocks, block_starts),
    )

    def grad_step(query_total, operands):
        key_block, value_block, start = operands
        probs = block_probs(key_block, start)
        prob_grad = jnp.einsum(
            "hqd,hkd->hqk", attended_grad, value_block, preferred_element_type=jnp.float32
        )
        score_grad = (probs * (prob_grad - delta[..., None])).astype(jnp.bfloat16)
        query_total = (
            query_total
            + jnp.einsum("hqk,hkd->hqd", score_grad, key_block, preferred_element_type=jnp.float32)
            * score_scale
        )
        key_grad = (
            jnp.einsum("hqk,hqd->hkd", score_grad, query_heads, preferred_element_type=jnp.float32)
            * score_scale
        )
        value_grad = jnp.einsum(
            "hqk,hqd->hkd",
            probs.astype(jnp.bfloat16),
            attended_grad,
            preferred_element_type=jnp.float32,
        )
        return (query_total, (key_grad, value_grad))

    query_total, (key_stack, value_stack) = lax.scan(
        grad_step,
        jnp.zeros((local_kv, head_rows, HEAD_SIZE), jnp.float32),
        (key_blocks, value_blocks, block_starts),
    )
    key_back, value_back = (
        lax.psum_scatter(
            by_rows(key_stack).astype(jnp.bfloat16), "expert", scatter_dimension=0, tiled=True
        ).astype(jnp.float32),
        lax.psum_scatter(
            by_rows(value_stack).astype(jnp.bfloat16), "expert", scatter_dimension=0, tiled=True
        ).astype(jnp.float32),
    )
    query_grad = (
        unrotate(
            row_major(query_total).reshape(rows_here, local_heads, HEAD_SIZE),
            cosine_table,
            sine_table,
        )
        .astype(jnp.bfloat16)
        .reshape(rows_here, local_heads * HEAD_SIZE)
    )
    key_grad = (
        unrotate(key_back.reshape(rows_here, local_kv, HEAD_SIZE), cosine_table, sine_table)
        .astype(jnp.bfloat16)
        .reshape(rows_here, local_kv * HEAD_SIZE)
    )
    value_grad = value_back.astype(jnp.bfloat16)
    grad_query = matmul_tn(first_normed, query_grad)
    grad_key = matmul_tn(first_normed, key_grad)
    grad_value = matmul_tn(first_normed, value_grad)
    first_part = (
        matmul_nt(query_grad, w_query)
        + matmul_nt(key_grad, key_weight)
        + matmul_nt(value_grad, value_weight)
    )
    first_grad = lax.psum(first_part.astype(jnp.bfloat16), "tensor").astype(jnp.float32)
    grad_first = jnp.sum(first_grad * first_unit, axis=0)
    grad_input = (
        residual_grad + norm_back(first_grad, first_unit, first_scale, first_gain)
    ).astype(jnp.bfloat16)
    dense = lax.psum(
        (grad_query, grad_key, grad_value, grad_output, grad_router, grad_first, grad_second),
        ("dp", "expert"),
    )
    expert_sums = (
        lax.psum(grad_gate.astype(jnp.bfloat16), "dp").astype(jnp.float32),
        lax.psum(grad_up.astype(jnp.bfloat16), "dp").astype(jnp.float32),
        lax.psum(grad_down.astype(jnp.bfloat16), "dp").astype(jnp.float32),
    )
    return (
        block_output,
        grad_input,
        dense[5],
        dense[0],
        dense[1],
        dense[2],
        dense[3],
        dense[6],
        dense[4],
        expert_sums[0],
        expert_sums[1],
        expert_sums[2],
    )


BF = jnp.bfloat16
F32 = jnp.float32
MIB = 1 << 20


def vmem_spec():
    return pl.BlockSpec(memory_space=pltpu.VMEM)


def smem_spec():
    return pl.BlockSpec(memory_space=pltpu.SMEM)


def allowed_pairs(scal_ref, rows):
    side = scal_ref[0]
    here = lax.broadcasted_iota(jnp.int32, (rows, 1), 0)
    keys = lax.broadcasted_iota(jnp.int32, (1, 2 * rows), 1)
    query_place = side * rows + here
    key_place = jnp.where(keys < rows, side * rows + keys, (1 - side) * rows + keys - rows)
    span = 2 * PIC

    def piece(places):
        window = places // span
        within = places - window * span
        start = jnp.where(window == 0, scal_ref[1], scal_ref[2])
        inside = (within >= start) & (within < start + PIC)
        return jnp.where(inside, window, -1)

    query_piece = piece(query_place)
    key_piece = piece(key_place)
    return (key_place <= query_place) | ((key_piece == query_piece) & (query_piece >= 0))


def attend_kernel(scal_ref, q_ref, k_ref, v_ref, wo_ref, att_ref, lse_ref, part_ref):
    rows = q_ref.shape[0]
    heads = q_ref.shape[1] // HEAD_SIZE
    sharing = q_ref.shape[1] // k_ref.shape[1]
    allowed = allowed_pairs(scal_ref, rows)
    pieces = []
    for head in range(heads):
        at = head * HEAD_SIZE
        kv = head // sharing * HEAD_SIZE
        query = q_ref[:, at : at + HEAD_SIZE]
        key = k_ref[:, kv : kv + HEAD_SIZE]
        value = v_ref[:, kv : kv + HEAD_SIZE]
        scores = jnp.where(allowed, matmul_nt(query, key) * (HEAD_SIZE**-0.5), masked_score)
        peak = jnp.max(scores, axis=1, keepdims=True)
        weights = jnp.exp(scores - peak)
        total = jnp.sum(weights, axis=1, keepdims=True)
        probs = (weights * (1.0 / total)).astype(BF)
        pieces.append(matmul(probs, value))
        lse_ref[:, head : head + 1] = peak + jnp.log(total)
    attended = jnp.concatenate(pieces, axis=1).astype(BF)
    att_ref[...] = attended
    part_ref[...] = matmul(attended, wo_ref[...]).astype(BF)


def attend(scal, query, key, value, w_output):
    rows, wide = query.shape
    return pl.pallas_call(
        attend_kernel,
        out_shape=(
            jax.ShapeDtypeStruct((rows, wide), BF),
            jax.ShapeDtypeStruct((rows, 128), F32),
            jax.ShapeDtypeStruct((rows, w_output.shape[1]), BF),
        ),
        in_specs=[smem_spec()] + [vmem_spec()] * 4,
        out_specs=(vmem_spec(),) * 3,
        compiler_params=pltpu.CompilerParams(vmem_limit_bytes=48 * MIB),
        name="attend",
    )(scal, query, key, value, w_output)


def turn(values, first):
    wide = values.shape[1]
    half = HEAD_SIZE // 2
    return jnp.where(
        first, -pltpu.roll(values, wide - half, 1), pltpu.roll(values, half, 1)
    )


def attend_back_kernel(
    scal_ref, q_ref, k_ref, v_ref, lse_ref, att_ref, low_ref, wo_ref, cos_ref, sin_ref,
    dq_ref, dk_ref, dv_ref, dwo_ref,
):
    rows, wide = q_ref.shape
    heads = wide // HEAD_SIZE
    sharing = q_ref.shape[1] // k_ref.shape[1]
    scale = HEAD_SIZE**-0.5
    low = low_ref[...]
    dwo_ref[...] = matmul_tn(att_ref[...], low)
    att_grad = matmul_nt(low, wo_ref[...]).astype(BF)
    allowed = allowed_pairs(scal_ref, rows)
    query_parts, key_parts, value_parts = [], [], []
    for head in range(heads):
        at = head * HEAD_SIZE
        kv = head // sharing * HEAD_SIZE
        query = q_ref[:, at : at + HEAD_SIZE]
        key = k_ref[:, kv : kv + HEAD_SIZE]
        value = v_ref[:, kv : kv + HEAD_SIZE]
        grad = att_grad[:, at : at + HEAD_SIZE]
        scores = jnp.where(allowed, matmul_nt(query, key) * scale, masked_score)
        probs = jnp.exp(scores - lse_ref[:, head : head + 1])
        prob_grad = matmul_nt(grad, value)
        delta = jnp.sum(probs * prob_grad, axis=1, keepdims=True)
        score_grad = (probs * (prob_grad - delta)).astype(BF)
        query_parts.append(matmul(score_grad, key) * scale)
        key_part = matmul_tn(score_grad, query) * scale
        value_part = matmul_tn(probs.astype(BF), grad)
        if head % sharing == 0:
            key_parts.append(key_part)
            value_parts.append(value_part)
        else:
            key_parts[-1] = key_parts[-1] + key_part
            value_parts[-1] = value_parts[-1] + value_part
    dk_ref[...] = jnp.concatenate(key_parts, axis=1).astype(BF)
    dv_ref[...] = jnp.concatenate(value_parts, axis=1).astype(BF)
    rotated = jnp.concatenate(query_parts, axis=1)
    lane = lax.broadcasted_iota(jnp.int32, (1, wide), 1)
    first = lane % HEAD_SIZE < HEAD_SIZE // 2
    cosines = jnp.concatenate([cos_ref[...]] * (wide // 128), axis=1)
    sines = jnp.concatenate([sin_ref[...]] * (wide // 128), axis=1)
    dq_ref[...] = (rotated * cosines - turn(rotated, first) * sines).astype(BF)


def attend_back(scal, query, key, value, lse, attended, low, w_output, cosines, sines):
    rows, wide = query.shape
    return pl.pallas_call(
        attend_back_kernel,
        out_shape=(
            jax.ShapeDtypeStruct((rows, wide), BF),
            jax.ShapeDtypeStruct(key.shape, BF),
            jax.ShapeDtypeStruct(value.shape, BF),
            jax.ShapeDtypeStruct(w_output.shape, F32),
        ),
        in_specs=[smem_spec()] + [vmem_spec()] * 9,
        out_specs=(vmem_spec(),) * 4,
        compiler_params=pltpu.CompilerParams(vmem_limit_bytes=56 * MIB),
        name="attend_back",
    )(scal, query, key, value, lse, attended, low, w_output, cosines, sines)


CHUNK = 256
GROUP = 4


def expert_kernel(last, *refs):
    if last:
        (
            scal_ref, n_ref, nt_ref, g_ref, chosen_ref, kept_ref, wr_ref, wg_ref, wu_ref, wd_ref, mix_in, back_in, gg_in,
            dwg_ref, dwu_ref, dwd_ref, mix_ref, back_ref, route_ref,
            gates, kept_gates, gate_grads, mix, back, wgs, wus, ghs, ght, dgs, dus,
        ) = refs
    else:
        (
            scal_ref, n_ref, g_ref, chosen_ref, kept_ref, wr_ref, wg_ref, wu_ref, wd_ref,
            dwg_ref, dwu_ref, dwd_ref, mix_ref, back_ref, gg_ref, nt_ref,
            gates, kept_gates, gate_grads, mix, back, wgs, wus, ghs, ght, dgs, dus,
        ) = refs
    step = pl.program_id(0)
    tokens, width = n_ref.shape
    experts_all = wr_ref.shape[1]
    group, _, hid = wg_ref.shape
    chunks = tokens // CHUNK
    lane = lax.broadcasted_iota(jnp.int32, (1, experts_all), 1)

    @pl.when(step == 0)
    def _():
        def start(at, carry):
            rows = pl.ds(pl.multiple_of(at * CHUNK, CHUNK), CHUNK)
            chosen = chosen_ref[rows, :] > 0.0
            logits = jnp.where(chosen, matmul(n_ref[rows, :], wr_ref[...]), masked_score)
            raised = jnp.exp(logits - jnp.max(logits, axis=1, keepdims=True))
            raised = jnp.where(chosen, raised, 0.0)
            gate = raised / jnp.sum(raised, axis=1, keepdims=True)
            gates[rows, :] = gate
            kept_gates[rows, :] = gate * kept_ref[rows, :]
            if last:
                mix[rows, :] = mix_in[rows, :].astype(F32)
                back[rows, :] = back_in[rows, :].astype(F32)
                gate_grads[rows, :] = gg_in[rows, :]
            else:
                mix[rows, :] = jnp.zeros((CHUNK, width), F32)
                back[rows, :] = jnp.zeros((CHUNK, width), F32)
                gate_grads[rows, :] = jnp.zeros((CHUNK, experts_all), F32)
            return carry

        lax.fori_loop(0, chunks, start, 0)
        if not last:
            for at in range(chunks):
                nt_ref[:, at * CHUNK : (at + 1) * CHUNK] = n_ref[at * CHUNK : (at + 1) * CHUNK, :].T

    for expert in range(group):
        wgs[:, expert * hid : (expert + 1) * hid] = wg_ref[expert]
        wus[:, expert * hid : (expert + 1) * hid] = wu_ref[expert]
    column = scal_ref[1] * (experts_all // 2) + scal_ref[0] * (experts_all // 4) + step * group

    def forward(at, carry):
        rows = pl.ds(pl.multiple_of(at * CHUNK, CHUNK), CHUNK)
        token = n_ref[rows, :]
        down = wd_ref[...].reshape(group * hid, width)
        gate_in = matmul(token, wgs[...])
        up_in = matmul(token, wus[...])
        pulled = matmul_nt(g_ref[rows, :], down)
        sig = 0.5 * jnp.tanh(0.5 * gate_in) + 0.5
        silu = gate_in * sig
        hidden = silu * up_in
        kept = kept_gates[rows, :]
        weights = []
        products = hidden * pulled
        grads = gate_grads[rows, :]
        for expert in range(group):
            here = lane == column + expert
            gate = jnp.sum(jnp.where(here, kept, 0.0), axis=1, keepdims=True)
            weights.append(jnp.broadcast_to(gate, (CHUNK, hid)))
            product = jnp.sum(products[:, expert * hid : (expert + 1) * hid], axis=1, keepdims=True)
            grads = grads + jnp.where(here, product, 0.0)
        gate_grads[rows, :] = grads
        weight = jnp.concatenate(weights, axis=1)
        gated = (hidden * weight).astype(BF)
        pulled = pulled * weight
        up_grad = (pulled * silu).astype(BF)
        gate_grad = (pulled * up_in * (sig + silu * (1.0 - sig))).astype(BF)
        ghs[rows, :] = gated
        dgs[rows, :] = gate_grad
        dus[rows, :] = up_grad
        mix[rows, :] += matmul(gated, down)
        back[rows, :] += matmul_nt(gate_grad, wgs[...]) + matmul_nt(up_grad, wus[...])
        return carry

    lax.fori_loop(0, chunks, forward, 0)
    for at in range(chunks):
        ght[:, at * CHUNK : (at + 1) * CHUNK] = ghs[at * CHUNK : (at + 1) * CHUNK, :].T

    def weights_grad(at, carry):
        rows = pl.ds(pl.multiple_of(at * CHUNK, CHUNK), CHUNK)
        turned = nt_ref[rows, :]
        gate_part = matmul(turned, dgs[...]).astype(BF)
        up_part = matmul(turned, dus[...]).astype(BF)
        for expert in range(group):
            dwg_ref[expert, rows, :] = gate_part[:, expert * hid : (expert + 1) * hid]
            dwu_ref[expert, rows, :] = up_part[:, expert * hid : (expert + 1) * hid]
        return carry

    lax.fori_loop(0, width // CHUNK, weights_grad, 0)
    for at in range(group * hid // CHUNK):
        part = matmul(ght[at * CHUNK : (at + 1) * CHUNK, :], g_ref[...]).astype(BF)
        for inner in range(CHUNK // hid):
            dwd_ref[at * (CHUNK // hid) + inner] = part[inner * hid : (inner + 1) * hid, :]

    @pl.when(step == pl.num_programs(0) - 1)
    def _():
        if last:
            route_ref[...] = jnp.zeros(route_ref.shape, F32)

        def finish(at, carry):
            rows = pl.ds(pl.multiple_of(at * CHUNK, CHUNK), CHUNK)
            mix_ref[rows, :] = mix[rows, :].astype(BF)
            if last:
                grads = gate_grads[rows, :] * kept_gates[rows, :]
                chosen_grad = grads - gates[rows, :] * jnp.sum(grads, axis=1, keepdims=True)
                low = chosen_grad.astype(BF)
                back_ref[rows, :] = (back[rows, :] + matmul_nt(low, wr_ref[...])).astype(BF)
                route_ref[...] += matmul_tn(low, n_ref[rows, :])
            else:
                back_ref[rows, :] = back[rows, :].astype(BF)
                gg_ref[rows, :] = gate_grads[rows, :]
            return carry

        lax.fori_loop(0, chunks, finish, 0)


def experts(last, scal, normed, turned, upstream, chosen, kept, w_router, w_gate, w_up, w_down, mix, back, gate_grads):
    tokens, width = normed.shape
    count, _, hid = w_gate.shape
    half = count // 2
    steps = half // GROUP
    experts_all = w_router.shape[1]
    whole = lambda step, scal: (0, 0)
    full = lambda array: pl.BlockSpec(array.shape, whole)
    picked = lambda step, scal: (scal[0] * steps + step, 0, 0)
    own = lambda step, scal: (step, 0, 0)
    rows_block = pl.BlockSpec((tokens, width), whole)
    narrow_block = pl.BlockSpec((tokens, experts_all), whole)
    args = [normed] + ([turned] if last else []) + [upstream, chosen, kept, w_router]
    specs = [full(array) for array in args]
    args += [w_gate, w_up, w_down]
    specs += [
        pl.BlockSpec((GROUP, width, hid), picked),
        pl.BlockSpec((GROUP, width, hid), picked),
        pl.BlockSpec((GROUP, hid, width), picked),
    ]
    if last:
        args += [mix, back, gate_grads]
        specs += [rows_block, rows_block, narrow_block]
    out_shape = [
        jax.ShapeDtypeStruct((half, width, hid), BF),
        jax.ShapeDtypeStruct((half, width, hid), BF),
        jax.ShapeDtypeStruct((half, hid, width), BF),
        jax.ShapeDtypeStruct((tokens, width), BF),
        jax.ShapeDtypeStruct((tokens, width), BF),
    ]
    out_specs = [
        pl.BlockSpec((GROUP, width, hid), own),
        pl.BlockSpec((GROUP, width, hid), own),
        pl.BlockSpec((GROUP, hid, width), own),
        rows_block,
        rows_block,
    ]
    if last:
        out_shape += [jax.ShapeDtypeStruct((experts_all, width), F32)]
        out_specs += [pl.BlockSpec((experts_all, width), whole)]
    else:
        out_shape += [
            jax.ShapeDtypeStruct((tokens, experts_all), F32),
            jax.ShapeDtypeStruct((width, tokens), BF),
        ]
        out_specs += [narrow_block, pl.BlockSpec((width, tokens), whole)]
    return pl.pallas_call(
        functools.partial(expert_kernel, last),
        out_shape=out_shape,
        grid_spec=pltpu.PrefetchScalarGridSpec(
            num_scalar_prefetch=1,
            grid=(steps,),
            in_specs=specs,
            out_specs=out_specs,
            scratch_shapes=[
                pltpu.VMEM((tokens, experts_all), F32),
                pltpu.VMEM((tokens, experts_all), F32),
                pltpu.VMEM((tokens, experts_all), F32),
                pltpu.VMEM((tokens, width), F32),
                pltpu.VMEM((tokens, width), F32),
                pltpu.VMEM((width, GROUP * hid), BF),
                pltpu.VMEM((width, GROUP * hid), BF),
                pltpu.VMEM((tokens, GROUP * hid), BF),
                pltpu.VMEM((GROUP * hid, tokens), BF),
                pltpu.VMEM((tokens, GROUP * hid), BF),
                pltpu.VMEM((tokens, GROUP * hid), BF),
            ],
        ),
        compiler_params=pltpu.CompilerParams(
            dimension_semantics=("arbitrary",), vmem_limit_bytes=60 * MIB
        ),
        cost_estimate=pl.CostEstimate(
            flops=18 * tokens * width * half * hid,
            bytes_accessed=12 * half * width * hid + 16 * tokens * width,
            transcendentals=tokens * half * hid,
        ),
        name="experts_last" if last else "experts_first",
    )(scal, *args)


def swap(array, axis, bit):
    size = lax.axis_size(axis)
    return lax.ppermute(array, axis, [(at, at ^ bit) for at in range(size)])


def fast_device(
    block_input, first_gain, w_query, key_weight, value_weight, w_output, second_gain, w_router,
    w_gate, w_up, w_down, expert_ids, slot_index, piece_start_offsets, upstream,
):
    rows, width = block_input.shape
    local_heads = w_query.shape[1] // HEAD_SIZE
    local_kv = key_weight.shape[1] // HEAD_SIZE
    experts_all = w_router.shape[1]
    side = lax.axis_index("expert")
    core = lax.axis_index("dp") % 2
    feature_start = lax.axis_index("tensor") * (width // 4)
    scal = jnp.concatenate([side[None].astype(jnp.int32), piece_start_offsets[0]])

    axis_row = jnp.arange(experts_all, dtype=jnp.int32)[None, None, :]
    hits = (expert_ids[:, :, None] == axis_row)
    chosen = jnp.sum(hits.astype(F32), axis=1)
    kept = jnp.sum((hits & (slot_index >= 0)[:, :, None]).astype(F32), axis=1)
    marks = jnp.concatenate([chosen, kept], axis=1).astype(BF)
    marks = jnp.concatenate([marks, swap(marks, "expert", 1)], axis=0).astype(F32)
    chosen, kept = marks[:, :experts_all], marks[:, experts_all:]
    upstream_all = jnp.concatenate([upstream, swap(upstream, "expert", 1)], axis=0)

    positions = side * rows + jnp.arange(rows, dtype=jnp.int32)
    cosine_table, sine_table = rope_tables(positions)
    cosines = jnp.tile(cosine_table, (1, 4))
    sines = jnp.tile(sine_table, (1, 4))
    inputs = block_input.astype(F32)
    first_scale = norm_scale(inputs)
    first_unit = inputs * first_scale
    first_normed = (first_unit * first_gain).astype(BF)
    query_rot = apply_rotary(
        matmul(first_normed, w_query).reshape(rows, local_heads, HEAD_SIZE), cosine_table, sine_table
    ).astype(BF).reshape(rows, local_heads * HEAD_SIZE)
    key_rot = apply_rotary(
        matmul(first_normed, key_weight).reshape(rows, local_kv, HEAD_SIZE), cosine_table, sine_table
    ).astype(BF).reshape(rows, local_kv * HEAD_SIZE)
    value_low = matmul(first_normed, value_weight).astype(BF)
    both = jnp.concatenate([key_rot, value_low], axis=1)
    both = jnp.concatenate([both, swap(both, "expert", 1)], axis=0)
    keys, values = both[:, : local_kv * HEAD_SIZE], both[:, local_kv * HEAD_SIZE :]

    attended, lse, part = attend(scal, query_rot, keys, values, w_output)
    residual = inputs + lax.psum(part, "tensor").astype(F32)
    second_scale = norm_scale(residual)
    second_unit = residual * second_scale
    second_normed = (second_unit * second_gain).astype(BF)
    normed_all = jnp.concatenate([second_normed, swap(second_normed, "expert", 1)], axis=0)

    away = jnp.stack([1 - core, side]).astype(jnp.int32)
    home = jnp.stack([core, side]).astype(jnp.int32)
    dwg0, dwu0, dwd0, mix, back, gate_grads, turned = experts(
        False, away, normed_all, None, upstream_all, chosen, kept, w_router, w_gate, w_up, w_down, None, None, None
    )
    sent = [swap(item, "dp", 1) for item in (dwd0, dwg0, dwu0)]
    dwg1, dwu1, dwd1, mix, back, route = experts(
        True, home, normed_all, turned, upstream_all, chosen, kept, w_router, w_gate, w_up, w_down, mix, back, gate_grads
    )
    pairs = [
        (mine.astype(F32) + other.astype(F32)).astype(BF) for mine, other in zip((dwd1, dwg1, dwu1), sent)
    ]
    crossed = [swap(item, "dp", 2) for item in pairs]
    sums = [(mine.astype(F32) + other.astype(F32)).astype(BF) for mine, other in zip(pairs, crossed)]
    others = [swap(item, "dp", 1) for item in sums]
    expert_sums = [
        jnp.where(core == 0, jnp.concatenate([mine, other], axis=0), jnp.concatenate([other, mine], axis=0)).astype(F32)
        for mine, other in zip(sums, others)
    ]

    mixed = lax.psum_scatter(mix, "tensor", scatter_dimension=1, tiled=True)
    mixed = mixed[:rows].astype(F32) + swap(mixed[rows:], "expert", 1).astype(F32)
    block_output = (
        lax.dynamic_slice_in_dim(residual, feature_start, width // 4, 1) + mixed
    ).astype(BF)

    own_back = (back[:rows].astype(F32) + swap(back[rows:], "expert", 1).astype(F32)).astype(BF)
    second_grad = lax.psum(own_back, "tensor").astype(F32)
    grad_second = jnp.sum(second_grad * second_unit, axis=0)
    residual_grad = upstream.astype(F32) + norm_back(second_grad, second_unit, second_scale, second_gain)
    residual_low = residual_grad.astype(BF)

    query_grad, dk, dv, grad_output = attend_back(
        scal, query_rot, keys, values, lse, attended, residual_low, w_output, cosines, sines
    )
    dboth = jnp.concatenate([dk, dv], axis=1)
    dboth = dboth[:rows].astype(F32) + swap(dboth[rows:], "expert", 1).astype(F32)
    key_back, value_back = dboth[:, : local_kv * HEAD_SIZE], dboth[:, local_kv * HEAD_SIZE :]
    key_grad = unrotate(
        key_back.reshape(rows, local_kv, HEAD_SIZE), cosine_table, sine_table
    ).astype(BF).reshape(rows, local_kv * HEAD_SIZE)
    value_grad = value_back.astype(BF)
    grad_query = matmul_tn(first_normed, query_grad)
    grad_key = matmul_tn(first_normed, key_grad)
    grad_value = matmul_tn(first_normed, value_grad)
    first_part = (
        matmul_nt(query_grad, w_query) + matmul_nt(key_grad, key_weight) + matmul_nt(value_grad, value_weight)
    )
    first_grad = lax.psum(first_part.astype(BF), "tensor").astype(F32)
    grad_first = jnp.sum(first_grad * first_unit, axis=0)
    grad_input = (residual_grad + norm_back(first_grad, first_unit, first_scale, first_gain)).astype(BF)
    dense = lax.psum((grad_query, grad_key, grad_value, grad_output, grad_first, grad_second), ("dp", "expert"))
    grad_router = lax.psum(route, ("dp", "expert", "tensor")).T
    return (
        block_output, grad_input, dense[4], dense[0], dense[1], dense[2], dense[3], dense[5], grad_router,
        expert_sums[1], expert_sums[2], expert_sums[0],
    )


def solution(mesh):
    fast = mesh.shape["expert"] == 2 and mesh.shape["dp"] == 4 and mesh.shape["tensor"] == 4
    placed = (
        P(("dp", "expert"), None),
        P(),
        P(None, "tensor"),
        P(None, "tensor"),
        P(None, "tensor"),
        P("tensor", None),
        P(),
        P(),
        P("expert", None, "tensor"),
        P("expert", None, "tensor"),
        P("expert", "tensor", None),
        P(("dp", "expert"), None),
        P(("dp", "expert"), None),
        P("dp", None),
        P(("dp", "expert"), None),
    )
    return jax.shard_map(
        fast_device if fast else general_device,
        mesh=mesh,
        in_specs=placed,
        out_specs=(
            P(("dp", "expert"), "tensor"),
            P(("dp", "expert"), None),
            P(),
            P(None, "tensor"),
            P(None, "tensor"),
            P(None, "tensor"),
            P("tensor", None),
            P(),
            P(),
            P("expert", None, "tensor"),
            P("expert", None, "tensor"),
            P("expert", "tensor", None),
        ),
        check_vma=False,
    )
```

```python
import functools
import math

import jax
import jax.numpy as jnp
from jax import lax
from jax.experimental import pallas as pl
from jax.experimental.pallas import tpu as pltpu
from jax.sharding import PartitionSpec as P

HEAD_SIZE = 64
TOPK = 8
PIC = 256


epsilon = 1e-06
rope_base = 10000.0
masked_score = -1e30


def rope_tables(positions):
    steps = jnp.arange(HEAD_SIZE // 2, dtype=jnp.float32)
    inverse = jnp.exp(steps * (-2.0 * math.log(rope_base) / HEAD_SIZE))
    angle = positions.astype(jnp.float32)[:, None] * inverse[None, :]
    return (jnp.cos(angle), jnp.sin(angle))


def apply_rotary(values, cosine_table, sine_table):
    half = values.shape[-1] // 2
    first = values[..., :half]
    second = values[..., half:]
    cosine_table = cosine_table[:, None, :]
    sine_table = sine_table[:, None, :]
    return jnp.concatenate(
        [first * cosine_table - second * sine_table, second * cosine_table + first * sine_table],
        axis=-1,
    )


def unrotate(values, cosine_table, sine_table):
    half = values.shape[-1] // 2
    first = values[..., :half]
    second = values[..., half:]
    cosine_table = cosine_table[:, None, :]
    sine_table = sine_table[:, None, :]
    return jnp.concatenate(
        [first * cosine_table + second * sine_table, second * cosine_table - first * sine_table],
        axis=-1,
    )


def piece_ids(positions, offsets):
    span = 2 * PIC
    window = positions // span
    within = positions - window * span
    count = offsets.shape[0]
    match = window[:, None] == jnp.arange(count, dtype=jnp.int32)[None, :]
    start = jnp.sum(jnp.where(match, offsets[None, :], 0), axis=1)
    inside = (window < count) & (within >= start) & (within < start + PIC)
    return jnp.where(inside, window, -1)


def matmul(left, right):
    return jnp.dot(left, right, preferred_element_type=jnp.float32)


def matmul_nt(left, right):
    return lax.dot_general(
        left, right, (((1,), (1,)), ((), ())), preferred_element_type=jnp.float32
    )


def matmul_tn(left, right):
    return lax.dot_general(
        left, right, (((0,), (0,)), ((), ())), preferred_element_type=jnp.float32
    )


def norm_scale(values):
    return lax.rsqrt(jnp.mean(values * values, axis=-1, keepdims=True) + epsilon)


def norm_back(grad, unit, scale, gain):
    weighted = grad * gain
    return scale * (weighted - unit * jnp.mean(weighted * unit, axis=-1, keepdims=True))


def general_device(
    block_input,
    first_gain,
    w_query,
    key_weight,
    value_weight,
    w_output,
    second_gain,
    w_router,
    w_gate,
    w_up,
    w_down,
    expert_ids,
    slot_index,
    piece_start_offsets,
    upstream,
):
    rows_here = block_input.shape[0]
    width = block_input.shape[1]
    groups = lax.axis_size("expert")
    length = rows_here * groups
    local_heads = w_query.shape[1] // HEAD_SIZE
    local_kv = key_weight.shape[1] // HEAD_SIZE
    sharing = local_heads // local_kv
    head_rows = sharing * rows_here
    experts_all = w_router.shape[1]
    capacity = TOPK * rows_here // experts_all
    slots_all = experts_all * capacity
    score_scale = HEAD_SIZE ** (-0.5)
    positions = lax.axis_index("expert") * rows_here + jnp.arange(rows_here, dtype=jnp.int32)
    cosine_table, sine_table = rope_tables(positions)
    inputs = block_input.astype(jnp.float32)
    first_scale = norm_scale(inputs)
    first_unit = inputs * first_scale
    first_normed = (first_unit * first_gain).astype(jnp.bfloat16)
    query_rot = apply_rotary(
        matmul(first_normed, w_query).reshape(rows_here, local_heads, HEAD_SIZE),
        cosine_table,
        sine_table,
    ).astype(jnp.bfloat16)
    key_rot = (
        apply_rotary(
            matmul(first_normed, key_weight).reshape(rows_here, local_kv, HEAD_SIZE),
            cosine_table,
            sine_table,
        )
        .astype(jnp.bfloat16)
        .reshape(rows_here, local_kv * HEAD_SIZE)
    )
    value_low = matmul(first_normed, value_weight).astype(jnp.bfloat16)
    keys_all, values_all = (
        lax.all_gather(key_rot, "expert", axis=0, tiled=True),
        lax.all_gather(value_low, "expert", axis=0, tiled=True),
    )
    block = min(512, length)
    blocks = length // block

    def by_block(array):
        return array.reshape(blocks, block, local_kv, HEAD_SIZE).transpose(0, 2, 1, 3)

    def by_rows(stacked):
        return stacked.transpose(0, 2, 1, 3).reshape(length, local_kv * HEAD_SIZE)

    def head_major(array):
        return (
            array.reshape(rows_here, local_kv, sharing, HEAD_SIZE)
            .transpose(1, 2, 0, 3)
            .reshape(local_kv, head_rows, HEAD_SIZE)
        )

    def row_major(array):
        return (
            array.reshape(local_kv, sharing, rows_here, HEAD_SIZE)
            .transpose(2, 0, 1, 3)
            .reshape(rows_here, local_heads * HEAD_SIZE)
        )

    key_blocks = by_block(keys_all)
    value_blocks = by_block(values_all)
    block_starts = jnp.arange(blocks, dtype=jnp.int32) * block
    query_heads = head_major(query_rot.reshape(rows_here, local_heads * HEAD_SIZE))
    offsets = piece_start_offsets[0]
    key_pieces = piece_ids(jnp.arange(length, dtype=jnp.int32), offsets)
    query_pieces = jnp.tile(piece_ids(positions, offsets), sharing)
    query_places = jnp.tile(positions, sharing)

    def block_scores(key_block, start):
        places = start + jnp.arange(block, dtype=jnp.int32)
        pieces = lax.dynamic_slice_in_dim(key_pieces, start, block)
        causal = places[None, :] <= query_places[:, None]
        same = (pieces[None, :] == query_pieces[:, None]) & (query_pieces[:, None] >= 0)
        scores = (
            jnp.einsum("hqd,hkd->hqk", query_heads, key_block, preferred_element_type=jnp.float32)
            * score_scale
        )
        return (scores, (causal | same)[None])

    def max_step(carry, operands):
        running_max, running_sum = carry
        key_block, start = operands
        scores, allowed = block_scores(key_block, start)
        scores = jnp.where(allowed, scores, masked_score)
        new_max = jnp.maximum(running_max, jnp.max(scores, axis=-1))
        weights = jnp.where(allowed, jnp.exp(scores - new_max[..., None]), 0.0)
        new_sum = running_sum * jnp.exp(running_max - new_max) + jnp.sum(weights, axis=-1)
        return ((new_max, new_sum), None)

    start_max = jnp.full((local_kv, head_rows), masked_score, jnp.float32)
    start_sum = jnp.zeros((local_kv, head_rows), jnp.float32)
    (row_max, row_sum), _ = lax.scan(max_step, (start_max, start_sum), (key_blocks, block_starts))
    log_total = row_max + jnp.log(row_sum)

    def block_probs(key_block, start):
        scores, allowed = block_scores(key_block, start)
        return jnp.where(allowed, jnp.exp(scores - log_total[..., None]), 0.0)

    def value_step(total, operands):
        key_block, value_block, start = operands
        probs = block_probs(key_block, start).astype(jnp.bfloat16)
        return (
            total
            + jnp.einsum("hqk,hkd->hqd", probs, value_block, preferred_element_type=jnp.float32),
            None,
        )

    mixed_output, _ = lax.scan(
        value_step,
        jnp.zeros((local_kv, head_rows, HEAD_SIZE), jnp.float32),
        (key_blocks, value_blocks, block_starts),
    )
    attended = row_major(mixed_output).astype(jnp.bfloat16)
    attention = lax.psum(matmul(attended, w_output), "tensor")
    residual = inputs + attention
    second_scale = norm_scale(residual)
    second_unit = residual * second_scale
    second_normed = (second_unit * second_gain).astype(jnp.bfloat16)
    logits = matmul(second_normed, w_router)
    chosen = jnp.take_along_axis(logits, expert_ids, axis=1)
    gates = jax.nn.softmax(chosen, axis=-1)
    row_ids = jnp.arange(rows_here, dtype=jnp.int32)
    flat = jnp.where(slot_index >= 0, expert_ids * capacity + slot_index, slots_all)
    selector = (
        jnp.zeros((slots_all, rows_here), jnp.bfloat16)
        .at[flat.reshape(-1), jnp.repeat(row_ids, TOPK)]
        .set(1.0, mode="drop")
    )
    dispatched = (
        matmul(selector, second_normed).astype(jnp.bfloat16).reshape(experts_all, capacity, width)
    )
    expert_rows = lax.all_to_all(dispatched, "expert", split_axis=0, concat_axis=1, tiled=True)
    gate_in = jnp.einsum("ebd,edf->ebf", expert_rows, w_gate, preferred_element_type=jnp.float32)
    up_in = jnp.einsum("ebd,edf->ebf", expert_rows, w_up, preferred_element_type=jnp.float32)
    sigmoid_gate = jax.nn.sigmoid(gate_in)
    silu_gate = gate_in * sigmoid_gate
    hidden = (silu_gate * up_in).astype(jnp.bfloat16)
    partial_out = jnp.einsum("ebf,efd->ebd", hidden, w_down, preferred_element_type=jnp.float32)
    expert_part = lax.psum_scatter(
        partial_out.astype(jnp.bfloat16), "tensor", scatter_dimension=2, tiled=True
    )
    returned = lax.all_to_all(expert_part, "expert", split_axis=1, concat_axis=0, tiled=True)
    quarter = returned.shape[2]
    padded_out = jnp.concatenate(
        [returned.reshape(slots_all, quarter), jnp.zeros((1, quarter), jnp.bfloat16)], axis=0
    )
    feature_start = lax.axis_index("tensor") * quarter
    grad_full = upstream.astype(jnp.float32)
    grad_part = lax.dynamic_slice_in_dim(grad_full, feature_start, quarter, 1)
    mixture = jnp.zeros((rows_here, quarter), jnp.float32)
    gate_terms = []
    for pick in range(TOPK):
        picked = padded_out[flat[:, pick]].astype(jnp.float32)
        mixture = mixture + gates[:, pick : pick + 1] * picked
        gate_terms.append(jnp.sum(grad_part * picked, axis=1))
    gate_part = jnp.stack(gate_terms, axis=1)
    block_output = (lax.dynamic_slice_in_dim(residual, feature_start, quarter, 1) + mixture).astype(
        jnp.bfloat16
    )
    slot_gates = (
        jnp.zeros((slots_all + 1,), jnp.float32)
        .at[flat.reshape(-1)]
        .set(gates.reshape(-1))[:slots_all]
    )
    grad_slots = (
        (matmul(selector, upstream) * slot_gates[:, None])
        .astype(jnp.bfloat16)
        .reshape(experts_all, capacity, width)
    )
    grad_rows_in = lax.all_to_all(grad_slots, "expert", split_axis=0, concat_axis=1, tiled=True)
    hidden_grad = jnp.einsum(
        "ebd,efd->ebf", grad_rows_in, w_down, preferred_element_type=jnp.float32
    )
    grad_down = jnp.einsum("ebf,ebd->efd", hidden, grad_rows_in, preferred_element_type=jnp.float32)
    gate_in_grad = (
        hidden_grad * up_in * (sigmoid_gate * (1.0 + gate_in * (1.0 - sigmoid_gate)))
    ).astype(jnp.bfloat16)
    up_in_grad = (hidden_grad * silu_gate).astype(jnp.bfloat16)
    grad_gate = jnp.einsum(
        "ebd,ebf->edf", expert_rows, gate_in_grad, preferred_element_type=jnp.float32
    )
    grad_up = jnp.einsum(
        "ebd,ebf->edf", expert_rows, up_in_grad, preferred_element_type=jnp.float32
    )
    rows_part = jnp.einsum("ebf,edf->ebd", gate_in_grad, w_gate, preferred_element_type=jnp.float32)
    rows_part = rows_part + jnp.einsum(
        "ebf,edf->ebd", up_in_grad, w_up, preferred_element_type=jnp.float32
    )
    rows_back = lax.all_to_all(
        rows_part.astype(jnp.bfloat16), "expert", split_axis=1, concat_axis=0, tiled=True
    ).astype(rows_part.dtype)
    padded_back = jnp.concatenate(
        [rows_back.reshape(slots_all, width), jnp.zeros((1, width), jnp.float32)], axis=0
    )
    second_part = jnp.zeros((rows_here, width), jnp.float32)
    for pick in range(TOPK):
        second_part = second_part + padded_back[flat[:, pick]]
    second_sum, gate_grads = (
        lax.psum(second_part.astype(jnp.bfloat16), "tensor").astype(jnp.float32),
        lax.psum(gate_part.astype(jnp.bfloat16), "tensor").astype(jnp.float32),
    )
    chosen_grad = gates * (gate_grads - jnp.sum(gates * gate_grads, axis=1, keepdims=True))
    expert_axis = jnp.arange(experts_all, dtype=jnp.int32)
    logit_grad = jnp.zeros((rows_here, experts_all), jnp.float32)
    for pick in range(TOPK):
        logit_grad = logit_grad + jnp.where(
            expert_ids[:, pick : pick + 1] == expert_axis[None, :],
            chosen_grad[:, pick : pick + 1],
            0.0,
        )
    logit_low = logit_grad.astype(jnp.bfloat16)
    grad_router = matmul_tn(second_normed, logit_low)
    second_grad = second_sum + matmul_nt(logit_low, w_router)
    grad_second = jnp.sum(second_grad * second_unit, axis=0)
    residual_grad = grad_full + norm_back(second_grad, second_unit, second_scale, second_gain)
    residual_low = residual_grad.astype(jnp.bfloat16)
    grad_output = matmul_tn(attended, residual_low)
    attended_grad = head_major(matmul_nt(residual_low, w_output).astype(jnp.bfloat16))

    def delta_step(total, operands):
        key_block, value_block, start = operands
        probs = block_probs(key_block, start)
        prob_grad = jnp.einsum(
            "hqd,hkd->hqk", attended_grad, value_block, preferred_element_type=jnp.float32
        )
        return (total + jnp.sum(probs * prob_grad, axis=-1), None)

    delta, _ = lax.scan(
        delta_step,
        jnp.zeros((local_kv, head_rows), jnp.float32),
        (key_blocks, value_blocks, block_starts),
    )

    def grad_step(query_total, operands):
        key_block, value_block, start = operands
        probs = block_probs(key_block, start)
        prob_grad = jnp.einsum(
            "hqd,hkd->hqk", attended_grad, value_block, preferred_element_type=jnp.float32
        )
        score_grad = (probs * (prob_grad - delta[..., None])).astype(jnp.bfloat16)
        query_total = (
            query_total
            + jnp.einsum("hqk,hkd->hqd", score_grad, key_block, preferred_element_type=jnp.float32)
            * score_scale
        )
        key_grad = (
            jnp.einsum("hqk,hqd->hkd", score_grad, query_heads, preferred_element_type=jnp.float32)
            * score_scale
        )
        value_grad = jnp.einsum(
            "hqk,hqd->hkd",
            probs.astype(jnp.bfloat16),
            attended_grad,
            preferred_element_type=jnp.float32,
        )
        return (query_total, (key_grad, value_grad))

    query_total, (key_stack, value_stack) = lax.scan(
        grad_step,
        jnp.zeros((local_kv, head_rows, HEAD_SIZE), jnp.float32),
        (key_blocks, value_blocks, block_starts),
    )
    key_back, value_back = (
        lax.psum_scatter(
            by_rows(key_stack).astype(jnp.bfloat16), "expert", scatter_dimension=0, tiled=True
        ).astype(jnp.float32),
        lax.psum_scatter(
            by_rows(value_stack).astype(jnp.bfloat16), "expert", scatter_dimension=0, tiled=True
        ).astype(jnp.float32),
    )
    query_grad = (
        unrotate(
            row_major(query_total).reshape(rows_here, local_heads, HEAD_SIZE),
            cosine_table,
            sine_table,
        )
        .astype(jnp.bfloat16)
        .reshape(rows_here, local_heads * HEAD_SIZE)
    )
    key_grad = (
        unrotate(key_back.reshape(rows_here, local_kv, HEAD_SIZE), cosine_table, sine_table)
        .astype(jnp.bfloat16)
        .reshape(rows_here, local_kv * HEAD_SIZE)
    )
    value_grad = value_back.astype(jnp.bfloat16)
    grad_query = matmul_tn(first_normed, query_grad)
    grad_key = matmul_tn(first_normed, key_grad)
    grad_value = matmul_tn(first_normed, value_grad)
    first_part = (
        matmul_nt(query_grad, w_query)
        + matmul_nt(key_grad, key_weight)
        + matmul_nt(value_grad, value_weight)
    )
    first_grad = lax.psum(first_part.astype(jnp.bfloat16), "tensor").astype(jnp.float32)
    grad_first = jnp.sum(first_grad * first_unit, axis=0)
    grad_input = (
        residual_grad + norm_back(first_grad, first_unit, first_scale, first_gain)
    ).astype(jnp.bfloat16)
    dense = lax.psum(
        (grad_query, grad_key, grad_value, grad_output, grad_router, grad_first, grad_second),
        ("dp", "expert"),
    )
    expert_sums = (
        lax.psum(grad_gate.astype(jnp.bfloat16), "dp").astype(jnp.float32),
        lax.psum(grad_up.astype(jnp.bfloat16), "dp").astype(jnp.float32),
        lax.psum(grad_down.astype(jnp.bfloat16), "dp").astype(jnp.float32),
    )
    return (
        block_output,
        grad_input,
        dense[5],
        dense[0],
        dense[1],
        dense[2],
        dense[3],
        dense[6],
        dense[4],
        expert_sums[0],
        expert_sums[1],
        expert_sums[2],
    )


BF = jnp.bfloat16
F32 = jnp.float32
MIB = 1 << 20


def vmem_spec():
    return pl.BlockSpec(memory_space=pltpu.VMEM)


def smem_spec():
    return pl.BlockSpec(memory_space=pltpu.SMEM)


def allowed_pairs(scal_ref, rows):
    side = scal_ref[0]
    here = lax.broadcasted_iota(jnp.int32, (rows, 1), 0)
    keys = lax.broadcasted_iota(jnp.int32, (1, 2 * rows), 1)
    query_place = side * rows + here
    key_place = jnp.where(keys < rows, side * rows + keys, (1 - side) * rows + keys - rows)
    span = 2 * PIC

    def piece(places):
        window = places // span
        within = places - window * span
        start = jnp.where(window == 0, scal_ref[1], scal_ref[2])
        inside = (within >= start) & (within < start + PIC)
        return jnp.where(inside, window, -1)

    query_piece = piece(query_place)
    key_piece = piece(key_place)
    return (key_place <= query_place) | ((key_piece == query_piece) & (query_piece >= 0))


def attend_kernel(scal_ref, q_ref, k_ref, v_ref, wo_ref, att_ref, lse_ref, part_ref):
    rows = q_ref.shape[0]
    heads = q_ref.shape[1] // HEAD_SIZE
    sharing = q_ref.shape[1] // k_ref.shape[1]
    allowed = allowed_pairs(scal_ref, rows)
    pieces = []
    for head in range(heads):
        at = head * HEAD_SIZE
        kv = head // sharing * HEAD_SIZE
        query = q_ref[:, at : at + HEAD_SIZE]
        key = k_ref[:, kv : kv + HEAD_SIZE]
        value = v_ref[:, kv : kv + HEAD_SIZE]
        scores = jnp.where(allowed, matmul_nt(query, key) * (HEAD_SIZE**-0.5), masked_score)
        peak = jnp.max(scores, axis=1, keepdims=True)
        weights = jnp.exp(scores - peak)
        total = jnp.sum(weights, axis=1, keepdims=True)
        probs = (weights * (1.0 / total)).astype(BF)
        pieces.append(matmul(probs, value))
        lse_ref[:, head : head + 1] = peak + jnp.log(total)
    attended = jnp.concatenate(pieces, axis=1).astype(BF)
    att_ref[...] = attended
    part_ref[...] = matmul(attended, wo_ref[...]).astype(BF)


def attend(scal, query, key, value, w_output):
    rows, wide = query.shape
    return pl.pallas_call(
        attend_kernel,
        out_shape=(
            jax.ShapeDtypeStruct((rows, wide), BF),
            jax.ShapeDtypeStruct((rows, 128), F32),
            jax.ShapeDtypeStruct((rows, w_output.shape[1]), BF),
        ),
        in_specs=[smem_spec()] + [vmem_spec()] * 4,
        out_specs=(vmem_spec(),) * 3,
        compiler_params=pltpu.CompilerParams(vmem_limit_bytes=48 * MIB),
        name="attend",
    )(scal, query, key, value, w_output)


def turn(values, first):
    wide = values.shape[1]
    half = HEAD_SIZE // 2
    return jnp.where(
        first, -pltpu.roll(values, wide - half, 1), pltpu.roll(values, half, 1)
    )


def attend_back_kernel(
    scal_ref, q_ref, k_ref, v_ref, lse_ref, att_ref, low_ref, wo_ref, cos_ref, sin_ref,
    dq_ref, dk_ref, dv_ref, dwo_ref,
):
    rows, wide = q_ref.shape
    heads = wide // HEAD_SIZE
    sharing = q_ref.shape[1] // k_ref.shape[1]
    scale = HEAD_SIZE**-0.5
    low = low_ref[...]
    dwo_ref[...] = matmul_tn(att_ref[...], low)
    att_grad = matmul_nt(low, wo_ref[...]).astype(BF)
    allowed = allowed_pairs(scal_ref, rows)
    query_parts, key_parts, value_parts = [], [], []
    for head in range(heads):
        at = head * HEAD_SIZE
        kv = head // sharing * HEAD_SIZE
        query = q_ref[:, at : at + HEAD_SIZE]
        key = k_ref[:, kv : kv + HEAD_SIZE]
        value = v_ref[:, kv : kv + HEAD_SIZE]
        grad = att_grad[:, at : at + HEAD_SIZE]
        scores = jnp.where(allowed, matmul_nt(query, key) * scale, masked_score)
        probs = jnp.exp(scores - lse_ref[:, head : head + 1])
        prob_grad = matmul_nt(grad, value)
        delta = jnp.sum(probs * prob_grad, axis=1, keepdims=True)
        score_grad = (probs * (prob_grad - delta)).astype(BF)
        query_parts.append(matmul(score_grad, key) * scale)
        key_part = matmul_tn(score_grad, query) * scale
        value_part = matmul_tn(probs.astype(BF), grad)
        if head % sharing == 0:
            key_parts.append(key_part)
            value_parts.append(value_part)
        else:
            key_parts[-1] = key_parts[-1] + key_part
            value_parts[-1] = value_parts[-1] + value_part
    dk_ref[...] = jnp.concatenate(key_parts, axis=1).astype(BF)
    dv_ref[...] = jnp.concatenate(value_parts, axis=1).astype(BF)
    rotated = jnp.concatenate(query_parts, axis=1)
    lane = lax.broadcasted_iota(jnp.int32, (1, wide), 1)
    first = lane % HEAD_SIZE < HEAD_SIZE // 2
    cosines = jnp.concatenate([cos_ref[...]] * (wide // 128), axis=1)
    sines = jnp.concatenate([sin_ref[...]] * (wide // 128), axis=1)
    dq_ref[...] = (rotated * cosines - turn(rotated, first) * sines).astype(BF)


def attend_back(scal, query, key, value, lse, attended, low, w_output, cosines, sines):
    rows, wide = query.shape
    return pl.pallas_call(
        attend_back_kernel,
        out_shape=(
            jax.ShapeDtypeStruct((rows, wide), BF),
            jax.ShapeDtypeStruct(key.shape, BF),
            jax.ShapeDtypeStruct(value.shape, BF),
            jax.ShapeDtypeStruct(w_output.shape, F32),
        ),
        in_specs=[smem_spec()] + [vmem_spec()] * 9,
        out_specs=(vmem_spec(),) * 4,
        compiler_params=pltpu.CompilerParams(vmem_limit_bytes=56 * MIB),
        name="attend_back",
    )(scal, query, key, value, lse, attended, low, w_output, cosines, sines)


CHUNK = 256
GROUP = 4


def expert_kernel(last, *refs):
    if last:
        (
            scal_ref, n_ref, nt_ref, g_ref, chosen_ref, kept_ref, wr_ref, wg_ref, wu_ref, wd_ref, mix_in, back_in, gg_in,
            dwg_ref, dwu_ref, dwd_ref, mix_ref, back_ref, route_ref,
            gates, kept_gates, gate_grads, mix, back, wgs, wus, ghs, ght, dgs, dus,
        ) = refs
    else:
        (
            scal_ref, n_ref, g_ref, chosen_ref, kept_ref, wr_ref, wg_ref, wu_ref, wd_ref,
            dwg_ref, dwu_ref, dwd_ref, mix_ref, back_ref, gg_ref, nt_ref,
            gates, kept_gates, gate_grads, mix, back, wgs, wus, ghs, ght, dgs, dus,
        ) = refs
    step = pl.program_id(0)
    tokens, width = n_ref.shape
    experts_all = wr_ref.shape[1]
    group, _, hid = wg_ref.shape
    chunks = tokens // CHUNK
    lane = lax.broadcasted_iota(jnp.int32, (1, experts_all), 1)

    @pl.when(step == 0)
    def _():
        def start(at, carry):
            rows = pl.ds(pl.multiple_of(at * CHUNK, CHUNK), CHUNK)
            chosen = chosen_ref[rows, :] > 0.0
            logits = jnp.where(chosen, matmul(n_ref[rows, :], wr_ref[...]), masked_score)
            raised = jnp.exp(logits - jnp.max(logits, axis=1, keepdims=True))
            raised = jnp.where(chosen, raised, 0.0)
            gate = raised / jnp.sum(raised, axis=1, keepdims=True)
            gates[rows, :] = gate
            kept_gates[rows, :] = gate * kept_ref[rows, :]
            if last:
                mix[rows, :] = mix_in[rows, :].astype(F32)
                back[rows, :] = back_in[rows, :].astype(F32)
                gate_grads[rows, :] = gg_in[rows, :]
            else:
                mix[rows, :] = jnp.zeros((CHUNK, width), F32)
                back[rows, :] = jnp.zeros((CHUNK, width), F32)
                gate_grads[rows, :] = jnp.zeros((CHUNK, experts_all), F32)
            return carry

        lax.fori_loop(0, chunks, start, 0)
        if not last:
            for at in range(chunks):
                nt_ref[:, at * CHUNK : (at + 1) * CHUNK] = n_ref[at * CHUNK : (at + 1) * CHUNK, :].T

    for expert in range(group):
        wgs[:, expert * hid : (expert + 1) * hid] = wg_ref[expert]
        wus[:, expert * hid : (expert + 1) * hid] = wu_ref[expert]
    column = scal_ref[1] * (experts_all // 2) + scal_ref[0] * (experts_all // 4) + step * group

    def forward(at, carry):
        rows = pl.ds(pl.multiple_of(at * CHUNK, CHUNK), CHUNK)
        token = n_ref[rows, :]
        down = wd_ref[...].reshape(group * hid, width)
        gate_in = matmul(token, wgs[...])
        up_in = matmul(token, wus[...])
        pulled = matmul_nt(g_ref[rows, :], down)
        sig = 0.5 * jnp.tanh(0.5 * gate_in) + 0.5
        silu = gate_in * sig
        hidden = silu * up_in
        kept = kept_gates[rows, :]
        weights = []
        products = hidden * pulled
        grads = gate_grads[rows, :]
        for expert in range(group):
            here = lane == column + expert
            gate = jnp.sum(jnp.where(here, kept, 0.0), axis=1, keepdims=True)
            weights.append(jnp.broadcast_to(gate, (CHUNK, hid)))
            product = jnp.sum(products[:, expert * hid : (expert + 1) * hid], axis=1, keepdims=True)
            grads = grads + jnp.where(here, product, 0.0)
        gate_grads[rows, :] = grads
        weight = jnp.concatenate(weights, axis=1)
        gated = (hidden * weight).astype(BF)
        pulled = pulled * weight
        up_grad = (pulled * silu).astype(BF)
        gate_grad = (pulled * up_in * (sig + silu * (1.0 - sig))).astype(BF)
        ghs[rows, :] = gated
        dgs[rows, :] = gate_grad
        dus[rows, :] = up_grad
        mix[rows, :] += matmul(gated, down)
        back[rows, :] += matmul_nt(gate_grad, wgs[...]) + matmul_nt(up_grad, wus[...])
        return carry

    lax.fori_loop(0, chunks, forward, 0)
    for at in range(chunks):
        ght[:, at * CHUNK : (at + 1) * CHUNK] = ghs[at * CHUNK : (at + 1) * CHUNK, :].T

    def weights_grad(at, carry):
        rows = pl.ds(pl.multiple_of(at * CHUNK, CHUNK), CHUNK)
        turned = nt_ref[rows, :]
        gate_part = matmul(turned, dgs[...]).astype(BF)
        up_part = matmul(turned, dus[...]).astype(BF)
        for expert in range(group):
            dwg_ref[expert, rows, :] = gate_part[:, expert * hid : (expert + 1) * hid]
            dwu_ref[expert, rows, :] = up_part[:, expert * hid : (expert + 1) * hid]
        return carry

    lax.fori_loop(0, width // CHUNK, weights_grad, 0)
    for at in range(group * hid // CHUNK):
        part = matmul(ght[at * CHUNK : (at + 1) * CHUNK, :], g_ref[...]).astype(BF)
        for inner in range(CHUNK // hid):
            dwd_ref[at * (CHUNK // hid) + inner] = part[inner * hid : (inner + 1) * hid, :]

    @pl.when(step == pl.num_programs(0) - 1)
    def _():
        if last:
            route_ref[...] = jnp.zeros(route_ref.shape, F32)

        def finish(at, carry):
            rows = pl.ds(pl.multiple_of(at * CHUNK, CHUNK), CHUNK)
            mix_ref[rows, :] = mix[rows, :].astype(BF)
            if last:
                grads = gate_grads[rows, :] * kept_gates[rows, :]
                chosen_grad = grads - gates[rows, :] * jnp.sum(grads, axis=1, keepdims=True)
                low = chosen_grad.astype(BF)
                back_ref[rows, :] = (back[rows, :] + matmul_nt(low, wr_ref[...])).astype(BF)
                route_ref[...] += matmul_tn(low, n_ref[rows, :])
            else:
                back_ref[rows, :] = back[rows, :].astype(BF)
                gg_ref[rows, :] = gate_grads[rows, :]
            return carry

        lax.fori_loop(0, chunks, finish, 0)


def experts(last, scal, normed, turned, upstream, chosen, kept, w_router, w_gate, w_up, w_down, mix, back, gate_grads):
    tokens, width = normed.shape
    count, _, hid = w_gate.shape
    half = count // 2
    steps = half // GROUP
    experts_all = w_router.shape[1]
    whole = lambda step, scal: (0, 0)
    full = lambda array: pl.BlockSpec(array.shape, whole)
    picked = lambda step, scal: (scal[0] * steps + step, 0, 0)
    own = lambda step, scal: (step, 0, 0)
    rows_block = pl.BlockSpec((tokens, width), whole)
    narrow_block = pl.BlockSpec((tokens, experts_all), whole)
    args = [normed] + ([turned] if last else []) + [upstream, chosen, kept, w_router]
    specs = [full(array) for array in args]
    args += [w_gate, w_up, w_down]
    specs += [
        pl.BlockSpec((GROUP, width, hid), picked),
        pl.BlockSpec((GROUP, width, hid), picked),
        pl.BlockSpec((GROUP, hid, width), picked),
    ]
    if last:
        args += [mix, back, gate_grads]
        specs += [rows_block, rows_block, narrow_block]
    out_shape = [
        jax.ShapeDtypeStruct((half, width, hid), BF),
        jax.ShapeDtypeStruct((half, width, hid), BF),
        jax.ShapeDtypeStruct((half, hid, width), BF),
        jax.ShapeDtypeStruct((tokens, width), BF),
        jax.ShapeDtypeStruct((tokens, width), BF),
    ]
    out_specs = [
        pl.BlockSpec((GROUP, width, hid), own),
        pl.BlockSpec((GROUP, width, hid), own),
        pl.BlockSpec((GROUP, hid, width), own),
        rows_block,
        rows_block,
    ]
    if last:
        out_shape += [jax.ShapeDtypeStruct((experts_all, width), F32)]
        out_specs += [pl.BlockSpec((experts_all, width), whole)]
    else:
        out_shape += [
            jax.ShapeDtypeStruct((tokens, experts_all), F32),
            jax.ShapeDtypeStruct((width, tokens), BF),
        ]
        out_specs += [narrow_block, pl.BlockSpec((width, tokens), whole)]
    return pl.pallas_call(
        functools.partial(expert_kernel, last),
        out_shape=out_shape,
        grid_spec=pltpu.PrefetchScalarGridSpec(
            num_scalar_prefetch=1,
            grid=(steps,),
            in_specs=specs,
            out_specs=out_specs,
            scratch_shapes=[
                pltpu.VMEM((tokens, experts_all), F32),
                pltpu.VMEM((tokens, experts_all), F32),
                pltpu.VMEM((tokens, experts_all), F32),
                pltpu.VMEM((tokens, width), F32),
                pltpu.VMEM((tokens, width), F32),
                pltpu.VMEM((width, GROUP * hid), BF),
                pltpu.VMEM((width, GROUP * hid), BF),
                pltpu.VMEM((tokens, GROUP * hid), BF),
                pltpu.VMEM((GROUP * hid, tokens), BF),
                pltpu.VMEM((tokens, GROUP * hid), BF),
                pltpu.VMEM((tokens, GROUP * hid), BF),
            ],
        ),
        compiler_params=pltpu.CompilerParams(
            dimension_semantics=("arbitrary",), vmem_limit_bytes=60 * MIB
        ),
        cost_estimate=pl.CostEstimate(
            flops=18 * tokens * width * half * hid,
            bytes_accessed=12 * half * width * hid + 16 * tokens * width,
            transcendentals=tokens * half * hid,
        ),
        name="experts_last" if last else "experts_first",
    )(scal, *args)


MESH = pl.DeviceIdType.MESH
PART = 32


def meet(partners):
    barrier = pltpu.get_barrier_semaphore()
    count = 0
    for here, device in partners:
        here = jnp.asarray(here)

        @pl.when(here)
        def _():
            pl.semaphore_signal(barrier, inc=1, device_id=device, device_id_type=MESH)

        count = count + here.astype(jnp.int32)
    pl.semaphore_wait(barrier, count)


def line_partners():
    place = lax.axis_index("tensor")
    last = lax.axis_size("tensor") - 1
    return [(place > 0, {"tensor": place - 1}), (place < last, {"tensor": place + 1})]


class Line:
    def __init__(self, parts, term, from_left, from_right, to_right, to_left, sems):
        self.place = lax.axis_index("tensor")
        self.last = lax.axis_size("tensor") - 1
        self.parts = parts
        self.term = term
        self.from_left, self.from_right = from_left, from_right
        self.to_right, self.to_left = to_right, to_left
        self.sems = sems

    def copy(self, way, at):
        near = jnp.where(self.place < self.last, self.place + 1, self.place - 1)
        far = jnp.where(self.place > 0, self.place - 1, self.place + 1)
        source, target, device = (
            (self.to_right, self.from_left, near) if way == 0 else (self.to_left, self.from_right, far)
        )
        return pltpu.make_async_remote_copy(
            src_ref=source.at[at],
            dst_ref=target.at[at],
            send_sem=self.sems.at[2 * way, at],
            recv_sem=self.sems.at[2 * way + 1, at],
            device_id={"tensor": device},
            device_id_type=MESH,
        )

    def clear(self):
        @pl.when(self.place == 0)
        def _():
            self.from_left[...] = jnp.zeros(self.from_left.shape, self.from_left.dtype)

        @pl.when(self.place == self.last)
        def _():
            self.from_right[...] = jnp.zeros(self.from_right.shape, self.from_right.dtype)

    def step(self, at):
        for way in range(2):
            part = at - (self.place if way == 0 else self.last - self.place)
            has_source = self.place > 0 if way == 0 else self.place < self.last
            has_target = self.place < self.last if way == 0 else self.place > 0
            arrived = self.from_left if way == 0 else self.from_right
            leaving = self.to_right if way == 0 else self.to_left
            valid = (part >= 0) & (part < self.parts)

            @pl.when(valid & has_source)
            def _():
                self.copy(way, part).wait_recv()

            @pl.when(valid & has_target)
            def _():
                leaving[part] = (self.term(part) + arrived[part].astype(F32)).astype(BF)
                self.copy(way, part).start()

    def total(self, part):
        return self.term(part) + self.from_left[part].astype(F32) + self.from_right[part].astype(F32)

    def drain(self):
        def wait(part, carry):
            @pl.when(self.place < self.last)
            def _():
                self.copy(0, part).wait_send()

            @pl.when(self.place > 0)
            def _():
                self.copy(1, part).wait_send()

            return carry

        lax.fori_loop(0, self.parts, wait, 0)


def line_scratch(parts, width):
    return [pltpu.VMEM((parts, PART, width), BF)] * 4 + [pltpu.SemaphoreType.DMA((4, parts))]


def peer_copy(source, target, sems, at):
    return pltpu.make_async_remote_copy(
        src_ref=source,
        dst_ref=target,
        send_sem=sems.at[0, at],
        recv_sem=sems.at[1, at],
        device_id={"expert": 1 - lax.axis_index("expert")},
        device_id_type=MESH,
    )


def scale_of(values):
    return lax.rsqrt(jnp.mean(values * values, axis=-1, keepdims=True) + epsilon)


def residual_kernel(
    part_ref, x_ref, gain_ref, res_ref, n_ref, from_left, from_right, to_right, to_left, sems, peer_sems
):
    parts = part_ref.shape[0]
    line = Line(parts, lambda at: part_ref[at].astype(F32), from_left, from_right, to_right, to_left, sems)
    line.clear()
    meet(line_partners() + [(True, {"expert": 1 - lax.axis_index("expert")})])

    def body(at, carry):
        line.step(at)
        part = at - line.last

        @pl.when(part >= 0)
        def _():
            residual = x_ref[part].astype(F32) + line.total(part)
            res_ref[part] = residual
            unit = residual * scale_of(residual)
            n_ref[0, part] = (unit * gain_ref[...]).astype(BF)
            peer_copy(n_ref.at[0, part], n_ref.at[1, part], peer_sems, part).start()

        return carry

    lax.fori_loop(0, parts + line.last, body, 0)
    line.drain()

    def wait(part, carry):
        peer_copy(n_ref.at[0, part], n_ref.at[1, part], peer_sems, part).wait()
        return carry

    lax.fori_loop(0, parts, wait, 0)


def residual_norm(part, block_input, gain):
    rows, width = block_input.shape
    parts = rows // PART
    residual, normed = pl.pallas_call(
        residual_kernel,
        out_shape=(
            jax.ShapeDtypeStruct((parts, PART, width), F32),
            jax.ShapeDtypeStruct((2, parts, PART, width), BF),
        ),
        in_specs=[vmem_spec()] * 3,
        out_specs=(vmem_spec(),) * 2,
        scratch_shapes=line_scratch(parts, width) + [pltpu.SemaphoreType.DMA((2, parts))],
        compiler_params=pltpu.CompilerParams(
            collective_id=0, has_side_effects=True, vmem_limit_bytes=40 * MIB
        ),
        name="residual_norm",
    )(part.reshape(parts, PART, width), block_input.reshape(parts, PART, width), gain[None])
    return residual, normed.reshape(2 * rows, width)


def residual_grad_kernel(
    back_ref, route_ref, res_ref, up_ref, gain_ref, grad_ref, low_ref, second_ref, route_out,
    from_left, from_right, to_right, to_left, sems, peer_sems, arrived, terms,
):
    parts = back_ref.shape[1]
    line = Line(parts + 1, lambda at: terms[at], from_left, from_right, to_right, to_left, sems)
    line.clear()
    meet(line_partners() + [(True, {"expert": 1 - lax.axis_index("expert")})])

    def send(part, carry):
        peer_copy(back_ref.at[1, part], arrived.at[part], peer_sems, part).start()
        return carry

    lax.fori_loop(0, parts, send, 0)
    terms[parts] = route_ref[...]
    second_ref[...] = jnp.zeros(second_ref.shape, F32)

    def body(at, carry):
        @pl.when(at < parts)
        def _():
            peer_copy(back_ref.at[1, at], arrived.at[at], peer_sems, at).wait_recv()
            terms[at] = back_ref[0, at].astype(F32) + arrived[at].astype(F32)

        line.step(at)
        part = at - line.last

        @pl.when((part >= 0) & (part < parts))
        def _():
            grad = line.total(part)
            residual = res_ref[part]
            scale = scale_of(residual)
            unit = residual * scale
            second_ref[...] += jnp.sum(grad * unit, axis=0, keepdims=True)
            result = up_ref[part].astype(F32) + norm_back(grad, unit, scale, gain_ref[...])
            grad_ref[part] = result
            low_ref[part] = result.astype(BF)

        return carry

    lax.fori_loop(0, parts + 1 + line.last, body, 0)
    route_out[...] = line.total(parts)
    line.drain()

    def wait(part, carry):
        peer_copy(back_ref.at[1, part], arrived.at[part], peer_sems, part).wait_send()
        return carry

    lax.fori_loop(0, parts, wait, 0)


def residual_gradient(back, route, residual, upstream, gain):
    rows, width = upstream.shape
    parts = rows // PART
    grad, low, second, route = pl.pallas_call(
        residual_grad_kernel,
        out_shape=(
            jax.ShapeDtypeStruct((parts, PART, width), F32),
            jax.ShapeDtypeStruct((parts, PART, width), BF),
            jax.ShapeDtypeStruct((1, width), F32),
            jax.ShapeDtypeStruct(route.shape, F32),
        ),
        in_specs=[vmem_spec()] * 5,
        out_specs=(vmem_spec(),) * 4,
        scratch_shapes=line_scratch(parts + 1, width)
        + [
            pltpu.SemaphoreType.DMA((2, parts)),
            pltpu.VMEM((parts, PART, width), BF),
            pltpu.VMEM((parts + 1, PART, width), F32),
        ],
        compiler_params=pltpu.CompilerParams(
            collective_id=1, has_side_effects=True, vmem_limit_bytes=48 * MIB
        ),
        name="residual_grad",
    )(
        back.reshape(2, parts, PART, width), route, residual, upstream.reshape(parts, PART, width), gain[None]
    )
    return grad, low.reshape(rows, width), second[0], route


def input_grad_kernel(
    part_ref, x_ref, res_grad_ref, gain_ref, grad_ref, first_ref, from_left, from_right, to_right, to_left, sems
):
    parts = part_ref.shape[0]
    line = Line(parts, lambda at: part_ref[at], from_left, from_right, to_right, to_left, sems)
    line.clear()
    meet(line_partners())
    first_ref[...] = jnp.zeros(first_ref.shape, F32)

    def body(at, carry):
        line.step(at)
        part = at - line.last

        @pl.when(part >= 0)
        def _():
            grad = line.total(part)
            values = x_ref[part].astype(F32)
            scale = scale_of(values)
            unit = values * scale
            first_ref[...] += jnp.sum(grad * unit, axis=0, keepdims=True)
            grad_ref[part] = (res_grad_ref[part] + norm_back(grad, unit, scale, gain_ref[...])).astype(BF)

        return carry

    lax.fori_loop(0, parts + line.last, body, 0)
    line.drain()


def input_gradient(first_part, block_input, residual_grad, gain):
    rows, width = block_input.shape
    parts = rows // PART
    grad, first = pl.pallas_call(
        input_grad_kernel,
        out_shape=(
            jax.ShapeDtypeStruct((parts, PART, width), BF),
            jax.ShapeDtypeStruct((1, width), F32),
        ),
        in_specs=[vmem_spec()] * 4,
        out_specs=(vmem_spec(),) * 2,
        scratch_shapes=line_scratch(parts, width),
        compiler_params=pltpu.CompilerParams(
            collective_id=2, has_side_effects=True, vmem_limit_bytes=40 * MIB
        ),
        name="input_grad",
    )(first_part.reshape(parts, PART, width), block_input.reshape(parts, PART, width), residual_grad, gain[None])
    return grad.reshape(rows, width), first[0]


def swap(array, axis, bit):
    size = lax.axis_size(axis)
    return lax.ppermute(array, axis, [(at, at ^ bit) for at in range(size)])


def fast_device(
    block_input, first_gain, w_query, key_weight, value_weight, w_output, second_gain, w_router,
    w_gate, w_up, w_down, expert_ids, slot_index, piece_start_offsets, upstream,
):
    rows, width = block_input.shape
    local_heads = w_query.shape[1] // HEAD_SIZE
    local_kv = key_weight.shape[1] // HEAD_SIZE
    experts_all = w_router.shape[1]
    side = lax.axis_index("expert")
    core = lax.axis_index("dp") % 2
    feature_start = lax.axis_index("tensor") * (width // 4)
    scal = jnp.concatenate([side[None].astype(jnp.int32), piece_start_offsets[0]])

    axis_row = jnp.arange(experts_all, dtype=jnp.int32)[None, None, :]
    hits = (expert_ids[:, :, None] == axis_row)
    chosen = jnp.sum(hits.astype(F32), axis=1)
    kept = jnp.sum((hits & (slot_index >= 0)[:, :, None]).astype(F32), axis=1)
    marks = jnp.concatenate([chosen, kept], axis=1).astype(BF)
    marks = jnp.concatenate([marks, swap(marks, "expert", 1)], axis=0).astype(F32)
    chosen, kept = marks[:, :experts_all], marks[:, experts_all:]
    upstream_all = jnp.concatenate([upstream, swap(upstream, "expert", 1)], axis=0)

    positions = side * rows + jnp.arange(rows, dtype=jnp.int32)
    cosine_table, sine_table = rope_tables(positions)
    cosines = jnp.tile(cosine_table, (1, 4))
    sines = jnp.tile(sine_table, (1, 4))
    inputs = block_input.astype(F32)
    first_scale = norm_scale(inputs)
    first_unit = inputs * first_scale
    first_normed = (first_unit * first_gain).astype(BF)
    query_rot = apply_rotary(
        matmul(first_normed, w_query).reshape(rows, local_heads, HEAD_SIZE), cosine_table, sine_table
    ).astype(BF).reshape(rows, local_heads * HEAD_SIZE)
    key_rot = apply_rotary(
        matmul(first_normed, key_weight).reshape(rows, local_kv, HEAD_SIZE), cosine_table, sine_table
    ).astype(BF).reshape(rows, local_kv * HEAD_SIZE)
    value_low = matmul(first_normed, value_weight).astype(BF)
    both = jnp.concatenate([key_rot, value_low], axis=1)
    both = jnp.concatenate([both, swap(both, "expert", 1)], axis=0)
    keys, values = both[:, : local_kv * HEAD_SIZE], both[:, local_kv * HEAD_SIZE :]

    attended, lse, part = attend(scal, query_rot, keys, values, w_output)
    residual, normed_all = residual_norm(part, block_input, second_gain)

    away = jnp.stack([1 - core, side]).astype(jnp.int32)
    home = jnp.stack([core, side]).astype(jnp.int32)
    dwg0, dwu0, dwd0, mix, back, gate_grads, turned = experts(
        False, away, normed_all, None, upstream_all, chosen, kept, w_router, w_gate, w_up, w_down, None, None, None
    )
    sent = [swap(item, "dp", 1) for item in (dwd0, dwg0, dwu0)]
    dwg1, dwu1, dwd1, mix, back, route = experts(
        True, home, normed_all, turned, upstream_all, chosen, kept, w_router, w_gate, w_up, w_down, mix, back, gate_grads
    )
    pairs = [
        (mine.astype(F32) + other.astype(F32)).astype(BF) for mine, other in zip((dwd1, dwg1, dwu1), sent)
    ]
    crossed = [swap(item, "dp", 2) for item in pairs]
    sums = [(mine.astype(F32) + other.astype(F32)).astype(BF) for mine, other in zip(pairs, crossed)]
    others = [swap(item, "dp", 1) for item in sums]
    expert_sums = [
        jnp.where(core == 0, jnp.concatenate([mine, other], axis=0), jnp.concatenate([other, mine], axis=0)).astype(F32)
        for mine, other in zip(sums, others)
    ]

    mixed = lax.psum_scatter(mix, "tensor", scatter_dimension=1, tiled=True)
    mixed = mixed[:rows].astype(F32) + swap(mixed[rows:], "expert", 1).astype(F32)
    block_output = (
        lax.dynamic_slice_in_dim(residual.reshape(rows, width), feature_start, width // 4, 1) + mixed
    ).astype(BF)

    residual_grad, residual_low, grad_second, route = residual_gradient(back, route, residual, upstream, second_gain)

    query_grad, dk, dv, grad_output = attend_back(
        scal, query_rot, keys, values, lse, attended, residual_low, w_output, cosines, sines
    )
    dboth = jnp.concatenate([dk, dv], axis=1)
    dboth = dboth[:rows].astype(F32) + swap(dboth[rows:], "expert", 1).astype(F32)
    key_back, value_back = dboth[:, : local_kv * HEAD_SIZE], dboth[:, local_kv * HEAD_SIZE :]
    key_grad = unrotate(
        key_back.reshape(rows, local_kv, HEAD_SIZE), cosine_table, sine_table
    ).astype(BF).reshape(rows, local_kv * HEAD_SIZE)
    value_grad = value_back.astype(BF)
    grad_query = matmul_tn(first_normed, query_grad)
    grad_key = matmul_tn(first_normed, key_grad)
    grad_value = matmul_tn(first_normed, value_grad)
    first_part = (
        matmul_nt(query_grad, w_query) + matmul_nt(key_grad, key_weight) + matmul_nt(value_grad, value_weight)
    )
    grad_input, grad_first = input_gradient(first_part, block_input, residual_grad, first_gain)
    early = lax.psum((grad_output.astype(BF), route.astype(BF), grad_second.astype(BF)), ("dp", "expert"))
    late = lax.psum(
        (grad_query.astype(BF), grad_key.astype(BF), grad_value.astype(BF), grad_first.astype(BF)), ("dp", "expert")
    )
    early = [item.astype(F32) for item in early]
    late = [item.astype(F32) for item in late]
    return (
        block_output, grad_input, late[3], late[0], late[1], late[2], early[0], early[2], early[1].T,
        expert_sums[1], expert_sums[2], expert_sums[0],
    )


def solution(mesh):
    fast = mesh.shape["expert"] == 2 and mesh.shape["dp"] == 4 and mesh.shape["tensor"] == 4
    placed = (
        P(("dp", "expert"), None),
        P(),
        P(None, "tensor"),
        P(None, "tensor"),
        P(None, "tensor"),
        P("tensor", None),
        P(),
        P(),
        P("expert", None, "tensor"),
        P("expert", None, "tensor"),
        P("expert", "tensor", None),
        P(("dp", "expert"), None),
        P(("dp", "expert"), None),
        P("dp", None),
        P(("dp", "expert"), None),
    )
    return jax.shard_map(
        fast_device if fast else general_device,
        mesh=mesh,
        in_specs=placed,
        out_specs=(
            P(("dp", "expert"), "tensor"),
            P(("dp", "expert"), None),
            P(),
            P(None, "tensor"),
            P(None, "tensor"),
            P(None, "tensor"),
            P("tensor", None),
            P(),
            P(),
            P("expert", None, "tensor"),
            P("expert", None, "tensor"),
            P("expert", "tensor", None),
        ),
        check_vma=False,
    )
```

```python
import functools
import math

import jax
import jax.numpy as jnp
from jax import lax
from jax.experimental import pallas as pl
from jax.experimental.pallas import tpu as pltpu
from jax.sharding import PartitionSpec as P

HEAD_SIZE = 64
TOPK = 8
PIC = 256


epsilon = 1e-06
rope_base = 10000.0
masked_score = -1e30


def rope_tables(positions):
    steps = jnp.arange(HEAD_SIZE // 2, dtype=jnp.float32)
    inverse = jnp.exp(steps * (-2.0 * math.log(rope_base) / HEAD_SIZE))
    angle = positions.astype(jnp.float32)[:, None] * inverse[None, :]
    return (jnp.cos(angle), jnp.sin(angle))


def apply_rotary(values, cosine_table, sine_table):
    half = values.shape[-1] // 2
    first = values[..., :half]
    second = values[..., half:]
    cosine_table = cosine_table[:, None, :]
    sine_table = sine_table[:, None, :]
    return jnp.concatenate(
        [first * cosine_table - second * sine_table, second * cosine_table + first * sine_table],
        axis=-1,
    )


def unrotate(values, cosine_table, sine_table):
    half = values.shape[-1] // 2
    first = values[..., :half]
    second = values[..., half:]
    cosine_table = cosine_table[:, None, :]
    sine_table = sine_table[:, None, :]
    return jnp.concatenate(
        [first * cosine_table + second * sine_table, second * cosine_table - first * sine_table],
        axis=-1,
    )


def piece_ids(positions, offsets):
    span = 2 * PIC
    window = positions // span
    within = positions - window * span
    count = offsets.shape[0]
    match = window[:, None] == jnp.arange(count, dtype=jnp.int32)[None, :]
    start = jnp.sum(jnp.where(match, offsets[None, :], 0), axis=1)
    inside = (window < count) & (within >= start) & (within < start + PIC)
    return jnp.where(inside, window, -1)


def matmul(left, right):
    return jnp.dot(left, right, preferred_element_type=jnp.float32)


def matmul_nt(left, right):
    return lax.dot_general(
        left, right, (((1,), (1,)), ((), ())), preferred_element_type=jnp.float32
    )


def matmul_tn(left, right):
    return lax.dot_general(
        left, right, (((0,), (0,)), ((), ())), preferred_element_type=jnp.float32
    )


def norm_scale(values):
    return lax.rsqrt(jnp.mean(values * values, axis=-1, keepdims=True) + epsilon)


def norm_back(grad, unit, scale, gain):
    weighted = grad * gain
    return scale * (weighted - unit * jnp.mean(weighted * unit, axis=-1, keepdims=True))


def general_device(
    block_input,
    first_gain,
    w_query,
    key_weight,
    value_weight,
    w_output,
    second_gain,
    w_router,
    w_gate,
    w_up,
    w_down,
    expert_ids,
    slot_index,
    piece_start_offsets,
    upstream,
):
    rows_here = block_input.shape[0]
    width = block_input.shape[1]
    groups = lax.axis_size("expert")
    length = rows_here * groups
    local_heads = w_query.shape[1] // HEAD_SIZE
    local_kv = key_weight.shape[1] // HEAD_SIZE
    sharing = local_heads // local_kv
    head_rows = sharing * rows_here
    experts_all = w_router.shape[1]
    capacity = TOPK * rows_here // experts_all
    slots_all = experts_all * capacity
    score_scale = HEAD_SIZE ** (-0.5)
    positions = lax.axis_index("expert") * rows_here + jnp.arange(rows_here, dtype=jnp.int32)
    cosine_table, sine_table = rope_tables(positions)
    inputs = block_input.astype(jnp.float32)
    first_scale = norm_scale(inputs)
    first_unit = inputs * first_scale
    first_normed = (first_unit * first_gain).astype(jnp.bfloat16)
    query_rot = apply_rotary(
        matmul(first_normed, w_query).reshape(rows_here, local_heads, HEAD_SIZE),
        cosine_table,
        sine_table,
    ).astype(jnp.bfloat16)
    key_rot = (
        apply_rotary(
            matmul(first_normed, key_weight).reshape(rows_here, local_kv, HEAD_SIZE),
            cosine_table,
            sine_table,
        )
        .astype(jnp.bfloat16)
        .reshape(rows_here, local_kv * HEAD_SIZE)
    )
    value_low = matmul(first_normed, value_weight).astype(jnp.bfloat16)
    keys_all, values_all = (
        lax.all_gather(key_rot, "expert", axis=0, tiled=True),
        lax.all_gather(value_low, "expert", axis=0, tiled=True),
    )
    block = min(512, length)
    blocks = length // block

    def by_block(array):
        return array.reshape(blocks, block, local_kv, HEAD_SIZE).transpose(0, 2, 1, 3)

    def by_rows(stacked):
        return stacked.transpose(0, 2, 1, 3).reshape(length, local_kv * HEAD_SIZE)

    def head_major(array):
        return (
            array.reshape(rows_here, local_kv, sharing, HEAD_SIZE)
            .transpose(1, 2, 0, 3)
            .reshape(local_kv, head_rows, HEAD_SIZE)
        )

    def row_major(array):
        return (
            array.reshape(local_kv, sharing, rows_here, HEAD_SIZE)
            .transpose(2, 0, 1, 3)
            .reshape(rows_here, local_heads * HEAD_SIZE)
        )

    key_blocks = by_block(keys_all)
    value_blocks = by_block(values_all)
    block_starts = jnp.arange(blocks, dtype=jnp.int32) * block
    query_heads = head_major(query_rot.reshape(rows_here, local_heads * HEAD_SIZE))
    offsets = piece_start_offsets[0]
    key_pieces = piece_ids(jnp.arange(length, dtype=jnp.int32), offsets)
    query_pieces = jnp.tile(piece_ids(positions, offsets), sharing)
    query_places = jnp.tile(positions, sharing)

    def block_scores(key_block, start):
        places = start + jnp.arange(block, dtype=jnp.int32)
        pieces = lax.dynamic_slice_in_dim(key_pieces, start, block)
        causal = places[None, :] <= query_places[:, None]
        same = (pieces[None, :] == query_pieces[:, None]) & (query_pieces[:, None] >= 0)
        scores = (
            jnp.einsum("hqd,hkd->hqk", query_heads, key_block, preferred_element_type=jnp.float32)
            * score_scale
        )
        return (scores, (causal | same)[None])

    def max_step(carry, operands):
        running_max, running_sum = carry
        key_block, start = operands
        scores, allowed = block_scores(key_block, start)
        scores = jnp.where(allowed, scores, masked_score)
        new_max = jnp.maximum(running_max, jnp.max(scores, axis=-1))
        weights = jnp.where(allowed, jnp.exp(scores - new_max[..., None]), 0.0)
        new_sum = running_sum * jnp.exp(running_max - new_max) + jnp.sum(weights, axis=-1)
        return ((new_max, new_sum), None)

    start_max = jnp.full((local_kv, head_rows), masked_score, jnp.float32)
    start_sum = jnp.zeros((local_kv, head_rows), jnp.float32)
    (row_max, row_sum), _ = lax.scan(max_step, (start_max, start_sum), (key_blocks, block_starts))
    log_total = row_max + jnp.log(row_sum)

    def block_probs(key_block, start):
        scores, allowed = block_scores(key_block, start)
        return jnp.where(allowed, jnp.exp(scores - log_total[..., None]), 0.0)

    def value_step(total, operands):
        key_block, value_block, start = operands
        probs = block_probs(key_block, start).astype(jnp.bfloat16)
        return (
            total
            + jnp.einsum("hqk,hkd->hqd", probs, value_block, preferred_element_type=jnp.float32),
            None,
        )

    mixed_output, _ = lax.scan(
        value_step,
        jnp.zeros((local_kv, head_rows, HEAD_SIZE), jnp.float32),
        (key_blocks, value_blocks, block_starts),
    )
    attended = row_major(mixed_output).astype(jnp.bfloat16)
    attention = lax.psum(matmul(attended, w_output), "tensor")
    residual = inputs + attention
    second_scale = norm_scale(residual)
    second_unit = residual * second_scale
    second_normed = (second_unit * second_gain).astype(jnp.bfloat16)
    logits = matmul(second_normed, w_router)
    chosen = jnp.take_along_axis(logits, expert_ids, axis=1)
    gates = jax.nn.softmax(chosen, axis=-1)
    row_ids = jnp.arange(rows_here, dtype=jnp.int32)
    flat = jnp.where(slot_index >= 0, expert_ids * capacity + slot_index, slots_all)
    selector = (
        jnp.zeros((slots_all, rows_here), jnp.bfloat16)
        .at[flat.reshape(-1), jnp.repeat(row_ids, TOPK)]
        .set(1.0, mode="drop")
    )
    dispatched = (
        matmul(selector, second_normed).astype(jnp.bfloat16).reshape(experts_all, capacity, width)
    )
    expert_rows = lax.all_to_all(dispatched, "expert", split_axis=0, concat_axis=1, tiled=True)
    gate_in = jnp.einsum("ebd,edf->ebf", expert_rows, w_gate, preferred_element_type=jnp.float32)
    up_in = jnp.einsum("ebd,edf->ebf", expert_rows, w_up, preferred_element_type=jnp.float32)
    sigmoid_gate = jax.nn.sigmoid(gate_in)
    silu_gate = gate_in * sigmoid_gate
    hidden = (silu_gate * up_in).astype(jnp.bfloat16)
    partial_out = jnp.einsum("ebf,efd->ebd", hidden, w_down, preferred_element_type=jnp.float32)
    expert_part = lax.psum_scatter(
        partial_out.astype(jnp.bfloat16), "tensor", scatter_dimension=2, tiled=True
    )
    returned = lax.all_to_all(expert_part, "expert", split_axis=1, concat_axis=0, tiled=True)
    quarter = returned.shape[2]
    padded_out = jnp.concatenate(
        [returned.reshape(slots_all, quarter), jnp.zeros((1, quarter), jnp.bfloat16)], axis=0
    )
    feature_start = lax.axis_index("tensor") * quarter
    grad_full = upstream.astype(jnp.float32)
    grad_part = lax.dynamic_slice_in_dim(grad_full, feature_start, quarter, 1)
    mixture = jnp.zeros((rows_here, quarter), jnp.float32)
    gate_terms = []
    for pick in range(TOPK):
        picked = padded_out[flat[:, pick]].astype(jnp.float32)
        mixture = mixture + gates[:, pick : pick + 1] * picked
        gate_terms.append(jnp.sum(grad_part * picked, axis=1))
    gate_part = jnp.stack(gate_terms, axis=1)
    block_output = (lax.dynamic_slice_in_dim(residual, feature_start, quarter, 1) + mixture).astype(
        jnp.bfloat16
    )
    slot_gates = (
        jnp.zeros((slots_all + 1,), jnp.float32)
        .at[flat.reshape(-1)]
        .set(gates.reshape(-1))[:slots_all]
    )
    grad_slots = (
        (matmul(selector, upstream) * slot_gates[:, None])
        .astype(jnp.bfloat16)
        .reshape(experts_all, capacity, width)
    )
    grad_rows_in = lax.all_to_all(grad_slots, "expert", split_axis=0, concat_axis=1, tiled=True)
    hidden_grad = jnp.einsum(
        "ebd,efd->ebf", grad_rows_in, w_down, preferred_element_type=jnp.float32
    )
    grad_down = jnp.einsum("ebf,ebd->efd", hidden, grad_rows_in, preferred_element_type=jnp.float32)
    gate_in_grad = (
        hidden_grad * up_in * (sigmoid_gate * (1.0 + gate_in * (1.0 - sigmoid_gate)))
    ).astype(jnp.bfloat16)
    up_in_grad = (hidden_grad * silu_gate).astype(jnp.bfloat16)
    grad_gate = jnp.einsum(
        "ebd,ebf->edf", expert_rows, gate_in_grad, preferred_element_type=jnp.float32
    )
    grad_up = jnp.einsum(
        "ebd,ebf->edf", expert_rows, up_in_grad, preferred_element_type=jnp.float32
    )
    rows_part = jnp.einsum("ebf,edf->ebd", gate_in_grad, w_gate, preferred_element_type=jnp.float32)
    rows_part = rows_part + jnp.einsum(
        "ebf,edf->ebd", up_in_grad, w_up, preferred_element_type=jnp.float32
    )
    rows_back = lax.all_to_all(
        rows_part.astype(jnp.bfloat16), "expert", split_axis=1, concat_axis=0, tiled=True
    ).astype(rows_part.dtype)
    padded_back = jnp.concatenate(
        [rows_back.reshape(slots_all, width), jnp.zeros((1, width), jnp.float32)], axis=0
    )
    second_part = jnp.zeros((rows_here, width), jnp.float32)
    for pick in range(TOPK):
        second_part = second_part + padded_back[flat[:, pick]]
    second_sum, gate_grads = (
        lax.psum(second_part.astype(jnp.bfloat16), "tensor").astype(jnp.float32),
        lax.psum(gate_part.astype(jnp.bfloat16), "tensor").astype(jnp.float32),
    )
    chosen_grad = gates * (gate_grads - jnp.sum(gates * gate_grads, axis=1, keepdims=True))
    expert_axis = jnp.arange(experts_all, dtype=jnp.int32)
    logit_grad = jnp.zeros((rows_here, experts_all), jnp.float32)
    for pick in range(TOPK):
        logit_grad = logit_grad + jnp.where(
            expert_ids[:, pick : pick + 1] == expert_axis[None, :],
            chosen_grad[:, pick : pick + 1],
            0.0,
        )
    logit_low = logit_grad.astype(jnp.bfloat16)
    grad_router = matmul_tn(second_normed, logit_low)
    second_grad = second_sum + matmul_nt(logit_low, w_router)
    grad_second = jnp.sum(second_grad * second_unit, axis=0)
    residual_grad = grad_full + norm_back(second_grad, second_unit, second_scale, second_gain)
    residual_low = residual_grad.astype(jnp.bfloat16)
    grad_output = matmul_tn(attended, residual_low)
    attended_grad = head_major(matmul_nt(residual_low, w_output).astype(jnp.bfloat16))

    def delta_step(total, operands):
        key_block, value_block, start = operands
        probs = block_probs(key_block, start)
        prob_grad = jnp.einsum(
            "hqd,hkd->hqk", attended_grad, value_block, preferred_element_type=jnp.float32
        )
        return (total + jnp.sum(probs * prob_grad, axis=-1), None)

    delta, _ = lax.scan(
        delta_step,
        jnp.zeros((local_kv, head_rows), jnp.float32),
        (key_blocks, value_blocks, block_starts),
    )

    def grad_step(query_total, operands):
        key_block, value_block, start = operands
        probs = block_probs(key_block, start)
        prob_grad = jnp.einsum(
            "hqd,hkd->hqk", attended_grad, value_block, preferred_element_type=jnp.float32
        )
        score_grad = (probs * (prob_grad - delta[..., None])).astype(jnp.bfloat16)
        query_total = (
            query_total
            + jnp.einsum("hqk,hkd->hqd", score_grad, key_block, preferred_element_type=jnp.float32)
            * score_scale
        )
        key_grad = (
            jnp.einsum("hqk,hqd->hkd", score_grad, query_heads, preferred_element_type=jnp.float32)
            * score_scale
        )
        value_grad = jnp.einsum(
            "hqk,hqd->hkd",
            probs.astype(jnp.bfloat16),
            attended_grad,
            preferred_element_type=jnp.float32,
        )
        return (query_total, (key_grad, value_grad))

    query_total, (key_stack, value_stack) = lax.scan(
        grad_step,
        jnp.zeros((local_kv, head_rows, HEAD_SIZE), jnp.float32),
        (key_blocks, value_blocks, block_starts),
    )
    key_back, value_back = (
        lax.psum_scatter(
            by_rows(key_stack).astype(jnp.bfloat16), "expert", scatter_dimension=0, tiled=True
        ).astype(jnp.float32),
        lax.psum_scatter(
            by_rows(value_stack).astype(jnp.bfloat16), "expert", scatter_dimension=0, tiled=True
        ).astype(jnp.float32),
    )
    query_grad = (
        unrotate(
            row_major(query_total).reshape(rows_here, local_heads, HEAD_SIZE),
            cosine_table,
            sine_table,
        )
        .astype(jnp.bfloat16)
        .reshape(rows_here, local_heads * HEAD_SIZE)
    )
    key_grad = (
        unrotate(key_back.reshape(rows_here, local_kv, HEAD_SIZE), cosine_table, sine_table)
        .astype(jnp.bfloat16)
        .reshape(rows_here, local_kv * HEAD_SIZE)
    )
    value_grad = value_back.astype(jnp.bfloat16)
    grad_query = matmul_tn(first_normed, query_grad)
    grad_key = matmul_tn(first_normed, key_grad)
    grad_value = matmul_tn(first_normed, value_grad)
    first_part = (
        matmul_nt(query_grad, w_query)
        + matmul_nt(key_grad, key_weight)
        + matmul_nt(value_grad, value_weight)
    )
    first_grad = lax.psum(first_part.astype(jnp.bfloat16), "tensor").astype(jnp.float32)
    grad_first = jnp.sum(first_grad * first_unit, axis=0)
    grad_input = (
        residual_grad + norm_back(first_grad, first_unit, first_scale, first_gain)
    ).astype(jnp.bfloat16)
    dense = lax.psum(
        (grad_query, grad_key, grad_value, grad_output, grad_router, grad_first, grad_second),
        ("dp", "expert"),
    )
    expert_sums = (
        lax.psum(grad_gate.astype(jnp.bfloat16), "dp").astype(jnp.float32),
        lax.psum(grad_up.astype(jnp.bfloat16), "dp").astype(jnp.float32),
        lax.psum(grad_down.astype(jnp.bfloat16), "dp").astype(jnp.float32),
    )
    return (
        block_output,
        grad_input,
        dense[5],
        dense[0],
        dense[1],
        dense[2],
        dense[3],
        dense[6],
        dense[4],
        expert_sums[0],
        expert_sums[1],
        expert_sums[2],
    )


BF = jnp.bfloat16
F32 = jnp.float32
MIB = 1 << 20


def vmem_spec():
    return pl.BlockSpec(memory_space=pltpu.VMEM)


def smem_spec():
    return pl.BlockSpec(memory_space=pltpu.SMEM)


def allowed_pairs(scal_ref, rows):
    side = scal_ref[0]
    here = lax.broadcasted_iota(jnp.int32, (rows, 1), 0)
    keys = lax.broadcasted_iota(jnp.int32, (1, 2 * rows), 1)
    query_place = side * rows + here
    key_place = jnp.where(keys < rows, side * rows + keys, (1 - side) * rows + keys - rows)
    span = 2 * PIC

    def piece(places):
        window = places // span
        within = places - window * span
        start = jnp.where(window == 0, scal_ref[1], scal_ref[2])
        inside = (within >= start) & (within < start + PIC)
        return jnp.where(inside, window, -1)

    query_piece = piece(query_place)
    key_piece = piece(key_place)
    return (key_place <= query_place) | ((key_piece == query_piece) & (query_piece >= 0))


def attend_kernel(scal_ref, q_ref, k_ref, v_ref, wo_ref, att_ref, lse_ref, part_ref):
    rows = q_ref.shape[0]
    heads = q_ref.shape[1] // HEAD_SIZE
    sharing = q_ref.shape[1] // k_ref.shape[1]
    allowed = allowed_pairs(scal_ref, rows)
    pieces = []
    for head in range(heads):
        at = head * HEAD_SIZE
        kv = head // sharing * HEAD_SIZE
        query = q_ref[:, at : at + HEAD_SIZE]
        key = k_ref[:, kv : kv + HEAD_SIZE]
        value = v_ref[:, kv : kv + HEAD_SIZE]
        scores = jnp.where(allowed, matmul_nt(query, key) * (HEAD_SIZE**-0.5), masked_score)
        peak = jnp.max(scores, axis=1, keepdims=True)
        weights = jnp.exp(scores - peak)
        total = jnp.sum(weights, axis=1, keepdims=True)
        probs = (weights * (1.0 / total)).astype(BF)
        pieces.append(matmul(probs, value))
        lse_ref[:, head : head + 1] = peak + jnp.log(total)
    attended = jnp.concatenate(pieces, axis=1).astype(BF)
    att_ref[...] = attended
    part_ref[...] = matmul(attended, wo_ref[...]).astype(BF)


def attend(scal, query, key, value, w_output):
    rows, wide = query.shape
    return pl.pallas_call(
        attend_kernel,
        out_shape=(
            jax.ShapeDtypeStruct((rows, wide), BF),
            jax.ShapeDtypeStruct((rows, 128), F32),
            jax.ShapeDtypeStruct((rows, w_output.shape[1]), BF),
        ),
        in_specs=[smem_spec()] + [vmem_spec()] * 4,
        out_specs=(vmem_spec(),) * 3,
        compiler_params=pltpu.CompilerParams(vmem_limit_bytes=48 * MIB),
        name="attend",
    )(scal, query, key, value, w_output)


def turn(values, first):
    wide = values.shape[1]
    half = HEAD_SIZE // 2
    return jnp.where(
        first, -pltpu.roll(values, wide - half, 1), pltpu.roll(values, half, 1)
    )


def attend_back_kernel(
    scal_ref, q_ref, k_ref, v_ref, lse_ref, att_ref, low_ref, wo_ref, cos_ref, sin_ref,
    dq_ref, dk_ref, dv_ref, dwo_ref,
):
    rows, wide = q_ref.shape
    heads = wide // HEAD_SIZE
    sharing = q_ref.shape[1] // k_ref.shape[1]
    scale = HEAD_SIZE**-0.5
    low = low_ref[...]
    dwo_ref[...] = matmul_tn(att_ref[...], low)
    att_grad = matmul_nt(low, wo_ref[...]).astype(BF)
    allowed = allowed_pairs(scal_ref, rows)
    query_parts, key_parts, value_parts = [], [], []
    for head in range(heads):
        at = head * HEAD_SIZE
        kv = head // sharing * HEAD_SIZE
        query = q_ref[:, at : at + HEAD_SIZE]
        key = k_ref[:, kv : kv + HEAD_SIZE]
        value = v_ref[:, kv : kv + HEAD_SIZE]
        grad = att_grad[:, at : at + HEAD_SIZE]
        scores = jnp.where(allowed, matmul_nt(query, key) * scale, masked_score)
        probs = jnp.exp(scores - lse_ref[:, head : head + 1])
        prob_grad = matmul_nt(grad, value)
        delta = jnp.sum(probs * prob_grad, axis=1, keepdims=True)
        score_grad = (probs * (prob_grad - delta)).astype(BF)
        query_parts.append(matmul(score_grad, key) * scale)
        key_part = matmul_tn(score_grad, query) * scale
        value_part = matmul_tn(probs.astype(BF), grad)
        if head % sharing == 0:
            key_parts.append(key_part)
            value_parts.append(value_part)
        else:
            key_parts[-1] = key_parts[-1] + key_part
            value_parts[-1] = value_parts[-1] + value_part
    dk_ref[...] = jnp.concatenate(key_parts, axis=1).astype(BF)
    dv_ref[...] = jnp.concatenate(value_parts, axis=1).astype(BF)
    rotated = jnp.concatenate(query_parts, axis=1)
    lane = lax.broadcasted_iota(jnp.int32, (1, wide), 1)
    first = lane % HEAD_SIZE < HEAD_SIZE // 2
    cosines = jnp.concatenate([cos_ref[...]] * (wide // 128), axis=1)
    sines = jnp.concatenate([sin_ref[...]] * (wide // 128), axis=1)
    dq_ref[...] = (rotated * cosines - turn(rotated, first) * sines).astype(BF)


def attend_back(scal, query, key, value, lse, attended, low, w_output, cosines, sines):
    rows, wide = query.shape
    return pl.pallas_call(
        attend_back_kernel,
        out_shape=(
            jax.ShapeDtypeStruct((rows, wide), BF),
            jax.ShapeDtypeStruct(key.shape, BF),
            jax.ShapeDtypeStruct(value.shape, BF),
            jax.ShapeDtypeStruct(w_output.shape, F32),
        ),
        in_specs=[smem_spec()] + [vmem_spec()] * 9,
        out_specs=(vmem_spec(),) * 4,
        compiler_params=pltpu.CompilerParams(vmem_limit_bytes=56 * MIB),
        name="attend_back",
    )(scal, query, key, value, lse, attended, low, w_output, cosines, sines)


MESH = pl.DeviceIdType.MESH
PART = 32
LAG = 3
LINK_COST = pl.CostEstimate(flops=4 * 10**10, bytes_accessed=10**7, transcendentals=0)


def meet(partners):
    barrier = pltpu.get_barrier_semaphore()
    count = 0
    for here, device in partners:
        here = jnp.asarray(here)

        @pl.when(here)
        def _():
            pl.semaphore_signal(barrier, inc=1, device_id=device, device_id_type=MESH)

        count = count + here.astype(jnp.int32)
    pl.semaphore_wait(barrier, count)


def line_partners():
    place = lax.axis_index("tensor")
    last = lax.axis_size("tensor") - 1
    return [(place > 0, {"tensor": place - 1}), (place < last, {"tensor": place + 1})]


class Line:
    def __init__(self, parts, term, from_left, from_right, to_right, to_left, sems):
        self.place = lax.axis_index("tensor")
        self.last = lax.axis_size("tensor") - 1
        self.parts = parts
        self.term = term
        self.from_left, self.from_right = from_left, from_right
        self.to_right, self.to_left = to_right, to_left
        self.sems = sems

    def copy(self, way, at):
        near = jnp.where(self.place < self.last, self.place + 1, self.place - 1)
        far = jnp.where(self.place > 0, self.place - 1, self.place + 1)
        source, target, device = (
            (self.to_right, self.from_left, near) if way == 0 else (self.to_left, self.from_right, far)
        )
        return pltpu.make_async_remote_copy(
            src_ref=source.at[at],
            dst_ref=target.at[at],
            send_sem=self.sems.at[2 * way, at],
            recv_sem=self.sems.at[2 * way + 1, at],
            device_id={"tensor": device},
            device_id_type=MESH,
        )

    def clear(self):
        @pl.when(self.place == 0)
        def _():
            self.from_left[...] = jnp.zeros(self.from_left.shape, self.from_left.dtype)

        @pl.when(self.place == self.last)
        def _():
            self.from_right[...] = jnp.zeros(self.from_right.shape, self.from_right.dtype)

    def step(self, at):
        for way in range(2):
            part = at - LAG * (self.place if way == 0 else self.last - self.place)
            has_source = self.place > 0 if way == 0 else self.place < self.last
            has_target = self.place < self.last if way == 0 else self.place > 0
            arrived = self.from_left if way == 0 else self.from_right
            leaving = self.to_right if way == 0 else self.to_left
            valid = (part >= 0) & (part < self.parts)

            @pl.when(valid & has_source)
            def _():
                self.copy(way, part).wait_recv()

            @pl.when(valid & has_target)
            def _():
                leaving[part] = (self.term(part) + arrived[part].astype(F32)).astype(BF)
                self.copy(way, part).start()

    def total(self, part):
        return self.term(part) + self.from_left[part].astype(F32) + self.from_right[part].astype(F32)

    def drain(self):
        def wait(part, carry):
            @pl.when(self.place < self.last)
            def _():
                self.copy(0, part).wait_send()

            @pl.when(self.place > 0)
            def _():
                self.copy(1, part).wait_send()

            return carry

        lax.fori_loop(0, self.parts, wait, 0)


def line_scratch(parts, width):
    return [pltpu.VMEM((parts, PART, width), BF)] * 4 + [pltpu.SemaphoreType.DMA((4, parts))]


def peer_copy(source, target, sems, at):
    return pltpu.make_async_remote_copy(
        src_ref=source,
        dst_ref=target,
        send_sem=sems.at[0, at],
        recv_sem=sems.at[1, at],
        device_id={"expert": 1 - lax.axis_index("expert")},
        device_id_type=MESH,
    )


def scale_of(values):
    return lax.rsqrt(jnp.mean(values * values, axis=-1, keepdims=True) + epsilon)


def residual_kernel(
    part_ref, x_ref, gain_ref, res_ref, n_ref, from_left, from_right, to_right, to_left, sems, peer_sems
):
    parts = part_ref.shape[0]
    line = Line(parts, lambda at: part_ref[at].astype(F32), from_left, from_right, to_right, to_left, sems)
    line.clear()
    meet(line_partners() + [(True, {"expert": 1 - lax.axis_index("expert")})])

    def body(at, carry):
        line.step(at)
        part = at - LAG * line.last

        @pl.when(part >= 0)
        def _():
            residual = x_ref[part].astype(F32) + line.total(part)
            res_ref[part] = residual
            unit = residual * scale_of(residual)
            n_ref[0, part] = (unit * gain_ref[...]).astype(BF)
            peer_copy(n_ref.at[0, part], n_ref.at[1, part], peer_sems, part).start()

        return carry

    lax.fori_loop(0, parts + LAG * line.last, body, 0)
    line.drain()

    def wait(part, carry):
        peer_copy(n_ref.at[0, part], n_ref.at[1, part], peer_sems, part).wait()
        return carry

    lax.fori_loop(0, parts, wait, 0)


def residual_norm(part, block_input, gain):
    rows, width = block_input.shape
    parts = rows // PART
    residual, normed = pl.pallas_call(
        residual_kernel,
        out_shape=(
            jax.ShapeDtypeStruct((parts, PART, width), F32),
            jax.ShapeDtypeStruct((2, parts, PART, width), BF),
        ),
        in_specs=[vmem_spec()] * 3,
        out_specs=(vmem_spec(),) * 2,
        scratch_shapes=line_scratch(parts, width) + [pltpu.SemaphoreType.DMA((2, parts))],
        compiler_params=pltpu.CompilerParams(
            collective_id=0, has_side_effects=True, vmem_limit_bytes=40 * MIB
        ),
        cost_estimate=LINK_COST,
        name="residual_norm",
    )(part.reshape(parts, PART, width), block_input.reshape(parts, PART, width), gain[None])
    return residual, normed.reshape(2 * rows, width)


def residual_grad_kernel(
    back_ref, route_ref, res_ref, up_ref, gain_ref, grad_ref, low_ref, second_ref, route_out,
    from_left, from_right, to_right, to_left, sems, peer_sems, arrived, terms,
):
    parts = back_ref.shape[1]
    line = Line(parts + 1, lambda at: terms[at], from_left, from_right, to_right, to_left, sems)
    line.clear()
    meet(line_partners() + [(True, {"expert": 1 - lax.axis_index("expert")})])

    def send(part, carry):
        peer_copy(back_ref.at[1, part], arrived.at[part], peer_sems, part).start()
        return carry

    lax.fori_loop(0, parts, send, 0)
    terms[parts] = route_ref[...]
    second_ref[...] = jnp.zeros(second_ref.shape, F32)

    def body(at, carry):
        @pl.when(at < parts)
        def _():
            peer_copy(back_ref.at[1, at], arrived.at[at], peer_sems, at).wait_recv()
            terms[at] = back_ref[0, at].astype(F32) + arrived[at].astype(F32)

        line.step(at)
        part = at - LAG * line.last

        @pl.when((part >= 0) & (part < parts))
        def _():
            grad = line.total(part)
            residual = res_ref[part]
            scale = scale_of(residual)
            unit = residual * scale
            second_ref[...] += jnp.sum(grad * unit, axis=0, keepdims=True)
            result = up_ref[part].astype(F32) + norm_back(grad, unit, scale, gain_ref[...])
            grad_ref[part] = result
            low_ref[part] = result.astype(BF)

        return carry

    lax.fori_loop(0, parts + 1 + LAG * line.last, body, 0)
    route_out[...] = line.total(parts)
    line.drain()

    def wait(part, carry):
        peer_copy(back_ref.at[1, part], arrived.at[part], peer_sems, part).wait_send()
        return carry

    lax.fori_loop(0, parts, wait, 0)


def residual_gradient(back, route, residual, upstream, gain):
    rows, width = upstream.shape
    parts = rows // PART
    grad, low, second, route = pl.pallas_call(
        residual_grad_kernel,
        out_shape=(
            jax.ShapeDtypeStruct((parts, PART, width), F32),
            jax.ShapeDtypeStruct((parts, PART, width), BF),
            jax.ShapeDtypeStruct((1, width), F32),
            jax.ShapeDtypeStruct(route.shape, F32),
        ),
        in_specs=[vmem_spec()] * 5,
        out_specs=(vmem_spec(),) * 4,
        scratch_shapes=line_scratch(parts + 1, width)
        + [
            pltpu.SemaphoreType.DMA((2, parts)),
            pltpu.VMEM((parts, PART, width), BF),
            pltpu.VMEM((parts + 1, PART, width), F32),
        ],
        compiler_params=pltpu.CompilerParams(
            collective_id=1, has_side_effects=True, vmem_limit_bytes=48 * MIB
        ),
        cost_estimate=LINK_COST,
        name="residual_grad",
    )(
        back.reshape(2, parts, PART, width), route, residual, upstream.reshape(parts, PART, width), gain[None]
    )
    return grad, low.reshape(rows, width), second[0], route


def input_grad_kernel(
    part_ref, x_ref, res_grad_ref, gain_ref, grad_ref, first_ref, from_left, from_right, to_right, to_left, sems
):
    parts = part_ref.shape[0]
    line = Line(parts, lambda at: part_ref[at], from_left, from_right, to_right, to_left, sems)
    line.clear()
    meet(line_partners())
    first_ref[...] = jnp.zeros(first_ref.shape, F32)

    def body(at, carry):
        line.step(at)
        part = at - LAG * line.last

        @pl.when(part >= 0)
        def _():
            grad = line.total(part)
            values = x_ref[part].astype(F32)
            scale = scale_of(values)
            unit = values * scale
            first_ref[...] += jnp.sum(grad * unit, axis=0, keepdims=True)
            grad_ref[part] = (res_grad_ref[part] + norm_back(grad, unit, scale, gain_ref[...])).astype(BF)

        return carry

    lax.fori_loop(0, parts + LAG * line.last, body, 0)
    line.drain()


def input_gradient(first_part, block_input, residual_grad, gain):
    rows, width = block_input.shape
    parts = rows // PART
    grad, first = pl.pallas_call(
        input_grad_kernel,
        out_shape=(
            jax.ShapeDtypeStruct((parts, PART, width), BF),
            jax.ShapeDtypeStruct((1, width), F32),
        ),
        in_specs=[vmem_spec()] * 4,
        out_specs=(vmem_spec(),) * 2,
        scratch_shapes=line_scratch(parts, width),
        compiler_params=pltpu.CompilerParams(
            collective_id=2, has_side_effects=True, vmem_limit_bytes=40 * MIB
        ),
        cost_estimate=LINK_COST,
        name="input_grad",
    )(first_part.reshape(parts, PART, width), block_input.reshape(parts, PART, width), residual_grad, gain[None])
    return grad.reshape(rows, width), first[0]


CHUNK = 512
GROUP = 4


def expert_kernel(
    n_ref, g_ref, chosen_ref, kept_ref, wr_ref, wg_ref, wu_ref, wd_ref,
    dwg_ref, dwu_ref, dwd_ref, mix_ref, back_ref, route_ref,
    gates, kept_gates, gate_grads, mix, back, nt, wgs, wus, ght, dgs, dus,
    out_g, out_u, out_d, in_g, in_u, in_d, sems,
):
    step = pl.program_id(0)
    steps = pl.num_programs(0) // 2
    side = lax.axis_index("expert")
    dp = lax.axis_index("dp")
    core = lax.rem(dp, 2)
    other = {"dp": dp + 1 - 2 * core}
    tokens, width = n_ref.shape
    experts_all = wr_ref.shape[1]
    group, _, hid = wg_ref.shape
    chunks = tokens // CHUNK
    lane = lax.broadcasted_iota(jnp.int32, (1, experts_all), 1)

    def copies(slot):
        return [
            pltpu.make_async_remote_copy(
                src_ref=source.at[slot], dst_ref=target.at[slot],
                send_sem=sems.at[0, kind, slot], recv_sem=sems.at[1, kind, slot],
                device_id=other, device_id_type=MESH,
            )
            for kind, (source, target) in enumerate(((out_g, in_g), (out_u, in_u), (out_d, in_d)))
        ]

    @pl.when(step == 0)
    def _():
        meet([(True, other)])

        def start(at, carry):
            rows = pl.ds(pl.multiple_of(at * CHUNK, CHUNK), CHUNK)
            chosen = chosen_ref[rows, :] > 0.0
            logits = jnp.where(chosen, matmul(n_ref[rows, :], wr_ref[...]), masked_score)
            raised = jnp.exp(logits - jnp.max(logits, axis=1, keepdims=True))
            raised = jnp.where(chosen, raised, 0.0)
            gate = raised / jnp.sum(raised, axis=1, keepdims=True)
            gates[rows, :] = gate
            kept_gates[rows, :] = gate * kept_ref[rows, :]
            mix[rows, :] = jnp.zeros((CHUNK, width), F32)
            back[rows, :] = jnp.zeros((CHUNK, width), F32)
            gate_grads[rows, :] = jnp.zeros((CHUNK, experts_all), F32)
            return carry

        lax.fori_loop(0, chunks, start, 0)
        for at in range(chunks):
            nt[:, at * CHUNK : (at + 1) * CHUNK] = n_ref[at * CHUNK : (at + 1) * CHUNK, :].T

    for expert in range(group):
        wgs[:, expert * hid : (expert + 1) * hid] = wg_ref[expert]
        wus[:, expert * hid : (expert + 1) * hid] = wu_ref[expert]
    first = step < steps
    block = jnp.where(first, (1 - core) * steps + step, core * steps + step - steps)
    column = side * (experts_all // 2) + block * group

    for at in range(chunks):
        rows = slice(at * CHUNK, (at + 1) * CHUNK)
        token = n_ref[rows, :]
        down = wd_ref[...].reshape(group * hid, width)
        gate_in = matmul(token, wgs[...])
        up_in = matmul(token, wus[...])
        pulled = matmul_nt(g_ref[rows, :], down)
        sig = 0.5 * jnp.tanh(0.5 * gate_in) + 0.5
        silu = gate_in * sig
        hidden = silu * up_in
        kept = kept_gates[rows, :]
        weights = []
        products = hidden * pulled
        grads = gate_grads[rows, :]
        for expert in range(group):
            here = lane == column + expert
            gate = jnp.sum(jnp.where(here, kept, 0.0), axis=1, keepdims=True)
            weights.append(jnp.broadcast_to(gate, (CHUNK, hid)))
            product = jnp.sum(products[:, expert * hid : (expert + 1) * hid], axis=1, keepdims=True)
            grads = grads + jnp.where(here, product, 0.0)
        gate_grads[rows, :] = grads
        weight = jnp.concatenate(weights, axis=1)
        gated = (hidden * weight).astype(BF)
        pulled = pulled * weight
        up_grad = (pulled * silu).astype(BF)
        gate_grad = (pulled * up_in * (sig + silu * (1.0 - sig))).astype(BF)
        ght[:, rows] = gated.T
        dgs[rows, :] = gate_grad
        dus[rows, :] = up_grad
        mix[rows, :] += matmul(gated, down)
        back[rows, :] += matmul_nt(gate_grad, wgs[...]) + matmul_nt(up_grad, wus[...])

    def weight_grads(store_rows, store_down):
        for at in range(width // CHUNK):
            rows = slice(at * CHUNK, (at + 1) * CHUNK)
            turned = nt[rows, :]
            gate_part = matmul(turned, dgs[...])
            up_part = matmul(turned, dus[...])
            for expert in range(group):
                inner = slice(expert * hid, (expert + 1) * hid)
                store_rows(expert, rows, gate_part[:, inner], up_part[:, inner])
        down_part = matmul(ght[...], g_ref[...])
        for expert in range(group):
            store_down(expert, down_part[expert * hid : (expert + 1) * hid, :])

    @pl.when(first)
    def _():
        def store_rows(expert, rows, gate_part, up_part):
            out_g[step, expert, rows, :] = gate_part.astype(BF)
            out_u[step, expert, rows, :] = up_part.astype(BF)

        def store_down(expert, part):
            out_d[step, expert] = part.astype(BF)

        weight_grads(store_rows, store_down)
        for copy in copies(step):
            copy.start()

    @pl.when(step >= steps)
    def _():
        slot = step - steps
        for copy in copies(slot):
            copy.wait_recv()

        def store_rows(expert, rows, gate_part, up_part):
            dwg_ref[expert, rows, :] = (gate_part + in_g[slot, expert, rows, :].astype(F32)).astype(BF)
            dwu_ref[expert, rows, :] = (up_part + in_u[slot, expert, rows, :].astype(F32)).astype(BF)

        def store_down(expert, part):
            dwd_ref[expert] = (part + in_d[slot, expert].astype(F32)).astype(BF)

        weight_grads(store_rows, store_down)
        for copy in copies(slot):
            copy.wait_send()

    @pl.when(step == 2 * steps - 1)
    def _():
        route_ref[...] = jnp.zeros(route_ref.shape, F32)

        def finish(at, carry):
            rows = pl.ds(pl.multiple_of(at * CHUNK, CHUNK), CHUNK)
            mix_ref[rows, :] = mix[rows, :].astype(BF)
            grads = gate_grads[rows, :] * kept_gates[rows, :]
            chosen_grad = grads - gates[rows, :] * jnp.sum(grads, axis=1, keepdims=True)
            low = chosen_grad.astype(BF)
            back_ref[rows, :] = (back[rows, :] + matmul_nt(low, wr_ref[...])).astype(BF)
            route_ref[...] += matmul_tn(low, n_ref[rows, :])
            return carry

        lax.fori_loop(0, chunks, finish, 0)


def experts(normed, upstream, chosen, kept, w_router, w_gate, w_up, w_down):
    tokens, width = normed.shape
    count, _, hid = w_gate.shape
    half = count // 2
    steps = half // GROUP
    experts_all = w_router.shape[1]
    once = pl.Buffered(1)
    whole = lambda step: (0, 0)

    def picked(step):
        core = lax.rem(lax.axis_index("dp"), 2)
        return (jnp.where(step < steps, (1 - core) * steps + step, core * steps + step - steps), 0, 0)

    own = lambda step: (jnp.maximum(step - steps, 0), 0, 0)
    args = [normed, upstream, chosen, kept, w_router]
    specs = [pl.BlockSpec(array.shape, whole, pipeline_mode=once) for array in args]
    up_block, down_block = (GROUP, width, hid), (GROUP, hid, width)
    specs += [pl.BlockSpec(up_block, picked), pl.BlockSpec(up_block, picked), pl.BlockSpec(down_block, picked)]
    gate_scratch = pltpu.VMEM((tokens, experts_all), F32)
    rows_scratch = pltpu.VMEM((tokens, width), F32)
    swap_scratch = [
        pltpu.VMEM((steps,) + up_block, BF),
        pltpu.VMEM((steps,) + up_block, BF),
        pltpu.VMEM((steps,) + down_block, BF),
    ]
    return pl.pallas_call(
        expert_kernel,
        out_shape=[
            jax.ShapeDtypeStruct((half, width, hid), BF),
            jax.ShapeDtypeStruct((half, width, hid), BF),
            jax.ShapeDtypeStruct((half, hid, width), BF),
            jax.ShapeDtypeStruct((tokens, width), BF),
            jax.ShapeDtypeStruct((tokens, width), BF),
            jax.ShapeDtypeStruct((experts_all, width), F32),
        ],
        grid=(2 * steps,),
        in_specs=specs,
        out_specs=[
            pl.BlockSpec(up_block, own),
            pl.BlockSpec(up_block, own),
            pl.BlockSpec(down_block, own),
            pl.BlockSpec((tokens, width), whole, pipeline_mode=once),
            pl.BlockSpec((tokens, width), whole, pipeline_mode=once),
            pl.BlockSpec((experts_all, width), whole, pipeline_mode=once),
        ],
        scratch_shapes=[
            gate_scratch, gate_scratch, gate_scratch, rows_scratch, rows_scratch,
            pltpu.VMEM((width, tokens), BF),
            pltpu.VMEM((width, GROUP * hid), BF),
            pltpu.VMEM((width, GROUP * hid), BF),
            pltpu.VMEM((GROUP * hid, tokens), BF),
            pltpu.VMEM((tokens, GROUP * hid), BF),
            pltpu.VMEM((tokens, GROUP * hid), BF),
        ]
        + swap_scratch
        + swap_scratch
        + [pltpu.SemaphoreType.DMA((2, 3, steps))],
        compiler_params=pltpu.CompilerParams(
            dimension_semantics=("arbitrary",), collective_id=3, has_side_effects=True, vmem_limit_bytes=60 * MIB
        ),
        cost_estimate=pl.CostEstimate(
            flops=18 * tokens * width * count * hid,
            bytes_accessed=12 * count * width * hid,
            transcendentals=tokens * count * hid,
        ),
        name="experts",
    )(*args, w_gate, w_up, w_down)


def combine_kernel(core_ref, mine_ref, crossed_ref, other_ref, other_crossed_ref, out_ref):
    here = pl.program_id(0) == 0

    @pl.when(here)
    def _():
        out_ref[...] = mine_ref[...].astype(F32) + crossed_ref[...].astype(F32)

    @pl.when(jnp.logical_not(here))
    def _():
        out_ref[...] = other_ref[...].astype(F32) + other_crossed_ref[...].astype(F32)


def combine(core, mine, crossed, other, other_crossed):
    half, high, wide = mine.shape
    step = 2
    count = half // step
    block = (step, high, wide)
    first = pl.BlockSpec(block, lambda part, at, core: (jnp.where(part == 0, at, count - 1), 0, 0))
    second = pl.BlockSpec(block, lambda part, at, core: (jnp.where(part == 0, 0, at), 0, 0))
    return pl.pallas_call(
        combine_kernel,
        out_shape=jax.ShapeDtypeStruct((2 * half, high, wide), F32),
        grid_spec=pltpu.PrefetchScalarGridSpec(
            num_scalar_prefetch=1,
            grid=(2, count),
            in_specs=[first, first, second, second],
            out_specs=pl.BlockSpec(
                block, lambda part, at, core: (jnp.where(part == 0, core[0], 1 - core[0]) * count + at, 0, 0)
            ),
        ),
        compiler_params=pltpu.CompilerParams(vmem_limit_bytes=32 * MIB),
        cost_estimate=pl.CostEstimate(flops=4 * half * high * wide, bytes_accessed=16 * half * high * wide, transcendentals=0),
        name="combine",
    )(core, mine, crossed, other, other_crossed)


def swap(array, axis, bit):
    size = lax.axis_size(axis)
    return lax.ppermute(array, axis, [(at, at ^ bit) for at in range(size)])


def fast_device(
    block_input, first_gain, w_query, key_weight, value_weight, w_output, second_gain, w_router,
    w_gate, w_up, w_down, expert_ids, slot_index, piece_start_offsets, upstream,
):
    rows, width = block_input.shape
    local_heads = w_query.shape[1] // HEAD_SIZE
    local_kv = key_weight.shape[1] // HEAD_SIZE
    experts_all = w_router.shape[1]
    side = lax.axis_index("expert")
    core = lax.axis_index("dp") % 2
    feature_start = lax.axis_index("tensor") * (width // 4)
    scal = jnp.concatenate([side[None].astype(jnp.int32), piece_start_offsets[0]])

    axis_row = jnp.arange(experts_all, dtype=jnp.int32)[None, None, :]
    hits = (expert_ids[:, :, None] == axis_row)
    chosen = jnp.sum(hits.astype(F32), axis=1)
    kept = jnp.sum((hits & (slot_index >= 0)[:, :, None]).astype(F32), axis=1)
    marks = jnp.concatenate([chosen, kept], axis=1).astype(BF)
    marks = jnp.concatenate([marks, swap(marks, "expert", 1)], axis=0).astype(F32)
    chosen, kept = marks[:, :experts_all], marks[:, experts_all:]
    upstream_all = jnp.concatenate([upstream, swap(upstream, "expert", 1)], axis=0)

    positions = side * rows + jnp.arange(rows, dtype=jnp.int32)
    cosine_table, sine_table = rope_tables(positions)
    cosines = jnp.tile(cosine_table, (1, 4))
    sines = jnp.tile(sine_table, (1, 4))
    inputs = block_input.astype(F32)
    first_scale = norm_scale(inputs)
    first_unit = inputs * first_scale
    first_normed = (first_unit * first_gain).astype(BF)
    query_rot = apply_rotary(
        matmul(first_normed, w_query).reshape(rows, local_heads, HEAD_SIZE), cosine_table, sine_table
    ).astype(BF).reshape(rows, local_heads * HEAD_SIZE)
    key_rot = apply_rotary(
        matmul(first_normed, key_weight).reshape(rows, local_kv, HEAD_SIZE), cosine_table, sine_table
    ).astype(BF).reshape(rows, local_kv * HEAD_SIZE)
    value_low = matmul(first_normed, value_weight).astype(BF)
    both = jnp.concatenate([key_rot, value_low], axis=1)
    both = jnp.concatenate([both, swap(both, "expert", 1)], axis=0)
    keys, values = both[:, : local_kv * HEAD_SIZE], both[:, local_kv * HEAD_SIZE :]

    attended, lse, part = attend(scal, query_rot, keys, values, w_output)
    residual, normed_all = residual_norm(part, block_input, second_gain)

    dwg, dwu, dwd, mix, back, route = experts(
        normed_all, upstream_all, chosen, kept, w_router, w_gate, w_up, w_down
    )
    pairs = (dwd, dwg, dwu)
    crossed = [swap(item, "dp", 2) for item in pairs]
    pairs_other = [swap(item, "dp", 1) for item in pairs]

    residual_grad, residual_low, grad_second, route = residual_gradient(back, route, residual, upstream, second_gain)

    query_grad, dk, dv, grad_output = attend_back(
        scal, query_rot, keys, values, lse, attended, residual_low, w_output, cosines, sines
    )
    dboth = jnp.concatenate([dk, dv], axis=1)
    dboth = dboth[:rows].astype(F32) + swap(dboth[rows:], "expert", 1).astype(F32)
    key_back, value_back = dboth[:, : local_kv * HEAD_SIZE], dboth[:, local_kv * HEAD_SIZE :]
    key_grad = unrotate(
        key_back.reshape(rows, local_kv, HEAD_SIZE), cosine_table, sine_table
    ).astype(BF).reshape(rows, local_kv * HEAD_SIZE)
    value_grad = value_back.astype(BF)
    grad_query = matmul_tn(first_normed, query_grad)
    grad_key = matmul_tn(first_normed, key_grad)
    grad_value = matmul_tn(first_normed, value_grad)
    first_part = (
        matmul_nt(query_grad, w_query) + matmul_nt(key_grad, key_weight) + matmul_nt(value_grad, value_weight)
    )
    grad_input, grad_first = input_gradient(first_part, block_input, residual_grad, first_gain)
    mix, grad_input = lax.optimization_barrier((mix, grad_input))
    mixed = lax.psum_scatter(mix, "tensor", scatter_dimension=1, tiled=True)
    mixed = mixed[:rows].astype(F32) + swap(mixed[rows:], "expert", 1).astype(F32)
    block_output = (
        lax.dynamic_slice_in_dim(residual.reshape(rows, width), feature_start, width // 4, 1) + mixed
    ).astype(BF)

    core_row = core[None].astype(jnp.int32)
    expert_sums = [
        combine(core_row, mine, other, away, swap(other, "dp", 1))
        for mine, other, away in zip(pairs, crossed, pairs_other)
    ]
    early = lax.psum((grad_output.astype(BF), route.astype(BF), grad_second.astype(BF)), ("dp", "expert"))
    late = lax.psum(
        (grad_query.astype(BF), grad_key.astype(BF), grad_value.astype(BF), grad_first.astype(BF)), ("dp", "expert")
    )
    early = [item.astype(F32) for item in early]
    late = [item.astype(F32) for item in late]
    return (
        block_output, grad_input, late[3], late[0], late[1], late[2], early[0], early[2], early[1].T,
        expert_sums[1], expert_sums[2], expert_sums[0],
    )


def solution(mesh):
    fast = mesh.shape["expert"] == 2 and mesh.shape["dp"] == 4 and mesh.shape["tensor"] == 4
    placed = (
        P(("dp", "expert"), None),
        P(),
        P(None, "tensor"),
        P(None, "tensor"),
        P(None, "tensor"),
        P("tensor", None),
        P(),
        P(),
        P("expert", None, "tensor"),
        P("expert", None, "tensor"),
        P("expert", "tensor", None),
        P(("dp", "expert"), None),
        P(("dp", "expert"), None),
        P("dp", None),
        P(("dp", "expert"), None),
    )
    return jax.shard_map(
        fast_device if fast else general_device,
        mesh=mesh,
        in_specs=placed,
        out_specs=(
            P(("dp", "expert"), "tensor"),
            P(("dp", "expert"), None),
            P(),
            P(None, "tensor"),
            P(None, "tensor"),
            P(None, "tensor"),
            P("tensor", None),
            P(),
            P(),
            P("expert", None, "tensor"),
            P("expert", None, "tensor"),
            P("expert", "tensor", None),
        ),
        check_vma=False,
    )
```

```python
import functools
import math

import jax
import jax.numpy as jnp
from jax import lax
from jax.experimental import pallas as pl
from jax.experimental.pallas import tpu as pltpu
from jax.sharding import PartitionSpec as P

HEAD_SIZE = 64
TOPK = 8
PIC = 256


epsilon = 1e-06
rope_base = 10000.0
masked_score = -1e30


def rope_tables(positions):
    steps = jnp.arange(HEAD_SIZE // 2, dtype=jnp.float32)
    inverse = jnp.exp(steps * (-2.0 * math.log(rope_base) / HEAD_SIZE))
    angle = positions.astype(jnp.float32)[:, None] * inverse[None, :]
    return (jnp.cos(angle), jnp.sin(angle))


def apply_rotary(values, cosine_table, sine_table):
    half = values.shape[-1] // 2
    first = values[..., :half]
    second = values[..., half:]
    cosine_table = cosine_table[:, None, :]
    sine_table = sine_table[:, None, :]
    return jnp.concatenate(
        [first * cosine_table - second * sine_table, second * cosine_table + first * sine_table],
        axis=-1,
    )


def unrotate(values, cosine_table, sine_table):
    half = values.shape[-1] // 2
    first = values[..., :half]
    second = values[..., half:]
    cosine_table = cosine_table[:, None, :]
    sine_table = sine_table[:, None, :]
    return jnp.concatenate(
        [first * cosine_table + second * sine_table, second * cosine_table - first * sine_table],
        axis=-1,
    )


def piece_ids(positions, offsets):
    span = 2 * PIC
    window = positions // span
    within = positions - window * span
    count = offsets.shape[0]
    match = window[:, None] == jnp.arange(count, dtype=jnp.int32)[None, :]
    start = jnp.sum(jnp.where(match, offsets[None, :], 0), axis=1)
    inside = (window < count) & (within >= start) & (within < start + PIC)
    return jnp.where(inside, window, -1)


def matmul(left, right):
    return jnp.dot(left, right, preferred_element_type=jnp.float32)


def matmul_nt(left, right):
    return lax.dot_general(
        left, right, (((1,), (1,)), ((), ())), preferred_element_type=jnp.float32
    )


def matmul_tn(left, right):
    return lax.dot_general(
        left, right, (((0,), (0,)), ((), ())), preferred_element_type=jnp.float32
    )


def norm_scale(values):
    return lax.rsqrt(jnp.mean(values * values, axis=-1, keepdims=True) + epsilon)


def norm_back(grad, unit, scale, gain):
    weighted = grad * gain
    return scale * (weighted - unit * jnp.mean(weighted * unit, axis=-1, keepdims=True))


def general_device(
    block_input,
    first_gain,
    w_query,
    key_weight,
    value_weight,
    w_output,
    second_gain,
    w_router,
    w_gate,
    w_up,
    w_down,
    expert_ids,
    slot_index,
    piece_start_offsets,
    upstream,
):
    rows_here = block_input.shape[0]
    width = block_input.shape[1]
    groups = lax.axis_size("expert")
    length = rows_here * groups
    local_heads = w_query.shape[1] // HEAD_SIZE
    local_kv = key_weight.shape[1] // HEAD_SIZE
    sharing = local_heads // local_kv
    head_rows = sharing * rows_here
    experts_all = w_router.shape[1]
    capacity = TOPK * rows_here // experts_all
    slots_all = experts_all * capacity
    score_scale = HEAD_SIZE ** (-0.5)
    positions = lax.axis_index("expert") * rows_here + jnp.arange(rows_here, dtype=jnp.int32)
    cosine_table, sine_table = rope_tables(positions)
    inputs = block_input.astype(jnp.float32)
    first_scale = norm_scale(inputs)
    first_unit = inputs * first_scale
    first_normed = (first_unit * first_gain).astype(jnp.bfloat16)
    query_rot = apply_rotary(
        matmul(first_normed, w_query).reshape(rows_here, local_heads, HEAD_SIZE),
        cosine_table,
        sine_table,
    ).astype(jnp.bfloat16)
    key_rot = (
        apply_rotary(
            matmul(first_normed, key_weight).reshape(rows_here, local_kv, HEAD_SIZE),
            cosine_table,
            sine_table,
        )
        .astype(jnp.bfloat16)
        .reshape(rows_here, local_kv * HEAD_SIZE)
    )
    value_low = matmul(first_normed, value_weight).astype(jnp.bfloat16)
    keys_all, values_all = (
        lax.all_gather(key_rot, "expert", axis=0, tiled=True),
        lax.all_gather(value_low, "expert", axis=0, tiled=True),
    )
    block = min(512, length)
    blocks = length // block

    def by_block(array):
        return array.reshape(blocks, block, local_kv, HEAD_SIZE).transpose(0, 2, 1, 3)

    def by_rows(stacked):
        return stacked.transpose(0, 2, 1, 3).reshape(length, local_kv * HEAD_SIZE)

    def head_major(array):
        return (
            array.reshape(rows_here, local_kv, sharing, HEAD_SIZE)
            .transpose(1, 2, 0, 3)
            .reshape(local_kv, head_rows, HEAD_SIZE)
        )

    def row_major(array):
        return (
            array.reshape(local_kv, sharing, rows_here, HEAD_SIZE)
            .transpose(2, 0, 1, 3)
            .reshape(rows_here, local_heads * HEAD_SIZE)
        )

    key_blocks = by_block(keys_all)
    value_blocks = by_block(values_all)
    block_starts = jnp.arange(blocks, dtype=jnp.int32) * block
    query_heads = head_major(query_rot.reshape(rows_here, local_heads * HEAD_SIZE))
    offsets = piece_start_offsets[0]
    key_pieces = piece_ids(jnp.arange(length, dtype=jnp.int32), offsets)
    query_pieces = jnp.tile(piece_ids(positions, offsets), sharing)
    query_places = jnp.tile(positions, sharing)

    def block_scores(key_block, start):
        places = start + jnp.arange(block, dtype=jnp.int32)
        pieces = lax.dynamic_slice_in_dim(key_pieces, start, block)
        causal = places[None, :] <= query_places[:, None]
        same = (pieces[None, :] == query_pieces[:, None]) & (query_pieces[:, None] >= 0)
        scores = (
            jnp.einsum("hqd,hkd->hqk", query_heads, key_block, preferred_element_type=jnp.float32)
            * score_scale
        )
        return (scores, (causal | same)[None])

    def max_step(carry, operands):
        running_max, running_sum = carry
        key_block, start = operands
        scores, allowed = block_scores(key_block, start)
        scores = jnp.where(allowed, scores, masked_score)
        new_max = jnp.maximum(running_max, jnp.max(scores, axis=-1))
        weights = jnp.where(allowed, jnp.exp(scores - new_max[..., None]), 0.0)
        new_sum = running_sum * jnp.exp(running_max - new_max) + jnp.sum(weights, axis=-1)
        return ((new_max, new_sum), None)

    start_max = jnp.full((local_kv, head_rows), masked_score, jnp.float32)
    start_sum = jnp.zeros((local_kv, head_rows), jnp.float32)
    (row_max, row_sum), _ = lax.scan(max_step, (start_max, start_sum), (key_blocks, block_starts))
    log_total = row_max + jnp.log(row_sum)

    def block_probs(key_block, start):
        scores, allowed = block_scores(key_block, start)
        return jnp.where(allowed, jnp.exp(scores - log_total[..., None]), 0.0)

    def value_step(total, operands):
        key_block, value_block, start = operands
        probs = block_probs(key_block, start).astype(jnp.bfloat16)
        return (
            total
            + jnp.einsum("hqk,hkd->hqd", probs, value_block, preferred_element_type=jnp.float32),
            None,
        )

    mixed_output, _ = lax.scan(
        value_step,
        jnp.zeros((local_kv, head_rows, HEAD_SIZE), jnp.float32),
        (key_blocks, value_blocks, block_starts),
    )
    attended = row_major(mixed_output).astype(jnp.bfloat16)
    attention = lax.psum(matmul(attended, w_output), "tensor")
    residual = inputs + attention
    second_scale = norm_scale(residual)
    second_unit = residual * second_scale
    second_normed = (second_unit * second_gain).astype(jnp.bfloat16)
    logits = matmul(second_normed, w_router)
    chosen = jnp.take_along_axis(logits, expert_ids, axis=1)
    gates = jax.nn.softmax(chosen, axis=-1)
    row_ids = jnp.arange(rows_here, dtype=jnp.int32)
    flat = jnp.where(slot_index >= 0, expert_ids * capacity + slot_index, slots_all)
    selector = (
        jnp.zeros((slots_all, rows_here), jnp.bfloat16)
        .at[flat.reshape(-1), jnp.repeat(row_ids, TOPK)]
        .set(1.0, mode="drop")
    )
    dispatched = (
        matmul(selector, second_normed).astype(jnp.bfloat16).reshape(experts_all, capacity, width)
    )
    expert_rows = lax.all_to_all(dispatched, "expert", split_axis=0, concat_axis=1, tiled=True)
    gate_in = jnp.einsum("ebd,edf->ebf", expert_rows, w_gate, preferred_element_type=jnp.float32)
    up_in = jnp.einsum("ebd,edf->ebf", expert_rows, w_up, preferred_element_type=jnp.float32)
    sigmoid_gate = jax.nn.sigmoid(gate_in)
    silu_gate = gate_in * sigmoid_gate
    hidden = (silu_gate * up_in).astype(jnp.bfloat16)
    partial_out = jnp.einsum("ebf,efd->ebd", hidden, w_down, preferred_element_type=jnp.float32)
    expert_part = lax.psum_scatter(
        partial_out.astype(jnp.bfloat16), "tensor", scatter_dimension=2, tiled=True
    )
    returned = lax.all_to_all(expert_part, "expert", split_axis=1, concat_axis=0, tiled=True)
    quarter = returned.shape[2]
    padded_out = jnp.concatenate(
        [returned.reshape(slots_all, quarter), jnp.zeros((1, quarter), jnp.bfloat16)], axis=0
    )
    feature_start = lax.axis_index("tensor") * quarter
    grad_full = upstream.astype(jnp.float32)
    grad_part = lax.dynamic_slice_in_dim(grad_full, feature_start, quarter, 1)
    mixture = jnp.zeros((rows_here, quarter), jnp.float32)
    gate_terms = []
    for pick in range(TOPK):
        picked = padded_out[flat[:, pick]].astype(jnp.float32)
        mixture = mixture + gates[:, pick : pick + 1] * picked
        gate_terms.append(jnp.sum(grad_part * picked, axis=1))
    gate_part = jnp.stack(gate_terms, axis=1)
    block_output = (lax.dynamic_slice_in_dim(residual, feature_start, quarter, 1) + mixture).astype(
        jnp.bfloat16
    )
    slot_gates = (
        jnp.zeros((slots_all + 1,), jnp.float32)
        .at[flat.reshape(-1)]
        .set(gates.reshape(-1))[:slots_all]
    )
    grad_slots = (
        (matmul(selector, upstream) * slot_gates[:, None])
        .astype(jnp.bfloat16)
        .reshape(experts_all, capacity, width)
    )
    grad_rows_in = lax.all_to_all(grad_slots, "expert", split_axis=0, concat_axis=1, tiled=True)
    hidden_grad = jnp.einsum(
        "ebd,efd->ebf", grad_rows_in, w_down, preferred_element_type=jnp.float32
    )
    grad_down = jnp.einsum("ebf,ebd->efd", hidden, grad_rows_in, preferred_element_type=jnp.float32)
    gate_in_grad = (
        hidden_grad * up_in * (sigmoid_gate * (1.0 + gate_in * (1.0 - sigmoid_gate)))
    ).astype(jnp.bfloat16)
    up_in_grad = (hidden_grad * silu_gate).astype(jnp.bfloat16)
    grad_gate = jnp.einsum(
        "ebd,ebf->edf", expert_rows, gate_in_grad, preferred_element_type=jnp.float32
    )
    grad_up = jnp.einsum(
        "ebd,ebf->edf", expert_rows, up_in_grad, preferred_element_type=jnp.float32
    )
    rows_part = jnp.einsum("ebf,edf->ebd", gate_in_grad, w_gate, preferred_element_type=jnp.float32)
    rows_part = rows_part + jnp.einsum(
        "ebf,edf->ebd", up_in_grad, w_up, preferred_element_type=jnp.float32
    )
    rows_back = lax.all_to_all(
        rows_part.astype(jnp.bfloat16), "expert", split_axis=1, concat_axis=0, tiled=True
    ).astype(rows_part.dtype)
    padded_back = jnp.concatenate(
        [rows_back.reshape(slots_all, width), jnp.zeros((1, width), jnp.float32)], axis=0
    )
    second_part = jnp.zeros((rows_here, width), jnp.float32)
    for pick in range(TOPK):
        second_part = second_part + padded_back[flat[:, pick]]
    second_sum, gate_grads = (
        lax.psum(second_part.astype(jnp.bfloat16), "tensor").astype(jnp.float32),
        lax.psum(gate_part.astype(jnp.bfloat16), "tensor").astype(jnp.float32),
    )
    chosen_grad = gates * (gate_grads - jnp.sum(gates * gate_grads, axis=1, keepdims=True))
    expert_axis = jnp.arange(experts_all, dtype=jnp.int32)
    logit_grad = jnp.zeros((rows_here, experts_all), jnp.float32)
    for pick in range(TOPK):
        logit_grad = logit_grad + jnp.where(
            expert_ids[:, pick : pick + 1] == expert_axis[None, :],
            chosen_grad[:, pick : pick + 1],
            0.0,
        )
    logit_low = logit_grad.astype(jnp.bfloat16)
    grad_router = matmul_tn(second_normed, logit_low)
    second_grad = second_sum + matmul_nt(logit_low, w_router)
    grad_second = jnp.sum(second_grad * second_unit, axis=0)
    residual_grad = grad_full + norm_back(second_grad, second_unit, second_scale, second_gain)
    residual_low = residual_grad.astype(jnp.bfloat16)
    grad_output = matmul_tn(attended, residual_low)
    attended_grad = head_major(matmul_nt(residual_low, w_output).astype(jnp.bfloat16))

    def delta_step(total, operands):
        key_block, value_block, start = operands
        probs = block_probs(key_block, start)
        prob_grad = jnp.einsum(
            "hqd,hkd->hqk", attended_grad, value_block, preferred_element_type=jnp.float32
        )
        return (total + jnp.sum(probs * prob_grad, axis=-1), None)

    delta, _ = lax.scan(
        delta_step,
        jnp.zeros((local_kv, head_rows), jnp.float32),
        (key_blocks, value_blocks, block_starts),
    )

    def grad_step(query_total, operands):
        key_block, value_block, start = operands
        probs = block_probs(key_block, start)
        prob_grad = jnp.einsum(
            "hqd,hkd->hqk", attended_grad, value_block, preferred_element_type=jnp.float32
        )
        score_grad = (probs * (prob_grad - delta[..., None])).astype(jnp.bfloat16)
        query_total = (
            query_total
            + jnp.einsum("hqk,hkd->hqd", score_grad, key_block, preferred_element_type=jnp.float32)
            * score_scale
        )
        key_grad = (
            jnp.einsum("hqk,hqd->hkd", score_grad, query_heads, preferred_element_type=jnp.float32)
            * score_scale
        )
        value_grad = jnp.einsum(
            "hqk,hqd->hkd",
            probs.astype(jnp.bfloat16),
            attended_grad,
            preferred_element_type=jnp.float32,
        )
        return (query_total, (key_grad, value_grad))

    query_total, (key_stack, value_stack) = lax.scan(
        grad_step,
        jnp.zeros((local_kv, head_rows, HEAD_SIZE), jnp.float32),
        (key_blocks, value_blocks, block_starts),
    )
    key_back, value_back = (
        lax.psum_scatter(
            by_rows(key_stack).astype(jnp.bfloat16), "expert", scatter_dimension=0, tiled=True
        ).astype(jnp.float32),
        lax.psum_scatter(
            by_rows(value_stack).astype(jnp.bfloat16), "expert", scatter_dimension=0, tiled=True
        ).astype(jnp.float32),
    )
    query_grad = (
        unrotate(
            row_major(query_total).reshape(rows_here, local_heads, HEAD_SIZE),
            cosine_table,
            sine_table,
        )
        .astype(jnp.bfloat16)
        .reshape(rows_here, local_heads * HEAD_SIZE)
    )
    key_grad = (
        unrotate(key_back.reshape(rows_here, local_kv, HEAD_SIZE), cosine_table, sine_table)
        .astype(jnp.bfloat16)
        .reshape(rows_here, local_kv * HEAD_SIZE)
    )
    value_grad = value_back.astype(jnp.bfloat16)
    grad_query = matmul_tn(first_normed, query_grad)
    grad_key = matmul_tn(first_normed, key_grad)
    grad_value = matmul_tn(first_normed, value_grad)
    first_part = (
        matmul_nt(query_grad, w_query)
        + matmul_nt(key_grad, key_weight)
        + matmul_nt(value_grad, value_weight)
    )
    first_grad = lax.psum(first_part.astype(jnp.bfloat16), "tensor").astype(jnp.float32)
    grad_first = jnp.sum(first_grad * first_unit, axis=0)
    grad_input = (
        residual_grad + norm_back(first_grad, first_unit, first_scale, first_gain)
    ).astype(jnp.bfloat16)
    dense = lax.psum(
        (grad_query, grad_key, grad_value, grad_output, grad_router, grad_first, grad_second),
        ("dp", "expert"),
    )
    expert_sums = (
        lax.psum(grad_gate.astype(jnp.bfloat16), "dp").astype(jnp.float32),
        lax.psum(grad_up.astype(jnp.bfloat16), "dp").astype(jnp.float32),
        lax.psum(grad_down.astype(jnp.bfloat16), "dp").astype(jnp.float32),
    )
    return (
        block_output,
        grad_input,
        dense[5],
        dense[0],
        dense[1],
        dense[2],
        dense[3],
        dense[6],
        dense[4],
        expert_sums[0],
        expert_sums[1],
        expert_sums[2],
    )


BF = jnp.bfloat16
F32 = jnp.float32
MIB = 1 << 20


def vmem_spec():
    return pl.BlockSpec(memory_space=pltpu.VMEM)


def smem_spec():
    return pl.BlockSpec(memory_space=pltpu.SMEM)


def allowed_pairs(scal_ref, rows):
    side = scal_ref[0]
    here = lax.broadcasted_iota(jnp.int32, (rows, 1), 0)
    keys = lax.broadcasted_iota(jnp.int32, (1, 2 * rows), 1)
    query_place = side * rows + here
    key_place = jnp.where(keys < rows, side * rows + keys, (1 - side) * rows + keys - rows)
    span = 2 * PIC

    def piece(places):
        window = places // span
        within = places - window * span
        start = jnp.where(window == 0, scal_ref[1], scal_ref[2])
        inside = (within >= start) & (within < start + PIC)
        return jnp.where(inside, window, -1)

    query_piece = piece(query_place)
    key_piece = piece(key_place)
    return (key_place <= query_place) | ((key_piece == query_piece) & (query_piece >= 0))


def attend_kernel(scal_ref, q_ref, k_ref, v_ref, wo_ref, att_ref, lse_ref, part_ref):
    rows = q_ref.shape[0]
    heads = q_ref.shape[1] // HEAD_SIZE
    sharing = q_ref.shape[1] // k_ref.shape[1]
    allowed = allowed_pairs(scal_ref, rows)
    pieces = []
    for head in range(heads):
        at = head * HEAD_SIZE
        kv = head // sharing * HEAD_SIZE
        query = q_ref[:, at : at + HEAD_SIZE]
        key = k_ref[:, kv : kv + HEAD_SIZE]
        value = v_ref[:, kv : kv + HEAD_SIZE]
        scores = jnp.where(allowed, matmul_nt(query, key) * (HEAD_SIZE**-0.5), masked_score)
        peak = jnp.max(scores, axis=1, keepdims=True)
        weights = jnp.exp(scores - peak)
        total = jnp.sum(weights, axis=1, keepdims=True)
        probs = (weights * (1.0 / total)).astype(BF)
        pieces.append(matmul(probs, value))
        lse_ref[:, head : head + 1] = peak + jnp.log(total)
    attended = jnp.concatenate(pieces, axis=1).astype(BF)
    att_ref[...] = attended
    part_ref[...] = matmul(attended, wo_ref[...]).astype(BF)


def attend(scal, query, key, value, w_output):
    rows, wide = query.shape
    return pl.pallas_call(
        attend_kernel,
        out_shape=(
            jax.ShapeDtypeStruct((rows, wide), BF),
            jax.ShapeDtypeStruct((rows, 128), F32),
            jax.ShapeDtypeStruct((rows, w_output.shape[1]), BF),
        ),
        in_specs=[smem_spec()] + [vmem_spec()] * 4,
        out_specs=(vmem_spec(),) * 3,
        compiler_params=pltpu.CompilerParams(vmem_limit_bytes=48 * MIB),
        name="attend",
    )(scal, query, key, value, w_output)


def turn(values, first):
    wide = values.shape[1]
    half = HEAD_SIZE // 2
    return jnp.where(
        first, -pltpu.roll(values, wide - half, 1), pltpu.roll(values, half, 1)
    )


def attend_back_kernel(
    scal_ref, q_ref, k_ref, v_ref, lse_ref, att_ref, low_ref, wo_ref, cos_ref, sin_ref,
    dq_ref, dk_ref, dv_ref, dwo_ref,
):
    rows, wide = q_ref.shape
    heads = wide // HEAD_SIZE
    sharing = q_ref.shape[1] // k_ref.shape[1]
    scale = HEAD_SIZE**-0.5
    low = low_ref[...]
    dwo_ref[...] = matmul_tn(att_ref[...], low)
    att_grad = matmul_nt(low, wo_ref[...]).astype(BF)
    allowed = allowed_pairs(scal_ref, rows)
    query_parts, key_parts, value_parts = [], [], []
    for head in range(heads):
        at = head * HEAD_SIZE
        kv = head // sharing * HEAD_SIZE
        query = q_ref[:, at : at + HEAD_SIZE]
        key = k_ref[:, kv : kv + HEAD_SIZE]
        value = v_ref[:, kv : kv + HEAD_SIZE]
        grad = att_grad[:, at : at + HEAD_SIZE]
        scores = jnp.where(allowed, matmul_nt(query, key) * scale, masked_score)
        probs = jnp.exp(scores - lse_ref[:, head : head + 1])
        prob_grad = matmul_nt(grad, value)
        delta = jnp.sum(probs * prob_grad, axis=1, keepdims=True)
        score_grad = (probs * (prob_grad - delta)).astype(BF)
        query_parts.append(matmul(score_grad, key) * scale)
        key_part = matmul_tn(score_grad, query) * scale
        value_part = matmul_tn(probs.astype(BF), grad)
        if head % sharing == 0:
            key_parts.append(key_part)
            value_parts.append(value_part)
        else:
            key_parts[-1] = key_parts[-1] + key_part
            value_parts[-1] = value_parts[-1] + value_part
    dk_ref[...] = jnp.concatenate(key_parts, axis=1).astype(BF)
    dv_ref[...] = jnp.concatenate(value_parts, axis=1).astype(BF)
    rotated = jnp.concatenate(query_parts, axis=1)
    lane = lax.broadcasted_iota(jnp.int32, (1, wide), 1)
    first = lane % HEAD_SIZE < HEAD_SIZE // 2
    cosines = jnp.concatenate([cos_ref[...]] * (wide // 128), axis=1)
    sines = jnp.concatenate([sin_ref[...]] * (wide // 128), axis=1)
    dq_ref[...] = (rotated * cosines - turn(rotated, first) * sines).astype(BF)


def attend_back(scal, query, key, value, lse, attended, low, w_output, cosines, sines):
    rows, wide = query.shape
    return pl.pallas_call(
        attend_back_kernel,
        out_shape=(
            jax.ShapeDtypeStruct((rows, wide), BF),
            jax.ShapeDtypeStruct(key.shape, BF),
            jax.ShapeDtypeStruct(value.shape, BF),
            jax.ShapeDtypeStruct(w_output.shape, F32),
        ),
        in_specs=[smem_spec()] + [vmem_spec()] * 9,
        out_specs=(vmem_spec(),) * 4,
        compiler_params=pltpu.CompilerParams(vmem_limit_bytes=56 * MIB),
        name="attend_back",
    )(scal, query, key, value, lse, attended, low, w_output, cosines, sines)


MESH = pl.DeviceIdType.MESH
PART = 32
LAG = 3
LINK_COST = pl.CostEstimate(flops=4 * 10**10, bytes_accessed=10**7, transcendentals=0)


def meet(partners):
    barrier = pltpu.get_barrier_semaphore()
    count = 0
    for here, device in partners:
        here = jnp.asarray(here)

        @pl.when(here)
        def _():
            pl.semaphore_signal(barrier, inc=1, device_id=device, device_id_type=MESH)

        count = count + here.astype(jnp.int32)
    pl.semaphore_wait(barrier, count)


def line_partners():
    place = lax.axis_index("tensor")
    last = lax.axis_size("tensor") - 1
    return [(place > 0, {"tensor": place - 1}), (place < last, {"tensor": place + 1})]


class Line:
    def __init__(self, parts, term, from_left, from_right, to_right, to_left, sems):
        self.place = lax.axis_index("tensor")
        self.last = lax.axis_size("tensor") - 1
        self.parts = parts
        self.term = term
        self.from_left, self.from_right = from_left, from_right
        self.to_right, self.to_left = to_right, to_left
        self.sems = sems

    def copy(self, way, at):
        near = jnp.where(self.place < self.last, self.place + 1, self.place - 1)
        far = jnp.where(self.place > 0, self.place - 1, self.place + 1)
        source, target, device = (
            (self.to_right, self.from_left, near) if way == 0 else (self.to_left, self.from_right, far)
        )
        return pltpu.make_async_remote_copy(
            src_ref=source.at[at],
            dst_ref=target.at[at],
            send_sem=self.sems.at[2 * way, at],
            recv_sem=self.sems.at[2 * way + 1, at],
            device_id={"tensor": device},
            device_id_type=MESH,
        )

    def clear(self):
        @pl.when(self.place == 0)
        def _():
            self.from_left[...] = jnp.zeros(self.from_left.shape, self.from_left.dtype)

        @pl.when(self.place == self.last)
        def _():
            self.from_right[...] = jnp.zeros(self.from_right.shape, self.from_right.dtype)

    def step(self, at):
        for way in range(2):
            part = at - LAG * (self.place if way == 0 else self.last - self.place)
            has_source = self.place > 0 if way == 0 else self.place < self.last
            has_target = self.place < self.last if way == 0 else self.place > 0
            arrived = self.from_left if way == 0 else self.from_right
            leaving = self.to_right if way == 0 else self.to_left
            valid = (part >= 0) & (part < self.parts)

            @pl.when(valid & has_source)
            def _():
                self.copy(way, part).wait_recv()

            @pl.when(valid & has_target)
            def _():
                leaving[part] = (self.term(part) + arrived[part].astype(F32)).astype(BF)
                self.copy(way, part).start()

    def total(self, part):
        return self.term(part) + self.from_left[part].astype(F32) + self.from_right[part].astype(F32)

    def drain(self):
        def wait(part, carry):
            @pl.when(self.place < self.last)
            def _():
                self.copy(0, part).wait_send()

            @pl.when(self.place > 0)
            def _():
                self.copy(1, part).wait_send()

            return carry

        lax.fori_loop(0, self.parts, wait, 0)


def line_scratch(parts, width):
    return [pltpu.VMEM((parts, PART, width), BF)] * 4 + [pltpu.SemaphoreType.DMA((4, parts))]


def peer_copy(source, target, sems, at):
    return pltpu.make_async_remote_copy(
        src_ref=source,
        dst_ref=target,
        send_sem=sems.at[0, at],
        recv_sem=sems.at[1, at],
        device_id={"expert": 1 - lax.axis_index("expert")},
        device_id_type=MESH,
    )


def scale_of(values):
    return lax.rsqrt(jnp.mean(values * values, axis=-1, keepdims=True) + epsilon)


def residual_kernel(
    part_ref, x_ref, gain_ref, res_ref, n_ref, from_left, from_right, to_right, to_left, sems, peer_sems
):
    parts = part_ref.shape[0]
    line = Line(parts, lambda at: part_ref[at].astype(F32), from_left, from_right, to_right, to_left, sems)
    line.clear()
    meet(line_partners() + [(True, {"expert": 1 - lax.axis_index("expert")})])

    def body(at, carry):
        line.step(at)
        part = at - LAG * line.last

        @pl.when(part >= 0)
        def _():
            residual = x_ref[part].astype(F32) + line.total(part)
            res_ref[part] = residual
            unit = residual * scale_of(residual)
            n_ref[0, part] = (unit * gain_ref[...]).astype(BF)
            peer_copy(n_ref.at[0, part], n_ref.at[1, part], peer_sems, part).start()

        return carry

    lax.fori_loop(0, parts + LAG * line.last, body, 0)
    line.drain()

    def wait(part, carry):
        peer_copy(n_ref.at[0, part], n_ref.at[1, part], peer_sems, part).wait()
        return carry

    lax.fori_loop(0, parts, wait, 0)


def residual_norm(part, block_input, gain):
    rows, width = block_input.shape
    parts = rows // PART
    residual, normed = pl.pallas_call(
        residual_kernel,
        out_shape=(
            jax.ShapeDtypeStruct((parts, PART, width), F32),
            jax.ShapeDtypeStruct((2, parts, PART, width), BF),
        ),
        in_specs=[vmem_spec()] * 3,
        out_specs=(vmem_spec(),) * 2,
        scratch_shapes=line_scratch(parts, width) + [pltpu.SemaphoreType.DMA((2, parts))],
        compiler_params=pltpu.CompilerParams(
            collective_id=0, has_side_effects=True, vmem_limit_bytes=40 * MIB
        ),
        cost_estimate=LINK_COST,
        name="residual_norm",
    )(part.reshape(parts, PART, width), block_input.reshape(parts, PART, width), gain[None])
    return residual, normed.reshape(2 * rows, width)


UNIT = 512


def residual_grad_kernel(
    back_ref, route_ref, res_ref, up_ref, gain_ref, wr_ref, marks_ref,
    far_n, far_g, far_on, far_og, wg_hbm, wu_hbm, wd_hbm, pg_hbm, pu_hbm, pd_hbm,
    grad_ref, low_ref, second_ref, route_out, sg_hbm, su_hbm, sd_hbm,
    from_left, from_right, to_right, to_left, sems, peer_sems, arrived, terms,
    tokens_n, tokens_g, turned, kept_gates, gates_w, ups_w, downs_w, pair_g, pair_u, pair_d, ght, dgs, dus,
    row_sems, weight_sems, pair_sems, out_sems,
):
    parts = back_ref.shape[1]
    core = lax.rem(lax.axis_index("dp"), 2)
    side = lax.axis_index("expert")
    groups, group, width, hid = pair_g.shape
    experts_all = wr_ref.shape[1]
    line = Line(parts + 1, lambda at: terms[at], from_left, from_right, to_right, to_left, sems)
    line.clear()
    meet(line_partners() + [(True, {"expert": 1 - side})])

    def send(part, carry):
        peer_copy(back_ref.at[1, part], arrived.at[part], peer_sems, part).start()
        return carry

    lax.fori_loop(0, parts, send, 0)

    half = tokens_n.shape[0] // 2
    row_copies = [
        pltpu.make_async_copy(source, target.at[pl.ds(place * half, half), :], row_sems.at[kind, place])
        for place, pair in enumerate(((far_n, far_g), (far_on, far_og)))
        for kind, (source, target) in enumerate(zip(pair, (tokens_n, tokens_g)))
    ]
    weight_copies, pair_copies, out_copies = [], [], []
    for at in range(groups):
        first = core * (groups * group) + at * group
        weight_copies.append(
            [
                pltpu.make_async_copy(
                    source.at[first + expert],
                    target.at[at, :, pl.ds(expert * hid, hid)],
                    weight_sems.at[at, kind, expert],
                )
                for expert in range(group)
                for kind, (source, target) in enumerate(((wg_hbm, gates_w), (wu_hbm, ups_w)))
            ]
            + [pltpu.make_async_copy(wd_hbm.at[pl.ds(first, group)], downs_w.at[at], weight_sems.at[at, 2, 0])]
        )
        sources = (pg_hbm, pu_hbm, pd_hbm)
        held = (pair_g, pair_u, pair_d)
        targets = (sg_hbm, su_hbm, sd_hbm)
        pair_copies.append(
            [
                pltpu.make_async_copy(sources[kind].at[pl.ds(at * group, group)], held[kind].at[at], pair_sems.at[at, kind])
                for kind in range(3)
            ]
        )
        out_copies.append(
            [
                pltpu.make_async_copy(held[kind].at[at], targets[kind].at[pl.ds(at * group, group)], out_sems.at[at, kind])
                for kind in range(3)
            ]
        )
    for copy in row_copies[:2] + weight_copies[0] + row_copies[2:] + pair_copies[0] + weight_copies[1] + pair_copies[1]:
        copy.start()
    terms[parts] = route_ref[...]
    second_ref[...] = jnp.zeros(second_ref.shape, F32)
    chunks = 2 * half // UNIT
    units = chunks + 3

    def compute(at):
        for where in range(groups):
            unit = at - where * units

            @pl.when(unit == 0)
            def _():
                for copy in weight_copies[where]:
                    copy.wait()

            if where == 0:

                @pl.when(unit == 0)
                def _():
                    for copy in row_copies[:2]:
                        copy.wait()

                @pl.when(unit == half // UNIT)
                def _():
                    for copy in row_copies[2:]:
                        copy.wait()

            @pl.when(unit == chunks)
            def _():
                for copy in pair_copies[where]:
                    copy.wait()

        where = at // units
        unit = at - where * units

        @pl.when(unit < chunks)
        def _():
            place = pl.multiple_of(unit * UNIT, UNIT)
            rows = pl.ds(place, UNIT)
            token = tokens_n[rows, :]

            @pl.when(where == 0)
            def _():
                kept_gates[rows, :] = route_gates(token, marks_ref[rows, :], wr_ref[...])[1]
                turned[:, rows] = token.T

            down = downs_w[where].reshape(group * hid, width)
            column = side * (experts_all // 2) + (core * groups + where) * group
            pulled = matmul_nt(tokens_g[rows, :], down)
            weight = spread_gates(kept_gates[rows, :], column, group, hid)
            _, gated, gate_grad, up_grad = hidden_terms(token, pulled, weight, gates_w[where], ups_w[where])
            ght[:, rows] = gated.T
            dgs[rows, :] = gate_grad
            dus[rows, :] = up_grad

        @pl.when((unit >= chunks) & (unit < chunks + 2))
        def _():
            rows = pl.ds(pl.multiple_of((unit - chunks) * (width // 2), width // 2), width // 2)
            for source, held in ((dgs, pair_g), (dus, pair_u)):
                part = matmul(turned[rows, :], source[...])
                for expert in range(group):
                    more = part[:, expert * hid : (expert + 1) * hid]
                    held[where, expert, rows, :] = (held[where, expert, rows, :].astype(F32) + more).astype(BF)

        @pl.when(unit == chunks + 2)
        def _():
            part = matmul(ght[...], tokens_g[...])
            for expert in range(group):
                more = part[expert * hid : (expert + 1) * hid, :]
                pair_d[where, expert] = (pair_d[where, expert].astype(F32) + more).astype(BF)

        for where in range(groups):

            @pl.when(at == where * units + units - 1)
            def _():
                for copy in out_copies[where]:
                    copy.start()

    def body(at, carry):
        @pl.when(at < parts)
        def _():
            peer_copy(back_ref.at[1, at], arrived.at[at], peer_sems, at).wait_recv()
            terms[at] = back_ref[0, at].astype(F32) + arrived[at].astype(F32)

        line.step(at)
        part = at - LAG * line.last

        @pl.when((part >= 0) & (part < parts))
        def _():
            grad = line.total(part)
            residual = res_ref[part]
            scale = scale_of(residual)
            unit = residual * scale
            second_ref[...] += jnp.sum(grad * unit, axis=0, keepdims=True)
            result = up_ref[part].astype(F32) + norm_back(grad, unit, scale, gain_ref[...])
            grad_ref[part] = result
            low_ref[part] = result.astype(BF)

        @pl.when((at >= FIRST_UNIT) & (at < FIRST_UNIT + groups * units))
        def _():
            compute(at - FIRST_UNIT)

        return carry

    lax.fori_loop(0, parts + 1 + LAG * line.last, body, 0)
    route_out[...] = line.total(parts)
    line.drain()

    def wait(part, carry):
        peer_copy(back_ref.at[1, part], arrived.at[part], peer_sems, part).wait_send()
        return carry

    lax.fori_loop(0, parts, wait, 0)
    for copies in out_copies:
        for copy in copies:
            copy.wait()


FIRST_UNIT = 3


def residual_gradient(back, route, residual, upstream, gain, w_router, marks, far_rows, w_gate, w_up, w_down, pairs):
    rows, width = upstream.shape
    parts = rows // PART
    half, _, hid = pairs[0].shape
    groups = half // GROUP
    tokens = 2 * far_rows[0].shape[0]
    any_spec = pl.BlockSpec(memory_space=pl.ANY)
    grad, low, second, route, *sums = pl.pallas_call(
        residual_grad_kernel,
        out_shape=[
            jax.ShapeDtypeStruct((parts, PART, width), F32),
            jax.ShapeDtypeStruct((parts, PART, width), BF),
            jax.ShapeDtypeStruct((1, width), F32),
            jax.ShapeDtypeStruct(route.shape, F32),
        ]
        + [jax.ShapeDtypeStruct(pair.shape, BF) for pair in pairs],
        in_specs=[vmem_spec()] * 7 + [any_spec] * 10,
        out_specs=[vmem_spec()] * 4 + [any_spec] * 3,
        scratch_shapes=line_scratch(parts + 1, width)
        + [
            pltpu.SemaphoreType.DMA((2, parts)),
            pltpu.VMEM((parts, PART, width), BF),
            pltpu.VMEM((parts + 1, PART, width), F32),
            pltpu.VMEM((tokens, width), BF),
            pltpu.VMEM((tokens, width), BF),
            pltpu.VMEM((width, tokens), BF),
            pltpu.VMEM((tokens, w_router.shape[1]), F32),
            pltpu.VMEM((groups, width, GROUP * hid), BF),
            pltpu.VMEM((groups, width, GROUP * hid), BF),
            pltpu.VMEM((groups, GROUP, hid, width), BF),
            pltpu.VMEM((groups, GROUP, width, hid), BF),
            pltpu.VMEM((groups, GROUP, width, hid), BF),
            pltpu.VMEM((groups, GROUP, hid, width), BF),
            pltpu.VMEM((GROUP * hid, tokens), BF),
            pltpu.VMEM((tokens, GROUP * hid), BF),
            pltpu.VMEM((tokens, GROUP * hid), BF),
            pltpu.SemaphoreType.DMA((2, 2)),
            pltpu.SemaphoreType.DMA((groups, 3, GROUP)),
            pltpu.SemaphoreType.DMA((groups, 3)),
            pltpu.SemaphoreType.DMA((groups, 3)),
        ],
        compiler_params=pltpu.CompilerParams(
            collective_id=1, has_side_effects=True, vmem_limit_bytes=60 * MIB
        ),
        cost_estimate=LINK_COST,
        name="residual_grad",
    )(
        back.reshape(2, parts, PART, width), route, residual, upstream.reshape(parts, PART, width), gain[None],
        w_router, marks, *far_rows, w_gate, w_up, w_down, *pairs,
    )
    return grad, low.reshape(rows, width), second[0], route, sums


def input_grad_kernel(
    part_ref, x_ref, res_grad_ref, gain_ref, grad_ref, first_ref, from_left, from_right, to_right, to_left, sems
):
    parts = part_ref.shape[0]
    line = Line(parts, lambda at: part_ref[at], from_left, from_right, to_right, to_left, sems)
    line.clear()
    meet(line_partners())
    first_ref[...] = jnp.zeros(first_ref.shape, F32)

    def body(at, carry):
        line.step(at)
        part = at - LAG * line.last

        @pl.when(part >= 0)
        def _():
            grad = line.total(part)
            values = x_ref[part].astype(F32)
            scale = scale_of(values)
            unit = values * scale
            first_ref[...] += jnp.sum(grad * unit, axis=0, keepdims=True)
            grad_ref[part] = (res_grad_ref[part] + norm_back(grad, unit, scale, gain_ref[...])).astype(BF)

        return carry

    lax.fori_loop(0, parts + LAG * line.last, body, 0)
    line.drain()


def input_gradient(first_part, block_input, residual_grad, gain):
    rows, width = block_input.shape
    parts = rows // PART
    grad, first = pl.pallas_call(
        input_grad_kernel,
        out_shape=(
            jax.ShapeDtypeStruct((parts, PART, width), BF),
            jax.ShapeDtypeStruct((1, width), F32),
        ),
        in_specs=[vmem_spec()] * 4,
        out_specs=(vmem_spec(),) * 2,
        scratch_shapes=line_scratch(parts, width),
        compiler_params=pltpu.CompilerParams(
            collective_id=2, has_side_effects=True, vmem_limit_bytes=40 * MIB
        ),
        cost_estimate=LINK_COST,
        name="input_grad",
    )(first_part.reshape(parts, PART, width), block_input.reshape(parts, PART, width), residual_grad, gain[None])
    return grad.reshape(rows, width), first[0]


CHUNK = 512
GROUP = 4


def route_gates(token, marks, w_router):
    experts_all = w_router.shape[1]
    chosen = marks[:, :experts_all].astype(F32)
    kept = marks[:, experts_all:].astype(F32)
    logits = jnp.where(chosen > 0.0, matmul(token, w_router), masked_score)
    raised = jnp.exp(logits - jnp.max(logits, axis=1, keepdims=True)) * chosen
    gate = raised / jnp.sum(raised, axis=1, keepdims=True)
    return gate, gate * kept


def hidden_terms(token, pulled, weight, gate_weights, up_weights):
    gate_in = matmul(token, gate_weights)
    up_in = matmul(token, up_weights)
    sig = 0.5 * jnp.tanh(0.5 * gate_in) + 0.5
    silu = gate_in * sig
    hidden = silu * up_in
    gated = (hidden * weight).astype(BF)
    scaled = pulled * weight
    up_grad = (scaled * silu).astype(BF)
    gate_grad = (scaled * up_in * (sig + silu * (1.0 - sig))).astype(BF)
    return hidden, gated, gate_grad, up_grad


def spread_gates(kept, column, group, hid):
    lane = lax.broadcasted_iota(jnp.int32, (1, kept.shape[1]), 1)
    weights = []
    for expert in range(group):
        gate = jnp.sum(jnp.where(lane == column + expert, kept, 0.0), axis=1, keepdims=True)
        weights.append(jnp.broadcast_to(gate, (kept.shape[0], hid)))
    return jnp.concatenate(weights, axis=1)


def expert_kernel(
    n_ref, g_ref, marks_ref, wr_ref, n_hbm, wg_ref, wu_ref, wd_ref,
    dwg_ref, dwu_ref, dwd_ref, mix_ref, back_ref, route_ref, far_ref, far_other_ref,
    gates, kept_gates, gate_grads, mix, back, nt, wgs, wus, ght, dgs, dus,
    out_g, out_u, out_d, in_g, in_u, in_d, sems, far_sems,
):
    step = pl.program_id(0)
    steps = pl.num_programs(0) // 2
    side = lax.axis_index("expert")
    dp = lax.axis_index("dp")
    core = lax.rem(dp, 2)
    other = {"dp": dp + 1 - 2 * core}
    beside = {"dp": lax.rem(dp + 2, 4)}
    tokens, width = n_ref.shape
    experts_all = wr_ref.shape[1]
    group, _, hid = wg_ref.shape
    chunks = tokens // CHUNK
    lane = lax.broadcasted_iota(jnp.int32, (1, experts_all), 1)

    def copies(slot):
        return [
            pltpu.make_async_remote_copy(
                src_ref=source.at[slot], dst_ref=target.at[slot],
                send_sem=sems.at[0, kind, slot], recv_sem=sems.at[1, kind, slot],
                device_id=other, device_id_type=MESH,
            )
            for kind, (source, target) in enumerate(((out_g, in_g), (out_u, in_u), (out_d, in_d)))
        ]

    def far_copy(kind, source, target, device):
        return pltpu.make_async_remote_copy(
            src_ref=source, dst_ref=target, send_sem=far_sems.at[0, kind], recv_sem=far_sems.at[1, kind],
            device_id=device, device_id_type=MESH,
        )

    cross = far_copy(0, n_hbm, far_ref, beside)
    share = far_copy(1, far_ref, far_other_ref, other)

    @pl.when(step == 0)
    def _():
        meet([(True, other), (True, beside)])
        cross.start()

        def start(at, carry):
            rows = pl.ds(pl.multiple_of(at * CHUNK, CHUNK), CHUNK)
            gate, kept_gate = route_gates(n_ref[rows, :], marks_ref[rows, :], wr_ref[...])
            gates[rows, :] = gate
            kept_gates[rows, :] = kept_gate
            mix[rows, :] = jnp.zeros((CHUNK, width), F32)
            back[rows, :] = jnp.zeros((CHUNK, width), F32)
            gate_grads[rows, :] = jnp.zeros((CHUNK, experts_all), F32)
            return carry

        lax.fori_loop(0, chunks, start, 0)
        for at in range(chunks):
            nt[:, at * CHUNK : (at + 1) * CHUNK] = n_ref[at * CHUNK : (at + 1) * CHUNK, :].T

    for expert in range(group):
        wgs[:, expert * hid : (expert + 1) * hid] = wg_ref[expert]
        wus[:, expert * hid : (expert + 1) * hid] = wu_ref[expert]
    first = step < steps
    block = jnp.where(first, (1 - core) * steps + step, core * steps + step - steps)
    column = side * (experts_all // 2) + block * group

    for at in range(chunks):
        rows = slice(at * CHUNK, (at + 1) * CHUNK)
        token = n_ref[rows, :]
        down = wd_ref[...].reshape(group * hid, width)
        pulled = matmul_nt(g_ref[rows, :], down)
        weight = spread_gates(kept_gates[rows, :], column, group, hid)
        hidden, gated, gate_grad, up_grad = hidden_terms(token, pulled, weight, wgs[...], wus[...])
        products = hidden * pulled
        grads = gate_grads[rows, :]
        for expert in range(group):
            product = jnp.sum(products[:, expert * hid : (expert + 1) * hid], axis=1, keepdims=True)
            grads = grads + jnp.where(lane == column + expert, product, 0.0)
        gate_grads[rows, :] = grads
        ght[:, rows] = gated.T
        dgs[rows, :] = gate_grad
        dus[rows, :] = up_grad
        mix[rows, :] += matmul(gated, down)
        back[rows, :] += matmul_nt(gate_grad, wgs[...]) + matmul_nt(up_grad, wus[...])

    def weight_grads(store_rows, store_down):
        for at in range(width // CHUNK):
            rows = slice(at * CHUNK, (at + 1) * CHUNK)
            turned = nt[rows, :]
            gate_part = matmul(turned, dgs[...])
            up_part = matmul(turned, dus[...])
            for expert in range(group):
                inner = slice(expert * hid, (expert + 1) * hid)
                store_rows(expert, rows, gate_part[:, inner], up_part[:, inner])
        down_part = matmul(ght[...], g_ref[...])
        for expert in range(group):
            store_down(expert, down_part[expert * hid : (expert + 1) * hid, :])

    @pl.when(first)
    def _():
        def store_rows(expert, rows, gate_part, up_part):
            out_g[step, expert, rows, :] = gate_part.astype(BF)
            out_u[step, expert, rows, :] = up_part.astype(BF)

        def store_down(expert, part):
            out_d[step, expert] = part.astype(BF)

        weight_grads(store_rows, store_down)
        for copy in copies(step):
            copy.start()

    @pl.when(step >= steps)
    def _():
        slot = step - steps
        for copy in copies(slot):
            copy.wait_recv()

        def store_rows(expert, rows, gate_part, up_part):
            dwg_ref[expert, rows, :] = (gate_part + in_g[slot, expert, rows, :].astype(F32)).astype(BF)
            dwu_ref[expert, rows, :] = (up_part + in_u[slot, expert, rows, :].astype(F32)).astype(BF)

        def store_down(expert, part):
            dwd_ref[expert] = (part + in_d[slot, expert].astype(F32)).astype(BF)

        weight_grads(store_rows, store_down)
        for copy in copies(slot):
            copy.wait_send()

    @pl.when(step == 2 * steps - 1)
    def _():
        cross.wait_recv()
        share.start()
        route_ref[...] = jnp.zeros(route_ref.shape, F32)

        def finish(at, carry):
            rows = pl.ds(pl.multiple_of(at * CHUNK, CHUNK), CHUNK)
            mix_ref[rows, :] = mix[rows, :].astype(BF)
            grads = gate_grads[rows, :] * kept_gates[rows, :]
            chosen_grad = grads - gates[rows, :] * jnp.sum(grads, axis=1, keepdims=True)
            low = chosen_grad.astype(BF)
            back_ref[rows, :] = (back[rows, :] + matmul_nt(low, wr_ref[...])).astype(BF)
            route_ref[...] += matmul_tn(low, n_ref[rows, :])
            return carry

        lax.fori_loop(0, chunks, finish, 0)
        cross.wait_send()
        share.wait()


def experts(normed, upstream, marks, w_router, w_gate, w_up, w_down):
    tokens, width = normed.shape
    count, _, hid = w_gate.shape
    half = count // 2
    steps = half // GROUP
    experts_all = w_router.shape[1]
    once = pl.Buffered(1)
    whole = lambda step: (0, 0)

    def picked(step):
        core = lax.rem(lax.axis_index("dp"), 2)
        return (jnp.where(step < steps, (1 - core) * steps + step, core * steps + step - steps), 0, 0)

    own = lambda step: (jnp.maximum(step - steps, 0), 0, 0)
    args = [normed, upstream, marks, w_router]
    specs = [pl.BlockSpec(array.shape, whole, pipeline_mode=once) for array in args]
    args += [normed]
    specs += [pl.BlockSpec(memory_space=pl.ANY)]
    up_block, down_block = (GROUP, width, hid), (GROUP, hid, width)
    specs += [pl.BlockSpec(up_block, picked), pl.BlockSpec(up_block, picked), pl.BlockSpec(down_block, picked)]
    gate_scratch = pltpu.VMEM((tokens, experts_all), F32)
    rows_scratch = pltpu.VMEM((tokens, width), F32)
    swap_scratch = [
        pltpu.VMEM((steps,) + up_block, BF),
        pltpu.VMEM((steps,) + up_block, BF),
        pltpu.VMEM((steps,) + down_block, BF),
    ]
    return pl.pallas_call(
        expert_kernel,
        out_shape=[
            jax.ShapeDtypeStruct((half, width, hid), BF),
            jax.ShapeDtypeStruct((half, width, hid), BF),
            jax.ShapeDtypeStruct((half, hid, width), BF),
            jax.ShapeDtypeStruct((tokens, width), BF),
            jax.ShapeDtypeStruct((tokens, width), BF),
            jax.ShapeDtypeStruct((experts_all, width), F32),
            jax.ShapeDtypeStruct((tokens, width), BF),
            jax.ShapeDtypeStruct((tokens, width), BF),
        ],
        grid=(2 * steps,),
        in_specs=specs,
        out_specs=[
            pl.BlockSpec(up_block, own),
            pl.BlockSpec(up_block, own),
            pl.BlockSpec(down_block, own),
            pl.BlockSpec((tokens, width), whole, pipeline_mode=once),
            pl.BlockSpec((tokens, width), whole, pipeline_mode=once),
            pl.BlockSpec((experts_all, width), whole, pipeline_mode=once),
            pl.BlockSpec(memory_space=pl.ANY),
            pl.BlockSpec(memory_space=pl.ANY),
        ],
        scratch_shapes=[
            gate_scratch, gate_scratch, gate_scratch, rows_scratch, rows_scratch,
            pltpu.VMEM((width, tokens), BF),
            pltpu.VMEM((width, GROUP * hid), BF),
            pltpu.VMEM((width, GROUP * hid), BF),
            pltpu.VMEM((GROUP * hid, tokens), BF),
            pltpu.VMEM((tokens, GROUP * hid), BF),
            pltpu.VMEM((tokens, GROUP * hid), BF),
        ]
        + swap_scratch
        + swap_scratch
        + [pltpu.SemaphoreType.DMA((2, 3, steps)), pltpu.SemaphoreType.DMA((2, 2))],
        compiler_params=pltpu.CompilerParams(
            dimension_semantics=("arbitrary",), collective_id=3, has_side_effects=True, vmem_limit_bytes=60 * MIB
        ),
        cost_estimate=pl.CostEstimate(
            flops=18 * tokens * width * count * hid,
            bytes_accessed=12 * count * width * hid,
            transcendentals=tokens * count * hid,
        ),
        name="experts",
    )(*args, w_gate, w_up, w_down)


def widen_kernel(core_ref, mine_ref, other_ref, out_ref):
    here = pl.program_id(0) == 0

    @pl.when(here)
    def _():
        out_ref[...] = mine_ref[...].astype(F32)

    @pl.when(jnp.logical_not(here))
    def _():
        out_ref[...] = other_ref[...].astype(F32)


def widen(core, mine, other):
    half, high, wide = mine.shape
    step = 4
    count = half // step
    block = (step, high, wide)
    return pl.pallas_call(
        widen_kernel,
        out_shape=jax.ShapeDtypeStruct((2 * half, high, wide), F32),
        grid_spec=pltpu.PrefetchScalarGridSpec(
            num_scalar_prefetch=1,
            grid=(2, count),
            in_specs=[
                pl.BlockSpec(block, lambda part, at, core: (jnp.where(part == 0, at, count - 1), 0, 0)),
                pl.BlockSpec(block, lambda part, at, core: (jnp.where(part == 0, 0, at), 0, 0)),
            ],
            out_specs=pl.BlockSpec(
                block, lambda part, at, core: (jnp.where(part == 0, core[0], 1 - core[0]) * count + at, 0, 0)
            ),
        ),
        compiler_params=pltpu.CompilerParams(vmem_limit_bytes=32 * MIB),
        cost_estimate=pl.CostEstimate(flops=2 * half * high * wide, bytes_accessed=12 * half * high * wide, transcendentals=0),
        name="widen",
    )(core, mine, other)


def swap(array, axis, bit):
    size = lax.axis_size(axis)
    return lax.ppermute(array, axis, [(at, at ^ bit) for at in range(size)])


def fast_device(
    block_input, first_gain, w_query, key_weight, value_weight, w_output, second_gain, w_router,
    w_gate, w_up, w_down, expert_ids, slot_index, piece_start_offsets, upstream,
):
    rows, width = block_input.shape
    local_heads = w_query.shape[1] // HEAD_SIZE
    local_kv = key_weight.shape[1] // HEAD_SIZE
    experts_all = w_router.shape[1]
    side = lax.axis_index("expert")
    core = lax.axis_index("dp") % 2
    feature_start = lax.axis_index("tensor") * (width // 4)
    scal = jnp.concatenate([side[None].astype(jnp.int32), piece_start_offsets[0]])

    axis_row = jnp.arange(experts_all, dtype=jnp.int32)[None, None, :]
    hits = (expert_ids[:, :, None] == axis_row)
    chosen = jnp.sum(hits.astype(F32), axis=1)
    kept = jnp.sum((hits & (slot_index >= 0)[:, :, None]).astype(F32), axis=1)
    marks = jnp.concatenate([chosen, kept], axis=1).astype(BF)
    marks = jnp.concatenate([marks, swap(marks, "expert", 1)], axis=0)
    far_marks = swap(marks, "dp", 2)
    far_marks = jnp.concatenate([far_marks, swap(far_marks, "dp", 1)], axis=0)
    upstream_all = jnp.concatenate([upstream, swap(upstream, "expert", 1)], axis=0)
    far_up = swap(upstream_all, "dp", 2)
    far_other_up = swap(far_up, "dp", 1)

    positions = side * rows + jnp.arange(rows, dtype=jnp.int32)
    cosine_table, sine_table = rope_tables(positions)
    cosines = jnp.tile(cosine_table, (1, 4))
    sines = jnp.tile(sine_table, (1, 4))
    inputs = block_input.astype(F32)
    first_scale = norm_scale(inputs)
    first_unit = inputs * first_scale
    first_normed = (first_unit * first_gain).astype(BF)
    query_rot = apply_rotary(
        matmul(first_normed, w_query).reshape(rows, local_heads, HEAD_SIZE), cosine_table, sine_table
    ).astype(BF).reshape(rows, local_heads * HEAD_SIZE)
    key_rot = apply_rotary(
        matmul(first_normed, key_weight).reshape(rows, local_kv, HEAD_SIZE), cosine_table, sine_table
    ).astype(BF).reshape(rows, local_kv * HEAD_SIZE)
    value_low = matmul(first_normed, value_weight).astype(BF)
    both = jnp.concatenate([key_rot, value_low], axis=1)
    both = jnp.concatenate([both, swap(both, "expert", 1)], axis=0)
    keys, values = both[:, : local_kv * HEAD_SIZE], both[:, local_kv * HEAD_SIZE :]

    attended, lse, part = attend(scal, query_rot, keys, values, w_output)
    residual, normed_all = residual_norm(part, block_input, second_gain)

    normed_all, far_up, far_other_up, far_marks = lax.optimization_barrier(
        (normed_all, far_up, far_other_up, far_marks)
    )
    dwg, dwu, dwd, mix, back, route, far_normed, far_other_normed = experts(
        normed_all, upstream_all, marks, w_router, w_gate, w_up, w_down
    )
    residual_grad, residual_low, grad_second, route, sums = residual_gradient(
        back, route, residual, upstream, second_gain, w_router, far_marks,
        (far_normed, far_up, far_other_normed, far_other_up), w_gate, w_up, w_down, (dwg, dwu, dwd),
    )

    query_grad, dk, dv, grad_output = attend_back(
        scal, query_rot, keys, values, lse, attended, residual_low, w_output, cosines, sines
    )
    dboth = jnp.concatenate([dk, dv], axis=1)
    dboth = dboth[:rows].astype(F32) + swap(dboth[rows:], "expert", 1).astype(F32)
    key_back, value_back = dboth[:, : local_kv * HEAD_SIZE], dboth[:, local_kv * HEAD_SIZE :]
    key_grad = unrotate(
        key_back.reshape(rows, local_kv, HEAD_SIZE), cosine_table, sine_table
    ).astype(BF).reshape(rows, local_kv * HEAD_SIZE)
    value_grad = value_back.astype(BF)
    grad_query = matmul_tn(first_normed, query_grad)
    grad_key = matmul_tn(first_normed, key_grad)
    grad_value = matmul_tn(first_normed, value_grad)
    first_part = (
        matmul_nt(query_grad, w_query) + matmul_nt(key_grad, key_weight) + matmul_nt(value_grad, value_weight)
    )
    grad_input, grad_first = input_gradient(first_part, block_input, residual_grad, first_gain)
    mix, grad_input = lax.optimization_barrier((mix, grad_input))
    mixed = lax.psum_scatter(mix, "tensor", scatter_dimension=1, tiled=True)
    mixed = mixed[:rows].astype(F32) + swap(mixed[rows:], "expert", 1).astype(F32)
    block_output = (
        lax.dynamic_slice_in_dim(residual.reshape(rows, width), feature_start, width // 4, 1) + mixed
    ).astype(BF)

    core_row = core[None].astype(jnp.int32)
    expert_sums = [widen(core_row, item, swap(item, "dp", 1)) for item in sums]
    early = lax.psum((grad_output.astype(BF), route.astype(BF), grad_second.astype(BF)), ("dp", "expert"))
    late = lax.psum(
        (grad_query.astype(BF), grad_key.astype(BF), grad_value.astype(BF), grad_first.astype(BF)), ("dp", "expert")
    )
    early = [item.astype(F32) for item in early]
    late = [item.astype(F32) for item in late]
    return (
        block_output, grad_input, late[3], late[0], late[1], late[2], early[0], early[2], early[1].T,
        expert_sums[0], expert_sums[1], expert_sums[2],
    )


def solution(mesh):
    fast = mesh.shape["expert"] == 2 and mesh.shape["dp"] == 4 and mesh.shape["tensor"] == 4
    placed = (
        P(("dp", "expert"), None),
        P(),
        P(None, "tensor"),
        P(None, "tensor"),
        P(None, "tensor"),
        P("tensor", None),
        P(),
        P(),
        P("expert", None, "tensor"),
        P("expert", None, "tensor"),
        P("expert", "tensor", None),
        P(("dp", "expert"), None),
        P(("dp", "expert"), None),
        P("dp", None),
        P(("dp", "expert"), None),
    )
    return jax.shard_map(
        fast_device if fast else general_device,
        mesh=mesh,
        in_specs=placed,
        out_specs=(
            P(("dp", "expert"), "tensor"),
            P(("dp", "expert"), None),
            P(),
            P(None, "tensor"),
            P(None, "tensor"),
            P(None, "tensor"),
            P("tensor", None),
            P(),
            P(),
            P("expert", None, "tensor"),
            P("expert", None, "tensor"),
            P("expert", "tensor", None),
        ),
        check_vma=False,
    )
```

```python
import functools
import math

import jax
import jax.numpy as jnp
from jax import lax
from jax.experimental import pallas as pl
from jax.experimental.pallas import tpu as pltpu
from jax.sharding import PartitionSpec as P

HEAD_SIZE = 64
TOPK = 8
PIC = 256


epsilon = 1e-06
rope_base = 10000.0
masked_score = -1e30


def rope_tables(positions):
    steps = jnp.arange(HEAD_SIZE // 2, dtype=jnp.float32)
    inverse = jnp.exp(steps * (-2.0 * math.log(rope_base) / HEAD_SIZE))
    angle = positions.astype(jnp.float32)[:, None] * inverse[None, :]
    return (jnp.cos(angle), jnp.sin(angle))


def apply_rotary(values, cosine_table, sine_table):
    half = values.shape[-1] // 2
    first = values[..., :half]
    second = values[..., half:]
    cosine_table = cosine_table[:, None, :]
    sine_table = sine_table[:, None, :]
    return jnp.concatenate(
        [first * cosine_table - second * sine_table, second * cosine_table + first * sine_table],
        axis=-1,
    )


def unrotate(values, cosine_table, sine_table):
    half = values.shape[-1] // 2
    first = values[..., :half]
    second = values[..., half:]
    cosine_table = cosine_table[:, None, :]
    sine_table = sine_table[:, None, :]
    return jnp.concatenate(
        [first * cosine_table + second * sine_table, second * cosine_table - first * sine_table],
        axis=-1,
    )


def piece_ids(positions, offsets):
    span = 2 * PIC
    window = positions // span
    within = positions - window * span
    count = offsets.shape[0]
    match = window[:, None] == jnp.arange(count, dtype=jnp.int32)[None, :]
    start = jnp.sum(jnp.where(match, offsets[None, :], 0), axis=1)
    inside = (window < count) & (within >= start) & (within < start + PIC)
    return jnp.where(inside, window, -1)


def matmul(left, right):
    return jnp.dot(left, right, preferred_element_type=jnp.float32)


def matmul_nt(left, right):
    return lax.dot_general(
        left, right, (((1,), (1,)), ((), ())), preferred_element_type=jnp.float32
    )


def matmul_tn(left, right):
    return lax.dot_general(
        left, right, (((0,), (0,)), ((), ())), preferred_element_type=jnp.float32
    )


def norm_scale(values):
    return lax.rsqrt(jnp.mean(values * values, axis=-1, keepdims=True) + epsilon)


def norm_back(grad, unit, scale, gain):
    weighted = grad * gain
    return scale * (weighted - unit * jnp.mean(weighted * unit, axis=-1, keepdims=True))


def general_device(
    block_input,
    first_gain,
    w_query,
    key_weight,
    value_weight,
    w_output,
    second_gain,
    w_router,
    w_gate,
    w_up,
    w_down,
    expert_ids,
    slot_index,
    piece_start_offsets,
    upstream,
):
    rows_here = block_input.shape[0]
    width = block_input.shape[1]
    groups = lax.axis_size("expert")
    length = rows_here * groups
    local_heads = w_query.shape[1] // HEAD_SIZE
    local_kv = key_weight.shape[1] // HEAD_SIZE
    sharing = local_heads // local_kv
    head_rows = sharing * rows_here
    experts_all = w_router.shape[1]
    capacity = TOPK * rows_here // experts_all
    slots_all = experts_all * capacity
    score_scale = HEAD_SIZE ** (-0.5)
    positions = lax.axis_index("expert") * rows_here + jnp.arange(rows_here, dtype=jnp.int32)
    cosine_table, sine_table = rope_tables(positions)
    inputs = block_input.astype(jnp.float32)
    first_scale = norm_scale(inputs)
    first_unit = inputs * first_scale
    first_normed = (first_unit * first_gain).astype(jnp.bfloat16)
    query_rot = apply_rotary(
        matmul(first_normed, w_query).reshape(rows_here, local_heads, HEAD_SIZE),
        cosine_table,
        sine_table,
    ).astype(jnp.bfloat16)
    key_rot = (
        apply_rotary(
            matmul(first_normed, key_weight).reshape(rows_here, local_kv, HEAD_SIZE),
            cosine_table,
            sine_table,
        )
        .astype(jnp.bfloat16)
        .reshape(rows_here, local_kv * HEAD_SIZE)
    )
    value_low = matmul(first_normed, value_weight).astype(jnp.bfloat16)
    keys_all, values_all = (
        lax.all_gather(key_rot, "expert", axis=0, tiled=True),
        lax.all_gather(value_low, "expert", axis=0, tiled=True),
    )
    block = min(512, length)
    blocks = length // block

    def by_block(array):
        return array.reshape(blocks, block, local_kv, HEAD_SIZE).transpose(0, 2, 1, 3)

    def by_rows(stacked):
        return stacked.transpose(0, 2, 1, 3).reshape(length, local_kv * HEAD_SIZE)

    def head_major(array):
        return (
            array.reshape(rows_here, local_kv, sharing, HEAD_SIZE)
            .transpose(1, 2, 0, 3)
            .reshape(local_kv, head_rows, HEAD_SIZE)
        )

    def row_major(array):
        return (
            array.reshape(local_kv, sharing, rows_here, HEAD_SIZE)
            .transpose(2, 0, 1, 3)
            .reshape(rows_here, local_heads * HEAD_SIZE)
        )

    key_blocks = by_block(keys_all)
    value_blocks = by_block(values_all)
    block_starts = jnp.arange(blocks, dtype=jnp.int32) * block
    query_heads = head_major(query_rot.reshape(rows_here, local_heads * HEAD_SIZE))
    offsets = piece_start_offsets[0]
    key_pieces = piece_ids(jnp.arange(length, dtype=jnp.int32), offsets)
    query_pieces = jnp.tile(piece_ids(positions, offsets), sharing)
    query_places = jnp.tile(positions, sharing)

    def block_scores(key_block, start):
        places = start + jnp.arange(block, dtype=jnp.int32)
        pieces = lax.dynamic_slice_in_dim(key_pieces, start, block)
        causal = places[None, :] <= query_places[:, None]
        same = (pieces[None, :] == query_pieces[:, None]) & (query_pieces[:, None] >= 0)
        scores = (
            jnp.einsum("hqd,hkd->hqk", query_heads, key_block, preferred_element_type=jnp.float32)
            * score_scale
        )
        return (scores, (causal | same)[None])

    def max_step(carry, operands):
        running_max, running_sum = carry
        key_block, start = operands
        scores, allowed = block_scores(key_block, start)
        scores = jnp.where(allowed, scores, masked_score)
        new_max = jnp.maximum(running_max, jnp.max(scores, axis=-1))
        weights = jnp.where(allowed, jnp.exp(scores - new_max[..., None]), 0.0)
        new_sum = running_sum * jnp.exp(running_max - new_max) + jnp.sum(weights, axis=-1)
        return ((new_max, new_sum), None)

    start_max = jnp.full((local_kv, head_rows), masked_score, jnp.float32)
    start_sum = jnp.zeros((local_kv, head_rows), jnp.float32)
    (row_max, row_sum), _ = lax.scan(max_step, (start_max, start_sum), (key_blocks, block_starts))
    log_total = row_max + jnp.log(row_sum)

    def block_probs(key_block, start):
        scores, allowed = block_scores(key_block, start)
        return jnp.where(allowed, jnp.exp(scores - log_total[..., None]), 0.0)

    def value_step(total, operands):
        key_block, value_block, start = operands
        probs = block_probs(key_block, start).astype(jnp.bfloat16)
        return (
            total
            + jnp.einsum("hqk,hkd->hqd", probs, value_block, preferred_element_type=jnp.float32),
            None,
        )

    mixed_output, _ = lax.scan(
        value_step,
        jnp.zeros((local_kv, head_rows, HEAD_SIZE), jnp.float32),
        (key_blocks, value_blocks, block_starts),
    )
    attended = row_major(mixed_output).astype(jnp.bfloat16)
    attention = lax.psum(matmul(attended, w_output), "tensor")
    residual = inputs + attention
    second_scale = norm_scale(residual)
    second_unit = residual * second_scale
    second_normed = (second_unit * second_gain).astype(jnp.bfloat16)
    logits = matmul(second_normed, w_router)
    chosen = jnp.take_along_axis(logits, expert_ids, axis=1)
    gates = jax.nn.softmax(chosen, axis=-1)
    row_ids = jnp.arange(rows_here, dtype=jnp.int32)
    flat = jnp.where(slot_index >= 0, expert_ids * capacity + slot_index, slots_all)
    selector = (
        jnp.zeros((slots_all, rows_here), jnp.bfloat16)
        .at[flat.reshape(-1), jnp.repeat(row_ids, TOPK)]
        .set(1.0, mode="drop")
    )
    dispatched = (
        matmul(selector, second_normed).astype(jnp.bfloat16).reshape(experts_all, capacity, width)
    )
    expert_rows = lax.all_to_all(dispatched, "expert", split_axis=0, concat_axis=1, tiled=True)
    gate_in = jnp.einsum("ebd,edf->ebf", expert_rows, w_gate, preferred_element_type=jnp.float32)
    up_in = jnp.einsum("ebd,edf->ebf", expert_rows, w_up, preferred_element_type=jnp.float32)
    sigmoid_gate = jax.nn.sigmoid(gate_in)
    silu_gate = gate_in * sigmoid_gate
    hidden = (silu_gate * up_in).astype(jnp.bfloat16)
    partial_out = jnp.einsum("ebf,efd->ebd", hidden, w_down, preferred_element_type=jnp.float32)
    expert_part = lax.psum_scatter(
        partial_out.astype(jnp.bfloat16), "tensor", scatter_dimension=2, tiled=True
    )
    returned = lax.all_to_all(expert_part, "expert", split_axis=1, concat_axis=0, tiled=True)
    quarter = returned.shape[2]
    padded_out = jnp.concatenate(
        [returned.reshape(slots_all, quarter), jnp.zeros((1, quarter), jnp.bfloat16)], axis=0
    )
    feature_start = lax.axis_index("tensor") * quarter
    grad_full = upstream.astype(jnp.float32)
    grad_part = lax.dynamic_slice_in_dim(grad_full, feature_start, quarter, 1)
    mixture = jnp.zeros((rows_here, quarter), jnp.float32)
    gate_terms = []
    for pick in range(TOPK):
        picked = padded_out[flat[:, pick]].astype(jnp.float32)
        mixture = mixture + gates[:, pick : pick + 1] * picked
        gate_terms.append(jnp.sum(grad_part * picked, axis=1))
    gate_part = jnp.stack(gate_terms, axis=1)
    block_output = (lax.dynamic_slice_in_dim(residual, feature_start, quarter, 1) + mixture).astype(
        jnp.bfloat16
    )
    slot_gates = (
        jnp.zeros((slots_all + 1,), jnp.float32)
        .at[flat.reshape(-1)]
        .set(gates.reshape(-1))[:slots_all]
    )
    grad_slots = (
        (matmul(selector, upstream) * slot_gates[:, None])
        .astype(jnp.bfloat16)
        .reshape(experts_all, capacity, width)
    )
    grad_rows_in = lax.all_to_all(grad_slots, "expert", split_axis=0, concat_axis=1, tiled=True)
    hidden_grad = jnp.einsum(
        "ebd,efd->ebf", grad_rows_in, w_down, preferred_element_type=jnp.float32
    )
    grad_down = jnp.einsum("ebf,ebd->efd", hidden, grad_rows_in, preferred_element_type=jnp.float32)
    gate_in_grad = (
        hidden_grad * up_in * (sigmoid_gate * (1.0 + gate_in * (1.0 - sigmoid_gate)))
    ).astype(jnp.bfloat16)
    up_in_grad = (hidden_grad * silu_gate).astype(jnp.bfloat16)
    grad_gate = jnp.einsum(
        "ebd,ebf->edf", expert_rows, gate_in_grad, preferred_element_type=jnp.float32
    )
    grad_up = jnp.einsum(
        "ebd,ebf->edf", expert_rows, up_in_grad, preferred_element_type=jnp.float32
    )
    rows_part = jnp.einsum("ebf,edf->ebd", gate_in_grad, w_gate, preferred_element_type=jnp.float32)
    rows_part = rows_part + jnp.einsum(
        "ebf,edf->ebd", up_in_grad, w_up, preferred_element_type=jnp.float32
    )
    rows_back = lax.all_to_all(
        rows_part.astype(jnp.bfloat16), "expert", split_axis=1, concat_axis=0, tiled=True
    ).astype(rows_part.dtype)
    padded_back = jnp.concatenate(
        [rows_back.reshape(slots_all, width), jnp.zeros((1, width), jnp.float32)], axis=0
    )
    second_part = jnp.zeros((rows_here, width), jnp.float32)
    for pick in range(TOPK):
        second_part = second_part + padded_back[flat[:, pick]]
    second_sum, gate_grads = (
        lax.psum(second_part.astype(jnp.bfloat16), "tensor").astype(jnp.float32),
        lax.psum(gate_part.astype(jnp.bfloat16), "tensor").astype(jnp.float32),
    )
    chosen_grad = gates * (gate_grads - jnp.sum(gates * gate_grads, axis=1, keepdims=True))
    expert_axis = jnp.arange(experts_all, dtype=jnp.int32)
    logit_grad = jnp.zeros((rows_here, experts_all), jnp.float32)
    for pick in range(TOPK):
        logit_grad = logit_grad + jnp.where(
            expert_ids[:, pick : pick + 1] == expert_axis[None, :],
            chosen_grad[:, pick : pick + 1],
            0.0,
        )
    logit_low = logit_grad.astype(jnp.bfloat16)
    grad_router = matmul_tn(second_normed, logit_low)
    second_grad = second_sum + matmul_nt(logit_low, w_router)
    grad_second = jnp.sum(second_grad * second_unit, axis=0)
    residual_grad = grad_full + norm_back(second_grad, second_unit, second_scale, second_gain)
    residual_low = residual_grad.astype(jnp.bfloat16)
    grad_output = matmul_tn(attended, residual_low)
    attended_grad = head_major(matmul_nt(residual_low, w_output).astype(jnp.bfloat16))

    def delta_step(total, operands):
        key_block, value_block, start = operands
        probs = block_probs(key_block, start)
        prob_grad = jnp.einsum(
            "hqd,hkd->hqk", attended_grad, value_block, preferred_element_type=jnp.float32
        )
        return (total + jnp.sum(probs * prob_grad, axis=-1), None)

    delta, _ = lax.scan(
        delta_step,
        jnp.zeros((local_kv, head_rows), jnp.float32),
        (key_blocks, value_blocks, block_starts),
    )

    def grad_step(query_total, operands):
        key_block, value_block, start = operands
        probs = block_probs(key_block, start)
        prob_grad = jnp.einsum(
            "hqd,hkd->hqk", attended_grad, value_block, preferred_element_type=jnp.float32
        )
        score_grad = (probs * (prob_grad - delta[..., None])).astype(jnp.bfloat16)
        query_total = (
            query_total
            + jnp.einsum("hqk,hkd->hqd", score_grad, key_block, preferred_element_type=jnp.float32)
            * score_scale
        )
        key_grad = (
            jnp.einsum("hqk,hqd->hkd", score_grad, query_heads, preferred_element_type=jnp.float32)
            * score_scale
        )
        value_grad = jnp.einsum(
            "hqk,hqd->hkd",
            probs.astype(jnp.bfloat16),
            attended_grad,
            preferred_element_type=jnp.float32,
        )
        return (query_total, (key_grad, value_grad))

    query_total, (key_stack, value_stack) = lax.scan(
        grad_step,
        jnp.zeros((local_kv, head_rows, HEAD_SIZE), jnp.float32),
        (key_blocks, value_blocks, block_starts),
    )
    key_back, value_back = (
        lax.psum_scatter(
            by_rows(key_stack).astype(jnp.bfloat16), "expert", scatter_dimension=0, tiled=True
        ).astype(jnp.float32),
        lax.psum_scatter(
            by_rows(value_stack).astype(jnp.bfloat16), "expert", scatter_dimension=0, tiled=True
        ).astype(jnp.float32),
    )
    query_grad = (
        unrotate(
            row_major(query_total).reshape(rows_here, local_heads, HEAD_SIZE),
            cosine_table,
            sine_table,
        )
        .astype(jnp.bfloat16)
        .reshape(rows_here, local_heads * HEAD_SIZE)
    )
    key_grad = (
        unrotate(key_back.reshape(rows_here, local_kv, HEAD_SIZE), cosine_table, sine_table)
        .astype(jnp.bfloat16)
        .reshape(rows_here, local_kv * HEAD_SIZE)
    )
    value_grad = value_back.astype(jnp.bfloat16)
    grad_query = matmul_tn(first_normed, query_grad)
    grad_key = matmul_tn(first_normed, key_grad)
    grad_value = matmul_tn(first_normed, value_grad)
    first_part = (
        matmul_nt(query_grad, w_query)
        + matmul_nt(key_grad, key_weight)
        + matmul_nt(value_grad, value_weight)
    )
    first_grad = lax.psum(first_part.astype(jnp.bfloat16), "tensor").astype(jnp.float32)
    grad_first = jnp.sum(first_grad * first_unit, axis=0)
    grad_input = (
        residual_grad + norm_back(first_grad, first_unit, first_scale, first_gain)
    ).astype(jnp.bfloat16)
    dense = lax.psum(
        (grad_query, grad_key, grad_value, grad_output, grad_router, grad_first, grad_second),
        ("dp", "expert"),
    )
    expert_sums = (
        lax.psum(grad_gate.astype(jnp.bfloat16), "dp").astype(jnp.float32),
        lax.psum(grad_up.astype(jnp.bfloat16), "dp").astype(jnp.float32),
        lax.psum(grad_down.astype(jnp.bfloat16), "dp").astype(jnp.float32),
    )
    return (
        block_output,
        grad_input,
        dense[5],
        dense[0],
        dense[1],
        dense[2],
        dense[3],
        dense[6],
        dense[4],
        expert_sums[0],
        expert_sums[1],
        expert_sums[2],
    )


BF = jnp.bfloat16
F32 = jnp.float32
MIB = 1 << 20


def vmem_spec():
    return pl.BlockSpec(memory_space=pltpu.VMEM)


def smem_spec():
    return pl.BlockSpec(memory_space=pltpu.SMEM)


def allowed_pairs(scal_ref, rows):
    side = scal_ref[0]
    here = lax.broadcasted_iota(jnp.int32, (rows, 1), 0)
    keys = lax.broadcasted_iota(jnp.int32, (1, 2 * rows), 1)
    query_place = side * rows + here
    key_place = jnp.where(keys < rows, side * rows + keys, (1 - side) * rows + keys - rows)
    span = 2 * PIC

    def piece(places):
        window = places // span
        within = places - window * span
        start = jnp.where(window == 0, scal_ref[1], scal_ref[2])
        inside = (within >= start) & (within < start + PIC)
        return jnp.where(inside, window, -1)

    query_piece = piece(query_place)
    key_piece = piece(key_place)
    return (key_place <= query_place) | ((key_piece == query_piece) & (query_piece >= 0))


def attend_kernel(scal_ref, q_ref, k_ref, v_ref, wo_ref, att_ref, lse_ref, part_ref):
    rows = q_ref.shape[0]
    heads = q_ref.shape[1] // HEAD_SIZE
    sharing = q_ref.shape[1] // k_ref.shape[1]
    allowed = allowed_pairs(scal_ref, rows)
    pieces = []
    for head in range(heads):
        at = head * HEAD_SIZE
        kv = head // sharing * HEAD_SIZE
        query = q_ref[:, at : at + HEAD_SIZE]
        key = k_ref[:, kv : kv + HEAD_SIZE]
        value = v_ref[:, kv : kv + HEAD_SIZE]
        scores = jnp.where(allowed, matmul_nt(query, key) * (HEAD_SIZE**-0.5), masked_score)
        peak = jnp.max(scores, axis=1, keepdims=True)
        weights = jnp.exp(scores - peak)
        total = jnp.sum(weights, axis=1, keepdims=True)
        probs = (weights * (1.0 / total)).astype(BF)
        pieces.append(matmul(probs, value))
        lse_ref[:, head : head + 1] = peak + jnp.log(total)
    attended = jnp.concatenate(pieces, axis=1).astype(BF)
    att_ref[...] = attended
    part_ref[...] = matmul(attended, wo_ref[...]).astype(BF)


def attend(scal, query, key, value, w_output):
    rows, wide = query.shape
    return pl.pallas_call(
        attend_kernel,
        out_shape=(
            jax.ShapeDtypeStruct((rows, wide), BF),
            jax.ShapeDtypeStruct((rows, 128), F32),
            jax.ShapeDtypeStruct((rows, w_output.shape[1]), BF),
        ),
        in_specs=[smem_spec()] + [vmem_spec()] * 4,
        out_specs=(vmem_spec(),) * 3,
        compiler_params=pltpu.CompilerParams(vmem_limit_bytes=48 * MIB),
        name="attend",
    )(scal, query, key, value, w_output)


def turn(values, first):
    wide = values.shape[1]
    half = HEAD_SIZE // 2
    return jnp.where(
        first, -pltpu.roll(values, wide - half, 1), pltpu.roll(values, half, 1)
    )


def attend_back_kernel(
    scal_ref, q_ref, k_ref, v_ref, lse_ref, att_ref, low_ref, wo_ref, cos_ref, sin_ref,
    dq_ref, dk_ref, dv_ref, dwo_ref,
):
    rows, wide = q_ref.shape
    heads = wide // HEAD_SIZE
    sharing = q_ref.shape[1] // k_ref.shape[1]
    scale = HEAD_SIZE**-0.5
    low = low_ref[...]
    dwo_ref[...] = matmul_tn(att_ref[...], low)
    att_grad = matmul_nt(low, wo_ref[...]).astype(BF)
    allowed = allowed_pairs(scal_ref, rows)
    query_parts, key_parts, value_parts = [], [], []
    for head in range(heads):
        at = head * HEAD_SIZE
        kv = head // sharing * HEAD_SIZE
        query = q_ref[:, at : at + HEAD_SIZE]
        key = k_ref[:, kv : kv + HEAD_SIZE]
        value = v_ref[:, kv : kv + HEAD_SIZE]
        grad = att_grad[:, at : at + HEAD_SIZE]
        scores = jnp.where(allowed, matmul_nt(query, key) * scale, masked_score)
        probs = jnp.exp(scores - lse_ref[:, head : head + 1])
        prob_grad = matmul_nt(grad, value)
        delta = jnp.sum(probs * prob_grad, axis=1, keepdims=True)
        score_grad = (probs * (prob_grad - delta)).astype(BF)
        query_parts.append(matmul(score_grad, key) * scale)
        key_part = matmul_tn(score_grad, query) * scale
        value_part = matmul_tn(probs.astype(BF), grad)
        if head % sharing == 0:
            key_parts.append(key_part)
            value_parts.append(value_part)
        else:
            key_parts[-1] = key_parts[-1] + key_part
            value_parts[-1] = value_parts[-1] + value_part
    dk_ref[...] = jnp.concatenate(key_parts, axis=1).astype(BF)
    dv_ref[...] = jnp.concatenate(value_parts, axis=1).astype(BF)
    rotated = jnp.concatenate(query_parts, axis=1)
    lane = lax.broadcasted_iota(jnp.int32, (1, wide), 1)
    first = lane % HEAD_SIZE < HEAD_SIZE // 2
    cosines = jnp.concatenate([cos_ref[...]] * (wide // 128), axis=1)
    sines = jnp.concatenate([sin_ref[...]] * (wide // 128), axis=1)
    dq_ref[...] = (rotated * cosines - turn(rotated, first) * sines).astype(BF)


def attend_back(scal, query, key, value, lse, attended, low, w_output, cosines, sines):
    rows, wide = query.shape
    return pl.pallas_call(
        attend_back_kernel,
        out_shape=(
            jax.ShapeDtypeStruct((rows, wide), BF),
            jax.ShapeDtypeStruct(key.shape, BF),
            jax.ShapeDtypeStruct(value.shape, BF),
            jax.ShapeDtypeStruct(w_output.shape, F32),
        ),
        in_specs=[smem_spec()] + [vmem_spec()] * 9,
        out_specs=(vmem_spec(),) * 4,
        compiler_params=pltpu.CompilerParams(vmem_limit_bytes=56 * MIB),
        name="attend_back",
    )(scal, query, key, value, lse, attended, low, w_output, cosines, sines)


MESH = pl.DeviceIdType.MESH
PART = 32
LAG = 3
LINK_COST = pl.CostEstimate(flops=4 * 10**10, bytes_accessed=10**7, transcendentals=0)


def meet(partners):
    barrier = pltpu.get_barrier_semaphore()
    count = 0
    for here, device in partners:
        here = jnp.asarray(here)

        @pl.when(here)
        def _():
            pl.semaphore_signal(barrier, inc=1, device_id=device, device_id_type=MESH)

        count = count + here.astype(jnp.int32)
    pl.semaphore_wait(barrier, count)


def line_partners():
    place = lax.axis_index("tensor")
    last = lax.axis_size("tensor") - 1
    return [(place > 0, {"tensor": place - 1}), (place < last, {"tensor": place + 1})]


class Line:
    def __init__(self, parts, term, from_left, from_right, to_right, to_left, sems):
        self.place = lax.axis_index("tensor")
        self.last = lax.axis_size("tensor") - 1
        self.parts = parts
        self.term = term
        self.from_left, self.from_right = from_left, from_right
        self.to_right, self.to_left = to_right, to_left
        self.sems = sems

    def copy(self, way, at):
        near = jnp.where(self.place < self.last, self.place + 1, self.place - 1)
        far = jnp.where(self.place > 0, self.place - 1, self.place + 1)
        source, target, device = (
            (self.to_right, self.from_left, near) if way == 0 else (self.to_left, self.from_right, far)
        )
        return pltpu.make_async_remote_copy(
            src_ref=source.at[at],
            dst_ref=target.at[at],
            send_sem=self.sems.at[2 * way, at],
            recv_sem=self.sems.at[2 * way + 1, at],
            device_id={"tensor": device},
            device_id_type=MESH,
        )

    def clear(self):
        @pl.when(self.place == 0)
        def _():
            self.from_left[...] = jnp.zeros(self.from_left.shape, self.from_left.dtype)

        @pl.when(self.place == self.last)
        def _():
            self.from_right[...] = jnp.zeros(self.from_right.shape, self.from_right.dtype)

    def step(self, at):
        for way in range(2):
            part = at - LAG * (self.place if way == 0 else self.last - self.place)
            has_source = self.place > 0 if way == 0 else self.place < self.last
            has_target = self.place < self.last if way == 0 else self.place > 0
            arrived = self.from_left if way == 0 else self.from_right
            leaving = self.to_right if way == 0 else self.to_left
            valid = (part >= 0) & (part < self.parts)

            @pl.when(valid & has_source)
            def _():
                self.copy(way, part).wait_recv()

            @pl.when(valid & has_target)
            def _():
                leaving[part] = (self.term(part) + arrived[part].astype(F32)).astype(BF)
                self.copy(way, part).start()

    def total(self, part):
        return self.term(part) + self.from_left[part].astype(F32) + self.from_right[part].astype(F32)

    def drain(self):
        def wait(part, carry):
            @pl.when(self.place < self.last)
            def _():
                self.copy(0, part).wait_send()

            @pl.when(self.place > 0)
            def _():
                self.copy(1, part).wait_send()

            return carry

        lax.fori_loop(0, self.parts, wait, 0)


def line_scratch(parts, width):
    return [pltpu.VMEM((parts, PART, width), BF)] * 4 + [pltpu.SemaphoreType.DMA((4, parts))]


def peer_copy(source, target, sems, at):
    return pltpu.make_async_remote_copy(
        src_ref=source,
        dst_ref=target,
        send_sem=sems.at[0, at],
        recv_sem=sems.at[1, at],
        device_id={"expert": 1 - lax.axis_index("expert")},
        device_id_type=MESH,
    )


def scale_of(values):
    return lax.rsqrt(jnp.mean(values * values, axis=-1, keepdims=True) + epsilon)


def plain_copy(source, target, sems, at, device):
    return pltpu.make_async_remote_copy(
        src_ref=source, dst_ref=target, send_sem=sems.at[0, at], recv_sem=sems.at[1, at],
        device_id=device, device_id_type=MESH,
    )


def beside():
    return {"dp": lax.rem(lax.axis_index("dp") + 2, 4)}


def other_core():
    place = lax.axis_index("dp")
    return {"dp": place + 1 - 2 * lax.rem(place, 2)}


def residual_kernel(
    part_ref, x_ref, gain_ref, up_own, up_peer0, up_peer1, marks_ref,
    res_ref, n_ref, up_all, far_peer, far_marks,
    from_left, from_right, to_right, to_left, sems, peer_sems, far_sems, near_sems,
):
    parts = part_ref.shape[0]
    line = Line(parts, lambda at: part_ref[at].astype(F32), from_left, from_right, to_right, to_left, sems)
    line.clear()
    meet(line_partners() + [(True, {"expert": 1 - lax.axis_index("expert")}), (True, beside())])
    quarter = up_peer0.shape[0]
    far_copies = [
        plain_copy(marks_ref, far_marks, far_sems, 0, beside()),
        plain_copy(up_peer0, far_peer.at[pl.ds(0, quarter), :], far_sems, 1, beside()),
        plain_copy(up_peer1, far_peer.at[pl.ds(quarter, quarter), :], far_sems, 2, beside()),
    ]
    near_copies = [
        pltpu.make_async_copy(up_own, up_all.at[pl.ds(0, 2 * quarter), :], near_sems.at[0]),
        pltpu.make_async_copy(up_peer0, up_all.at[pl.ds(2 * quarter, quarter), :], near_sems.at[1]),
        pltpu.make_async_copy(up_peer1, up_all.at[pl.ds(3 * quarter, quarter), :], near_sems.at[2]),
    ]
    for copy in far_copies + near_copies:
        copy.start()

    def body(at, carry):
        line.step(at)
        part = at - LAG * line.last

        @pl.when(part >= 0)
        def _():
            residual = x_ref[part].astype(F32) + line.total(part)
            res_ref[part] = residual
            unit = residual * scale_of(residual)
            n_ref[0, part] = (unit * gain_ref[...]).astype(BF)
            peer_copy(n_ref.at[0, part], n_ref.at[1, part], peer_sems, part).start()

        return carry

    lax.fori_loop(0, parts + LAG * line.last, body, 0)
    line.drain()

    def wait(part, carry):
        peer_copy(n_ref.at[0, part], n_ref.at[1, part], peer_sems, part).wait()
        return carry

    lax.fori_loop(0, parts, wait, 0)
    for copy in far_copies + near_copies:
        copy.wait()


def residual_norm(part, block_input, gain, upstream, peer_up, marks):
    rows, width = block_input.shape
    parts = rows // PART
    any_spec = pl.BlockSpec(memory_space=pl.ANY)
    residual, normed, *rest = pl.pallas_call(
        residual_kernel,
        out_shape=(
            jax.ShapeDtypeStruct((parts, PART, width), F32),
            jax.ShapeDtypeStruct((2, parts, PART, width), BF),
            jax.ShapeDtypeStruct((2 * rows, width), BF),
            jax.ShapeDtypeStruct((rows, width), BF),
            jax.ShapeDtypeStruct(marks.shape, BF),
        ),
        in_specs=[vmem_spec()] * 3 + [any_spec] * 4,
        out_specs=(vmem_spec(),) * 2 + (any_spec,) * 3,
        scratch_shapes=line_scratch(parts, width)
        + [pltpu.SemaphoreType.DMA((2, parts)), pltpu.SemaphoreType.DMA((2, 3)), pltpu.SemaphoreType.DMA((3,))],
        compiler_params=pltpu.CompilerParams(
            collective_id=0, has_side_effects=True, vmem_limit_bytes=40 * MIB
        ),
        cost_estimate=LINK_COST,
        name="residual_norm",
    )(
        part.reshape(parts, PART, width), block_input.reshape(parts, PART, width), gain[None],
        upstream, *peer_up, marks,
    )
    return residual, normed.reshape(2 * rows, width), *rest


UNIT = 512


def residual_grad_kernel(
    back_ref, route_ref, res_ref, up_ref, gain_ref, wr_ref, mix_ref,
    far_n, far_on, far_g0, far_g1, far_og0, far_og1, far_m, far_om,
    wg_hbm, wu_hbm, wd_hbm, pg_hbm, pu_hbm, pd_hbm,
    grad_ref, low_ref, second_ref, route_out, mixed_ref, sg_hbm, su_hbm, sd_hbm,
    from_left, from_right, to_right, to_left, sems, peer_sems, arrived, terms,
    tokens_n, tokens_g, turned, kept_gates, gates_w, ups_w, downs_w, pair_g, pair_u, pair_d, ght, dgs, dus,
    row_sems, weight_sems, pair_sems, out_sems, mix_arrived, mix_sems, marks_ref,
):
    parts = back_ref.shape[1]
    core = lax.rem(lax.axis_index("dp"), 2)
    side = lax.axis_index("expert")
    groups, group, width, hid = pair_g.shape
    experts_all = wr_ref.shape[1]
    line = Line(parts + 1, lambda at: terms[at], from_left, from_right, to_right, to_left, sems)
    line.clear()
    meet(line_partners() + [(True, {"expert": 1 - side})])

    def send(part, carry):
        peer_copy(back_ref.at[1, part], arrived.at[part], peer_sems, part).start()
        return carry

    lax.fori_loop(0, parts, send, 0)

    def send_mix(part, carry):
        peer_copy(mix_ref.at[1, part], mix_arrived.at[part], mix_sems, part).start()
        return carry

    lax.fori_loop(0, parts, send_mix, 0)
    half = tokens_n.shape[0] // 2
    quarter = half // 2
    row_copies = []
    for place, (rows, first, second, marks) in enumerate(((far_n, far_g0, far_g1, far_m), (far_on, far_og0, far_og1, far_om))):
        at = place * half
        row_copies += [
            pltpu.make_async_copy(rows, tokens_n.at[pl.ds(at, half), :], row_sems.at[0, place]),
            pltpu.make_async_copy(first, tokens_g.at[pl.ds(at, quarter), :], row_sems.at[1, place]),
            pltpu.make_async_copy(second, tokens_g.at[pl.ds(at + quarter, quarter), :], row_sems.at[2, place]),
            pltpu.make_async_copy(marks, marks_ref.at[pl.ds(at, half), :], row_sems.at[3, place]),
        ]
    weight_copies, pair_copies, out_copies = [], [], []
    for at in range(groups):
        first = core * (groups * group) + at * group
        weight_copies.append(
            [
                pltpu.make_async_copy(
                    source.at[first + expert],
                    target.at[at, :, pl.ds(expert * hid, hid)],
                    weight_sems.at[at, kind, expert],
                )
                for expert in range(group)
                for kind, (source, target) in enumerate(((wg_hbm, gates_w), (wu_hbm, ups_w)))
            ]
            + [pltpu.make_async_copy(wd_hbm.at[pl.ds(first, group)], downs_w.at[at], weight_sems.at[at, 2, 0])]
        )
        sources = (pg_hbm, pu_hbm, pd_hbm)
        held = (pair_g, pair_u, pair_d)
        targets = (sg_hbm, su_hbm, sd_hbm)
        pair_copies.append(
            [
                pltpu.make_async_copy(sources[kind].at[pl.ds(at * group, group)], held[kind].at[at], pair_sems.at[at, kind])
                for kind in range(3)
            ]
        )
        out_copies.append(
            [
                pltpu.make_async_copy(held[kind].at[at], targets[kind].at[pl.ds(at * group, group)], out_sems.at[at, kind])
                for kind in range(3)
            ]
        )
    for copy in row_copies[:4] + weight_copies[0] + row_copies[4:] + pair_copies[0] + weight_copies[1] + pair_copies[1]:
        copy.start()
    terms[parts] = route_ref[...]
    second_ref[...] = jnp.zeros(second_ref.shape, F32)
    chunks = 2 * half // UNIT
    units = chunks + 3

    def compute(at):
        for where in range(groups):
            unit = at - where * units

            @pl.when(unit == 0)
            def _():
                for copy in weight_copies[where]:
                    copy.wait()

            if where == 0:

                @pl.when(unit == 0)
                def _():
                    for copy in row_copies[:4]:
                        copy.wait()

                @pl.when(unit == half // UNIT)
                def _():
                    for copy in row_copies[4:]:
                        copy.wait()

            @pl.when(unit == chunks)
            def _():
                for copy in pair_copies[where]:
                    copy.wait()

        where = at // units
        unit = at - where * units

        @pl.when(unit < chunks)
        def _():
            place = pl.multiple_of(unit * UNIT, UNIT)
            rows = pl.ds(place, UNIT)
            token = tokens_n[rows, :]

            @pl.when(where == 0)
            def _():
                kept_gates[rows, :] = route_gates(token, marks_ref[rows, :], wr_ref[...])[1]
                turned[:, rows] = token.T

            down = downs_w[where].reshape(group * hid, width)
            column = side * (experts_all // 2) + (core * groups + where) * group
            pulled = matmul_nt(tokens_g[rows, :], down)
            weight = spread_gates(kept_gates[rows, :], column, group, hid)
            _, gated, gate_grad, up_grad = hidden_terms(token, pulled, weight, gates_w[where], ups_w[where])
            ght[:, rows] = gated.T
            dgs[rows, :] = gate_grad
            dus[rows, :] = up_grad

        @pl.when((unit >= chunks) & (unit < chunks + 2))
        def _():
            rows = pl.ds(pl.multiple_of((unit - chunks) * (width // 2), width // 2), width // 2)
            for source, held in ((dgs, pair_g), (dus, pair_u)):
                part = matmul(turned[rows, :], source[...])
                for expert in range(group):
                    more = part[:, expert * hid : (expert + 1) * hid]
                    held[where, expert, rows, :] = (held[where, expert, rows, :].astype(F32) + more).astype(BF)

        @pl.when(unit == chunks + 2)
        def _():
            part = matmul(ght[...], tokens_g[...])
            for expert in range(group):
                more = part[expert * hid : (expert + 1) * hid, :]
                pair_d[where, expert] = (pair_d[where, expert].astype(F32) + more).astype(BF)

        for where in range(groups):

            @pl.when(at == where * units + units - 1)
            def _():
                for copy in out_copies[where]:
                    copy.start()

    def body(at, carry):
        @pl.when(at < parts)
        def _():
            peer_copy(back_ref.at[1, at], arrived.at[at], peer_sems, at).wait_recv()
            terms[at] = back_ref[0, at].astype(F32) + arrived[at].astype(F32)

        line.step(at)
        part = at - LAG * line.last

        @pl.when((part >= 0) & (part < parts))
        def _():
            grad = line.total(part)
            residual = res_ref[part]
            scale = scale_of(residual)
            unit = residual * scale
            second_ref[...] += jnp.sum(grad * unit, axis=0, keepdims=True)
            result = up_ref[part].astype(F32) + norm_back(grad, unit, scale, gain_ref[...])
            grad_ref[part] = result
            low_ref[part] = result.astype(BF)

        mixed = at - MIX_STEP

        @pl.when((mixed >= 0) & (mixed < parts))
        def _():
            peer_copy(mix_ref.at[1, mixed], mix_arrived.at[mixed], mix_sems, mixed).wait_recv()
            mixed_ref[mixed] = (mix_ref[0, mixed].astype(F32) + mix_arrived[mixed].astype(F32)).astype(BF)

        @pl.when((at >= FIRST_UNIT) & (at < FIRST_UNIT + groups * units))
        def _():
            compute(at - FIRST_UNIT)

        return carry

    lax.fori_loop(0, parts + 1 + LAG * line.last, body, 0)
    route_out[...] = line.total(parts)
    line.drain()

    def wait(part, carry):
        peer_copy(back_ref.at[1, part], arrived.at[part], peer_sems, part).wait_send()
        peer_copy(mix_ref.at[1, part], mix_arrived.at[part], mix_sems, part).wait_send()
        return carry

    lax.fori_loop(0, parts, wait, 0)
    for copies in out_copies:
        for copy in copies:
            copy.wait()


FIRST_UNIT = 3
MIX_STEP = 10


def residual_gradient(back, mix, route, residual, upstream, gain, w_router, far_rows, w_gate, w_up, w_down, pairs):
    rows, width = upstream.shape
    parts = rows // PART
    half, _, hid = pairs[0].shape
    groups = half // GROUP
    tokens = 2 * far_rows[0].shape[0]
    any_spec = pl.BlockSpec(memory_space=pl.ANY)
    grad, low, second, route, mixed, *sums = pl.pallas_call(
        residual_grad_kernel,
        out_shape=[
            jax.ShapeDtypeStruct((parts, PART, width), F32),
            jax.ShapeDtypeStruct((parts, PART, width), BF),
            jax.ShapeDtypeStruct((1, width), F32),
            jax.ShapeDtypeStruct(route.shape, F32),
            jax.ShapeDtypeStruct((parts, PART, width), BF),
        ]
        + [jax.ShapeDtypeStruct(pair.shape, BF) for pair in pairs],
        in_specs=[vmem_spec()] * 7 + [any_spec] * 14,
        out_specs=[vmem_spec()] * 5 + [any_spec] * 3,
        scratch_shapes=line_scratch(parts + 1, width)
        + [
            pltpu.SemaphoreType.DMA((2, parts)),
            pltpu.VMEM((parts, PART, width), BF),
            pltpu.VMEM((parts + 1, PART, width), F32),
            pltpu.VMEM((tokens, width), BF),
            pltpu.VMEM((tokens, width), BF),
            pltpu.VMEM((width, tokens), BF),
            pltpu.VMEM((tokens, w_router.shape[1]), F32),
            pltpu.VMEM((groups, width, GROUP * hid), BF),
            pltpu.VMEM((groups, width, GROUP * hid), BF),
            pltpu.VMEM((groups, GROUP, hid, width), BF),
            pltpu.VMEM((groups, GROUP, width, hid), BF),
            pltpu.VMEM((groups, GROUP, width, hid), BF),
            pltpu.VMEM((groups, GROUP, hid, width), BF),
            pltpu.VMEM((GROUP * hid, tokens), BF),
            pltpu.VMEM((tokens, GROUP * hid), BF),
            pltpu.VMEM((tokens, GROUP * hid), BF),
            pltpu.SemaphoreType.DMA((4, 2)),
            pltpu.SemaphoreType.DMA((groups, 3, GROUP)),
            pltpu.SemaphoreType.DMA((groups, 3)),
            pltpu.SemaphoreType.DMA((groups, 3)),
            pltpu.VMEM((parts, PART, width), BF),
            pltpu.SemaphoreType.DMA((2, parts)),
            pltpu.VMEM((tokens, 2 * w_router.shape[1]), BF),
        ],
        compiler_params=pltpu.CompilerParams(
            collective_id=1, has_side_effects=True, vmem_limit_bytes=60 * MIB
        ),
        cost_estimate=LINK_COST,
        name="residual_grad",
    )(
        back.reshape(2, parts, PART, width), route, residual, upstream.reshape(parts, PART, width), gain[None],
        w_router, mix.reshape(2, parts, PART, width), *far_rows, w_gate, w_up, w_down, *pairs,
    )
    return grad, low.reshape(rows, width), second, route, mixed.reshape(rows, width), sums


def input_grad_kernel(
    x_ref, res_grad_ref, gain_ref, n_ref, dq_ref, dk_ref, dv_ref, wq_ref, wk_ref, wv_ref, cos_ref, sin_ref,
    dwo_ref, route_ref, second_ref,
    grad_ref, gq_ref, gk_ref, gv_ref, go_ref, gr_ref, gs_ref, gf_ref,
    from_left, from_right, to_right, to_left, sems, terms, kv_in, kv_sems,
    wide, wide_core, wide_x, wide_y, wide_back, tall, tall_core, tall_x, tall_y, tall_back, rows2, rows_core, rows_x, rows_y, sum_sems,
):
    parts = x_ref.shape[0]
    rows = n_ref.shape[0]
    width = n_ref.shape[1]
    core = lax.rem(lax.axis_index("dp"), 2)
    peer = {"expert": 1 - lax.axis_index("expert")}
    kv = dk_ref.shape[1]
    queries = dq_ref.shape[1]
    line = Line(parts + 1, lambda at: terms[at], from_left, from_right, to_right, to_left, sems)
    line.clear()
    meet(line_partners() + [(True, peer), (True, beside()), (True, other_core())])
    key_copy = plain_copy(dk_ref.at[pl.ds(rows, rows), :], kv_in.at[0], kv_sems, 0, peer)
    value_copy = plain_copy(dv_ref.at[pl.ds(rows, rows), :], kv_in.at[1], kv_sems, 1, peer)
    key_copy.start()
    value_copy.start()

    half_tall = tall.shape[1]
    outs = dwo_ref.shape[0]
    for at in range(2):
        low, high = at * half_tall, (at + 1) * half_tall
        top = min(high, outs)
        tall[at, : top - low, :] = dwo_ref[low:top, :].astype(BF)
        if high > outs:
            tall[at, outs - low :, :] = route_ref[...].astype(BF)

    tall_steps = [
        plain_copy(tall.at[1 - core], tall_core, sum_sems, 0, other_core()),
        plain_copy(tall.at[core], tall_y, sum_sems, 1, peer),
        plain_copy(tall.at[core], tall_x, sum_sems, 2, beside()),
        plain_copy(tall.at[core], tall_back, sum_sems, 3, other_core()),
    ]
    wide_steps = [
        plain_copy(wide.at[1 - core], wide_core, sum_sems, 4, other_core()),
        plain_copy(wide.at[core], wide_x, sum_sems, 5, beside()),
        plain_copy(wide.at[core], wide_y, sum_sems, 6, peer),
        plain_copy(wide.at[core], wide_back, sum_sems, 7, other_core()),
    ]
    rows_steps = [
        plain_copy(rows2, rows_core, sum_sems, 8, other_core()),
        plain_copy(rows2, rows_y, sum_sems, 9, peer),
        plain_copy(rows2, rows_x, sum_sems, 10, beside()),
    ]
    tall_steps[0].start()

    def add(held, arrived):
        held[...] = (held[...].astype(F32) + arrived[...].astype(F32)).astype(BF)

    query_grad = dq_ref[...]
    by_rows = (parts, rows // parts, width)
    terms[pl.ds(0, parts)] = matmul_nt(query_grad, wq_ref[...]).reshape(by_rows)
    turned = n_ref[...].T
    query_part = matmul(turned, query_grad).astype(BF)
    for at in range(2):
        wide[at, :, :queries] = query_part[at * width // 2 : (at + 1) * width // 2, :]
    key_copy.wait_recv()
    value_copy.wait_recv()
    rotated = dk_ref[:rows, :].astype(F32) + kv_in[0].astype(F32)
    lane = lax.broadcasted_iota(jnp.int32, (1, kv), 1)
    first = lane % HEAD_SIZE < HEAD_SIZE // 2
    key_grad = (rotated * cos_ref[...] - turn(rotated, first) * sin_ref[...]).astype(BF)
    value_grad = (dv_ref[:rows, :].astype(F32) + kv_in[1].astype(F32)).astype(BF)
    more = matmul_nt(key_grad, wk_ref[...]) + matmul_nt(value_grad, wv_ref[...])
    terms[pl.ds(0, parts)] += more.reshape(by_rows)
    both_part = matmul(turned, jnp.concatenate([key_grad, value_grad], axis=1)).astype(BF)
    for at in range(2):
        wide[at, :, queries:] = both_part[at * width // 2 : (at + 1) * width // 2, :]
    wide_steps[0].start()

    def gain_part(at, total):
        values = x_ref[at].astype(F32)
        return total + jnp.sum(terms[at] * (values * scale_of(values)), axis=0, keepdims=True)

    first_sum = lax.fori_loop(0, parts, gain_part, jnp.zeros((1, width), F32))
    pad = jnp.zeros((rows2.shape[0] - 2, width), F32)
    rows2[...] = jnp.concatenate([first_sum, second_ref[...], pad], axis=0).astype(BF)
    rows_steps[0].start()

    def exchange(at):
        @pl.when(at == 0)
        def _():
            rows_steps[0].wait()
            add(rows2, rows_core)
            rows_steps[1].start()
            tall_steps[0].wait()
            add(tall.at[core], tall_core)
            tall_steps[1].start()

        @pl.when(at == 1)
        def _():
            wide_steps[0].wait()
            add(wide.at[core], wide_core)

        @pl.when(at == 2)
        def _():
            rows_steps[1].wait()
            add(rows2, rows_y)
            rows_steps[2].start()
            wide_steps[1].start()

        @pl.when(at == 5)
        def _():
            rows_steps[2].wait()
            add(rows2, rows_x)
            summed = rows2[...].astype(F32)
            terms[parts] = jnp.concatenate([summed[:1, :], jnp.zeros((PART - 1, width), F32)], axis=0)
            gs_ref[...] = summed[1:2, :]

        @pl.when(at == 8)
        def _():
            tall_steps[1].wait()
            add(tall.at[core], tall_y)
            tall_steps[2].start()

        @pl.when(at == 11)
        def _():
            wide_steps[1].wait()
            add(wide.at[core], wide_x)
            wide_steps[2].start()

        @pl.when(at == 18)
        def _():
            tall_steps[2].wait()
            add(tall.at[core], tall_x)
            tall_steps[3].start()

        @pl.when(at == 20)
        def _():
            wide_steps[2].wait()
            add(wide.at[core], wide_y)
            wide_steps[3].start()

    def body(at, carry):
        exchange(at)
        line.step(at)
        part = at - LAG * line.last

        @pl.when((part >= 0) & (part < parts))
        def _():
            grad = line.total(part)
            values = x_ref[part].astype(F32)
            scale = scale_of(values)
            unit = values * scale
            grad_ref[part] = (res_grad_ref[part] + norm_back(grad, unit, scale, gain_ref[...])).astype(BF)

        return carry

    lax.fori_loop(0, parts + 1 + LAG * line.last, body, 0)
    gf_ref[...] = line.total(parts)[:1, :]
    line.drain()
    key_copy.wait_send()
    value_copy.wait_send()
    tall_steps[3].wait()
    for at in range(2):
        low, high = at * half_tall, (at + 1) * half_tall
        top = min(high, outs)
        summed = jnp.where(core == at, tall[at].astype(F32), tall_back[...].astype(F32))
        go_ref[low:top, :] = summed[: top - low, :]
        if high > outs:
            gr_ref[...] = summed[outs - low :, :]
    wide_steps[3].wait()
    for at in range(2):
        span = slice(at * width // 2, (at + 1) * width // 2)
        summed = jnp.where(core == at, wide[at].astype(F32), wide_back[...].astype(F32))
        gq_ref[span, :] = summed[:, :queries]
        gk_ref[span, :] = summed[:, queries : queries + kv]
        gv_ref[span, :] = summed[:, queries + kv :]


def input_gradient(
    block_input, residual_grad, gain, normed, dq, dk, dv, w_query, key_weight, value_weight, cosines, sines,
    grad_output, route, second,
):
    rows, width = block_input.shape
    parts = rows // PART
    columns = w_query.shape[1] + 2 * key_weight.shape[1]
    tall = (grad_output.shape[0] + route.shape[0]) // 2
    wide_half = pltpu.VMEM((width // 2, columns), BF)
    tall_half = pltpu.VMEM((tall, width), BF)
    tile = pltpu.VMEM((16, width), BF)
    grad, *rest = pl.pallas_call(
        input_grad_kernel,
        out_shape=(
            jax.ShapeDtypeStruct((parts, PART, width), BF),
            jax.ShapeDtypeStruct(w_query.shape, F32),
            jax.ShapeDtypeStruct(key_weight.shape, F32),
            jax.ShapeDtypeStruct(value_weight.shape, F32),
            jax.ShapeDtypeStruct(grad_output.shape, F32),
            jax.ShapeDtypeStruct(route.shape, F32),
            jax.ShapeDtypeStruct((1, width), F32),
            jax.ShapeDtypeStruct((1, width), F32),
        ),
        in_specs=[vmem_spec()] * 15,
        out_specs=(vmem_spec(),) * 8,
        scratch_shapes=line_scratch(parts + 1, width)
        + [
            pltpu.VMEM((parts + 1, PART, width), F32),
            pltpu.VMEM((2, rows, key_weight.shape[1]), BF),
            pltpu.SemaphoreType.DMA((2, 2)),
            pltpu.VMEM((2, width // 2, columns), BF), wide_half, wide_half, wide_half, wide_half,
            pltpu.VMEM((2, tall, width), BF), tall_half, tall_half, tall_half, tall_half,
            tile, tile, tile, tile,
            pltpu.SemaphoreType.DMA((2, 11)),
        ],
        compiler_params=pltpu.CompilerParams(
            collective_id=2, has_side_effects=True, vmem_limit_bytes=56 * MIB
        ),
        cost_estimate=LINK_COST,
        name="input_grad",
    )(
        block_input.reshape(parts, PART, width), residual_grad, gain[None], normed, dq, dk, dv,
        w_query, key_weight, value_weight, cosines, sines, grad_output, route, second,
    )
    return grad.reshape(rows, width), *rest


CHUNK = 512
GROUP = 4


def route_gates(token, marks, w_router):
    experts_all = w_router.shape[1]
    chosen = marks[:, :experts_all].astype(F32)
    kept = marks[:, experts_all:].astype(F32)
    logits = jnp.where(chosen > 0.0, matmul(token, w_router), masked_score)
    raised = jnp.exp(logits - jnp.max(logits, axis=1, keepdims=True)) * chosen
    gate = raised / jnp.sum(raised, axis=1, keepdims=True)
    return gate, gate * kept


def hidden_terms(token, pulled, weight, gate_weights, up_weights):
    gate_in = matmul(token, gate_weights)
    up_in = matmul(token, up_weights)
    sig = 0.5 * jnp.tanh(0.5 * gate_in) + 0.5
    silu = gate_in * sig
    hidden = silu * up_in
    gated = (hidden * weight).astype(BF)
    scaled = pulled * weight
    up_grad = (scaled * silu).astype(BF)
    gate_grad = (scaled * up_in * (sig + silu * (1.0 - sig))).astype(BF)
    return hidden, gated, gate_grad, up_grad


def spread_gates(kept, column, group, hid):
    lane = lax.broadcasted_iota(jnp.int32, (1, kept.shape[1]), 1)
    weights = []
    for expert in range(group):
        gate = jnp.sum(jnp.where(lane == column + expert, kept, 0.0), axis=1, keepdims=True)
        weights.append(jnp.broadcast_to(gate, (kept.shape[0], hid)))
    return jnp.concatenate(weights, axis=1)


def expert_kernel(
    n_ref, g_ref, marks_ref, wr_ref, n_hbm, far_g0, far_g1, far_m, wg_ref, wu_ref, wd_ref,
    dwg_ref, dwu_ref, dwd_ref, mix_ref, back_ref, route_ref, far_n, far_on, far_og0, far_og1, far_om,
    gates, kept_gates, gate_grads, mix, back, nt, wgs, wus, ght, dgs, dus,
    out_g, out_u, out_d, in_g, in_u, in_d, sems, far_sems,
):
    step = pl.program_id(0)
    steps = pl.num_programs(0) // 2
    side = lax.axis_index("expert")
    dp = lax.axis_index("dp")
    core = lax.rem(dp, 2)
    other = other_core()
    tokens, width = n_ref.shape
    experts_all = wr_ref.shape[1]
    group, _, hid = wg_ref.shape
    chunks = tokens // CHUNK
    lane = lax.broadcasted_iota(jnp.int32, (1, experts_all), 1)

    def copies(slot):
        return [
            pltpu.make_async_remote_copy(
                src_ref=source.at[slot], dst_ref=target.at[slot],
                send_sem=sems.at[0, kind, slot], recv_sem=sems.at[1, kind, slot],
                device_id=other, device_id_type=MESH,
            )
            for kind, (source, target) in enumerate(((out_g, in_g), (out_u, in_u), (out_d, in_d)))
        ]

    half = tokens // 2
    cross = [
        plain_copy(n_hbm.at[pl.ds(at * half, half), :], far_n.at[pl.ds(at * half, half), :], far_sems, at, beside())
        for at in range(2)
    ]
    share = [
        plain_copy(far_n.at[pl.ds(at * half, half), :], far_on.at[pl.ds(at * half, half), :], far_sems, 2 + at, other)
        for at in range(2)
    ]
    early = [
        plain_copy(source, target, far_sems, 4 + at, other)
        for at, (source, target) in enumerate(((far_g0, far_og0), (far_g1, far_og1), (far_m, far_om)))
    ]

    @pl.when(step == 0)
    def _():
        meet([(True, other), (True, beside())])
        for copy in cross + early:
            copy.start()

        def start(at, carry):
            rows = pl.ds(pl.multiple_of(at * CHUNK, CHUNK), CHUNK)
            gate, kept_gate = route_gates(n_ref[rows, :], marks_ref[rows, :], wr_ref[...])
            gates[rows, :] = gate
            kept_gates[rows, :] = kept_gate
            mix[rows, :] = jnp.zeros((CHUNK, width), F32)
            back[rows, :] = jnp.zeros((CHUNK, width), F32)
            gate_grads[rows, :] = jnp.zeros((CHUNK, experts_all), F32)
            return carry

        lax.fori_loop(0, chunks, start, 0)
        for at in range(chunks):
            nt[:, at * CHUNK : (at + 1) * CHUNK] = n_ref[at * CHUNK : (at + 1) * CHUNK, :].T

    for expert in range(group):
        wgs[:, expert * hid : (expert + 1) * hid] = wg_ref[expert]
        wus[:, expert * hid : (expert + 1) * hid] = wu_ref[expert]
    first = step < steps
    block = jnp.where(first, (1 - core) * steps + step, core * steps + step - steps)
    column = side * (experts_all // 2) + block * group

    for at in range(chunks):
        rows = slice(at * CHUNK, (at + 1) * CHUNK)
        token = n_ref[rows, :]
        down = wd_ref[...].reshape(group * hid, width)
        pulled = matmul_nt(g_ref[rows, :], down)
        weight = spread_gates(kept_gates[rows, :], column, group, hid)
        hidden, gated, gate_grad, up_grad = hidden_terms(token, pulled, weight, wgs[...], wus[...])
        products = hidden * pulled
        grads = gate_grads[rows, :]
        for expert in range(group):
            product = jnp.sum(products[:, expert * hid : (expert + 1) * hid], axis=1, keepdims=True)
            grads = grads + jnp.where(lane == column + expert, product, 0.0)
        gate_grads[rows, :] = grads
        ght[:, rows] = gated.T
        dgs[rows, :] = gate_grad
        dus[rows, :] = up_grad
        mix[rows, :] += matmul(gated, down)
        back[rows, :] += matmul_nt(gate_grad, wgs[...]) + matmul_nt(up_grad, wus[...])

    def weight_grads(store_rows, store_down):
        for at in range(width // CHUNK):
            rows = slice(at * CHUNK, (at + 1) * CHUNK)
            turned = nt[rows, :]
            gate_part = matmul(turned, dgs[...])
            up_part = matmul(turned, dus[...])
            for expert in range(group):
                inner = slice(expert * hid, (expert + 1) * hid)
                store_rows(expert, rows, gate_part[:, inner], up_part[:, inner])
        down_part = matmul(ght[...], g_ref[...])
        for expert in range(group):
            store_down(expert, down_part[expert * hid : (expert + 1) * hid, :])

    @pl.when(first)
    def _():
        def store_rows(expert, rows, gate_part, up_part):
            out_g[step, expert, rows, :] = gate_part.astype(BF)
            out_u[step, expert, rows, :] = up_part.astype(BF)

        def store_down(expert, part):
            out_d[step, expert] = part.astype(BF)

        weight_grads(store_rows, store_down)
        for copy in copies(step):
            copy.start()

    @pl.when(step >= steps)
    def _():
        slot = step - steps
        for copy in copies(slot):
            copy.wait_recv()

        def store_rows(expert, rows, gate_part, up_part):
            dwg_ref[expert, rows, :] = (gate_part + in_g[slot, expert, rows, :].astype(F32)).astype(BF)
            dwu_ref[expert, rows, :] = (up_part + in_u[slot, expert, rows, :].astype(F32)).astype(BF)

        def store_down(expert, part):
            dwd_ref[expert] = (part + in_d[slot, expert].astype(F32)).astype(BF)

        weight_grads(store_rows, store_down)
        for copy in copies(slot):
            copy.wait_send()

    @pl.when(step == 2 * steps - 1)
    def _():
        for at in range(2):
            cross[at].wait_recv()
            share[at].start()
        route_ref[...] = jnp.zeros(route_ref.shape, F32)

        def finish(at, carry):
            rows = pl.ds(pl.multiple_of(at * CHUNK, CHUNK), CHUNK)
            mix_ref[rows, :] = mix[rows, :].astype(BF)
            grads = gate_grads[rows, :] * kept_gates[rows, :]
            chosen_grad = grads - gates[rows, :] * jnp.sum(grads, axis=1, keepdims=True)
            low = chosen_grad.astype(BF)
            back_ref[rows, :] = (back[rows, :] + matmul_nt(low, wr_ref[...])).astype(BF)
            route_ref[...] += matmul_tn(low, n_ref[rows, :])
            return carry

        lax.fori_loop(0, chunks, finish, 0)
        for copy in cross:
            copy.wait_send()
        for copy in share + early:
            copy.wait()


def experts(normed, upstream, marks, w_router, far_own, far_peer, far_marks, w_gate, w_up, w_down):
    tokens, width = normed.shape
    count, _, hid = w_gate.shape
    half = count // 2
    steps = half // GROUP
    experts_all = w_router.shape[1]
    once = pl.Buffered(1)
    whole = lambda step: (0, 0)

    def picked(step):
        core = lax.rem(lax.axis_index("dp"), 2)
        return (jnp.where(step < steps, (1 - core) * steps + step, core * steps + step - steps), 0, 0)

    own = lambda step: (jnp.maximum(step - steps, 0), 0, 0)
    args = [normed, upstream, marks, w_router]
    specs = [pl.BlockSpec(array.shape, whole, pipeline_mode=once) for array in args]
    args += [normed, far_own, far_peer, far_marks]
    specs += [pl.BlockSpec(memory_space=pl.ANY)] * 4
    up_block, down_block = (GROUP, width, hid), (GROUP, hid, width)
    specs += [pl.BlockSpec(up_block, picked), pl.BlockSpec(up_block, picked), pl.BlockSpec(down_block, picked)]
    gate_scratch = pltpu.VMEM((tokens, experts_all), F32)
    rows_scratch = pltpu.VMEM((tokens, width), F32)
    swap_scratch = [
        pltpu.VMEM((steps,) + up_block, BF),
        pltpu.VMEM((steps,) + up_block, BF),
        pltpu.VMEM((steps,) + down_block, BF),
    ]
    return pl.pallas_call(
        expert_kernel,
        out_shape=[
            jax.ShapeDtypeStruct((half, width, hid), BF),
            jax.ShapeDtypeStruct((half, width, hid), BF),
            jax.ShapeDtypeStruct((half, hid, width), BF),
            jax.ShapeDtypeStruct((tokens, width), BF),
            jax.ShapeDtypeStruct((tokens, width), BF),
            jax.ShapeDtypeStruct((experts_all, width), F32),
            jax.ShapeDtypeStruct((tokens, width), BF),
            jax.ShapeDtypeStruct((tokens, width), BF),
            jax.ShapeDtypeStruct(far_own.shape, BF),
            jax.ShapeDtypeStruct(far_peer.shape, BF),
            jax.ShapeDtypeStruct(far_marks.shape, BF),
        ],
        grid=(2 * steps,),
        in_specs=specs,
        out_specs=[
            pl.BlockSpec(up_block, own),
            pl.BlockSpec(up_block, own),
            pl.BlockSpec(down_block, own),
            pl.BlockSpec((tokens, width), whole, pipeline_mode=once),
            pl.BlockSpec((tokens, width), whole, pipeline_mode=once),
            pl.BlockSpec((experts_all, width), whole, pipeline_mode=once),
        ]
        + [pl.BlockSpec(memory_space=pl.ANY)] * 5,
        scratch_shapes=[
            gate_scratch, gate_scratch, gate_scratch, rows_scratch, rows_scratch,
            pltpu.VMEM((width, tokens), BF),
            pltpu.VMEM((width, GROUP * hid), BF),
            pltpu.VMEM((width, GROUP * hid), BF),
            pltpu.VMEM((GROUP * hid, tokens), BF),
            pltpu.VMEM((tokens, GROUP * hid), BF),
            pltpu.VMEM((tokens, GROUP * hid), BF),
        ]
        + swap_scratch
        + swap_scratch
        + [pltpu.SemaphoreType.DMA((2, 3, steps)), pltpu.SemaphoreType.DMA((2, 7))],
        compiler_params=pltpu.CompilerParams(
            dimension_semantics=("arbitrary",), collective_id=3, has_side_effects=True, vmem_limit_bytes=60 * MIB
        ),
        cost_estimate=pl.CostEstimate(
            flops=18 * tokens * width * count * hid,
            bytes_accessed=12 * count * width * hid,
            transcendentals=tokens * count * hid,
        ),
        name="experts",
    )(*args, w_gate, w_up, w_down)


def widen_kernel(core_ref, mine_ref, other_ref, out_ref):
    here = pl.program_id(0) == 0

    @pl.when(here)
    def _():
        out_ref[...] = mine_ref[...].astype(F32)

    @pl.when(jnp.logical_not(here))
    def _():
        out_ref[...] = other_ref[...].astype(F32)


def widen(core, mine, other):
    half, high, wide = mine.shape
    step = 4
    count = half // step
    block = (step, high, wide)
    return pl.pallas_call(
        widen_kernel,
        out_shape=jax.ShapeDtypeStruct((2 * half, high, wide), F32),
        grid_spec=pltpu.PrefetchScalarGridSpec(
            num_scalar_prefetch=1,
            grid=(2, count),
            in_specs=[
                pl.BlockSpec(block, lambda part, at, core: (jnp.where(part == 0, at, count - 1), 0, 0)),
                pl.BlockSpec(block, lambda part, at, core: (jnp.where(part == 0, 0, at), 0, 0)),
            ],
            out_specs=pl.BlockSpec(
                block, lambda part, at, core: (jnp.where(part == 0, core[0], 1 - core[0]) * count + at, 0, 0)
            ),
        ),
        compiler_params=pltpu.CompilerParams(vmem_limit_bytes=32 * MIB),
        cost_estimate=pl.CostEstimate(flops=2 * half * high * wide, bytes_accessed=12 * half * high * wide, transcendentals=0),
        name="widen",
    )(core, mine, other)


def swap(array, axis, bit):
    size = lax.axis_size(axis)
    return lax.ppermute(array, axis, [(at, at ^ bit) for at in range(size)])


def fast_device(
    block_input, first_gain, w_query, key_weight, value_weight, w_output, second_gain, w_router,
    w_gate, w_up, w_down, expert_ids, slot_index, piece_start_offsets, upstream,
):
    rows, width = block_input.shape
    local_heads = w_query.shape[1] // HEAD_SIZE
    local_kv = key_weight.shape[1] // HEAD_SIZE
    experts_all = w_router.shape[1]
    side = lax.axis_index("expert")
    core = lax.axis_index("dp") % 2
    feature_start = lax.axis_index("tensor") * (width // 4)
    scal = jnp.concatenate([side[None].astype(jnp.int32), piece_start_offsets[0]])

    axis_row = jnp.arange(experts_all, dtype=jnp.int32)[None, None, :]
    hits = (expert_ids[:, :, None] == axis_row)
    chosen = jnp.sum(hits.astype(F32), axis=1)
    kept = jnp.sum((hits & (slot_index >= 0)[:, :, None]).astype(F32), axis=1)
    marks = jnp.concatenate([chosen, kept], axis=1).astype(BF)
    marks = jnp.concatenate([marks, swap(marks, "expert", 1)], axis=0)
    far_up = swap(upstream, "dp", 2)
    peer_up = [swap(upstream[: rows // 2], "expert", 1)]

    positions = side * rows + jnp.arange(rows, dtype=jnp.int32)
    cosine_table, sine_table = rope_tables(positions)
    cosines = jnp.tile(cosine_table, (1, 4))
    sines = jnp.tile(sine_table, (1, 4))
    inputs = block_input.astype(F32)
    first_scale = norm_scale(inputs)
    first_unit = inputs * first_scale
    first_normed = (first_unit * first_gain).astype(BF)
    query_rot = apply_rotary(
        matmul(first_normed, w_query).reshape(rows, local_heads, HEAD_SIZE), cosine_table, sine_table
    ).astype(BF).reshape(rows, local_heads * HEAD_SIZE)
    key_rot = apply_rotary(
        matmul(first_normed, key_weight).reshape(rows, local_kv, HEAD_SIZE), cosine_table, sine_table
    ).astype(BF).reshape(rows, local_kv * HEAD_SIZE)
    value_low = matmul(first_normed, value_weight).astype(BF)
    both = jnp.concatenate([key_rot, value_low], axis=1)
    later, both = lax.optimization_barrier((upstream[rows // 2 :], both))
    peer_up.append(swap(later, "expert", 1))
    both = jnp.concatenate([both, swap(both, "expert", 1)], axis=0)
    keys, values = both[:, : local_kv * HEAD_SIZE], both[:, local_kv * HEAD_SIZE :]

    attended, lse, part = attend(scal, query_rot, keys, values, w_output)
    part, far_up = lax.optimization_barrier((part, far_up))
    residual, normed_all, upstream_all, far_peer_up, far_marks = residual_norm(
        part, block_input, second_gain, upstream, peer_up, marks
    )
    dwg, dwu, dwd, mix, back, route, *far = experts(
        normed_all, upstream_all, marks, w_router, far_up, far_peer_up, far_marks, w_gate, w_up, w_down
    )
    far_normed, far_other_normed, far_other_up, far_other_peer_up, far_other_marks = far
    residual_grad, residual_low, grad_second, route, mixed, sums = residual_gradient(
        back, mix, route, residual, upstream, second_gain, w_router,
        (
            far_normed, far_other_normed, far_up, far_peer_up, far_other_up, far_other_peer_up,
            far_marks, far_other_marks,
        ),
        w_gate, w_up, w_down, (dwg, dwu, dwd),
    )
    mixed = lax.psum_scatter(mixed, "tensor", scatter_dimension=1, tiled=True)

    query_grad, dk, dv, grad_output = attend_back(
        scal, query_rot, keys, values, lse, attended, residual_low, w_output, cosines, sines
    )
    grad_input, grad_query, grad_key, grad_value, grad_output, grad_router, grad_second, grad_first = input_gradient(
        block_input, residual_grad, first_gain, first_normed, query_grad, dk, dv, w_query, key_weight, value_weight,
        cosines, sines, grad_output, route, grad_second,
    )
    block_output = (
        lax.dynamic_slice_in_dim(residual.reshape(rows, width), feature_start, width // 4, 1) + mixed.astype(F32)
    ).astype(BF)
    core_row = core[None].astype(jnp.int32)
    expert_sums = [widen(core_row, item, swap(item, "dp", 1)) for item in sums]
    return (
        block_output, grad_input, grad_first[0], grad_query, grad_key, grad_value, grad_output, grad_second[0],
        grad_router.T, expert_sums[0], expert_sums[1], expert_sums[2],
    )


def solution(mesh):
    fast = mesh.shape["expert"] == 2 and mesh.shape["dp"] == 4 and mesh.shape["tensor"] == 4
    placed = (
        P(("dp", "expert"), None),
        P(),
        P(None, "tensor"),
        P(None, "tensor"),
        P(None, "tensor"),
        P("tensor", None),
        P(),
        P(),
        P("expert", None, "tensor"),
        P("expert", None, "tensor"),
        P("expert", "tensor", None),
        P(("dp", "expert"), None),
        P(("dp", "expert"), None),
        P("dp", None),
        P(("dp", "expert"), None),
    )
    return jax.shard_map(
        fast_device if fast else general_device,
        mesh=mesh,
        in_specs=placed,
        out_specs=(
            P(("dp", "expert"), "tensor"),
            P(("dp", "expert"), None),
            P(),
            P(None, "tensor"),
            P(None, "tensor"),
            P(None, "tensor"),
            P("tensor", None),
            P(),
            P(),
            P("expert", None, "tensor"),
            P("expert", None, "tensor"),
            P("expert", "tensor", None),
        ),
        check_vma=False,
    )
```

```python
import functools
import math

import jax
import jax.numpy as jnp
from jax import lax
from jax.experimental import pallas as pl
from jax.experimental.pallas import tpu as pltpu
from jax.sharding import PartitionSpec as P

HEAD_SIZE = 64
TOPK = 8
PIC = 256


epsilon = 1e-06
rope_base = 10000.0
masked_score = -1e30


def rope_tables(positions):
    steps = jnp.arange(HEAD_SIZE // 2, dtype=jnp.float32)
    inverse = jnp.exp(steps * (-2.0 * math.log(rope_base) / HEAD_SIZE))
    angle = positions.astype(jnp.float32)[:, None] * inverse[None, :]
    return (jnp.cos(angle), jnp.sin(angle))


def apply_rotary(values, cosine_table, sine_table):
    half = values.shape[-1] // 2
    first = values[..., :half]
    second = values[..., half:]
    cosine_table = cosine_table[:, None, :]
    sine_table = sine_table[:, None, :]
    return jnp.concatenate(
        [first * cosine_table - second * sine_table, second * cosine_table + first * sine_table],
        axis=-1,
    )


def unrotate(values, cosine_table, sine_table):
    half = values.shape[-1] // 2
    first = values[..., :half]
    second = values[..., half:]
    cosine_table = cosine_table[:, None, :]
    sine_table = sine_table[:, None, :]
    return jnp.concatenate(
        [first * cosine_table + second * sine_table, second * cosine_table - first * sine_table],
        axis=-1,
    )


def piece_ids(positions, offsets):
    span = 2 * PIC
    window = positions // span
    within = positions - window * span
    count = offsets.shape[0]
    match = window[:, None] == jnp.arange(count, dtype=jnp.int32)[None, :]
    start = jnp.sum(jnp.where(match, offsets[None, :], 0), axis=1)
    inside = (window < count) & (within >= start) & (within < start + PIC)
    return jnp.where(inside, window, -1)


def matmul(left, right):
    return jnp.dot(left, right, preferred_element_type=jnp.float32)


def matmul_nt(left, right):
    return lax.dot_general(
        left, right, (((1,), (1,)), ((), ())), preferred_element_type=jnp.float32
    )


def matmul_tn(left, right):
    return lax.dot_general(
        left, right, (((0,), (0,)), ((), ())), preferred_element_type=jnp.float32
    )


def norm_scale(values):
    return lax.rsqrt(jnp.mean(values * values, axis=-1, keepdims=True) + epsilon)


def norm_back(grad, unit, scale, gain):
    weighted = grad * gain
    return scale * (weighted - unit * jnp.mean(weighted * unit, axis=-1, keepdims=True))


def general_device(
    block_input,
    first_gain,
    w_query,
    key_weight,
    value_weight,
    w_output,
    second_gain,
    w_router,
    w_gate,
    w_up,
    w_down,
    expert_ids,
    slot_index,
    piece_start_offsets,
    upstream,
):
    rows_here = block_input.shape[0]
    width = block_input.shape[1]
    groups = lax.axis_size("expert")
    length = rows_here * groups
    local_heads = w_query.shape[1] // HEAD_SIZE
    local_kv = key_weight.shape[1] // HEAD_SIZE
    sharing = local_heads // local_kv
    head_rows = sharing * rows_here
    experts_all = w_router.shape[1]
    capacity = TOPK * rows_here // experts_all
    slots_all = experts_all * capacity
    score_scale = HEAD_SIZE ** (-0.5)
    positions = lax.axis_index("expert") * rows_here + jnp.arange(rows_here, dtype=jnp.int32)
    cosine_table, sine_table = rope_tables(positions)
    inputs = block_input.astype(jnp.float32)
    first_scale = norm_scale(inputs)
    first_unit = inputs * first_scale
    first_normed = (first_unit * first_gain).astype(jnp.bfloat16)
    query_rot = apply_rotary(
        matmul(first_normed, w_query).reshape(rows_here, local_heads, HEAD_SIZE),
        cosine_table,
        sine_table,
    ).astype(jnp.bfloat16)
    key_rot = (
        apply_rotary(
            matmul(first_normed, key_weight).reshape(rows_here, local_kv, HEAD_SIZE),
            cosine_table,
            sine_table,
        )
        .astype(jnp.bfloat16)
        .reshape(rows_here, local_kv * HEAD_SIZE)
    )
    value_low = matmul(first_normed, value_weight).astype(jnp.bfloat16)
    keys_all, values_all = (
        lax.all_gather(key_rot, "expert", axis=0, tiled=True),
        lax.all_gather(value_low, "expert", axis=0, tiled=True),
    )
    block = min(512, length)
    blocks = length // block

    def by_block(array):
        return array.reshape(blocks, block, local_kv, HEAD_SIZE).transpose(0, 2, 1, 3)

    def by_rows(stacked):
        return stacked.transpose(0, 2, 1, 3).reshape(length, local_kv * HEAD_SIZE)

    def head_major(array):
        return (
            array.reshape(rows_here, local_kv, sharing, HEAD_SIZE)
            .transpose(1, 2, 0, 3)
            .reshape(local_kv, head_rows, HEAD_SIZE)
        )

    def row_major(array):
        return (
            array.reshape(local_kv, sharing, rows_here, HEAD_SIZE)
            .transpose(2, 0, 1, 3)
            .reshape(rows_here, local_heads * HEAD_SIZE)
        )

    key_blocks = by_block(keys_all)
    value_blocks = by_block(values_all)
    block_starts = jnp.arange(blocks, dtype=jnp.int32) * block
    query_heads = head_major(query_rot.reshape(rows_here, local_heads * HEAD_SIZE))
    offsets = piece_start_offsets[0]
    key_pieces = piece_ids(jnp.arange(length, dtype=jnp.int32), offsets)
    query_pieces = jnp.tile(piece_ids(positions, offsets), sharing)
    query_places = jnp.tile(positions, sharing)

    def block_scores(key_block, start):
        places = start + jnp.arange(block, dtype=jnp.int32)
        pieces = lax.dynamic_slice_in_dim(key_pieces, start, block)
        causal = places[None, :] <= query_places[:, None]
        same = (pieces[None, :] == query_pieces[:, None]) & (query_pieces[:, None] >= 0)
        scores = (
            jnp.einsum("hqd,hkd->hqk", query_heads, key_block, preferred_element_type=jnp.float32)
            * score_scale
        )
        return (scores, (causal | same)[None])

    def max_step(carry, operands):
        running_max, running_sum = carry
        key_block, start = operands
        scores, allowed = block_scores(key_block, start)
        scores = jnp.where(allowed, scores, masked_score)
        new_max = jnp.maximum(running_max, jnp.max(scores, axis=-1))
        weights = jnp.where(allowed, jnp.exp(scores - new_max[..., None]), 0.0)
        new_sum = running_sum * jnp.exp(running_max - new_max) + jnp.sum(weights, axis=-1)
        return ((new_max, new_sum), None)

    start_max = jnp.full((local_kv, head_rows), masked_score, jnp.float32)
    start_sum = jnp.zeros((local_kv, head_rows), jnp.float32)
    (row_max, row_sum), _ = lax.scan(max_step, (start_max, start_sum), (key_blocks, block_starts))
    log_total = row_max + jnp.log(row_sum)

    def block_probs(key_block, start):
        scores, allowed = block_scores(key_block, start)
        return jnp.where(allowed, jnp.exp(scores - log_total[..., None]), 0.0)

    def value_step(total, operands):
        key_block, value_block, start = operands
        probs = block_probs(key_block, start).astype(jnp.bfloat16)
        return (
            total
            + jnp.einsum("hqk,hkd->hqd", probs, value_block, preferred_element_type=jnp.float32),
            None,
        )

    mixed_output, _ = lax.scan(
        value_step,
        jnp.zeros((local_kv, head_rows, HEAD_SIZE), jnp.float32),
        (key_blocks, value_blocks, block_starts),
    )
    attended = row_major(mixed_output).astype(jnp.bfloat16)
    attention = lax.psum(matmul(attended, w_output), "tensor")
    residual = inputs + attention
    second_scale = norm_scale(residual)
    second_unit = residual * second_scale
    second_normed = (second_unit * second_gain).astype(jnp.bfloat16)
    logits = matmul(second_normed, w_router)
    chosen = jnp.take_along_axis(logits, expert_ids, axis=1)
    gates = jax.nn.softmax(chosen, axis=-1)
    row_ids = jnp.arange(rows_here, dtype=jnp.int32)
    flat = jnp.where(slot_index >= 0, expert_ids * capacity + slot_index, slots_all)
    selector = (
        jnp.zeros((slots_all, rows_here), jnp.bfloat16)
        .at[flat.reshape(-1), jnp.repeat(row_ids, TOPK)]
        .set(1.0, mode="drop")
    )
    dispatched = (
        matmul(selector, second_normed).astype(jnp.bfloat16).reshape(experts_all, capacity, width)
    )
    expert_rows = lax.all_to_all(dispatched, "expert", split_axis=0, concat_axis=1, tiled=True)
    gate_in = jnp.einsum("ebd,edf->ebf", expert_rows, w_gate, preferred_element_type=jnp.float32)
    up_in = jnp.einsum("ebd,edf->ebf", expert_rows, w_up, preferred_element_type=jnp.float32)
    sigmoid_gate = jax.nn.sigmoid(gate_in)
    silu_gate = gate_in * sigmoid_gate
    hidden = (silu_gate * up_in).astype(jnp.bfloat16)
    partial_out = jnp.einsum("ebf,efd->ebd", hidden, w_down, preferred_element_type=jnp.float32)
    expert_part = lax.psum_scatter(
        partial_out.astype(jnp.bfloat16), "tensor", scatter_dimension=2, tiled=True
    )
    returned = lax.all_to_all(expert_part, "expert", split_axis=1, concat_axis=0, tiled=True)
    quarter = returned.shape[2]
    padded_out = jnp.concatenate(
        [returned.reshape(slots_all, quarter), jnp.zeros((1, quarter), jnp.bfloat16)], axis=0
    )
    feature_start = lax.axis_index("tensor") * quarter
    grad_full = upstream.astype(jnp.float32)
    grad_part = lax.dynamic_slice_in_dim(grad_full, feature_start, quarter, 1)
    mixture = jnp.zeros((rows_here, quarter), jnp.float32)
    gate_terms = []
    for pick in range(TOPK):
        picked = padded_out[flat[:, pick]].astype(jnp.float32)
        mixture = mixture + gates[:, pick : pick + 1] * picked
        gate_terms.append(jnp.sum(grad_part * picked, axis=1))
    gate_part = jnp.stack(gate_terms, axis=1)
    block_output = (lax.dynamic_slice_in_dim(residual, feature_start, quarter, 1) + mixture).astype(
        jnp.bfloat16
    )
    slot_gates = (
        jnp.zeros((slots_all + 1,), jnp.float32)
        .at[flat.reshape(-1)]
        .set(gates.reshape(-1))[:slots_all]
    )
    grad_slots = (
        (matmul(selector, upstream) * slot_gates[:, None])
        .astype(jnp.bfloat16)
        .reshape(experts_all, capacity, width)
    )
    grad_rows_in = lax.all_to_all(grad_slots, "expert", split_axis=0, concat_axis=1, tiled=True)
    hidden_grad = jnp.einsum(
        "ebd,efd->ebf", grad_rows_in, w_down, preferred_element_type=jnp.float32
    )
    grad_down = jnp.einsum("ebf,ebd->efd", hidden, grad_rows_in, preferred_element_type=jnp.float32)
    gate_in_grad = (
        hidden_grad * up_in * (sigmoid_gate * (1.0 + gate_in * (1.0 - sigmoid_gate)))
    ).astype(jnp.bfloat16)
    up_in_grad = (hidden_grad * silu_gate).astype(jnp.bfloat16)
    grad_gate = jnp.einsum(
        "ebd,ebf->edf", expert_rows, gate_in_grad, preferred_element_type=jnp.float32
    )
    grad_up = jnp.einsum(
        "ebd,ebf->edf", expert_rows, up_in_grad, preferred_element_type=jnp.float32
    )
    rows_part = jnp.einsum("ebf,edf->ebd", gate_in_grad, w_gate, preferred_element_type=jnp.float32)
    rows_part = rows_part + jnp.einsum(
        "ebf,edf->ebd", up_in_grad, w_up, preferred_element_type=jnp.float32
    )
    rows_back = lax.all_to_all(
        rows_part.astype(jnp.bfloat16), "expert", split_axis=1, concat_axis=0, tiled=True
    ).astype(rows_part.dtype)
    padded_back = jnp.concatenate(
        [rows_back.reshape(slots_all, width), jnp.zeros((1, width), jnp.float32)], axis=0
    )
    second_part = jnp.zeros((rows_here, width), jnp.float32)
    for pick in range(TOPK):
        second_part = second_part + padded_back[flat[:, pick]]
    second_sum, gate_grads = (
        lax.psum(second_part.astype(jnp.bfloat16), "tensor").astype(jnp.float32),
        lax.psum(gate_part.astype(jnp.bfloat16), "tensor").astype(jnp.float32),
    )
    chosen_grad = gates * (gate_grads - jnp.sum(gates * gate_grads, axis=1, keepdims=True))
    expert_axis = jnp.arange(experts_all, dtype=jnp.int32)
    logit_grad = jnp.zeros((rows_here, experts_all), jnp.float32)
    for pick in range(TOPK):
        logit_grad = logit_grad + jnp.where(
            expert_ids[:, pick : pick + 1] == expert_axis[None, :],
            chosen_grad[:, pick : pick + 1],
            0.0,
        )
    logit_low = logit_grad.astype(jnp.bfloat16)
    grad_router = matmul_tn(second_normed, logit_low)
    second_grad = second_sum + matmul_nt(logit_low, w_router)
    grad_second = jnp.sum(second_grad * second_unit, axis=0)
    residual_grad = grad_full + norm_back(second_grad, second_unit, second_scale, second_gain)
    residual_low = residual_grad.astype(jnp.bfloat16)
    grad_output = matmul_tn(attended, residual_low)
    attended_grad = head_major(matmul_nt(residual_low, w_output).astype(jnp.bfloat16))

    def delta_step(total, operands):
        key_block, value_block, start = operands
        probs = block_probs(key_block, start)
        prob_grad = jnp.einsum(
            "hqd,hkd->hqk", attended_grad, value_block, preferred_element_type=jnp.float32
        )
        return (total + jnp.sum(probs * prob_grad, axis=-1), None)

    delta, _ = lax.scan(
        delta_step,
        jnp.zeros((local_kv, head_rows), jnp.float32),
        (key_blocks, value_blocks, block_starts),
    )

    def grad_step(query_total, operands):
        key_block, value_block, start = operands
        probs = block_probs(key_block, start)
        prob_grad = jnp.einsum(
            "hqd,hkd->hqk", attended_grad, value_block, preferred_element_type=jnp.float32
        )
        score_grad = (probs * (prob_grad - delta[..., None])).astype(jnp.bfloat16)
        query_total = (
            query_total
            + jnp.einsum("hqk,hkd->hqd", score_grad, key_block, preferred_element_type=jnp.float32)
            * score_scale
        )
        key_grad = (
            jnp.einsum("hqk,hqd->hkd", score_grad, query_heads, preferred_element_type=jnp.float32)
            * score_scale
        )
        value_grad = jnp.einsum(
            "hqk,hqd->hkd",
            probs.astype(jnp.bfloat16),
            attended_grad,
            preferred_element_type=jnp.float32,
        )
        return (query_total, (key_grad, value_grad))

    query_total, (key_stack, value_stack) = lax.scan(
        grad_step,
        jnp.zeros((local_kv, head_rows, HEAD_SIZE), jnp.float32),
        (key_blocks, value_blocks, block_starts),
    )
    key_back, value_back = (
        lax.psum_scatter(
            by_rows(key_stack).astype(jnp.bfloat16), "expert", scatter_dimension=0, tiled=True
        ).astype(jnp.float32),
        lax.psum_scatter(
            by_rows(value_stack).astype(jnp.bfloat16), "expert", scatter_dimension=0, tiled=True
        ).astype(jnp.float32),
    )
    query_grad = (
        unrotate(
            row_major(query_total).reshape(rows_here, local_heads, HEAD_SIZE),
            cosine_table,
            sine_table,
        )
        .astype(jnp.bfloat16)
        .reshape(rows_here, local_heads * HEAD_SIZE)
    )
    key_grad = (
        unrotate(key_back.reshape(rows_here, local_kv, HEAD_SIZE), cosine_table, sine_table)
        .astype(jnp.bfloat16)
        .reshape(rows_here, local_kv * HEAD_SIZE)
    )
    value_grad = value_back.astype(jnp.bfloat16)
    grad_query = matmul_tn(first_normed, query_grad)
    grad_key = matmul_tn(first_normed, key_grad)
    grad_value = matmul_tn(first_normed, value_grad)
    first_part = (
        matmul_nt(query_grad, w_query)
        + matmul_nt(key_grad, key_weight)
        + matmul_nt(value_grad, value_weight)
    )
    first_grad = lax.psum(first_part.astype(jnp.bfloat16), "tensor").astype(jnp.float32)
    grad_first = jnp.sum(first_grad * first_unit, axis=0)
    grad_input = (
        residual_grad + norm_back(first_grad, first_unit, first_scale, first_gain)
    ).astype(jnp.bfloat16)
    dense = lax.psum(
        (grad_query, grad_key, grad_value, grad_output, grad_router, grad_first, grad_second),
        ("dp", "expert"),
    )
    expert_sums = (
        lax.psum(grad_gate.astype(jnp.bfloat16), "dp").astype(jnp.float32),
        lax.psum(grad_up.astype(jnp.bfloat16), "dp").astype(jnp.float32),
        lax.psum(grad_down.astype(jnp.bfloat16), "dp").astype(jnp.float32),
    )
    return (
        block_output,
        grad_input,
        dense[5],
        dense[0],
        dense[1],
        dense[2],
        dense[3],
        dense[6],
        dense[4],
        expert_sums[0],
        expert_sums[1],
        expert_sums[2],
    )


BF = jnp.bfloat16
F32 = jnp.float32
MIB = 1 << 20


def vmem_spec():
    return pl.BlockSpec(memory_space=pltpu.VMEM)


def smem_spec():
    return pl.BlockSpec(memory_space=pltpu.SMEM)


def allowed_pairs(offsets_ref, rows, start, count):
    side = lax.axis_index("expert")
    here = start + lax.broadcasted_iota(jnp.int32, (count, 1), 0)
    keys = lax.broadcasted_iota(jnp.int32, (1, 2 * rows), 1)
    query_place = side * rows + here
    key_place = jnp.where(keys < rows, side * rows + keys, (1 - side) * rows + keys - rows)
    span = 2 * PIC

    def piece(places):
        window = places // span
        within = places - window * span
        start = jnp.where(window == 0, offsets_ref[0, 0], offsets_ref[0, 1])
        inside = (within >= start) & (within < start + PIC)
        return jnp.where(inside, window, -1)

    query_piece = piece(query_place)
    key_piece = piece(key_place)
    return (key_place <= query_place) | ((key_piece == query_piece) & (query_piece >= 0))


def turn(values, first):
    wide = values.shape[1]
    half = HEAD_SIZE // 2
    return jnp.where(
        first, -pltpu.roll(values, wide - half, 1), pltpu.roll(values, half, 1)
    )


def attend_back_kernel(
    scal_ref, q_ref, k_ref, v_ref, lse_ref, att_ref, low_ref, wo_ref, cos_ref, sin_ref,
    dq_ref, dk_ref, dv_ref, dwo_ref,
):
    rows, wide = q_ref.shape
    heads = wide // HEAD_SIZE
    sharing = q_ref.shape[1] // k_ref.shape[1]
    scale = HEAD_SIZE**-0.5
    low = low_ref[...]
    dwo_ref[...] = matmul_tn(att_ref[...], low)
    att_grad = matmul_nt(low, wo_ref[...]).astype(BF)
    allowed = allowed_pairs(scal_ref, rows, 0, rows)
    query_parts, key_parts, value_parts = [], [], []
    for head in range(heads):
        at = head * HEAD_SIZE
        kv = head // sharing * HEAD_SIZE
        query = q_ref[:, at : at + HEAD_SIZE]
        key = k_ref[:, kv : kv + HEAD_SIZE]
        value = v_ref[:, kv : kv + HEAD_SIZE]
        grad = att_grad[:, at : at + HEAD_SIZE]
        scores = jnp.where(allowed, matmul_nt(query, key) * scale, masked_score)
        probs = jnp.exp(scores - lse_ref[:, head : head + 1])
        prob_grad = matmul_nt(grad, value)
        delta = jnp.sum(probs * prob_grad, axis=1, keepdims=True)
        score_grad = (probs * (prob_grad - delta)).astype(BF)
        query_parts.append(matmul(score_grad, key) * scale)
        key_part = matmul_tn(score_grad, query) * scale
        value_part = matmul_tn(probs.astype(BF), grad)
        if head % sharing == 0:
            key_parts.append(key_part)
            value_parts.append(value_part)
        else:
            key_parts[-1] = key_parts[-1] + key_part
            value_parts[-1] = value_parts[-1] + value_part
    dk_ref[...] = jnp.concatenate(key_parts, axis=1).astype(BF)
    dv_ref[...] = jnp.concatenate(value_parts, axis=1).astype(BF)
    rotated = jnp.concatenate(query_parts, axis=1)
    lane = lax.broadcasted_iota(jnp.int32, (1, wide), 1)
    first = lane % HEAD_SIZE < HEAD_SIZE // 2
    cosines = jnp.concatenate([cos_ref[...]] * (wide // 128), axis=1)
    sines = jnp.concatenate([sin_ref[...]] * (wide // 128), axis=1)
    dq_ref[...] = (rotated * cosines - turn(rotated, first) * sines).astype(BF)


def attend_back(scal, query, key, value, lse, attended, low, w_output, cosines, sines):
    rows, wide = query.shape
    return pl.pallas_call(
        attend_back_kernel,
        out_shape=(
            jax.ShapeDtypeStruct((rows, wide), BF),
            jax.ShapeDtypeStruct(key.shape, BF),
            jax.ShapeDtypeStruct(value.shape, BF),
            jax.ShapeDtypeStruct(w_output.shape, F32),
        ),
        in_specs=[smem_spec()] + [vmem_spec()] * 9,
        out_specs=(vmem_spec(),) * 4,
        compiler_params=pltpu.CompilerParams(vmem_limit_bytes=56 * MIB),
        name="attend_back",
    )(scal, query, key, value, lse, attended, low, w_output, cosines, sines)


MESH = pl.DeviceIdType.MESH
PART = 32
LAG = 3
LINK_COST = pl.CostEstimate(flops=4 * 10**10, bytes_accessed=10**7, transcendentals=0)


def meet(partners):
    barrier = pltpu.get_barrier_semaphore()
    count = 0
    for here, device in partners:
        here = jnp.asarray(here)

        @pl.when(here)
        def _():
            pl.semaphore_signal(barrier, inc=1, device_id=device, device_id_type=MESH)

        count = count + here.astype(jnp.int32)
    pl.semaphore_wait(barrier, count)


def line_partners():
    place = lax.axis_index("tensor")
    last = lax.axis_size("tensor") - 1
    return [(place > 0, {"tensor": place - 1}), (place < last, {"tensor": place + 1})]


class Line:
    def __init__(self, parts, term, from_left, from_right, to_right, to_left, sems):
        self.place = lax.axis_index("tensor")
        self.last = lax.axis_size("tensor") - 1
        self.parts = parts
        self.term = term
        self.from_left, self.from_right = from_left, from_right
        self.to_right, self.to_left = to_right, to_left
        self.sems = sems

    def copy(self, way, at):
        near = jnp.where(self.place < self.last, self.place + 1, self.place - 1)
        far = jnp.where(self.place > 0, self.place - 1, self.place + 1)
        source, target, device = (
            (self.to_right, self.from_left, near) if way == 0 else (self.to_left, self.from_right, far)
        )
        return pltpu.make_async_remote_copy(
            src_ref=source.at[at],
            dst_ref=target.at[at],
            send_sem=self.sems.at[2 * way, at],
            recv_sem=self.sems.at[2 * way + 1, at],
            device_id={"tensor": device},
            device_id_type=MESH,
        )

    def clear(self):
        @pl.when(self.place == 0)
        def _():
            self.from_left[...] = jnp.zeros(self.from_left.shape, self.from_left.dtype)

        @pl.when(self.place == self.last)
        def _():
            self.from_right[...] = jnp.zeros(self.from_right.shape, self.from_right.dtype)

    def step(self, at):
        for way in range(2):
            part = at - LAG * (self.place if way == 0 else self.last - self.place)
            has_source = self.place > 0 if way == 0 else self.place < self.last
            has_target = self.place < self.last if way == 0 else self.place > 0
            arrived = self.from_left if way == 0 else self.from_right
            leaving = self.to_right if way == 0 else self.to_left
            valid = (part >= 0) & (part < self.parts)

            @pl.when(valid & has_source)
            def _():
                self.copy(way, part).wait_recv()

            @pl.when(valid & has_target)
            def _():
                leaving[part] = (self.term(part) + arrived[part].astype(F32)).astype(BF)
                self.copy(way, part).start()

    def total(self, part):
        return self.term(part) + self.from_left[part].astype(F32) + self.from_right[part].astype(F32)

    def drain(self):
        def wait(part, carry):
            @pl.when(self.place < self.last)
            def _():
                self.copy(0, part).wait_send()

            @pl.when(self.place > 0)
            def _():
                self.copy(1, part).wait_send()

            return carry

        lax.fori_loop(0, self.parts, wait, 0)


def line_scratch(parts, width):
    return [pltpu.VMEM((parts, PART, width), BF)] * 4 + [pltpu.SemaphoreType.DMA((4, parts))]


def peer_copy(source, target, sems, at):
    return pltpu.make_async_remote_copy(
        src_ref=source,
        dst_ref=target,
        send_sem=sems.at[0, at],
        recv_sem=sems.at[1, at],
        device_id={"expert": 1 - lax.axis_index("expert")},
        device_id_type=MESH,
    )


def scale_of(values):
    return lax.rsqrt(jnp.mean(values * values, axis=-1, keepdims=True) + epsilon)


def plain_copy(source, target, sems, at, device):
    return pltpu.make_async_remote_copy(
        src_ref=source, dst_ref=target, send_sem=sems.at[0, at], recv_sem=sems.at[1, at],
        device_id=device, device_id_type=MESH,
    )


def beside():
    return {"dp": lax.rem(lax.axis_index("dp") + 2, 4)}


def other_core():
    place = lax.axis_index("dp")
    return {"dp": place + 1 - 2 * lax.rem(place, 2)}


EARLY = 160
BAND = 256


def front_kernel(
    offsets_ref, x_ref, gain1_ref, gain2_ref, wq_ref, wk_ref, wv_ref, wo_ref, cos_ref, sin_ref, ids_ref, slots_ref, up_hbm,
    n1_ref, q_ref, k_ref, v_ref, att_ref, lse_ref, res_ref, n_ref, marks_ref, far_marks, up_peer, far_up,
    from_left, from_right, to_right, to_left, sems, peer_sems, far_sems, terms,
):
    parts = x_ref.shape[0]
    rows, width = n1_ref.shape
    side = lax.axis_index("expert")
    peer = {"expert": 1 - side}
    line = Line(parts, lambda at: terms[at], from_left, from_right, to_right, to_left, sems)
    meet(line_partners() + [(True, peer), (True, beside())])
    early, late = pl.ds(0, EARLY), pl.ds(EARLY, rows - EARLY)
    up_early = plain_copy(up_hbm.at[early, :], up_peer.at[early, :], far_sems, 0, peer)
    up_late = plain_copy(up_hbm.at[late, :], up_peer.at[late, :], far_sems, 1, peer)
    up_cross = plain_copy(up_hbm, far_up, far_sems, 2, beside())
    key_copy = plain_copy(k_ref.at[0], k_ref.at[1], far_sems, 3, peer)
    value_copy = plain_copy(v_ref.at[0], v_ref.at[1], far_sems, 4, peer)
    marks_copy = plain_copy(marks_ref.at[0], marks_ref.at[1], far_sems, 5, peer)
    marks_cross = plain_copy(marks_ref, far_marks, far_sems, 6, beside())
    up_early.start()
    up_cross.start()
    line.clear()

    values = x_ref[...].reshape(rows, width).astype(F32)
    normed = (values * scale_of(values) * gain1_ref[...]).astype(BF)
    n1_ref[...] = normed
    queries, kv = q_ref.shape[1], k_ref.shape[2]

    def rotate(array):
        wide = array.shape[1]
        lane = lax.broadcasted_iota(jnp.int32, (1, wide), 1)
        first = lane % HEAD_SIZE < HEAD_SIZE // 2
        cosines = jnp.concatenate([cos_ref[...]] * (wide // 128), axis=1)
        sines = jnp.concatenate([sin_ref[...]] * (wide // 128), axis=1)
        return (array * cosines + turn(array, first) * sines).astype(BF)

    k_ref[0] = rotate(matmul(normed, wk_ref[...]))
    key_copy.start()
    v_ref[0] = matmul(normed, wv_ref[...]).astype(BF)
    value_copy.start()
    experts_all = marks_ref.shape[2] // 2
    lane = lax.broadcasted_iota(jnp.int32, (1, experts_all), 1)
    chosen = jnp.zeros((rows, experts_all), F32)
    kept = jnp.zeros((rows, experts_all), F32)
    for pick in range(ids_ref.shape[1]):
        hit = ids_ref[:, pick : pick + 1] == lane
        chosen = chosen + jnp.where(hit, 1.0, 0.0)
        kept = kept + jnp.where(hit & (slots_ref[:, pick : pick + 1] >= 0), 1.0, 0.0)
    marks_ref[0] = jnp.concatenate([chosen, kept], axis=1).astype(BF)
    marks_copy.start()
    up_late.start()
    q_ref[...] = rotate(matmul(normed, wq_ref[...]))
    key_copy.wait_recv()
    value_copy.wait_recv()
    sharing = queries // kv

    def attend(at):
        start = pl.multiple_of(at * BAND, BAND)
        band = pl.ds(start, BAND)
        allowed = allowed_pairs(offsets_ref, rows, start, BAND)
        pieces = []
        for head in range(queries // HEAD_SIZE):
            kv_at = head // sharing * HEAD_SIZE
            query = q_ref[band, head * HEAD_SIZE : (head + 1) * HEAD_SIZE]
            key = k_ref[:, :, kv_at : kv_at + HEAD_SIZE].reshape(2 * rows, HEAD_SIZE)
            value = v_ref[:, :, kv_at : kv_at + HEAD_SIZE].reshape(2 * rows, HEAD_SIZE)
            scores = jnp.where(allowed, matmul_nt(query, key) * (HEAD_SIZE**-0.5), masked_score)
            peak = jnp.max(scores, axis=1, keepdims=True)
            weights = jnp.exp(scores - peak)
            total = jnp.sum(weights, axis=1, keepdims=True)
            pieces.append(matmul((weights * (1.0 / total)).astype(BF), value))
            lse_ref[band, head : head + 1] = peak + jnp.log(total)
        attended = jnp.concatenate(pieces, axis=1).astype(BF)
        att_ref[band, :] = attended
        count = BAND // PART
        terms[pl.ds(at * count, count)] = matmul(attended, wo_ref[...]).reshape(count, PART, width)

    def body(at, carry):
        @pl.when(at < rows // BAND)
        def _():
            attend(at)

        @pl.when(at == 3)
        def _():
            marks_copy.wait_recv()
            marks_cross.start()

        line.step(at - 1)
        part = at - 1 - LAG * line.last

        @pl.when(part >= 0)
        def _():
            residual = x_ref[part].astype(F32) + line.total(part)
            res_ref[part] = residual
            unit = residual * scale_of(residual)
            n_ref[0, part] = (unit * gain2_ref[...]).astype(BF)
            peer_copy(n_ref.at[0, part], n_ref.at[1, part], peer_sems, part).start()

        return carry

    lax.fori_loop(0, 1 + parts + LAG * line.last, body, 0)
    line.drain()
    for copy in (key_copy, value_copy, marks_copy):
        copy.wait_send()
    for copy in (up_early, up_late, up_cross, marks_cross):
        copy.wait()

    def wait(part, carry):
        peer_copy(n_ref.at[0, part], n_ref.at[1, part], peer_sems, part).wait()
        return carry

    lax.fori_loop(0, parts, wait, 0)


def front(
    offsets, block_input, first_gain, second_gain, w_query, key_weight, value_weight, w_output, cosines, sines,
    expert_ids, slot_index, upstream, experts_all,
):
    rows, width = block_input.shape
    parts = rows // PART
    queries, kv = w_query.shape[1], key_weight.shape[1]
    any_spec = pl.BlockSpec(memory_space=pl.ANY)
    low = lambda *shape: jax.ShapeDtypeStruct(shape, BF)
    return pl.pallas_call(
        front_kernel,
        out_shape=(
            low(rows, width),
            low(rows, queries),
            low(2, rows, kv),
            low(2, rows, kv),
            low(rows, queries),
            jax.ShapeDtypeStruct((rows, 128), F32),
            jax.ShapeDtypeStruct((parts, PART, width), F32),
            low(2, parts, PART, width),
            low(2, rows, 2 * experts_all),
            low(2, rows, 2 * experts_all),
            low(rows, width),
            low(rows, width),
        ),
        in_specs=[smem_spec()] + [vmem_spec()] * 11 + [any_spec],
        out_specs=(vmem_spec(),) * 9 + (any_spec,) * 3,
        scratch_shapes=line_scratch(parts, width)
        + [
            pltpu.SemaphoreType.DMA((2, parts)),
            pltpu.SemaphoreType.DMA((2, 7)),
            pltpu.VMEM((parts, PART, width), F32),
        ],
        compiler_params=pltpu.CompilerParams(
            collective_id=0, has_side_effects=True, vmem_limit_bytes=60 * MIB
        ),
        cost_estimate=LINK_COST,
        name="front",
    )(
        offsets, block_input.reshape(parts, PART, width), first_gain[None], second_gain[None], w_query, key_weight,
        value_weight, w_output, cosines, sines, expert_ids, slot_index, upstream,
    )


UNIT = 512


def residual_grad_kernel(
    back_ref, route_ref, res_ref, up_ref, gain_ref, wr_ref, mix_ref,
    far_n, far_on, far_g0, far_g1, far_og0, far_og1, far_m, far_om,
    wg_hbm, wu_hbm, wd_hbm, pg_hbm, pu_hbm, pd_hbm,
    grad_ref, low_ref, second_ref, route_out, mixed_ref, sg_hbm, su_hbm, sd_hbm,
    from_left, from_right, to_right, to_left, sems, peer_sems, arrived, terms,
    tokens_n, tokens_g, turned, kept_gates, gates_w, ups_w, downs_w, pair_g, pair_u, pair_d, ght, dgs, dus,
    row_sems, weight_sems, pair_sems, out_sems, mix_arrived, mix_sems, marks_ref,
):
    parts = back_ref.shape[1]
    core = lax.rem(lax.axis_index("dp"), 2)
    side = lax.axis_index("expert")
    groups, group, width, hid = pair_g.shape
    experts_all = wr_ref.shape[1]
    line = Line(parts + 1, lambda at: terms[at], from_left, from_right, to_right, to_left, sems)
    line.clear()
    meet(line_partners() + [(True, {"expert": 1 - side})])

    def send(part, carry):
        peer_copy(back_ref.at[1, part], arrived.at[part], peer_sems, part).start()
        return carry

    lax.fori_loop(0, parts, send, 0)

    def send_mix(part, carry):
        peer_copy(mix_ref.at[1, part], mix_arrived.at[part], mix_sems, part).start()
        return carry

    lax.fori_loop(0, parts, send_mix, 0)
    half = tokens_n.shape[0] // 2
    quarter = half // 2
    row_copies = []
    for place, (rows, first, second, marks) in enumerate(((far_n, far_g0, far_g1, far_m), (far_on, far_og0, far_og1, far_om))):
        at = place * half
        row_copies += [
            pltpu.make_async_copy(rows, tokens_n.at[pl.ds(at, half), :], row_sems.at[0, place]),
            pltpu.make_async_copy(first, tokens_g.at[pl.ds(at, quarter), :], row_sems.at[1, place]),
            pltpu.make_async_copy(second, tokens_g.at[pl.ds(at + quarter, quarter), :], row_sems.at[2, place]),
            pltpu.make_async_copy(marks, marks_ref.at[pl.ds(at, half), :], row_sems.at[3, place]),
        ]
    weight_copies, pair_copies, out_copies = [], [], []
    for at in range(groups):
        first = core * (groups * group) + at * group
        weight_copies.append(
            [
                pltpu.make_async_copy(
                    source.at[first + expert],
                    target.at[at, :, pl.ds(expert * hid, hid)],
                    weight_sems.at[at, kind, expert],
                )
                for expert in range(group)
                for kind, (source, target) in enumerate(((wg_hbm, gates_w), (wu_hbm, ups_w)))
            ]
            + [pltpu.make_async_copy(wd_hbm.at[pl.ds(first, group)], downs_w.at[at], weight_sems.at[at, 2, 0])]
        )
        sources = (pg_hbm, pu_hbm, pd_hbm)
        held = (pair_g, pair_u, pair_d)
        targets = (sg_hbm, su_hbm, sd_hbm)
        pair_copies.append(
            [
                pltpu.make_async_copy(sources[kind].at[pl.ds(at * group, group)], held[kind].at[at], pair_sems.at[at, kind])
                for kind in range(3)
            ]
        )
        out_copies.append(
            [
                pltpu.make_async_copy(held[kind].at[at], targets[kind].at[pl.ds(at * group, group)], out_sems.at[at, kind])
                for kind in range(3)
            ]
        )
    for copy in row_copies[:4] + weight_copies[0] + row_copies[4:] + pair_copies[0] + weight_copies[1] + pair_copies[1]:
        copy.start()
    terms[parts] = route_ref[...]
    second_ref[...] = jnp.zeros(second_ref.shape, F32)
    chunks = 2 * half // UNIT
    units = chunks + 3

    def compute(at):
        for where in range(groups):
            unit = at - where * units

            @pl.when(unit == 0)
            def _():
                for copy in weight_copies[where]:
                    copy.wait()

            if where == 0:

                @pl.when(unit == 0)
                def _():
                    for copy in row_copies[:4]:
                        copy.wait()

                @pl.when(unit == half // UNIT)
                def _():
                    for copy in row_copies[4:]:
                        copy.wait()

            @pl.when(unit == chunks)
            def _():
                for copy in pair_copies[where]:
                    copy.wait()

        where = at // units
        unit = at - where * units

        @pl.when(unit < chunks)
        def _():
            place = pl.multiple_of(unit * UNIT, UNIT)
            rows = pl.ds(place, UNIT)
            token = tokens_n[rows, :]

            @pl.when(where == 0)
            def _():
                kept_gates[rows, :] = route_gates(token, marks_ref[rows, :], wr_ref[...])[1]
                turned[:, rows] = token.T

            down = downs_w[where].reshape(group * hid, width)
            column = side * (experts_all // 2) + (core * groups + where) * group
            pulled = matmul_nt(tokens_g[rows, :], down)
            weight = spread_gates(kept_gates[rows, :], column, group, hid)
            _, gated, gate_grad, up_grad = hidden_terms(token, pulled, weight, gates_w[where], ups_w[where])
            ght[:, rows] = gated.T
            dgs[rows, :] = gate_grad
            dus[rows, :] = up_grad

        @pl.when((unit >= chunks) & (unit < chunks + 2))
        def _():
            rows = pl.ds(pl.multiple_of((unit - chunks) * (width // 2), width // 2), width // 2)
            for source, held in ((dgs, pair_g), (dus, pair_u)):
                part = matmul(turned[rows, :], source[...])
                for expert in range(group):
                    more = part[:, expert * hid : (expert + 1) * hid]
                    held[where, expert, rows, :] = (held[where, expert, rows, :].astype(F32) + more).astype(BF)

        @pl.when(unit == chunks + 2)
        def _():
            part = matmul(ght[...], tokens_g[...])
            for expert in range(group):
                more = part[expert * hid : (expert + 1) * hid, :]
                pair_d[where, expert] = (pair_d[where, expert].astype(F32) + more).astype(BF)

        for where in range(groups):

            @pl.when(at == where * units + units - 1)
            def _():
                for copy in out_copies[where]:
                    copy.start()

    def body(at, carry):
        @pl.when(at < parts)
        def _():
            peer_copy(back_ref.at[1, at], arrived.at[at], peer_sems, at).wait_recv()
            terms[at] = back_ref[0, at].astype(F32) + arrived[at].astype(F32)

        line.step(at)
        part = at - LAG * line.last

        @pl.when((part >= 0) & (part < parts))
        def _():
            grad = line.total(part)
            residual = res_ref[part]
            scale = scale_of(residual)
            unit = residual * scale
            second_ref[...] += jnp.sum(grad * unit, axis=0, keepdims=True)
            result = up_ref[part].astype(F32) + norm_back(grad, unit, scale, gain_ref[...])
            grad_ref[part] = result
            low_ref[part] = result.astype(BF)

        mixed = at - MIX_STEP

        @pl.when((mixed >= 0) & (mixed < parts))
        def _():
            peer_copy(mix_ref.at[1, mixed], mix_arrived.at[mixed], mix_sems, mixed).wait_recv()
            mixed_ref[mixed] = (mix_ref[0, mixed].astype(F32) + mix_arrived[mixed].astype(F32)).astype(BF)

        @pl.when((at >= FIRST_UNIT) & (at < FIRST_UNIT + groups * units))
        def _():
            compute(at - FIRST_UNIT)

        return carry

    lax.fori_loop(0, parts + 1 + LAG * line.last, body, 0)
    route_out[...] = line.total(parts)
    line.drain()

    def wait(part, carry):
        peer_copy(back_ref.at[1, part], arrived.at[part], peer_sems, part).wait_send()
        peer_copy(mix_ref.at[1, part], mix_arrived.at[part], mix_sems, part).wait_send()
        return carry

    lax.fori_loop(0, parts, wait, 0)
    for copies in out_copies:
        for copy in copies:
            copy.wait()


FIRST_UNIT = 3
MIX_STEP = 10


def residual_gradient(back, mix, route, residual, upstream, gain, w_router, far_rows, w_gate, w_up, w_down, pairs):
    rows, width = upstream.shape
    parts = rows // PART
    half, _, hid = pairs[0].shape
    groups = half // GROUP
    tokens = 2 * far_rows[0].shape[0]
    any_spec = pl.BlockSpec(memory_space=pl.ANY)
    grad, low, second, route, mixed, *sums = pl.pallas_call(
        residual_grad_kernel,
        out_shape=[
            jax.ShapeDtypeStruct((parts, PART, width), F32),
            jax.ShapeDtypeStruct((parts, PART, width), BF),
            jax.ShapeDtypeStruct((1, width), F32),
            jax.ShapeDtypeStruct(route.shape, F32),
            jax.ShapeDtypeStruct((parts, PART, width), BF),
        ]
        + [jax.ShapeDtypeStruct(pair.shape, BF) for pair in pairs],
        in_specs=[vmem_spec()] * 7 + [any_spec] * 14,
        out_specs=[vmem_spec()] * 5 + [any_spec] * 3,
        scratch_shapes=line_scratch(parts + 1, width)
        + [
            pltpu.SemaphoreType.DMA((2, parts)),
            pltpu.VMEM((parts, PART, width), BF),
            pltpu.VMEM((parts + 1, PART, width), F32),
            pltpu.VMEM((tokens, width), BF),
            pltpu.VMEM((tokens, width), BF),
            pltpu.VMEM((width, tokens), BF),
            pltpu.VMEM((tokens, w_router.shape[1]), F32),
            pltpu.VMEM((groups, width, GROUP * hid), BF),
            pltpu.VMEM((groups, width, GROUP * hid), BF),
            pltpu.VMEM((groups, GROUP, hid, width), BF),
            pltpu.VMEM((groups, GROUP, width, hid), BF),
            pltpu.VMEM((groups, GROUP, width, hid), BF),
            pltpu.VMEM((groups, GROUP, hid, width), BF),
            pltpu.VMEM((GROUP * hid, tokens), BF),
            pltpu.VMEM((tokens, GROUP * hid), BF),
            pltpu.VMEM((tokens, GROUP * hid), BF),
            pltpu.SemaphoreType.DMA((4, 2)),
            pltpu.SemaphoreType.DMA((groups, 3, GROUP)),
            pltpu.SemaphoreType.DMA((groups, 3)),
            pltpu.SemaphoreType.DMA((groups, 3)),
            pltpu.VMEM((parts, PART, width), BF),
            pltpu.SemaphoreType.DMA((2, parts)),
            pltpu.VMEM((tokens, 2 * w_router.shape[1]), BF),
        ],
        compiler_params=pltpu.CompilerParams(
            collective_id=1, has_side_effects=True, vmem_limit_bytes=60 * MIB
        ),
        cost_estimate=LINK_COST,
        name="residual_grad",
    )(
        back.reshape(2, parts, PART, width), route, residual, upstream.reshape(parts, PART, width), gain[None],
        w_router, mix.reshape(2, parts, PART, width), *far_rows, w_gate, w_up, w_down, *pairs,
    )
    return grad, low.reshape(rows, width), second, route, mixed.reshape(rows, width), sums


def input_grad_kernel(
    x_ref, res_grad_ref, gain_ref, n_ref, dq_ref, dk_ref, dv_ref, wq_ref, wk_ref, wv_ref, cos_ref, sin_ref,
    dwo_ref, route_ref, second_ref,
    grad_ref, gq_ref, gk_ref, gv_ref, go_ref, gr_ref, gs_ref, gf_ref,
    from_left, from_right, to_right, to_left, sems, terms, kv_in, kv_sems,
    wide, wide_core, wide_x, wide_y, wide_back, tall, tall_core, tall_x, tall_y, tall_back, rows2, rows_core, rows_x, rows_y, sum_sems,
):
    parts = x_ref.shape[0]
    rows = n_ref.shape[0]
    width = n_ref.shape[1]
    core = lax.rem(lax.axis_index("dp"), 2)
    peer = {"expert": 1 - lax.axis_index("expert")}
    kv = dk_ref.shape[1]
    queries = dq_ref.shape[1]
    line = Line(parts + 1, lambda at: terms[at], from_left, from_right, to_right, to_left, sems)
    line.clear()
    meet(line_partners() + [(True, peer), (True, beside()), (True, other_core())])
    key_copy = plain_copy(dk_ref.at[pl.ds(rows, rows), :], kv_in.at[0], kv_sems, 0, peer)
    value_copy = plain_copy(dv_ref.at[pl.ds(rows, rows), :], kv_in.at[1], kv_sems, 1, peer)
    key_copy.start()
    value_copy.start()

    half_tall = tall.shape[1]
    outs = dwo_ref.shape[0]
    for at in range(2):
        low, high = at * half_tall, (at + 1) * half_tall
        top = min(high, outs)
        tall[at, : top - low, :] = dwo_ref[low:top, :].astype(BF)
        if high > outs:
            tall[at, outs - low :, :] = route_ref[...].astype(BF)

    tall_steps = [
        plain_copy(tall.at[1 - core], tall_core, sum_sems, 0, other_core()),
        plain_copy(tall.at[core], tall_y, sum_sems, 1, peer),
        plain_copy(tall.at[core], tall_x, sum_sems, 2, beside()),
        plain_copy(tall.at[core], tall_back, sum_sems, 3, other_core()),
    ]
    wide_steps = [
        plain_copy(wide.at[1 - core], wide_core, sum_sems, 4, other_core()),
        plain_copy(wide.at[core], wide_x, sum_sems, 5, beside()),
        plain_copy(wide.at[core], wide_y, sum_sems, 6, peer),
        plain_copy(wide.at[core], wide_back, sum_sems, 7, other_core()),
    ]
    rows_steps = [
        plain_copy(rows2, rows_core, sum_sems, 8, other_core()),
        plain_copy(rows2, rows_y, sum_sems, 9, peer),
        plain_copy(rows2, rows_x, sum_sems, 10, beside()),
    ]
    tall_steps[0].start()

    def add(held, arrived):
        held[...] = (held[...].astype(F32) + arrived[...].astype(F32)).astype(BF)

    query_grad = dq_ref[...]
    by_rows = (parts, rows // parts, width)
    terms[pl.ds(0, parts)] = matmul_nt(query_grad, wq_ref[...]).reshape(by_rows)
    turned = n_ref[...].T
    query_part = matmul(turned, query_grad).astype(BF)
    for at in range(2):
        wide[at, :, :queries] = query_part[at * width // 2 : (at + 1) * width // 2, :]
    key_copy.wait_recv()
    value_copy.wait_recv()
    rotated = dk_ref[:rows, :].astype(F32) + kv_in[0].astype(F32)
    lane = lax.broadcasted_iota(jnp.int32, (1, kv), 1)
    first = lane % HEAD_SIZE < HEAD_SIZE // 2
    key_grad = (rotated * cos_ref[...] - turn(rotated, first) * sin_ref[...]).astype(BF)
    value_grad = (dv_ref[:rows, :].astype(F32) + kv_in[1].astype(F32)).astype(BF)
    more = matmul_nt(key_grad, wk_ref[...]) + matmul_nt(value_grad, wv_ref[...])
    terms[pl.ds(0, parts)] += more.reshape(by_rows)
    both_part = matmul(turned, jnp.concatenate([key_grad, value_grad], axis=1)).astype(BF)
    for at in range(2):
        wide[at, :, queries:] = both_part[at * width // 2 : (at + 1) * width // 2, :]
    wide_steps[0].start()

    def gain_part(at, total):
        values = x_ref[at].astype(F32)
        return total + jnp.sum(terms[at] * (values * scale_of(values)), axis=0, keepdims=True)

    first_sum = lax.fori_loop(0, parts, gain_part, jnp.zeros((1, width), F32))
    pad = jnp.zeros((rows2.shape[0] - 2, width), F32)
    rows2[...] = jnp.concatenate([first_sum, second_ref[...], pad], axis=0).astype(BF)
    rows_steps[0].start()

    def exchange(at):
        @pl.when(at == 0)
        def _():
            rows_steps[0].wait()
            add(rows2, rows_core)
            rows_steps[1].start()
            tall_steps[0].wait()
            add(tall.at[core], tall_core)
            tall_steps[1].start()

        @pl.when(at == 1)
        def _():
            wide_steps[0].wait()
            add(wide.at[core], wide_core)

        @pl.when(at == 2)
        def _():
            rows_steps[1].wait()
            add(rows2, rows_y)
            rows_steps[2].start()
            wide_steps[1].start()

        @pl.when(at == 5)
        def _():
            rows_steps[2].wait()
            add(rows2, rows_x)
            summed = rows2[...].astype(F32)
            terms[parts] = jnp.concatenate([summed[:1, :], jnp.zeros((PART - 1, width), F32)], axis=0)
            gs_ref[...] = summed[1:2, :]

        @pl.when(at == 8)
        def _():
            tall_steps[1].wait()
            add(tall.at[core], tall_y)
            tall_steps[2].start()

        @pl.when(at == 11)
        def _():
            wide_steps[1].wait()
            add(wide.at[core], wide_x)
            wide_steps[2].start()

        @pl.when(at == 18)
        def _():
            tall_steps[2].wait()
            add(tall.at[core], tall_x)
            tall_steps[3].start()

        @pl.when(at == 20)
        def _():
            wide_steps[2].wait()
            add(wide.at[core], wide_y)
            wide_steps[3].start()

    def body(at, carry):
        exchange(at)
        line.step(at)
        part = at - LAG * line.last

        @pl.when((part >= 0) & (part < parts))
        def _():
            grad = line.total(part)
            values = x_ref[part].astype(F32)
            scale = scale_of(values)
            unit = values * scale
            grad_ref[part] = (res_grad_ref[part] + norm_back(grad, unit, scale, gain_ref[...])).astype(BF)

        return carry

    lax.fori_loop(0, parts + 1 + LAG * line.last, body, 0)
    gf_ref[...] = line.total(parts)[:1, :]
    line.drain()
    key_copy.wait_send()
    value_copy.wait_send()
    tall_steps[3].wait()
    for at in range(2):
        low, high = at * half_tall, (at + 1) * half_tall
        top = min(high, outs)
        summed = jnp.where(core == at, tall[at].astype(F32), tall_back[...].astype(F32))
        go_ref[low:top, :] = summed[: top - low, :]
        if high > outs:
            gr_ref[...] = summed[outs - low :, :]
    wide_steps[3].wait()
    for at in range(2):
        span = slice(at * width // 2, (at + 1) * width // 2)
        summed = jnp.where(core == at, wide[at].astype(F32), wide_back[...].astype(F32))
        gq_ref[span, :] = summed[:, :queries]
        gk_ref[span, :] = summed[:, queries : queries + kv]
        gv_ref[span, :] = summed[:, queries + kv :]


def input_gradient(
    block_input, residual_grad, gain, normed, dq, dk, dv, w_query, key_weight, value_weight, cosines, sines,
    grad_output, route, second,
):
    rows, width = block_input.shape
    parts = rows // PART
    columns = w_query.shape[1] + 2 * key_weight.shape[1]
    tall = (grad_output.shape[0] + route.shape[0]) // 2
    wide_half = pltpu.VMEM((width // 2, columns), BF)
    tall_half = pltpu.VMEM((tall, width), BF)
    tile = pltpu.VMEM((16, width), BF)
    grad, *rest = pl.pallas_call(
        input_grad_kernel,
        out_shape=(
            jax.ShapeDtypeStruct((parts, PART, width), BF),
            jax.ShapeDtypeStruct(w_query.shape, F32),
            jax.ShapeDtypeStruct(key_weight.shape, F32),
            jax.ShapeDtypeStruct(value_weight.shape, F32),
            jax.ShapeDtypeStruct(grad_output.shape, F32),
            jax.ShapeDtypeStruct(route.shape, F32),
            jax.ShapeDtypeStruct((1, width), F32),
            jax.ShapeDtypeStruct((1, width), F32),
        ),
        in_specs=[vmem_spec()] * 15,
        out_specs=(vmem_spec(),) * 8,
        scratch_shapes=line_scratch(parts + 1, width)
        + [
            pltpu.VMEM((parts + 1, PART, width), F32),
            pltpu.VMEM((2, rows, key_weight.shape[1]), BF),
            pltpu.SemaphoreType.DMA((2, 2)),
            pltpu.VMEM((2, width // 2, columns), BF), wide_half, wide_half, wide_half, wide_half,
            pltpu.VMEM((2, tall, width), BF), tall_half, tall_half, tall_half, tall_half,
            tile, tile, tile, tile,
            pltpu.SemaphoreType.DMA((2, 11)),
        ],
        compiler_params=pltpu.CompilerParams(
            collective_id=2, has_side_effects=True, vmem_limit_bytes=60 * MIB
        ),
        cost_estimate=LINK_COST,
        name="input_grad",
    )(
        block_input.reshape(parts, PART, width), residual_grad, gain[None], normed, dq, dk, dv,
        w_query, key_weight, value_weight, cosines, sines, grad_output, route, second,
    )
    return grad.reshape(rows, width), *rest


CHUNK = 512
GROUP = 4


def route_gates(token, marks, w_router):
    experts_all = w_router.shape[1]
    chosen = marks[:, :experts_all].astype(F32)
    kept = marks[:, experts_all:].astype(F32)
    logits = jnp.where(chosen > 0.0, matmul(token, w_router), masked_score)
    raised = jnp.exp(logits - jnp.max(logits, axis=1, keepdims=True)) * chosen
    gate = raised / jnp.sum(raised, axis=1, keepdims=True)
    return gate, gate * kept


def hidden_terms(token, pulled, weight, gate_weights, up_weights):
    gate_in = matmul(token, gate_weights)
    up_in = matmul(token, up_weights)
    sig = 0.5 * jnp.tanh(0.5 * gate_in) + 0.5
    silu = gate_in * sig
    hidden = silu * up_in
    gated = (hidden * weight).astype(BF)
    scaled = pulled * weight
    up_grad = (scaled * silu).astype(BF)
    gate_grad = (scaled * up_in * (sig + silu * (1.0 - sig))).astype(BF)
    return hidden, gated, gate_grad, up_grad


def spread_gates(kept, column, group, hid):
    lane = lax.broadcasted_iota(jnp.int32, (1, kept.shape[1]), 1)
    weights = []
    for expert in range(group):
        gate = jnp.sum(jnp.where(lane == column + expert, kept, 0.0), axis=1, keepdims=True)
        weights.append(jnp.broadcast_to(gate, (kept.shape[0], hid)))
    return jnp.concatenate(weights, axis=1)


def expert_kernel(
    n_ref, marks_ref, wr_ref, n_hbm, own_up, peer_up, far_g0, far_m, wg_ref, wu_ref, wd_ref,
    dwg_ref, dwu_ref, dwd_ref, mix_ref, back_ref, route_ref, far_n, far_on, far_g1, far_og0, far_og1, far_om,
    gates, kept_gates, gate_grads, mix, back, nt, wgs, wus, ght, dgs, dus,
    out_g, out_u, out_d, in_g, in_u, in_d, sems, far_sems, g_ref, up_sems,
):
    step = pl.program_id(0)
    steps = pl.num_programs(0) // 2
    side = lax.axis_index("expert")
    dp = lax.axis_index("dp")
    core = lax.rem(dp, 2)
    other = other_core()
    tokens, width = n_ref.shape
    experts_all = wr_ref.shape[1]
    group, _, hid = wg_ref.shape
    chunks = tokens // CHUNK
    lane = lax.broadcasted_iota(jnp.int32, (1, experts_all), 1)

    def copies(slot):
        return [
            pltpu.make_async_remote_copy(
                src_ref=source.at[slot], dst_ref=target.at[slot],
                send_sem=sems.at[0, kind, slot], recv_sem=sems.at[1, kind, slot],
                device_id=other, device_id_type=MESH,
            )
            for kind, (source, target) in enumerate(((out_g, in_g), (out_u, in_u), (out_d, in_d)))
        ]

    half = tokens // 2
    cross = [
        plain_copy(n_hbm.at[pl.ds(at * half, half), :], far_n.at[pl.ds(at * half, half), :], far_sems, at, beside())
        for at in range(2)
    ]
    share = [
        plain_copy(far_n.at[pl.ds(at * half, half), :], far_on.at[pl.ds(at * half, half), :], far_sems, 2 + at, other)
        for at in range(2)
    ]
    peer = {"expert": 1 - side}
    turn_up = plain_copy(far_g0, far_g1, far_sems, 4, peer)
    share_up = plain_copy(far_g1, far_og1, far_sems, 5, other)
    early = [
        plain_copy(source, target, far_sems, 6 + at, other)
        for at, (source, target) in enumerate(((far_g0, far_og0), (far_m, far_om)))
    ]
    loads = [
        pltpu.make_async_copy(source, g_ref.at[pl.ds(at * half, half), :], up_sems.at[at])
        for at, source in enumerate((own_up, peer_up))
    ]

    @pl.when(step == 0)
    def _():
        for copy in loads:
            copy.start()
        meet([(True, other), (True, beside()), (True, peer)])
        for copy in cross + early + [turn_up]:
            copy.start()

        def start(at, carry):
            rows = pl.ds(pl.multiple_of(at * CHUNK, CHUNK), CHUNK)
            gate, kept_gate = route_gates(n_ref[rows, :], marks_ref[rows, :], wr_ref[...])
            gates[rows, :] = gate
            kept_gates[rows, :] = kept_gate
            mix[rows, :] = jnp.zeros((CHUNK, width), F32)
            back[rows, :] = jnp.zeros((CHUNK, width), F32)
            gate_grads[rows, :] = jnp.zeros((CHUNK, experts_all), F32)
            return carry

        lax.fori_loop(0, chunks, start, 0)
        for at in range(chunks):
            nt[:, at * CHUNK : (at + 1) * CHUNK] = n_ref[at * CHUNK : (at + 1) * CHUNK, :].T
        for copy in loads:
            copy.wait()

    @pl.when(step == steps)
    def _():
        cross[0].wait_recv()
        share[0].start()
        turn_up.wait_recv()
        share_up.start()

    for expert in range(group):
        wgs[:, expert * hid : (expert + 1) * hid] = wg_ref[expert]
        wus[:, expert * hid : (expert + 1) * hid] = wu_ref[expert]
    first = step < steps
    block = jnp.where(first, (1 - core) * steps + step, core * steps + step - steps)
    column = side * (experts_all // 2) + block * group

    for at in range(chunks):
        rows = slice(at * CHUNK, (at + 1) * CHUNK)
        token = n_ref[rows, :]
        down = wd_ref[...].reshape(group * hid, width)
        pulled = matmul_nt(g_ref[rows, :], down)
        weight = spread_gates(kept_gates[rows, :], column, group, hid)
        hidden, gated, gate_grad, up_grad = hidden_terms(token, pulled, weight, wgs[...], wus[...])
        products = hidden * pulled
        grads = gate_grads[rows, :]
        for expert in range(group):
            product = jnp.sum(products[:, expert * hid : (expert + 1) * hid], axis=1, keepdims=True)
            grads = grads + jnp.where(lane == column + expert, product, 0.0)
        gate_grads[rows, :] = grads
        ght[:, rows] = gated.T
        dgs[rows, :] = gate_grad
        dus[rows, :] = up_grad
        mix[rows, :] += matmul(gated, down)
        back[rows, :] += matmul_nt(gate_grad, wgs[...]) + matmul_nt(up_grad, wus[...])

    def weight_grads(store_rows, store_down):
        for at in range(width // CHUNK):
            rows = slice(at * CHUNK, (at + 1) * CHUNK)
            turned = nt[rows, :]
            gate_part = matmul(turned, dgs[...])
            up_part = matmul(turned, dus[...])
            for expert in range(group):
                inner = slice(expert * hid, (expert + 1) * hid)
                store_rows(expert, rows, gate_part[:, inner], up_part[:, inner])
        down_part = matmul(ght[...], g_ref[...])
        for expert in range(group):
            store_down(expert, down_part[expert * hid : (expert + 1) * hid, :])

    @pl.when(first)
    def _():
        def store_rows(expert, rows, gate_part, up_part):
            out_g[step, expert, rows, :] = gate_part.astype(BF)
            out_u[step, expert, rows, :] = up_part.astype(BF)

        def store_down(expert, part):
            out_d[step, expert] = part.astype(BF)

        weight_grads(store_rows, store_down)
        for copy in copies(step):
            copy.start()

    @pl.when(step >= steps)
    def _():
        slot = step - steps
        for copy in copies(slot):
            copy.wait_recv()

        def store_rows(expert, rows, gate_part, up_part):
            dwg_ref[expert, rows, :] = (gate_part + in_g[slot, expert, rows, :].astype(F32)).astype(BF)
            dwu_ref[expert, rows, :] = (up_part + in_u[slot, expert, rows, :].astype(F32)).astype(BF)

        def store_down(expert, part):
            dwd_ref[expert] = (part + in_d[slot, expert].astype(F32)).astype(BF)

        weight_grads(store_rows, store_down)
        for copy in copies(slot):
            copy.wait_send()

    @pl.when(step == 2 * steps - 1)
    def _():
        cross[1].wait_recv()
        share[1].start()
        route_ref[...] = jnp.zeros(route_ref.shape, F32)

        def finish(at, carry):
            rows = pl.ds(pl.multiple_of(at * CHUNK, CHUNK), CHUNK)
            mix_ref[rows, :] = mix[rows, :].astype(BF)
            grads = gate_grads[rows, :] * kept_gates[rows, :]
            chosen_grad = grads - gates[rows, :] * jnp.sum(grads, axis=1, keepdims=True)
            low = chosen_grad.astype(BF)
            back_ref[rows, :] = (back[rows, :] + matmul_nt(low, wr_ref[...])).astype(BF)
            route_ref[...] += matmul_tn(low, n_ref[rows, :])
            return carry

        lax.fori_loop(0, chunks, finish, 0)
        for copy in cross + [turn_up]:
            copy.wait_send()
        for copy in share + early + [share_up]:
            copy.wait()


def experts(normed, marks, w_router, upstream, peer_up, far_up, far_marks, w_gate, w_up, w_down):
    tokens, width = normed.shape
    count, _, hid = w_gate.shape
    half = count // 2
    steps = half // GROUP
    experts_all = w_router.shape[1]
    once = pl.Buffered(1)
    whole = lambda step: (0, 0)

    def picked(step):
        core = lax.rem(lax.axis_index("dp"), 2)
        return (jnp.where(step < steps, (1 - core) * steps + step, core * steps + step - steps), 0, 0)

    own = lambda step: (jnp.maximum(step - steps, 0), 0, 0)
    args = [normed, marks, w_router]
    specs = [pl.BlockSpec(array.shape, whole, pipeline_mode=once) for array in args]
    args += [normed, upstream, peer_up, far_up, far_marks]
    specs += [pl.BlockSpec(memory_space=pl.ANY)] * 5
    up_block, down_block = (GROUP, width, hid), (GROUP, hid, width)
    specs += [pl.BlockSpec(up_block, picked), pl.BlockSpec(up_block, picked), pl.BlockSpec(down_block, picked)]
    gate_scratch = pltpu.VMEM((tokens, experts_all), F32)
    rows_scratch = pltpu.VMEM((tokens, width), F32)
    swap_scratch = [
        pltpu.VMEM((steps,) + up_block, BF),
        pltpu.VMEM((steps,) + up_block, BF),
        pltpu.VMEM((steps,) + down_block, BF),
    ]
    return pl.pallas_call(
        expert_kernel,
        out_shape=[
            jax.ShapeDtypeStruct((half, width, hid), BF),
            jax.ShapeDtypeStruct((half, width, hid), BF),
            jax.ShapeDtypeStruct((half, hid, width), BF),
            jax.ShapeDtypeStruct((tokens, width), BF),
            jax.ShapeDtypeStruct((tokens, width), BF),
            jax.ShapeDtypeStruct((experts_all, width), F32),
            jax.ShapeDtypeStruct((tokens, width), BF),
            jax.ShapeDtypeStruct((tokens, width), BF),
            jax.ShapeDtypeStruct(far_up.shape, BF),
            jax.ShapeDtypeStruct(far_up.shape, BF),
            jax.ShapeDtypeStruct(far_up.shape, BF),
            jax.ShapeDtypeStruct(far_marks.shape, BF),
        ],
        grid=(2 * steps,),
        in_specs=specs,
        out_specs=[
            pl.BlockSpec(up_block, own),
            pl.BlockSpec(up_block, own),
            pl.BlockSpec(down_block, own),
            pl.BlockSpec((tokens, width), whole, pipeline_mode=once),
            pl.BlockSpec((tokens, width), whole, pipeline_mode=once),
            pl.BlockSpec((experts_all, width), whole, pipeline_mode=once),
        ]
        + [pl.BlockSpec(memory_space=pl.ANY)] * 6,
        scratch_shapes=[
            gate_scratch, gate_scratch, gate_scratch, rows_scratch, rows_scratch,
            pltpu.VMEM((width, tokens), BF),
            pltpu.VMEM((width, GROUP * hid), BF),
            pltpu.VMEM((width, GROUP * hid), BF),
            pltpu.VMEM((GROUP * hid, tokens), BF),
            pltpu.VMEM((tokens, GROUP * hid), BF),
            pltpu.VMEM((tokens, GROUP * hid), BF),
        ]
        + swap_scratch
        + swap_scratch
        + [pltpu.SemaphoreType.DMA((2, 3, steps)), pltpu.SemaphoreType.DMA((2, 8)), pltpu.VMEM((tokens, width), BF), pltpu.SemaphoreType.DMA((2,))],
        compiler_params=pltpu.CompilerParams(
            dimension_semantics=("arbitrary",), collective_id=3, has_side_effects=True, vmem_limit_bytes=60 * MIB
        ),
        cost_estimate=pl.CostEstimate(
            flops=18 * tokens * width * count * hid,
            bytes_accessed=12 * count * width * hid,
            transcendentals=tokens * count * hid,
        ),
        name="experts",
    )(*args, w_gate, w_up, w_down)


def widen_kernel(core_ref, mine_ref, other_ref, out_ref):
    here = pl.program_id(0) == 0

    @pl.when(here)
    def _():
        out_ref[...] = mine_ref[...].astype(F32)

    @pl.when(jnp.logical_not(here))
    def _():
        out_ref[...] = other_ref[...].astype(F32)


def widen(core, mine, other):
    half, high, wide = mine.shape
    step = 4
    count = half // step
    block = (step, high, wide)
    return pl.pallas_call(
        widen_kernel,
        out_shape=jax.ShapeDtypeStruct((2 * half, high, wide), F32),
        grid_spec=pltpu.PrefetchScalarGridSpec(
            num_scalar_prefetch=1,
            grid=(2, count),
            in_specs=[
                pl.BlockSpec(block, lambda part, at, core: (jnp.where(part == 0, at, count - 1), 0, 0)),
                pl.BlockSpec(block, lambda part, at, core: (jnp.where(part == 0, 0, at), 0, 0)),
            ],
            out_specs=pl.BlockSpec(
                block, lambda part, at, core: (jnp.where(part == 0, core[0], 1 - core[0]) * count + at, 0, 0)
            ),
        ),
        compiler_params=pltpu.CompilerParams(vmem_limit_bytes=32 * MIB),
        cost_estimate=pl.CostEstimate(flops=2 * half * high * wide, bytes_accessed=12 * half * high * wide, transcendentals=0),
        name="widen",
    )(core, mine, other)


def swap(array, axis, bit):
    size = lax.axis_size(axis)
    return lax.ppermute(array, axis, [(at, at ^ bit) for at in range(size)])


def fast_device(
    block_input, first_gain, w_query, key_weight, value_weight, w_output, second_gain, w_router,
    w_gate, w_up, w_down, expert_ids, slot_index, piece_start_offsets, upstream,
):
    rows, width = block_input.shape
    experts_all = w_router.shape[1]
    core = lax.axis_index("dp") % 2
    feature_start = lax.axis_index("tensor") * (width // 4)
    positions = lax.axis_index("expert") * rows + jnp.arange(rows, dtype=jnp.int32)
    cosine_table, sine_table = rope_tables(positions)
    cosines = jnp.tile(cosine_table, (1, 4))
    sines = jnp.tile(sine_table, (1, 4))
    (
        first_normed, query_rot, keys, values, attended, lse, residual, normed_all, marks, far_marks, peer_up, far_up,
    ) = front(
        piece_start_offsets, block_input, first_gain, second_gain, w_query, key_weight, value_weight, w_output,
        cosines, sines, expert_ids, slot_index, upstream, experts_all,
    )
    keys, values = keys.reshape(2 * rows, -1), values.reshape(2 * rows, -1)
    normed_all = normed_all.reshape(2 * rows, width)
    marks = marks.reshape(2 * rows, 2 * experts_all)
    far_marks = far_marks.reshape(2 * rows, 2 * experts_all)
    dwg, dwu, dwd, mix, back, route, *far = experts(
        normed_all, marks, w_router, upstream, peer_up, far_up, far_marks, w_gate, w_up, w_down
    )
    far_normed, far_other_normed, far_peer_up, far_other_up, far_other_peer_up, far_other_marks = far
    residual_grad, residual_low, grad_second, route, mixed, sums = residual_gradient(
        back, mix, route, residual, upstream, second_gain, w_router,
        (
            far_normed, far_other_normed, far_up, far_peer_up, far_other_up, far_other_peer_up,
            far_marks, far_other_marks,
        ),
        w_gate, w_up, w_down, (dwg, dwu, dwd),
    )
    mixed = lax.psum_scatter(mixed, "tensor", scatter_dimension=1, tiled=True)

    query_grad, dk, dv, grad_output = attend_back(
        piece_start_offsets, query_rot, keys, values, lse, attended, residual_low, w_output, cosines, sines
    )
    grad_input, grad_query, grad_key, grad_value, grad_output, grad_router, grad_second, grad_first = input_gradient(
        block_input, residual_grad, first_gain, first_normed, query_grad, dk, dv, w_query, key_weight, value_weight,
        cosines, sines, grad_output, route, grad_second,
    )
    block_output = (
        lax.dynamic_slice_in_dim(residual.reshape(rows, width), feature_start, width // 4, 1) + mixed.astype(F32)
    ).astype(BF)
    core_row = core[None].astype(jnp.int32)
    expert_sums = [widen(core_row, item, swap(item, "dp", 1)) for item in sums]
    return (
        block_output, grad_input, grad_first[0], grad_query, grad_key, grad_value, grad_output, grad_second[0],
        grad_router.T, expert_sums[0], expert_sums[1], expert_sums[2],
    )


def solution(mesh):
    fast = mesh.shape["expert"] == 2 and mesh.shape["dp"] == 4 and mesh.shape["tensor"] == 4
    placed = (
        P(("dp", "expert"), None),
        P(),
        P(None, "tensor"),
        P(None, "tensor"),
        P(None, "tensor"),
        P("tensor", None),
        P(),
        P(),
        P("expert", None, "tensor"),
        P("expert", None, "tensor"),
        P("expert", "tensor", None),
        P(("dp", "expert"), None),
        P(("dp", "expert"), None),
        P("dp", None),
        P(("dp", "expert"), None),
    )
    return jax.shard_map(
        fast_device if fast else general_device,
        mesh=mesh,
        in_specs=placed,
        out_specs=(
            P(("dp", "expert"), "tensor"),
            P(("dp", "expert"), None),
            P(),
            P(None, "tensor"),
            P(None, "tensor"),
            P(None, "tensor"),
            P("tensor", None),
            P(),
            P(),
            P("expert", None, "tensor"),
            P("expert", None, "tensor"),
            P("expert", "tensor", None),
        ),
        check_vma=False,
    )
```

```python
import functools
import math

import jax
import jax.numpy as jnp
from jax import lax
from jax.experimental import pallas as pl
from jax.experimental.pallas import tpu as pltpu
from jax.sharding import PartitionSpec as P

HEAD_SIZE = 64
TOPK = 8
PIC = 256


epsilon = 1e-06
rope_base = 10000.0
masked_score = -1e30


def rope_tables(positions):
    steps = jnp.arange(HEAD_SIZE // 2, dtype=jnp.float32)
    inverse = jnp.exp(steps * (-2.0 * math.log(rope_base) / HEAD_SIZE))
    angle = positions.astype(jnp.float32)[:, None] * inverse[None, :]
    return (jnp.cos(angle), jnp.sin(angle))


def apply_rotary(values, cosine_table, sine_table):
    half = values.shape[-1] // 2
    first = values[..., :half]
    second = values[..., half:]
    cosine_table = cosine_table[:, None, :]
    sine_table = sine_table[:, None, :]
    return jnp.concatenate(
        [first * cosine_table - second * sine_table, second * cosine_table + first * sine_table],
        axis=-1,
    )


def unrotate(values, cosine_table, sine_table):
    half = values.shape[-1] // 2
    first = values[..., :half]
    second = values[..., half:]
    cosine_table = cosine_table[:, None, :]
    sine_table = sine_table[:, None, :]
    return jnp.concatenate(
        [first * cosine_table + second * sine_table, second * cosine_table - first * sine_table],
        axis=-1,
    )


def piece_ids(positions, offsets):
    span = 2 * PIC
    window = positions // span
    within = positions - window * span
    count = offsets.shape[0]
    match = window[:, None] == jnp.arange(count, dtype=jnp.int32)[None, :]
    start = jnp.sum(jnp.where(match, offsets[None, :], 0), axis=1)
    inside = (window < count) & (within >= start) & (within < start + PIC)
    return jnp.where(inside, window, -1)


def matmul(left, right):
    return jnp.dot(left, right, preferred_element_type=jnp.float32)


def matmul_nt(left, right):
    return lax.dot_general(
        left, right, (((1,), (1,)), ((), ())), preferred_element_type=jnp.float32
    )


def matmul_tn(left, right):
    return lax.dot_general(
        left, right, (((0,), (0,)), ((), ())), preferred_element_type=jnp.float32
    )


def norm_scale(values):
    return lax.rsqrt(jnp.mean(values * values, axis=-1, keepdims=True) + epsilon)


def norm_back(grad, unit, scale, gain):
    weighted = grad * gain
    return scale * (weighted - unit * jnp.mean(weighted * unit, axis=-1, keepdims=True))


def general_device(
    block_input,
    first_gain,
    w_query,
    key_weight,
    value_weight,
    w_output,
    second_gain,
    w_router,
    w_gate,
    w_up,
    w_down,
    expert_ids,
    slot_index,
    piece_start_offsets,
    upstream,
):
    rows_here = block_input.shape[0]
    width = block_input.shape[1]
    groups = lax.axis_size("expert")
    length = rows_here * groups
    local_heads = w_query.shape[1] // HEAD_SIZE
    local_kv = key_weight.shape[1] // HEAD_SIZE
    sharing = local_heads // local_kv
    head_rows = sharing * rows_here
    experts_all = w_router.shape[1]
    capacity = TOPK * rows_here // experts_all
    slots_all = experts_all * capacity
    score_scale = HEAD_SIZE ** (-0.5)
    positions = lax.axis_index("expert") * rows_here + jnp.arange(rows_here, dtype=jnp.int32)
    cosine_table, sine_table = rope_tables(positions)
    inputs = block_input.astype(jnp.float32)
    first_scale = norm_scale(inputs)
    first_unit = inputs * first_scale
    first_normed = (first_unit * first_gain).astype(jnp.bfloat16)
    query_rot = apply_rotary(
        matmul(first_normed, w_query).reshape(rows_here, local_heads, HEAD_SIZE),
        cosine_table,
        sine_table,
    ).astype(jnp.bfloat16)
    key_rot = (
        apply_rotary(
            matmul(first_normed, key_weight).reshape(rows_here, local_kv, HEAD_SIZE),
            cosine_table,
            sine_table,
        )
        .astype(jnp.bfloat16)
        .reshape(rows_here, local_kv * HEAD_SIZE)
    )
    value_low = matmul(first_normed, value_weight).astype(jnp.bfloat16)
    keys_all, values_all = (
        lax.all_gather(key_rot, "expert", axis=0, tiled=True),
        lax.all_gather(value_low, "expert", axis=0, tiled=True),
    )
    block = min(512, length)
    blocks = length // block

    def by_block(array):
        return array.reshape(blocks, block, local_kv, HEAD_SIZE).transpose(0, 2, 1, 3)

    def by_rows(stacked):
        return stacked.transpose(0, 2, 1, 3).reshape(length, local_kv * HEAD_SIZE)

    def head_major(array):
        return (
            array.reshape(rows_here, local_kv, sharing, HEAD_SIZE)
            .transpose(1, 2, 0, 3)
            .reshape(local_kv, head_rows, HEAD_SIZE)
        )

    def row_major(array):
        return (
            array.reshape(local_kv, sharing, rows_here, HEAD_SIZE)
            .transpose(2, 0, 1, 3)
            .reshape(rows_here, local_heads * HEAD_SIZE)
        )

    key_blocks = by_block(keys_all)
    value_blocks = by_block(values_all)
    block_starts = jnp.arange(blocks, dtype=jnp.int32) * block
    query_heads = head_major(query_rot.reshape(rows_here, local_heads * HEAD_SIZE))
    offsets = piece_start_offsets[0]
    key_pieces = piece_ids(jnp.arange(length, dtype=jnp.int32), offsets)
    query_pieces = jnp.tile(piece_ids(positions, offsets), sharing)
    query_places = jnp.tile(positions, sharing)

    def block_scores(key_block, start):
        places = start + jnp.arange(block, dtype=jnp.int32)
        pieces = lax.dynamic_slice_in_dim(key_pieces, start, block)
        causal = places[None, :] <= query_places[:, None]
        same = (pieces[None, :] == query_pieces[:, None]) & (query_pieces[:, None] >= 0)
        scores = (
            jnp.einsum("hqd,hkd->hqk", query_heads, key_block, preferred_element_type=jnp.float32)
            * score_scale
        )
        return (scores, (causal | same)[None])

    def max_step(carry, operands):
        running_max, running_sum = carry
        key_block, start = operands
        scores, allowed = block_scores(key_block, start)
        scores = jnp.where(allowed, scores, masked_score)
        new_max = jnp.maximum(running_max, jnp.max(scores, axis=-1))
        weights = jnp.where(allowed, jnp.exp(scores - new_max[..., None]), 0.0)
        new_sum = running_sum * jnp.exp(running_max - new_max) + jnp.sum(weights, axis=-1)
        return ((new_max, new_sum), None)

    start_max = jnp.full((local_kv, head_rows), masked_score, jnp.float32)
    start_sum = jnp.zeros((local_kv, head_rows), jnp.float32)
    (row_max, row_sum), _ = lax.scan(max_step, (start_max, start_sum), (key_blocks, block_starts))
    log_total = row_max + jnp.log(row_sum)

    def block_probs(key_block, start):
        scores, allowed = block_scores(key_block, start)
        return jnp.where(allowed, jnp.exp(scores - log_total[..., None]), 0.0)

    def value_step(total, operands):
        key_block, value_block, start = operands
        probs = block_probs(key_block, start).astype(jnp.bfloat16)
        return (
            total
            + jnp.einsum("hqk,hkd->hqd", probs, value_block, preferred_element_type=jnp.float32),
            None,
        )

    mixed_output, _ = lax.scan(
        value_step,
        jnp.zeros((local_kv, head_rows, HEAD_SIZE), jnp.float32),
        (key_blocks, value_blocks, block_starts),
    )
    attended = row_major(mixed_output).astype(jnp.bfloat16)
    attention = lax.psum(matmul(attended, w_output), "tensor")
    residual = inputs + attention
    second_scale = norm_scale(residual)
    second_unit = residual * second_scale
    second_normed = (second_unit * second_gain).astype(jnp.bfloat16)
    logits = matmul(second_normed, w_router)
    chosen = jnp.take_along_axis(logits, expert_ids, axis=1)
    gates = jax.nn.softmax(chosen, axis=-1)
    row_ids = jnp.arange(rows_here, dtype=jnp.int32)
    flat = jnp.where(slot_index >= 0, expert_ids * capacity + slot_index, slots_all)
    selector = (
        jnp.zeros((slots_all, rows_here), jnp.bfloat16)
        .at[flat.reshape(-1), jnp.repeat(row_ids, TOPK)]
        .set(1.0, mode="drop")
    )
    dispatched = (
        matmul(selector, second_normed).astype(jnp.bfloat16).reshape(experts_all, capacity, width)
    )
    expert_rows = lax.all_to_all(dispatched, "expert", split_axis=0, concat_axis=1, tiled=True)
    gate_in = jnp.einsum("ebd,edf->ebf", expert_rows, w_gate, preferred_element_type=jnp.float32)
    up_in = jnp.einsum("ebd,edf->ebf", expert_rows, w_up, preferred_element_type=jnp.float32)
    sigmoid_gate = jax.nn.sigmoid(gate_in)
    silu_gate = gate_in * sigmoid_gate
    hidden = (silu_gate * up_in).astype(jnp.bfloat16)
    partial_out = jnp.einsum("ebf,efd->ebd", hidden, w_down, preferred_element_type=jnp.float32)
    expert_part = lax.psum_scatter(
        partial_out.astype(jnp.bfloat16), "tensor", scatter_dimension=2, tiled=True
    )
    returned = lax.all_to_all(expert_part, "expert", split_axis=1, concat_axis=0, tiled=True)
    quarter = returned.shape[2]
    padded_out = jnp.concatenate(
        [returned.reshape(slots_all, quarter), jnp.zeros((1, quarter), jnp.bfloat16)], axis=0
    )
    feature_start = lax.axis_index("tensor") * quarter
    grad_full = upstream.astype(jnp.float32)
    grad_part = lax.dynamic_slice_in_dim(grad_full, feature_start, quarter, 1)
    mixture = jnp.zeros((rows_here, quarter), jnp.float32)
    gate_terms = []
    for pick in range(TOPK):
        picked = padded_out[flat[:, pick]].astype(jnp.float32)
        mixture = mixture + gates[:, pick : pick + 1] * picked
        gate_terms.append(jnp.sum(grad_part * picked, axis=1))
    gate_part = jnp.stack(gate_terms, axis=1)
    block_output = (lax.dynamic_slice_in_dim(residual, feature_start, quarter, 1) + mixture).astype(
        jnp.bfloat16
    )
    slot_gates = (
        jnp.zeros((slots_all + 1,), jnp.float32)
        .at[flat.reshape(-1)]
        .set(gates.reshape(-1))[:slots_all]
    )
    grad_slots = (
        (matmul(selector, upstream) * slot_gates[:, None])
        .astype(jnp.bfloat16)
        .reshape(experts_all, capacity, width)
    )
    grad_rows_in = lax.all_to_all(grad_slots, "expert", split_axis=0, concat_axis=1, tiled=True)
    hidden_grad = jnp.einsum(
        "ebd,efd->ebf", grad_rows_in, w_down, preferred_element_type=jnp.float32
    )
    grad_down = jnp.einsum("ebf,ebd->efd", hidden, grad_rows_in, preferred_element_type=jnp.float32)
    gate_in_grad = (
        hidden_grad * up_in * (sigmoid_gate * (1.0 + gate_in * (1.0 - sigmoid_gate)))
    ).astype(jnp.bfloat16)
    up_in_grad = (hidden_grad * silu_gate).astype(jnp.bfloat16)
    grad_gate = jnp.einsum(
        "ebd,ebf->edf", expert_rows, gate_in_grad, preferred_element_type=jnp.float32
    )
    grad_up = jnp.einsum(
        "ebd,ebf->edf", expert_rows, up_in_grad, preferred_element_type=jnp.float32
    )
    rows_part = jnp.einsum("ebf,edf->ebd", gate_in_grad, w_gate, preferred_element_type=jnp.float32)
    rows_part = rows_part + jnp.einsum(
        "ebf,edf->ebd", up_in_grad, w_up, preferred_element_type=jnp.float32
    )
    rows_back = lax.all_to_all(
        rows_part.astype(jnp.bfloat16), "expert", split_axis=1, concat_axis=0, tiled=True
    ).astype(rows_part.dtype)
    padded_back = jnp.concatenate(
        [rows_back.reshape(slots_all, width), jnp.zeros((1, width), jnp.float32)], axis=0
    )
    second_part = jnp.zeros((rows_here, width), jnp.float32)
    for pick in range(TOPK):
        second_part = second_part + padded_back[flat[:, pick]]
    second_sum, gate_grads = (
        lax.psum(second_part.astype(jnp.bfloat16), "tensor").astype(jnp.float32),
        lax.psum(gate_part.astype(jnp.bfloat16), "tensor").astype(jnp.float32),
    )
    chosen_grad = gates * (gate_grads - jnp.sum(gates * gate_grads, axis=1, keepdims=True))
    expert_axis = jnp.arange(experts_all, dtype=jnp.int32)
    logit_grad = jnp.zeros((rows_here, experts_all), jnp.float32)
    for pick in range(TOPK):
        logit_grad = logit_grad + jnp.where(
            expert_ids[:, pick : pick + 1] == expert_axis[None, :],
            chosen_grad[:, pick : pick + 1],
            0.0,
        )
    logit_low = logit_grad.astype(jnp.bfloat16)
    grad_router = matmul_tn(second_normed, logit_low)
    second_grad = second_sum + matmul_nt(logit_low, w_router)
    grad_second = jnp.sum(second_grad * second_unit, axis=0)
    residual_grad = grad_full + norm_back(second_grad, second_unit, second_scale, second_gain)
    residual_low = residual_grad.astype(jnp.bfloat16)
    grad_output = matmul_tn(attended, residual_low)
    attended_grad = head_major(matmul_nt(residual_low, w_output).astype(jnp.bfloat16))

    def delta_step(total, operands):
        key_block, value_block, start = operands
        probs = block_probs(key_block, start)
        prob_grad = jnp.einsum(
            "hqd,hkd->hqk", attended_grad, value_block, preferred_element_type=jnp.float32
        )
        return (total + jnp.sum(probs * prob_grad, axis=-1), None)

    delta, _ = lax.scan(
        delta_step,
        jnp.zeros((local_kv, head_rows), jnp.float32),
        (key_blocks, value_blocks, block_starts),
    )

    def grad_step(query_total, operands):
        key_block, value_block, start = operands
        probs = block_probs(key_block, start)
        prob_grad = jnp.einsum(
            "hqd,hkd->hqk", attended_grad, value_block, preferred_element_type=jnp.float32
        )
        score_grad = (probs * (prob_grad - delta[..., None])).astype(jnp.bfloat16)
        query_total = (
            query_total
            + jnp.einsum("hqk,hkd->hqd", score_grad, key_block, preferred_element_type=jnp.float32)
            * score_scale
        )
        key_grad = (
            jnp.einsum("hqk,hqd->hkd", score_grad, query_heads, preferred_element_type=jnp.float32)
            * score_scale
        )
        value_grad = jnp.einsum(
            "hqk,hqd->hkd",
            probs.astype(jnp.bfloat16),
            attended_grad,
            preferred_element_type=jnp.float32,
        )
        return (query_total, (key_grad, value_grad))

    query_total, (key_stack, value_stack) = lax.scan(
        grad_step,
        jnp.zeros((local_kv, head_rows, HEAD_SIZE), jnp.float32),
        (key_blocks, value_blocks, block_starts),
    )
    key_back, value_back = (
        lax.psum_scatter(
            by_rows(key_stack).astype(jnp.bfloat16), "expert", scatter_dimension=0, tiled=True
        ).astype(jnp.float32),
        lax.psum_scatter(
            by_rows(value_stack).astype(jnp.bfloat16), "expert", scatter_dimension=0, tiled=True
        ).astype(jnp.float32),
    )
    query_grad = (
        unrotate(
            row_major(query_total).reshape(rows_here, local_heads, HEAD_SIZE),
            cosine_table,
            sine_table,
        )
        .astype(jnp.bfloat16)
        .reshape(rows_here, local_heads * HEAD_SIZE)
    )
    key_grad = (
        unrotate(key_back.reshape(rows_here, local_kv, HEAD_SIZE), cosine_table, sine_table)
        .astype(jnp.bfloat16)
        .reshape(rows_here, local_kv * HEAD_SIZE)
    )
    value_grad = value_back.astype(jnp.bfloat16)
    grad_query = matmul_tn(first_normed, query_grad)
    grad_key = matmul_tn(first_normed, key_grad)
    grad_value = matmul_tn(first_normed, value_grad)
    first_part = (
        matmul_nt(query_grad, w_query)
        + matmul_nt(key_grad, key_weight)
        + matmul_nt(value_grad, value_weight)
    )
    first_grad = lax.psum(first_part.astype(jnp.bfloat16), "tensor").astype(jnp.float32)
    grad_first = jnp.sum(first_grad * first_unit, axis=0)
    grad_input = (
        residual_grad + norm_back(first_grad, first_unit, first_scale, first_gain)
    ).astype(jnp.bfloat16)
    dense = lax.psum(
        (grad_query, grad_key, grad_value, grad_output, grad_router, grad_first, grad_second),
        ("dp", "expert"),
    )
    expert_sums = (
        lax.psum(grad_gate.astype(jnp.bfloat16), "dp").astype(jnp.float32),
        lax.psum(grad_up.astype(jnp.bfloat16), "dp").astype(jnp.float32),
        lax.psum(grad_down.astype(jnp.bfloat16), "dp").astype(jnp.float32),
    )
    return (
        block_output,
        grad_input,
        dense[5],
        dense[0],
        dense[1],
        dense[2],
        dense[3],
        dense[6],
        dense[4],
        expert_sums[0],
        expert_sums[1],
        expert_sums[2],
    )


BF = jnp.bfloat16
F32 = jnp.float32
MIB = 1 << 20


def vmem_spec():
    return pl.BlockSpec(memory_space=pltpu.VMEM)


def smem_spec():
    return pl.BlockSpec(memory_space=pltpu.SMEM)


def allowed_pairs(offsets_ref, rows, start, count):
    side = lax.axis_index("expert")
    here = start + lax.broadcasted_iota(jnp.int32, (count, 1), 0)
    keys = lax.broadcasted_iota(jnp.int32, (1, 2 * rows), 1)
    query_place = side * rows + here
    key_place = jnp.where(keys < rows, side * rows + keys, (1 - side) * rows + keys - rows)
    span = 2 * PIC

    def piece(places):
        window = places // span
        within = places - window * span
        start = jnp.where(window == 0, offsets_ref[0, 0], offsets_ref[0, 1])
        inside = (within >= start) & (within < start + PIC)
        return jnp.where(inside, window, -1)

    query_piece = piece(query_place)
    key_piece = piece(key_place)
    return (key_place <= query_place) | ((key_piece == query_piece) & (query_piece >= 0))


def turn(values, first):
    wide = values.shape[1]
    half = HEAD_SIZE // 2
    return jnp.where(
        first, -pltpu.roll(values, wide - half, 1), pltpu.roll(values, half, 1)
    )


MESH = pl.DeviceIdType.MESH
PART = 32
LAG = 3
LINK_COST = pl.CostEstimate(flops=4 * 10**10, bytes_accessed=10**7, transcendentals=0)


def meet(partners):
    barrier = pltpu.get_barrier_semaphore()
    count = 0
    for here, device in partners:
        here = jnp.asarray(here)

        @pl.when(here)
        def _():
            pl.semaphore_signal(barrier, inc=1, device_id=device, device_id_type=MESH)

        count = count + here.astype(jnp.int32)
    pl.semaphore_wait(barrier, count)


def line_partners():
    place = lax.axis_index("tensor")
    last = lax.axis_size("tensor") - 1
    return [(place > 0, {"tensor": place - 1}), (place < last, {"tensor": place + 1})]


class Line:
    def __init__(self, parts, term, from_left, from_right, to_right, to_left, sems):
        self.place = lax.axis_index("tensor")
        self.last = lax.axis_size("tensor") - 1
        self.parts = parts
        self.term = term
        self.from_left, self.from_right = from_left, from_right
        self.to_right, self.to_left = to_right, to_left
        self.sems = sems

    def copy(self, way, at):
        near = jnp.where(self.place < self.last, self.place + 1, self.place - 1)
        far = jnp.where(self.place > 0, self.place - 1, self.place + 1)
        source, target, device = (
            (self.to_right, self.from_left, near) if way == 0 else (self.to_left, self.from_right, far)
        )
        return pltpu.make_async_remote_copy(
            src_ref=source.at[at],
            dst_ref=target.at[at],
            send_sem=self.sems.at[2 * way, at],
            recv_sem=self.sems.at[2 * way + 1, at],
            device_id={"tensor": device},
            device_id_type=MESH,
        )

    def clear(self):
        @pl.when(self.place == 0)
        def _():
            self.from_left[...] = jnp.zeros(self.from_left.shape, self.from_left.dtype)

        @pl.when(self.place == self.last)
        def _():
            self.from_right[...] = jnp.zeros(self.from_right.shape, self.from_right.dtype)

    def step(self, at):
        for way in range(2):
            part = at - LAG * (self.place if way == 0 else self.last - self.place)
            has_source = self.place > 0 if way == 0 else self.place < self.last
            has_target = self.place < self.last if way == 0 else self.place > 0
            arrived = self.from_left if way == 0 else self.from_right
            leaving = self.to_right if way == 0 else self.to_left
            valid = (part >= 0) & (part < self.parts)

            @pl.when(valid & has_source)
            def _():
                self.copy(way, part).wait_recv()

            @pl.when(valid & has_target)
            def _():
                leaving[part] = (self.term(part) + arrived[part].astype(F32)).astype(BF)
                self.copy(way, part).start()

    def total(self, part):
        return self.term(part) + self.from_left[part].astype(F32) + self.from_right[part].astype(F32)

    def drain(self):
        def wait(part, carry):
            @pl.when(self.place < self.last)
            def _():
                self.copy(0, part).wait_send()

            @pl.when(self.place > 0)
            def _():
                self.copy(1, part).wait_send()

            return carry

        lax.fori_loop(0, self.parts, wait, 0)


def line_scratch(parts, width):
    return [pltpu.VMEM((parts, PART, width), BF)] * 4 + [pltpu.SemaphoreType.DMA((4, parts))]


def peer_copy(source, target, sems, at):
    return pltpu.make_async_remote_copy(
        src_ref=source,
        dst_ref=target,
        send_sem=sems.at[0, at],
        recv_sem=sems.at[1, at],
        device_id={"expert": 1 - lax.axis_index("expert")},
        device_id_type=MESH,
    )


def scale_of(values):
    return lax.rsqrt(jnp.mean(values * values, axis=-1, keepdims=True) + epsilon)


def plain_copy(source, target, sems, at, device):
    return pltpu.make_async_remote_copy(
        src_ref=source, dst_ref=target, send_sem=sems.at[0, at], recv_sem=sems.at[1, at],
        device_id=device, device_id_type=MESH,
    )


def beside():
    return {"dp": lax.rem(lax.axis_index("dp") + 2, 4)}


def other_core():
    place = lax.axis_index("dp")
    return {"dp": place + 1 - 2 * lax.rem(place, 2)}


EARLY = 160
BAND = 256


def front_kernel(
    offsets_ref, x_ref, gain1_ref, gain2_ref, wq_ref, wk_ref, wv_ref, wo_ref, cos_ref, sin_ref, ids_ref, slots_ref, up_hbm,
    n1_ref, q_ref, k_ref, v_ref, att_ref, lse_ref, res_ref, n_ref, marks_ref, far_marks, up_peer, far_up,
    from_left, from_right, to_right, to_left, sems, peer_sems, far_sems, terms,
):
    parts = x_ref.shape[0]
    rows, width = n1_ref.shape
    side = lax.axis_index("expert")
    peer = {"expert": 1 - side}
    line = Line(parts, lambda at: terms[at], from_left, from_right, to_right, to_left, sems)
    meet(line_partners() + [(True, peer), (True, beside())])
    early, late = pl.ds(0, EARLY), pl.ds(EARLY, rows - EARLY)
    up_early = plain_copy(up_hbm.at[early, :], up_peer.at[early, :], far_sems, 0, peer)
    up_late = plain_copy(up_hbm.at[late, :], up_peer.at[late, :], far_sems, 1, peer)
    up_cross = plain_copy(up_hbm, far_up, far_sems, 2, beside())
    key_copy = plain_copy(k_ref.at[0], k_ref.at[1], far_sems, 3, peer)
    value_copy = plain_copy(v_ref.at[0], v_ref.at[1], far_sems, 4, peer)
    marks_copy = plain_copy(marks_ref.at[0], marks_ref.at[1], far_sems, 5, peer)
    marks_cross = plain_copy(marks_ref, far_marks, far_sems, 6, beside())
    up_early.start()
    up_cross.start()
    line.clear()

    values = x_ref[...].reshape(rows, width).astype(F32)
    normed = (values * scale_of(values) * gain1_ref[...]).astype(BF)
    n1_ref[...] = normed
    queries, kv = q_ref.shape[1], k_ref.shape[2]

    def rotate(array):
        wide = array.shape[1]
        lane = lax.broadcasted_iota(jnp.int32, (1, wide), 1)
        first = lane % HEAD_SIZE < HEAD_SIZE // 2
        cosines = jnp.concatenate([cos_ref[...]] * (wide // 128), axis=1)
        sines = jnp.concatenate([sin_ref[...]] * (wide // 128), axis=1)
        return (array * cosines + turn(array, first) * sines).astype(BF)

    k_ref[0] = rotate(matmul(normed, wk_ref[...]))
    key_copy.start()
    v_ref[0] = matmul(normed, wv_ref[...]).astype(BF)
    value_copy.start()
    experts_all = marks_ref.shape[2] // 2
    lane = lax.broadcasted_iota(jnp.int32, (1, experts_all), 1)
    chosen = jnp.zeros((rows, experts_all), F32)
    kept = jnp.zeros((rows, experts_all), F32)
    for pick in range(ids_ref.shape[1]):
        hit = ids_ref[:, pick : pick + 1] == lane
        chosen = chosen + jnp.where(hit, 1.0, 0.0)
        kept = kept + jnp.where(hit & (slots_ref[:, pick : pick + 1] >= 0), 1.0, 0.0)
    marks_ref[0] = jnp.concatenate([chosen, kept], axis=1).astype(BF)
    marks_copy.start()
    up_late.start()
    q_ref[...] = rotate(matmul(normed, wq_ref[...]))
    key_copy.wait_recv()
    value_copy.wait_recv()
    sharing = queries // kv

    def attend(at):
        start = pl.multiple_of(at * BAND, BAND)
        band = pl.ds(start, BAND)
        allowed = allowed_pairs(offsets_ref, rows, start, BAND)
        pieces = []
        for head in range(queries // HEAD_SIZE):
            kv_at = head // sharing * HEAD_SIZE
            query = q_ref[band, head * HEAD_SIZE : (head + 1) * HEAD_SIZE]
            key = k_ref[:, :, kv_at : kv_at + HEAD_SIZE].reshape(2 * rows, HEAD_SIZE)
            value = v_ref[:, :, kv_at : kv_at + HEAD_SIZE].reshape(2 * rows, HEAD_SIZE)
            scores = jnp.where(allowed, matmul_nt(query, key) * (HEAD_SIZE**-0.5), masked_score)
            peak = jnp.max(scores, axis=1, keepdims=True)
            weights = jnp.exp(scores - peak)
            total = jnp.sum(weights, axis=1, keepdims=True)
            pieces.append(matmul((weights * (1.0 / total)).astype(BF), value))
            lse_ref[band, head : head + 1] = peak + jnp.log(total)
        attended = jnp.concatenate(pieces, axis=1).astype(BF)
        att_ref[band, :] = attended
        count = BAND // PART
        terms[pl.ds(at * count, count)] = matmul(attended, wo_ref[...]).reshape(count, PART, width)

    def body(at, carry):
        @pl.when(at < rows // BAND)
        def _():
            attend(at)

        @pl.when(at == 3)
        def _():
            marks_copy.wait_recv()
            marks_cross.start()

        line.step(at - 1)
        part = at - 1 - LAG * line.last

        @pl.when(part >= 0)
        def _():
            residual = x_ref[part].astype(F32) + line.total(part)
            res_ref[part] = residual
            unit = residual * scale_of(residual)
            n_ref[0, part] = (unit * gain2_ref[...]).astype(BF)
            peer_copy(n_ref.at[0, part], n_ref.at[1, part], peer_sems, part).start()

        return carry

    lax.fori_loop(0, 1 + parts + LAG * line.last, body, 0)
    line.drain()
    for copy in (key_copy, value_copy, marks_copy):
        copy.wait_send()
    for copy in (up_early, up_late, up_cross, marks_cross):
        copy.wait()

    def wait(part, carry):
        peer_copy(n_ref.at[0, part], n_ref.at[1, part], peer_sems, part).wait()
        return carry

    lax.fori_loop(0, parts, wait, 0)


def front(
    offsets, block_input, first_gain, second_gain, w_query, key_weight, value_weight, w_output, cosines, sines,
    expert_ids, slot_index, upstream, experts_all,
):
    rows, width = block_input.shape
    parts = rows // PART
    queries, kv = w_query.shape[1], key_weight.shape[1]
    any_spec = pl.BlockSpec(memory_space=pl.ANY)
    low = lambda *shape: jax.ShapeDtypeStruct(shape, BF)
    return pl.pallas_call(
        front_kernel,
        out_shape=(
            low(rows, width),
            low(rows, queries),
            low(2, rows, kv),
            low(2, rows, kv),
            low(rows, queries),
            jax.ShapeDtypeStruct((rows, 128), F32),
            jax.ShapeDtypeStruct((parts, PART, width), F32),
            low(2, parts, PART, width),
            low(2, rows, 2 * experts_all),
            low(2, rows, 2 * experts_all),
            low(rows, width),
            low(rows, width),
        ),
        in_specs=[smem_spec()] + [vmem_spec()] * 11 + [any_spec],
        out_specs=(vmem_spec(),) * 9 + (any_spec,) * 3,
        scratch_shapes=line_scratch(parts, width)
        + [
            pltpu.SemaphoreType.DMA((2, parts)),
            pltpu.SemaphoreType.DMA((2, 7)),
            pltpu.VMEM((parts, PART, width), F32),
        ],
        compiler_params=pltpu.CompilerParams(
            collective_id=0, has_side_effects=True, vmem_limit_bytes=60 * MIB
        ),
        cost_estimate=LINK_COST,
        name="front",
    )(
        offsets, block_input.reshape(parts, PART, width), first_gain[None], second_gain[None], w_query, key_weight,
        value_weight, w_output, cosines, sines, expert_ids, slot_index, upstream,
    )


UNIT = 512


def residual_grad_kernel(
    back_ref, route_ref, res_ref, up_ref, gain_ref, wr_ref, mix_ref,
    far_n, far_on, far_g0, far_g1, far_og0, far_og1, far_m, far_om,
    wg_hbm, wu_hbm, wd_hbm, pg_hbm, pu_hbm, pd_hbm,
    grad_ref, low_ref, second_ref, route_out, mixed_ref, sg_hbm, su_hbm, sd_hbm, og_hbm, ou_hbm, od_hbm,
    from_left, from_right, to_right, to_left, sems, peer_sems, arrived, terms,
    tokens_n, tokens_g, turned, kept_gates, gates_w, ups_w, downs_w, pair_g, pair_u, pair_d, ght, dgs, dus,
    row_sems, weight_sems, pair_sems, out_sems, mix_arrived, mix_sems, marks_ref, share_sems,
):
    parts = back_ref.shape[1]
    core = lax.rem(lax.axis_index("dp"), 2)
    side = lax.axis_index("expert")
    groups, group, width, hid = pair_g.shape
    experts_all = wr_ref.shape[1]
    line = Line(parts + 1, lambda at: terms[at], from_left, from_right, to_right, to_left, sems)
    line.clear()
    meet(line_partners() + [(True, {"expert": 1 - side}), (True, other_core())])

    def send(part, carry):
        peer_copy(back_ref.at[1, part], arrived.at[part], peer_sems, part).start()
        return carry

    lax.fori_loop(0, parts, send, 0)

    def send_mix(part, carry):
        peer_copy(mix_ref.at[1, part], mix_arrived.at[part], mix_sems, part).start()
        return carry

    lax.fori_loop(0, parts, send_mix, 0)
    half = tokens_n.shape[0] // 2
    quarter = half // 2
    row_copies = []
    for place, (rows, first, second, marks) in enumerate(((far_n, far_g0, far_g1, far_m), (far_on, far_og0, far_og1, far_om))):
        at = place * half
        row_copies += [
            pltpu.make_async_copy(rows, tokens_n.at[pl.ds(at, half), :], row_sems.at[0, place]),
            pltpu.make_async_copy(first, tokens_g.at[pl.ds(at, quarter), :], row_sems.at[1, place]),
            pltpu.make_async_copy(second, tokens_g.at[pl.ds(at + quarter, quarter), :], row_sems.at[2, place]),
            pltpu.make_async_copy(marks, marks_ref.at[pl.ds(at, half), :], row_sems.at[3, place]),
        ]
    weight_copies, pair_copies, out_copies = [], [], []
    for at in range(groups):
        first = core * (groups * group) + at * group
        weight_copies.append(
            [
                pltpu.make_async_copy(
                    source.at[first + expert],
                    target.at[at, :, pl.ds(expert * hid, hid)],
                    weight_sems.at[at, kind, expert],
                )
                for expert in range(group)
                for kind, (source, target) in enumerate(((wg_hbm, gates_w), (wu_hbm, ups_w)))
            ]
            + [pltpu.make_async_copy(wd_hbm.at[pl.ds(first, group)], downs_w.at[at], weight_sems.at[at, 2, 0])]
        )
        sources = (pg_hbm, pu_hbm, pd_hbm)
        held = (pair_g, pair_u, pair_d)
        targets = (sg_hbm, su_hbm, sd_hbm)
        others = (og_hbm, ou_hbm, od_hbm)
        pair_copies.append(
            [
                pltpu.make_async_copy(sources[kind].at[pl.ds(at * group, group)], held[kind].at[at], pair_sems.at[at, kind])
                for kind in range(3)
            ]
        )
        out_copies.append(
            [
                pltpu.make_async_copy(held[kind].at[at], targets[kind].at[pl.ds(at * group, group)], out_sems.at[at, kind])
                for kind in range(3)
            ]
            + [
                plain_copy(
                    held[kind].at[at], others[kind].at[pl.ds(at * group, group)], share_sems.at[at], kind, other_core()
                )
                for kind in range(3)
            ]
        )
    for copy in row_copies[:4] + weight_copies[0] + row_copies[4:] + pair_copies[0] + weight_copies[1] + pair_copies[1]:
        copy.start()
    terms[parts] = route_ref[...]
    second_ref[...] = jnp.zeros(second_ref.shape, F32)
    chunks = 2 * half // UNIT
    units = chunks + 3

    def compute(at):
        for where in range(groups):
            unit = at - where * units

            @pl.when(unit == 0)
            def _():
                for copy in weight_copies[where]:
                    copy.wait()

            if where == 0:

                @pl.when(unit == 0)
                def _():
                    for copy in row_copies[:4]:
                        copy.wait()

                @pl.when(unit == half // UNIT)
                def _():
                    for copy in row_copies[4:]:
                        copy.wait()

            @pl.when(unit == chunks)
            def _():
                for copy in pair_copies[where]:
                    copy.wait()

        where = at // units
        unit = at - where * units

        @pl.when(unit < chunks)
        def _():
            place = pl.multiple_of(unit * UNIT, UNIT)
            rows = pl.ds(place, UNIT)
            token = tokens_n[rows, :]

            @pl.when(where == 0)
            def _():
                kept_gates[rows, :] = route_gates(token, marks_ref[rows, :], wr_ref[...])[1]
                turned[:, rows] = token.T

            down = downs_w[where].reshape(group * hid, width)
            column = side * (experts_all // 2) + (core * groups + where) * group
            pulled = matmul_nt(tokens_g[rows, :], down)
            weight = spread_gates(kept_gates[rows, :], column, group, hid)
            _, gated, gate_grad, up_grad = hidden_terms(token, pulled, weight, gates_w[where], ups_w[where])
            ght[:, rows] = gated.T
            dgs[rows, :] = gate_grad
            dus[rows, :] = up_grad

        @pl.when((unit >= chunks) & (unit < chunks + 2))
        def _():
            rows = pl.ds(pl.multiple_of((unit - chunks) * (width // 2), width // 2), width // 2)
            for source, held in ((dgs, pair_g), (dus, pair_u)):
                part = matmul(turned[rows, :], source[...])
                for expert in range(group):
                    more = part[:, expert * hid : (expert + 1) * hid]
                    held[where, expert, rows, :] = (held[where, expert, rows, :].astype(F32) + more).astype(BF)

        @pl.when(unit == chunks + 2)
        def _():
            part = matmul(ght[...], tokens_g[...])
            for expert in range(group):
                more = part[expert * hid : (expert + 1) * hid, :]
                pair_d[where, expert] = (pair_d[where, expert].astype(F32) + more).astype(BF)

        for where in range(groups):

            @pl.when(at == where * units + units - 1)
            def _():
                for copy in out_copies[where]:
                    copy.start()

    def add_mix(part):
        peer_copy(mix_ref.at[1, part], mix_arrived.at[part], mix_sems, part).wait_recv()
        mixed_ref[part] = (mix_ref[0, part].astype(F32) + mix_arrived[part].astype(F32)).astype(BF)

    def body(at, carry):
        @pl.when(at < parts)
        def _():
            peer_copy(back_ref.at[1, at], arrived.at[at], peer_sems, at).wait_recv()
            terms[at] = back_ref[0, at].astype(F32) + arrived[at].astype(F32)

        line.step(at)
        part = at - LAG * line.last

        @pl.when((part >= 0) & (part < parts))
        def _():
            grad = line.total(part)
            residual = res_ref[part]
            scale = scale_of(residual)
            unit = residual * scale
            second_ref[...] += jnp.sum(grad * unit, axis=0, keepdims=True)
            result = up_ref[part].astype(F32) + norm_back(grad, unit, scale, gain_ref[...])
            grad_ref[part] = result
            low_ref[part] = result.astype(BF)

        @pl.when(at >= MIX_STEP)
        def _():
            add_mix(at - MIX_STEP)

        @pl.when((at >= FIRST_UNIT) & (at < FIRST_UNIT + groups * units))
        def _():
            compute(at - FIRST_UNIT)

        return carry

    steps = parts + 1 + LAG * line.last
    lax.fori_loop(0, steps, body, 0)
    route_out[...] = line.total(parts)

    def rest(part, carry):
        add_mix(part)
        return carry

    lax.fori_loop(steps - MIX_STEP, parts, rest, 0)
    line.drain()

    def wait(part, carry):
        peer_copy(back_ref.at[1, part], arrived.at[part], peer_sems, part).wait_send()
        peer_copy(mix_ref.at[1, part], mix_arrived.at[part], mix_sems, part).wait_send()
        return carry

    lax.fori_loop(0, parts, wait, 0)
    for copies in out_copies:
        for copy in copies:
            copy.wait()


FIRST_UNIT = 3
MIX_STEP = 17


def residual_gradient(back, mix, route, residual, upstream, gain, w_router, far_rows, w_gate, w_up, w_down, pairs):
    rows, width = upstream.shape
    parts = rows // PART
    half, _, hid = pairs[0].shape
    groups = half // GROUP
    tokens = 2 * far_rows[0].shape[0]
    any_spec = pl.BlockSpec(memory_space=pl.ANY)
    grad, low, second, route, mixed, *sums = pl.pallas_call(
        residual_grad_kernel,
        out_shape=[
            jax.ShapeDtypeStruct((parts, PART, width), F32),
            jax.ShapeDtypeStruct((parts, PART, width), BF),
            jax.ShapeDtypeStruct((1, width), F32),
            jax.ShapeDtypeStruct(route.shape, F32),
            jax.ShapeDtypeStruct((parts, PART, width), BF),
        ]
        + [jax.ShapeDtypeStruct(pair.shape, BF) for pair in pairs] * 2,
        in_specs=[vmem_spec()] * 7 + [any_spec] * 14,
        out_specs=[vmem_spec()] * 5 + [any_spec] * 6,
        scratch_shapes=line_scratch(parts + 1, width)
        + [
            pltpu.SemaphoreType.DMA((2, parts)),
            pltpu.VMEM((parts, PART, width), BF),
            pltpu.VMEM((parts + 1, PART, width), F32),
            pltpu.VMEM((tokens, width), BF),
            pltpu.VMEM((tokens, width), BF),
            pltpu.VMEM((width, tokens), BF),
            pltpu.VMEM((tokens, w_router.shape[1]), F32),
            pltpu.VMEM((groups, width, GROUP * hid), BF),
            pltpu.VMEM((groups, width, GROUP * hid), BF),
            pltpu.VMEM((groups, GROUP, hid, width), BF),
            pltpu.VMEM((groups, GROUP, width, hid), BF),
            pltpu.VMEM((groups, GROUP, width, hid), BF),
            pltpu.VMEM((groups, GROUP, hid, width), BF),
            pltpu.VMEM((GROUP * hid, tokens), BF),
            pltpu.VMEM((tokens, GROUP * hid), BF),
            pltpu.VMEM((tokens, GROUP * hid), BF),
            pltpu.SemaphoreType.DMA((4, 2)),
            pltpu.SemaphoreType.DMA((groups, 3, GROUP)),
            pltpu.SemaphoreType.DMA((groups, 3)),
            pltpu.SemaphoreType.DMA((groups, 3)),
            pltpu.VMEM((parts, PART, width), BF),
            pltpu.SemaphoreType.DMA((2, parts)),
            pltpu.VMEM((tokens, 2 * w_router.shape[1]), BF),
            pltpu.SemaphoreType.DMA((groups, 2, 3)),
        ],
        compiler_params=pltpu.CompilerParams(
            collective_id=1, has_side_effects=True, vmem_limit_bytes=60 * MIB
        ),
        cost_estimate=LINK_COST,
        name="residual_grad",
    )(
        back.reshape(2, parts, PART, width), route, residual, upstream.reshape(parts, PART, width), gain[None],
        w_router, mix.reshape(2, parts, PART, width), *far_rows, w_gate, w_up, w_down, *pairs,
    )
    return grad, low.reshape(rows, width), second, route, mixed, sums


def input_grad_kernel(
    offsets_ref, x_ref, res_grad_ref, gain_ref, n_ref, wq_ref, wk_ref, wv_ref, wo_ref, cos_ref, sin_ref,
    q_ref, k_ref, v_ref, lse_ref, att_ref, low_ref, route_ref, second_ref, mix_ref, res_ref,
    grad_ref, wide_out, wide_back, tall_out, tall_back, gains_ref, block_ref,
    from_left, from_right, to_right, to_left, sems, terms, kv_out, kv_in, kv_sems,
    wide, wide_core, wide_x, wide_y, tall, tall_core, tall_x, tall_y, rows2, rows_core, rows_x, rows_y, sum_sems,
    mix_left, mix_right, mix_to_right, mix_to_left, mix_sems,
):
    parts = x_ref.shape[0]
    rows = n_ref.shape[0]
    width = n_ref.shape[1]
    core = lax.rem(lax.axis_index("dp"), 2)
    peer = {"expert": 1 - lax.axis_index("expert")}
    kv = wk_ref.shape[1]
    queries = wq_ref.shape[1]
    line = Line(parts + 1, lambda at: terms[at], from_left, from_right, to_right, to_left, sems)
    spread = Spread(mix_ref, mix_left, mix_right, mix_to_right, mix_to_left, mix_sems)
    line.clear()
    spread.clear()
    meet(line_partners() + [(True, peer), (True, beside()), (True, other_core())])
    spread.step(0)
    key_copy = plain_copy(kv_out.at[0, pl.ds(rows, rows), :], kv_in.at[0], kv_sems, 0, peer)
    value_copy = plain_copy(kv_out.at[1, pl.ds(rows, rows), :], kv_in.at[1], kv_sems, 1, peer)

    scale = HEAD_SIZE**-0.5
    low = low_ref[...]
    out_part = matmul(att_ref[...].T, low).astype(BF)
    att_grad = matmul_nt(low, wo_ref[...]).astype(BF)
    half_tall = tall.shape[1]
    outs = wo_ref.shape[0]
    for at in range(2):
        start, high = at * half_tall, (at + 1) * half_tall
        top = min(high, outs)
        tall[at, : top - start, :] = out_part[start:top, :]
        if high > outs:
            tall[at, outs - start :, :] = route_ref[...].astype(BF)

    tall_steps = [
        plain_copy(tall.at[1 - core], tall_core, sum_sems, 0, other_core()),
        plain_copy(tall.at[core], tall_y, sum_sems, 1, peer),
        plain_copy(tall.at[core], tall_x, sum_sems, 2, beside()),
        plain_copy(tall.at[core], tall_back, sum_sems, 3, other_core()),
    ]
    wide_steps = [
        plain_copy(wide.at[1 - core], wide_core, sum_sems, 4, other_core()),
        plain_copy(wide.at[core], wide_x, sum_sems, 5, beside()),
        plain_copy(wide.at[core], wide_y, sum_sems, 6, peer),
        plain_copy(wide.at[core], wide_back, sum_sems, 7, other_core()),
    ]
    rows_steps = [
        plain_copy(rows2, rows_core, sum_sems, 8, other_core()),
        plain_copy(rows2, rows_y, sum_sems, 9, peer),
        plain_copy(rows2, rows_x, sum_sems, 10, beside()),
    ]
    tall_steps[0].start()

    def add(held, arrived):
        held[...] = (held[...].astype(F32) + arrived[...].astype(F32)).astype(BF)

    allowed = allowed_pairs(offsets_ref, rows, 0, rows)
    sharing = queries // kv
    query_parts, key_parts, value_parts = [], [], []
    for head in range(queries // HEAD_SIZE):
        if head:
            spread.step(head)
        at = head * HEAD_SIZE
        kv_at = head // sharing * HEAD_SIZE
        query = q_ref[:, at : at + HEAD_SIZE]
        key = k_ref[:, kv_at : kv_at + HEAD_SIZE]
        value = v_ref[:, kv_at : kv_at + HEAD_SIZE]
        grad = att_grad[:, at : at + HEAD_SIZE]
        scores = jnp.where(allowed, matmul_nt(query, key) * scale, masked_score)
        probs = jnp.exp(scores - lse_ref[:, head : head + 1])
        prob_grad = matmul_nt(grad, value)
        delta = jnp.sum(probs * prob_grad, axis=1, keepdims=True)
        score_grad = (probs * (prob_grad - delta)).astype(BF)
        query_parts.append(matmul(score_grad, key) * scale)
        key_part = matmul_tn(score_grad, query) * scale
        value_part = matmul_tn(probs.astype(BF), grad)
        if head % sharing == 0:
            key_parts.append(key_part)
            value_parts.append(value_part)
        else:
            key_parts[-1] = key_parts[-1] + key_part
            value_parts[-1] = value_parts[-1] + value_part
    kv_out[0] = jnp.concatenate(key_parts, axis=1).astype(BF)
    key_copy.start()
    kv_out[1] = jnp.concatenate(value_parts, axis=1).astype(BF)
    value_copy.start()

    def rotate_back(array):
        wide_lanes = array.shape[1]
        lane = lax.broadcasted_iota(jnp.int32, (1, wide_lanes), 1)
        first = lane % HEAD_SIZE < HEAD_SIZE // 2
        cosines = jnp.concatenate([cos_ref[...]] * (wide_lanes // 128), axis=1)
        sines = jnp.concatenate([sin_ref[...]] * (wide_lanes // 128), axis=1)
        return (array * cosines - turn(array, first) * sines).astype(BF)

    query_grad = rotate_back(jnp.concatenate(query_parts, axis=1))
    by_rows = (parts, rows // parts, width)
    terms[pl.ds(0, parts)] = matmul_nt(query_grad, wq_ref[...]).reshape(by_rows)
    turned = n_ref[...].T
    query_part = matmul(turned, query_grad).astype(BF)
    for at in range(2):
        wide[at, :, :queries] = query_part[at * width // 2 : (at + 1) * width // 2, :]
    key_copy.wait_recv()
    value_copy.wait_recv()
    key_grad = rotate_back(kv_out[0, :rows, :].astype(F32) + kv_in[0].astype(F32))
    value_grad = (kv_out[1, :rows, :].astype(F32) + kv_in[1].astype(F32)).astype(BF)
    more = matmul_nt(key_grad, wk_ref[...]) + matmul_nt(value_grad, wv_ref[...])
    terms[pl.ds(0, parts)] += more.reshape(by_rows)
    both_part = matmul(turned, jnp.concatenate([key_grad, value_grad], axis=1)).astype(BF)
    for at in range(2):
        wide[at, :, queries:] = both_part[at * width // 2 : (at + 1) * width // 2, :]
    wide_steps[0].start()

    def gain_part(at, total):
        values = x_ref[at].astype(F32)
        return total + jnp.sum(terms[at] * (values * scale_of(values)), axis=0, keepdims=True)

    first_sum = lax.fori_loop(0, parts, gain_part, jnp.zeros((1, width), F32))
    pad = jnp.zeros((rows2.shape[0] - 2, width), F32)
    rows2[...] = jnp.concatenate([first_sum, second_ref[...], pad], axis=0).astype(BF)
    rows_steps[0].start()

    def exchange(at):
        @pl.when(at == 0)
        def _():
            rows_steps[0].wait()
            add(rows2, rows_core)
            rows_steps[1].start()
            tall_steps[0].wait()
            add(tall.at[core], tall_core)
            tall_steps[1].start()

        @pl.when(at == 1)
        def _():
            wide_steps[0].wait()
            add(wide.at[core], wide_core)

        @pl.when(at == 2)
        def _():
            rows_steps[1].wait()
            add(rows2, rows_y)
            rows_steps[2].start()
            wide_steps[1].start()

        @pl.when(at == 5)
        def _():
            rows_steps[2].wait()
            add(rows2, rows_x)
            summed = rows2[...].astype(F32)
            terms[parts] = jnp.concatenate([summed[:1, :], jnp.zeros((PART - 1, width), F32)], axis=0)
            gains_ref[1:2, :] = summed[1:2, :]

        @pl.when(at == 8)
        def _():
            tall_steps[1].wait()
            add(tall.at[core], tall_y)
            tall_steps[2].start()

        @pl.when(at == 11)
        def _():
            wide_steps[1].wait()
            add(wide.at[core], wide_x)
            wide_steps[2].start()

        @pl.when(at == 18)
        def _():
            tall_steps[2].wait()
            add(tall.at[core], tall_x)
            tall_steps[3].start()

        @pl.when(at == 20)
        def _():
            wide_steps[2].wait()
            add(wide.at[core], wide_y)
            wide_steps[3].start()

    heads = queries // HEAD_SIZE

    def body(at, carry):
        exchange(at)
        line.step(at)

        @pl.when((at % 2 == 0) & (at // 2 + heads < spread.steps))
        def _():
            spread.step(at // 2 + heads)

        @pl.when((at % 2 == 0) & (at // 2 + heads >= spread.first_whole) & (at // 2 + heads < spread.steps))
        def _():
            block = at // 2 + heads - spread.first_whole
            block_ref[block] = (res_ref[block, :, spread.own()] + spread.total(block)).astype(BF)

        part = at - LAG * line.last

        @pl.when((part >= 0) & (part < parts))
        def _():
            grad = line.total(part)
            values = x_ref[part].astype(F32)
            scale = scale_of(values)
            unit = values * scale
            grad_ref[part] = (res_grad_ref[part] + norm_back(grad, unit, scale, gain_ref[...])).astype(BF)

        return carry

    lax.fori_loop(0, parts + 1 + LAG * line.last, body, 0)
    gains_ref[0:1, :] = line.total(parts)[:1, :]
    line.drain()
    spread.drain()
    key_copy.wait_send()
    value_copy.wait_send()
    tall_steps[3].wait()
    wide_steps[3].wait()
    tall_out[...] = tall[core]
    wide_out[...] = wide[core]


class Spread:
    def __init__(self, term, from_left, from_right, to_right, to_left, sems):
        self.place = lax.axis_index("tensor")
        self.size = lax.axis_size("tensor")
        self.term = term
        self.blocks = term.shape[0]
        self.span = term.shape[2] // self.size
        self.from_left, self.from_right = from_left, from_right
        self.to_right, self.to_left = to_right, to_left
        self.sems = sems
        self.first_whole = 2 * (self.size - 1)
        self.steps = self.blocks + self.first_whole

    def copy(self, way, block, shard):
        last = self.size - 1
        near = jnp.where(self.place < last, self.place + 1, self.place - 1)
        far = jnp.where(self.place > 0, self.place - 1, self.place + 1)
        source, target, device = (
            (self.to_right, self.from_left, near) if way == 0 else (self.to_left, self.from_right, far)
        )
        return pltpu.make_async_remote_copy(
            src_ref=source.at[block, shard], dst_ref=target.at[block, shard],
            send_sem=self.sems.at[2 * way, block, shard], recv_sem=self.sems.at[2 * way + 1, block, shard],
            device_id={"tensor": device}, device_id_type=MESH,
        )

    def clear(self):
        @pl.when(self.place == 0)
        def _():
            self.from_left[...] = jnp.zeros(self.from_left.shape, BF)

        @pl.when(self.place == self.size - 1)
        def _():
            self.from_right[...] = jnp.zeros(self.from_right.shape, BF)

    def passes(self, way, shard):
        return self.place < shard if way == 0 else self.place > shard

    def has_source(self, way):
        return self.place > 0 if way == 0 else self.place < self.size - 1

    def step(self, at):
        for way in range(2):
            block = at - 2 * (self.place if way == 0 else self.size - 1 - self.place)
            valid = (block >= 0) & (block < self.blocks)
            arrived = self.from_left if way == 0 else self.from_right
            leaving = self.to_right if way == 0 else self.to_left
            for shard in range(self.size):
                here = valid & self.passes(way, shard)

                @pl.when(here & self.has_source(way))
                def _():
                    self.copy(way, block, shard).wait_recv()

                @pl.when(here)
                def _():
                    lanes = slice(shard * self.span, (shard + 1) * self.span)
                    own = self.term[block, :, lanes].astype(F32)
                    leaving[block, shard] = (own + arrived[block, shard].astype(F32)).astype(BF)
                    self.copy(way, block, shard).start()

    def own(self):
        return pl.ds(pl.multiple_of(self.place * self.span, self.span), self.span)

    def total(self, block):
        for way in range(2):

            @pl.when(self.has_source(way))
            def _():
                self.copy(way, block, self.place).wait_recv()

        sides = self.from_left[block, self.place].astype(F32) + self.from_right[block, self.place].astype(F32)
        return self.term[block, :, self.own()].astype(F32) + sides

    def drain(self):
        for way in range(2):
            for shard in range(self.size):

                @pl.when(self.passes(way, shard))
                def _():
                    for block in range(self.blocks):
                        self.copy(way, block, shard).wait_send()


BLOCK_ROWS = 128


def input_gradient(
    offsets, block_input, residual_grad, gain, normed, w_query, key_weight, value_weight, w_output, cosines, sines,
    query, keys, values, lse, attended, low, route, second, mixed, residual,
):
    rows, width = block_input.shape
    parts = rows // PART
    kv = key_weight.shape[1]
    columns = w_query.shape[1] + 2 * kv
    tall = (w_output.shape[0] + route.shape[0]) // 2
    size = lax.axis_size("tensor")
    blocks = rows // BLOCK_ROWS
    wide_half = pltpu.VMEM((width // 2, columns), BF)
    tall_half = pltpu.VMEM((tall, width), BF)
    tile = pltpu.VMEM((16, width), BF)
    mix_half = pltpu.VMEM((blocks, size, BLOCK_ROWS, width // size), BF)
    return pl.pallas_call(
        input_grad_kernel,
        out_shape=(
            jax.ShapeDtypeStruct((parts, PART, width), BF),
            jax.ShapeDtypeStruct((width // 2, columns), BF),
            jax.ShapeDtypeStruct((width // 2, columns), BF),
            jax.ShapeDtypeStruct((tall, width), BF),
            jax.ShapeDtypeStruct((tall, width), BF),
            jax.ShapeDtypeStruct((8, width), F32),
            jax.ShapeDtypeStruct((blocks, BLOCK_ROWS, width // size), BF),
        ),
        in_specs=[smem_spec()] + [vmem_spec()] * 20,
        out_specs=(vmem_spec(),) * 7,
        scratch_shapes=line_scratch(parts + 1, width)
        + [
            pltpu.VMEM((parts + 1, PART, width), F32),
            pltpu.VMEM((2, 2 * rows, kv), BF),
            pltpu.VMEM((2, rows, kv), BF),
            pltpu.SemaphoreType.DMA((2, 2)),
            pltpu.VMEM((2, width // 2, columns), BF), wide_half, wide_half, wide_half,
            pltpu.VMEM((2, tall, width), BF), tall_half, tall_half, tall_half,
            tile, tile, tile, tile,
            pltpu.SemaphoreType.DMA((2, 11)),
            mix_half, mix_half, mix_half, mix_half,
            pltpu.SemaphoreType.DMA((4, blocks, size)),
        ],
        compiler_params=pltpu.CompilerParams(
            collective_id=2, has_side_effects=True, vmem_limit_bytes=60 * MIB
        ),
        cost_estimate=LINK_COST,
        name="input_grad",
    )(
        offsets, block_input.reshape(parts, PART, width), residual_grad, gain[None], normed,
        w_query, key_weight, value_weight, w_output, cosines, sines, query, keys, values, lse, attended, low,
        route, second, mixed.reshape(blocks, BLOCK_ROWS, width), residual.reshape(blocks, BLOCK_ROWS, width),
    )


CHUNK = 512
GROUP = 4


def route_gates(token, marks, w_router):
    experts_all = w_router.shape[1]
    chosen = marks[:, :experts_all].astype(F32)
    kept = marks[:, experts_all:].astype(F32)
    logits = jnp.where(chosen > 0.0, matmul(token, w_router), masked_score)
    raised = jnp.exp(logits - jnp.max(logits, axis=1, keepdims=True)) * chosen
    gate = raised / jnp.sum(raised, axis=1, keepdims=True)
    return gate, gate * kept


def hidden_terms(token, pulled, weight, gate_weights, up_weights):
    gate_in = matmul(token, gate_weights)
    up_in = matmul(token, up_weights)
    sig = 0.5 * jnp.tanh(0.5 * gate_in) + 0.5
    silu = gate_in * sig
    hidden = silu * up_in
    gated = (hidden * weight).astype(BF)
    scaled = pulled * weight
    up_grad = (scaled * silu).astype(BF)
    gate_grad = (scaled * up_in * (sig + silu * (1.0 - sig))).astype(BF)
    return hidden, gated, gate_grad, up_grad


def spread_gates(kept, column, group, hid):
    lane = lax.broadcasted_iota(jnp.int32, (1, kept.shape[1]), 1)
    weights = []
    for expert in range(group):
        gate = jnp.sum(jnp.where(lane == column + expert, kept, 0.0), axis=1, keepdims=True)
        weights.append(jnp.broadcast_to(gate, (kept.shape[0], hid)))
    return jnp.concatenate(weights, axis=1)


def expert_kernel(
    n_ref, marks_ref, wr_ref, n_hbm, own_up, peer_up, far_g0, far_m, wg_ref, wu_ref, wd_ref,
    dwg_ref, dwu_ref, dwd_ref, mix_ref, back_ref, route_ref, far_n, far_on, far_g1, far_og0, far_og1, far_om,
    gates, kept_gates, gate_grads, mix, back, nt, wgs, wus, ght, dgs, dus,
    out_g, out_u, out_d, in_g, in_u, in_d, sems, far_sems, g_ref, up_sems,
):
    step = pl.program_id(0)
    steps = pl.num_programs(0) // 2
    side = lax.axis_index("expert")
    dp = lax.axis_index("dp")
    core = lax.rem(dp, 2)
    other = other_core()
    tokens, width = n_ref.shape
    experts_all = wr_ref.shape[1]
    group, _, hid = wg_ref.shape
    chunks = tokens // CHUNK
    lane = lax.broadcasted_iota(jnp.int32, (1, experts_all), 1)

    def copies(slot):
        return [
            pltpu.make_async_remote_copy(
                src_ref=source.at[slot], dst_ref=target.at[slot],
                send_sem=sems.at[0, kind, slot], recv_sem=sems.at[1, kind, slot],
                device_id=other, device_id_type=MESH,
            )
            for kind, (source, target) in enumerate(((out_g, in_g), (out_u, in_u), (out_d, in_d)))
        ]

    half = tokens // 2
    cross = [
        plain_copy(n_hbm.at[pl.ds(at * half, half), :], far_n.at[pl.ds(at * half, half), :], far_sems, at, beside())
        for at in range(2)
    ]
    share = [
        plain_copy(far_n.at[pl.ds(at * half, half), :], far_on.at[pl.ds(at * half, half), :], far_sems, 2 + at, other)
        for at in range(2)
    ]
    peer = {"expert": 1 - side}
    turn_up = plain_copy(far_g0, far_g1, far_sems, 4, peer)
    share_up = plain_copy(far_g1, far_og1, far_sems, 5, other)
    early = [
        plain_copy(source, target, far_sems, 6 + at, other)
        for at, (source, target) in enumerate(((far_g0, far_og0), (far_m, far_om)))
    ]
    loads = [
        pltpu.make_async_copy(source, g_ref.at[pl.ds(at * half, half), :], up_sems.at[at])
        for at, source in enumerate((own_up, peer_up))
    ]

    @pl.when(step == 0)
    def _():
        for copy in loads:
            copy.start()
        meet([(True, other), (True, beside()), (True, peer)])
        for copy in cross + early + [turn_up]:
            copy.start()

        def start(at, carry):
            rows = pl.ds(pl.multiple_of(at * CHUNK, CHUNK), CHUNK)
            gate, kept_gate = route_gates(n_ref[rows, :], marks_ref[rows, :], wr_ref[...])
            gates[rows, :] = gate
            kept_gates[rows, :] = kept_gate
            mix[rows, :] = jnp.zeros((CHUNK, width), F32)
            back[rows, :] = jnp.zeros((CHUNK, width), F32)
            gate_grads[rows, :] = jnp.zeros((CHUNK, experts_all), F32)
            return carry

        lax.fori_loop(0, chunks, start, 0)
        for at in range(chunks):
            nt[:, at * CHUNK : (at + 1) * CHUNK] = n_ref[at * CHUNK : (at + 1) * CHUNK, :].T
        for copy in loads:
            copy.wait()

    @pl.when(step == steps)
    def _():
        cross[0].wait_recv()
        share[0].start()
        turn_up.wait_recv()
        share_up.start()

    for expert in range(group):
        wgs[:, expert * hid : (expert + 1) * hid] = wg_ref[expert]
        wus[:, expert * hid : (expert + 1) * hid] = wu_ref[expert]
    first = step < steps
    block = jnp.where(first, (1 - core) * steps + step, core * steps + step - steps)
    column = side * (experts_all // 2) + block * group

    for at in range(chunks):
        rows = slice(at * CHUNK, (at + 1) * CHUNK)
        token = n_ref[rows, :]
        down = wd_ref[...].reshape(group * hid, width)
        pulled = matmul_nt(g_ref[rows, :], down)
        weight = spread_gates(kept_gates[rows, :], column, group, hid)
        hidden, gated, gate_grad, up_grad = hidden_terms(token, pulled, weight, wgs[...], wus[...])
        products = hidden * pulled
        grads = gate_grads[rows, :]
        for expert in range(group):
            product = jnp.sum(products[:, expert * hid : (expert + 1) * hid], axis=1, keepdims=True)
            grads = grads + jnp.where(lane == column + expert, product, 0.0)
        gate_grads[rows, :] = grads
        ght[:, rows] = gated.T
        dgs[rows, :] = gate_grad
        dus[rows, :] = up_grad
        mix[rows, :] += matmul(gated, down)
        back[rows, :] += matmul_nt(gate_grad, wgs[...]) + matmul_nt(up_grad, wus[...])

    def weight_grads(store_rows, store_down):
        for at in range(width // CHUNK):
            rows = slice(at * CHUNK, (at + 1) * CHUNK)
            turned = nt[rows, :]
            gate_part = matmul(turned, dgs[...])
            up_part = matmul(turned, dus[...])
            for expert in range(group):
                inner = slice(expert * hid, (expert + 1) * hid)
                store_rows(expert, rows, gate_part[:, inner], up_part[:, inner])
        down_part = matmul(ght[...], g_ref[...])
        for expert in range(group):
            store_down(expert, down_part[expert * hid : (expert + 1) * hid, :])

    @pl.when(first)
    def _():
        def store_rows(expert, rows, gate_part, up_part):
            out_g[step, expert, rows, :] = gate_part.astype(BF)
            out_u[step, expert, rows, :] = up_part.astype(BF)

        def store_down(expert, part):
            out_d[step, expert] = part.astype(BF)

        weight_grads(store_rows, store_down)
        for copy in copies(step):
            copy.start()

    @pl.when(step >= steps)
    def _():
        slot = step - steps
        for copy in copies(slot):
            copy.wait_recv()

        def store_rows(expert, rows, gate_part, up_part):
            dwg_ref[expert, rows, :] = (gate_part + in_g[slot, expert, rows, :].astype(F32)).astype(BF)
            dwu_ref[expert, rows, :] = (up_part + in_u[slot, expert, rows, :].astype(F32)).astype(BF)

        def store_down(expert, part):
            dwd_ref[expert] = (part + in_d[slot, expert].astype(F32)).astype(BF)

        weight_grads(store_rows, store_down)
        for copy in copies(slot):
            copy.wait_send()

    @pl.when(step == 2 * steps - 1)
    def _():
        cross[1].wait_recv()
        share[1].start()
        route_ref[...] = jnp.zeros(route_ref.shape, F32)

        def finish(at, carry):
            rows = pl.ds(pl.multiple_of(at * CHUNK, CHUNK), CHUNK)
            mix_ref[rows, :] = mix[rows, :].astype(BF)
            grads = gate_grads[rows, :] * kept_gates[rows, :]
            chosen_grad = grads - gates[rows, :] * jnp.sum(grads, axis=1, keepdims=True)
            low = chosen_grad.astype(BF)
            back_ref[rows, :] = (back[rows, :] + matmul_nt(low, wr_ref[...])).astype(BF)
            route_ref[...] += matmul_tn(low, n_ref[rows, :])
            return carry

        lax.fori_loop(0, chunks, finish, 0)
        for copy in cross + [turn_up]:
            copy.wait_send()
        for copy in share + early + [share_up]:
            copy.wait()


def experts(normed, marks, w_router, upstream, peer_up, far_up, far_marks, w_gate, w_up, w_down):
    tokens, width = normed.shape
    count, _, hid = w_gate.shape
    half = count // 2
    steps = half // GROUP
    experts_all = w_router.shape[1]
    once = pl.Buffered(1)
    whole = lambda step: (0, 0)

    def picked(step):
        core = lax.rem(lax.axis_index("dp"), 2)
        return (jnp.where(step < steps, (1 - core) * steps + step, core * steps + step - steps), 0, 0)

    own = lambda step: (jnp.maximum(step - steps, 0), 0, 0)
    args = [normed, marks, w_router]
    specs = [pl.BlockSpec(array.shape, whole, pipeline_mode=once) for array in args]
    args += [normed, upstream, peer_up, far_up, far_marks]
    specs += [pl.BlockSpec(memory_space=pl.ANY)] * 5
    up_block, down_block = (GROUP, width, hid), (GROUP, hid, width)
    specs += [pl.BlockSpec(up_block, picked), pl.BlockSpec(up_block, picked), pl.BlockSpec(down_block, picked)]
    gate_scratch = pltpu.VMEM((tokens, experts_all), F32)
    rows_scratch = pltpu.VMEM((tokens, width), F32)
    swap_scratch = [
        pltpu.VMEM((steps,) + up_block, BF),
        pltpu.VMEM((steps,) + up_block, BF),
        pltpu.VMEM((steps,) + down_block, BF),
    ]
    return pl.pallas_call(
        expert_kernel,
        out_shape=[
            jax.ShapeDtypeStruct((half, width, hid), BF),
            jax.ShapeDtypeStruct((half, width, hid), BF),
            jax.ShapeDtypeStruct((half, hid, width), BF),
            jax.ShapeDtypeStruct((tokens, width), BF),
            jax.ShapeDtypeStruct((tokens, width), BF),
            jax.ShapeDtypeStruct((experts_all, width), F32),
            jax.ShapeDtypeStruct((tokens, width), BF),
            jax.ShapeDtypeStruct((tokens, width), BF),
            jax.ShapeDtypeStruct(far_up.shape, BF),
            jax.ShapeDtypeStruct(far_up.shape, BF),
            jax.ShapeDtypeStruct(far_up.shape, BF),
            jax.ShapeDtypeStruct(far_marks.shape, BF),
        ],
        grid=(2 * steps,),
        in_specs=specs,
        out_specs=[
            pl.BlockSpec(up_block, own),
            pl.BlockSpec(up_block, own),
            pl.BlockSpec(down_block, own),
            pl.BlockSpec((tokens, width), whole, pipeline_mode=once),
            pl.BlockSpec((tokens, width), whole, pipeline_mode=once),
            pl.BlockSpec((experts_all, width), whole, pipeline_mode=once),
        ]
        + [pl.BlockSpec(memory_space=pl.ANY)] * 6,
        scratch_shapes=[
            gate_scratch, gate_scratch, gate_scratch, rows_scratch, rows_scratch,
            pltpu.VMEM((width, tokens), BF),
            pltpu.VMEM((width, GROUP * hid), BF),
            pltpu.VMEM((width, GROUP * hid), BF),
            pltpu.VMEM((GROUP * hid, tokens), BF),
            pltpu.VMEM((tokens, GROUP * hid), BF),
            pltpu.VMEM((tokens, GROUP * hid), BF),
        ]
        + swap_scratch
        + swap_scratch
        + [pltpu.SemaphoreType.DMA((2, 3, steps)), pltpu.SemaphoreType.DMA((2, 8)), pltpu.VMEM((tokens, width), BF), pltpu.SemaphoreType.DMA((2,))],
        compiler_params=pltpu.CompilerParams(
            dimension_semantics=("arbitrary",), collective_id=3, has_side_effects=True, vmem_limit_bytes=60 * MIB
        ),
        cost_estimate=pl.CostEstimate(
            flops=18 * tokens * width * count * hid,
            bytes_accessed=12 * count * width * hid,
            transcendentals=tokens * count * hid,
        ),
        name="experts",
    )(*args, w_gate, w_up, w_down)


def finish_kernel(core_ref, *refs):
    ins, outs = refs[:13], refs[13:]
    part, at = pl.program_id(0), pl.program_id(1)
    mine, other = ins[:3], ins[3:6]
    wide_mine, wide_other, tall_mine, tall_other, gains, grad, block = ins[6:]
    out_g, out_u, out_d, out_q, out_k, out_v, out_o, out_r, out_first, out_second, out_grad, out_block = outs
    for place, sources in enumerate((mine, other)):

        @pl.when(part == place)
        def _():
            for source, target in zip(sources, (out_g, out_u, out_d)):
                target[...] = source[...].astype(F32)

    core = core_ref[0]
    queries, kv = out_q.shape[1], out_k.shape[1]
    half = out_q.shape[0] // 2
    tall = tall_mine.shape[0]
    outs_rows = out_o.shape[0]

    @pl.when((part == 0) & (at == 0))
    def _():
        out_grad[...] = grad[...]
        out_block[...] = block[...]
        out_first[...] = gains[0:1, :]
        out_second[...] = gains[1:2, :]

    for place in range(2):

        @pl.when((part == 0) & (at == 1 + place))
        def _():
            own = core == place
            summed = jnp.where(own, wide_mine[...].astype(F32), wide_other[...].astype(F32))
            rows = slice(place * half, (place + 1) * half)
            out_q[rows, :] = summed[:, :queries]
            out_k[rows, :] = summed[:, queries : queries + kv]
            out_v[rows, :] = summed[:, queries + kv :]
            tall_sum = jnp.where(own, tall_mine[...].astype(F32), tall_other[...].astype(F32))
            top = min((place + 1) * tall, outs_rows)
            out_o[place * tall : top, :] = tall_sum[: top - place * tall, :]
            if place == 1:
                out_r[...] = tall_sum[top - place * tall :, :].T


def finish(core, sums, others, wide, wide_back, tall, tall_back, gains, grad, block, queries, outs_rows):
    half = sums[0].shape[0]
    width = grad.shape[1]
    kv = (wide.shape[1] - queries) // 2
    experts_all = 2 * tall.shape[0] - outs_rows
    whole = lambda shape: pl.BlockSpec(shape, lambda part, at, core: (0,) * len(shape), pipeline_mode=pl.Buffered(1))
    single = lambda array, index: pl.BlockSpec((1,) + array.shape[1:], index)
    first = lambda part, at, core: (jnp.where(part == 0, at, half - 1), 0, 0)
    second = lambda part, at, core: (jnp.where(part == 0, 0, at), 0, 0)
    placed = lambda part, at, core: (jnp.where(part == 0, core[0], 1 - core[0]) * half + at, 0, 0)
    rest = [wide, wide_back, tall, tall_back, gains, grad, block]
    wide_shape = lambda shape: jax.ShapeDtypeStruct(shape, F32)
    shapes = [
        (2 * wide.shape[0], queries), (2 * wide.shape[0], kv), (2 * wide.shape[0], kv),
        (outs_rows, width), (width, experts_all), (1, width), (1, width),
    ]
    return pl.pallas_call(
        finish_kernel,
        out_shape=[wide_shape((2 * half,) + item.shape[1:]) for item in sums]
        + [wide_shape(shape) for shape in shapes]
        + [jax.ShapeDtypeStruct(grad.shape, BF), jax.ShapeDtypeStruct(block.shape, BF)],
        grid_spec=pltpu.PrefetchScalarGridSpec(
            num_scalar_prefetch=1,
            grid=(2, half),
            in_specs=[single(item, first) for item in sums]
            + [single(item, second) for item in others]
            + [whole(item.shape) for item in rest],
            out_specs=[single(item, placed) for item in sums]
            + [whole(shape) for shape in shapes + [grad.shape, block.shape]],
        ),
        compiler_params=pltpu.CompilerParams(vmem_limit_bytes=60 * MIB),
        name="finish",
    )(core, *sums, *others, *rest)


def fast_device(
    block_input, first_gain, w_query, key_weight, value_weight, w_output, second_gain, w_router,
    w_gate, w_up, w_down, expert_ids, slot_index, piece_start_offsets, upstream,
):
    rows, width = block_input.shape
    experts_all = w_router.shape[1]
    core = lax.axis_index("dp") % 2
    positions = lax.axis_index("expert") * rows + jnp.arange(rows, dtype=jnp.int32)
    cosine_table, sine_table = rope_tables(positions)
    cosines = jnp.tile(cosine_table, (1, 4))
    sines = jnp.tile(sine_table, (1, 4))
    (
        first_normed, query_rot, keys, values, attended, lse, residual, normed_all, marks, far_marks, peer_up, far_up,
    ) = front(
        piece_start_offsets, block_input, first_gain, second_gain, w_query, key_weight, value_weight, w_output,
        cosines, sines, expert_ids, slot_index, upstream, experts_all,
    )
    keys, values = keys.reshape(2 * rows, -1), values.reshape(2 * rows, -1)
    normed_all = normed_all.reshape(2 * rows, width)
    marks = marks.reshape(2 * rows, 2 * experts_all)
    far_marks = far_marks.reshape(2 * rows, 2 * experts_all)
    dwg, dwu, dwd, mix, back, route, *far = experts(
        normed_all, marks, w_router, upstream, peer_up, far_up, far_marks, w_gate, w_up, w_down
    )
    far_normed, far_other_normed, far_peer_up, far_other_up, far_other_peer_up, far_other_marks = far
    residual_grad, residual_low, grad_second, route, mixed, sums = residual_gradient(
        back, mix, route, residual, upstream, second_gain, w_router,
        (
            far_normed, far_other_normed, far_up, far_peer_up, far_other_up, far_other_peer_up,
            far_marks, far_other_marks,
        ),
        w_gate, w_up, w_down, (dwg, dwu, dwd),
    )
    grad_input, wide, wide_back, tall, tall_back, gains, block_output = input_gradient(
        piece_start_offsets, block_input, residual_grad, first_gain, first_normed, w_query, key_weight, value_weight,
        w_output, cosines, sines, query_rot, keys, values, lse, attended, residual_low, route, grad_second, mixed, residual,
    )
    grad_gate, grad_up, grad_down, grad_query, grad_key, grad_value, grad_output, grad_router, first, second, grad, block = finish(
        core[None].astype(jnp.int32), sums[:3], sums[3:], wide, wide_back, tall, tall_back, gains,
        grad_input.reshape(rows, width), block_output.reshape(rows, width // 4), w_query.shape[1], w_output.shape[0],
    )
    return (
        block, grad, first[0], grad_query, grad_key, grad_value, grad_output, second[0], grad_router,
        grad_gate, grad_up, grad_down,
    )


def solution(mesh):
    fast = mesh.shape["expert"] == 2 and mesh.shape["dp"] == 4 and mesh.shape["tensor"] == 4
    placed = (
        P(("dp", "expert"), None),
        P(),
        P(None, "tensor"),
        P(None, "tensor"),
        P(None, "tensor"),
        P("tensor", None),
        P(),
        P(),
        P("expert", None, "tensor"),
        P("expert", None, "tensor"),
        P("expert", "tensor", None),
        P(("dp", "expert"), None),
        P(("dp", "expert"), None),
        P("dp", None),
        P(("dp", "expert"), None),
    )
    return jax.shard_map(
        fast_device if fast else general_device,
        mesh=mesh,
        in_specs=placed,
        out_specs=(
            P(("dp", "expert"), "tensor"),
            P(("dp", "expert"), None),
            P(),
            P(None, "tensor"),
            P(None, "tensor"),
            P(None, "tensor"),
            P("tensor", None),
            P(),
            P(),
            P("expert", None, "tensor"),
            P("expert", None, "tensor"),
            P("expert", "tensor", None),
        ),
        check_vma=False,
    )
```

```python
import functools
import math

import jax
import jax.numpy as jnp
from jax import lax
from jax.experimental import pallas as pl
from jax.experimental.pallas import tpu as pltpu
from jax.sharding import PartitionSpec as P

HEAD_SIZE = 64
TOPK = 8
PIC = 256


epsilon = 1e-06
rope_base = 10000.0
masked_score = -1e30


def rope_tables(positions):
    steps = jnp.arange(HEAD_SIZE // 2, dtype=jnp.float32)
    inverse = jnp.exp(steps * (-2.0 * math.log(rope_base) / HEAD_SIZE))
    angle = positions.astype(jnp.float32)[:, None] * inverse[None, :]
    return (jnp.cos(angle), jnp.sin(angle))


def apply_rotary(values, cosine_table, sine_table):
    half = values.shape[-1] // 2
    first = values[..., :half]
    second = values[..., half:]
    cosine_table = cosine_table[:, None, :]
    sine_table = sine_table[:, None, :]
    return jnp.concatenate(
        [first * cosine_table - second * sine_table, second * cosine_table + first * sine_table],
        axis=-1,
    )


def unrotate(values, cosine_table, sine_table):
    half = values.shape[-1] // 2
    first = values[..., :half]
    second = values[..., half:]
    cosine_table = cosine_table[:, None, :]
    sine_table = sine_table[:, None, :]
    return jnp.concatenate(
        [first * cosine_table + second * sine_table, second * cosine_table - first * sine_table],
        axis=-1,
    )


def piece_ids(positions, offsets):
    span = 2 * PIC
    window = positions // span
    within = positions - window * span
    count = offsets.shape[0]
    match = window[:, None] == jnp.arange(count, dtype=jnp.int32)[None, :]
    start = jnp.sum(jnp.where(match, offsets[None, :], 0), axis=1)
    inside = (window < count) & (within >= start) & (within < start + PIC)
    return jnp.where(inside, window, -1)


def matmul(left, right):
    return jnp.dot(left, right, preferred_element_type=jnp.float32)


def matmul_nt(left, right):
    return lax.dot_general(
        left, right, (((1,), (1,)), ((), ())), preferred_element_type=jnp.float32
    )


def matmul_tn(left, right):
    return lax.dot_general(
        left, right, (((0,), (0,)), ((), ())), preferred_element_type=jnp.float32
    )


def norm_scale(values):
    return lax.rsqrt(jnp.mean(values * values, axis=-1, keepdims=True) + epsilon)


def norm_back(grad, unit, scale, gain):
    weighted = grad * gain
    return scale * (weighted - unit * jnp.mean(weighted * unit, axis=-1, keepdims=True))


def general_device(
    block_input,
    first_gain,
    w_query,
    key_weight,
    value_weight,
    w_output,
    second_gain,
    w_router,
    w_gate,
    w_up,
    w_down,
    expert_ids,
    slot_index,
    piece_start_offsets,
    upstream,
):
    rows_here = block_input.shape[0]
    width = block_input.shape[1]
    groups = lax.axis_size("expert")
    length = rows_here * groups
    local_heads = w_query.shape[1] // HEAD_SIZE
    local_kv = key_weight.shape[1] // HEAD_SIZE
    sharing = local_heads // local_kv
    head_rows = sharing * rows_here
    experts_all = w_router.shape[1]
    capacity = TOPK * rows_here // experts_all
    slots_all = experts_all * capacity
    score_scale = HEAD_SIZE ** (-0.5)
    positions = lax.axis_index("expert") * rows_here + jnp.arange(rows_here, dtype=jnp.int32)
    cosine_table, sine_table = rope_tables(positions)
    inputs = block_input.astype(jnp.float32)
    first_scale = norm_scale(inputs)
    first_unit = inputs * first_scale
    first_normed = (first_unit * first_gain).astype(jnp.bfloat16)
    query_rot = apply_rotary(
        matmul(first_normed, w_query).reshape(rows_here, local_heads, HEAD_SIZE),
        cosine_table,
        sine_table,
    ).astype(jnp.bfloat16)
    key_rot = (
        apply_rotary(
            matmul(first_normed, key_weight).reshape(rows_here, local_kv, HEAD_SIZE),
            cosine_table,
            sine_table,
        )
        .astype(jnp.bfloat16)
        .reshape(rows_here, local_kv * HEAD_SIZE)
    )
    value_low = matmul(first_normed, value_weight).astype(jnp.bfloat16)
    keys_all, values_all = (
        lax.all_gather(key_rot, "expert", axis=0, tiled=True),
        lax.all_gather(value_low, "expert", axis=0, tiled=True),
    )
    block = min(512, length)
    blocks = length // block

    def by_block(array):
        return array.reshape(blocks, block, local_kv, HEAD_SIZE).transpose(0, 2, 1, 3)

    def by_rows(stacked):
        return stacked.transpose(0, 2, 1, 3).reshape(length, local_kv * HEAD_SIZE)

    def head_major(array):
        return (
            array.reshape(rows_here, local_kv, sharing, HEAD_SIZE)
            .transpose(1, 2, 0, 3)
            .reshape(local_kv, head_rows, HEAD_SIZE)
        )

    def row_major(array):
        return (
            array.reshape(local_kv, sharing, rows_here, HEAD_SIZE)
            .transpose(2, 0, 1, 3)
            .reshape(rows_here, local_heads * HEAD_SIZE)
        )

    key_blocks = by_block(keys_all)
    value_blocks = by_block(values_all)
    block_starts = jnp.arange(blocks, dtype=jnp.int32) * block
    query_heads = head_major(query_rot.reshape(rows_here, local_heads * HEAD_SIZE))
    offsets = piece_start_offsets[0]
    key_pieces = piece_ids(jnp.arange(length, dtype=jnp.int32), offsets)
    query_pieces = jnp.tile(piece_ids(positions, offsets), sharing)
    query_places = jnp.tile(positions, sharing)

    def block_scores(key_block, start):
        places = start + jnp.arange(block, dtype=jnp.int32)
        pieces = lax.dynamic_slice_in_dim(key_pieces, start, block)
        causal = places[None, :] <= query_places[:, None]
        same = (pieces[None, :] == query_pieces[:, None]) & (query_pieces[:, None] >= 0)
        scores = (
            jnp.einsum("hqd,hkd->hqk", query_heads, key_block, preferred_element_type=jnp.float32)
            * score_scale
        )
        return (scores, (causal | same)[None])

    def max_step(carry, operands):
        running_max, running_sum = carry
        key_block, start = operands
        scores, allowed = block_scores(key_block, start)
        scores = jnp.where(allowed, scores, masked_score)
        new_max = jnp.maximum(running_max, jnp.max(scores, axis=-1))
        weights = jnp.where(allowed, jnp.exp(scores - new_max[..., None]), 0.0)
        new_sum = running_sum * jnp.exp(running_max - new_max) + jnp.sum(weights, axis=-1)
        return ((new_max, new_sum), None)

    start_max = jnp.full((local_kv, head_rows), masked_score, jnp.float32)
    start_sum = jnp.zeros((local_kv, head_rows), jnp.float32)
    (row_max, row_sum), _ = lax.scan(max_step, (start_max, start_sum), (key_blocks, block_starts))
    log_total = row_max + jnp.log(row_sum)

    def block_probs(key_block, start):
        scores, allowed = block_scores(key_block, start)
        return jnp.where(allowed, jnp.exp(scores - log_total[..., None]), 0.0)

    def value_step(total, operands):
        key_block, value_block, start = operands
        probs = block_probs(key_block, start).astype(jnp.bfloat16)
        return (
            total
            + jnp.einsum("hqk,hkd->hqd", probs, value_block, preferred_element_type=jnp.float32),
            None,
        )

    mixed_output, _ = lax.scan(
        value_step,
        jnp.zeros((local_kv, head_rows, HEAD_SIZE), jnp.float32),
        (key_blocks, value_blocks, block_starts),
    )
    attended = row_major(mixed_output).astype(jnp.bfloat16)
    attention = lax.psum(matmul(attended, w_output), "tensor")
    residual = inputs + attention
    second_scale = norm_scale(residual)
    second_unit = residual * second_scale
    second_normed = (second_unit * second_gain).astype(jnp.bfloat16)
    logits = matmul(second_normed, w_router)
    chosen = jnp.take_along_axis(logits, expert_ids, axis=1)
    gates = jax.nn.softmax(chosen, axis=-1)
    row_ids = jnp.arange(rows_here, dtype=jnp.int32)
    flat = jnp.where(slot_index >= 0, expert_ids * capacity + slot_index, slots_all)
    selector = (
        jnp.zeros((slots_all, rows_here), jnp.bfloat16)
        .at[flat.reshape(-1), jnp.repeat(row_ids, TOPK)]
        .set(1.0, mode="drop")
    )
    dispatched = (
        matmul(selector, second_normed).astype(jnp.bfloat16).reshape(experts_all, capacity, width)
    )
    expert_rows = lax.all_to_all(dispatched, "expert", split_axis=0, concat_axis=1, tiled=True)
    gate_in = jnp.einsum("ebd,edf->ebf", expert_rows, w_gate, preferred_element_type=jnp.float32)
    up_in = jnp.einsum("ebd,edf->ebf", expert_rows, w_up, preferred_element_type=jnp.float32)
    sigmoid_gate = jax.nn.sigmoid(gate_in)
    silu_gate = gate_in * sigmoid_gate
    hidden = (silu_gate * up_in).astype(jnp.bfloat16)
    partial_out = jnp.einsum("ebf,efd->ebd", hidden, w_down, preferred_element_type=jnp.float32)
    expert_part = lax.psum_scatter(
        partial_out.astype(jnp.bfloat16), "tensor", scatter_dimension=2, tiled=True
    )
    returned = lax.all_to_all(expert_part, "expert", split_axis=1, concat_axis=0, tiled=True)
    quarter = returned.shape[2]
    padded_out = jnp.concatenate(
        [returned.reshape(slots_all, quarter), jnp.zeros((1, quarter), jnp.bfloat16)], axis=0
    )
    feature_start = lax.axis_index("tensor") * quarter
    grad_full = upstream.astype(jnp.float32)
    grad_part = lax.dynamic_slice_in_dim(grad_full, feature_start, quarter, 1)
    mixture = jnp.zeros((rows_here, quarter), jnp.float32)
    gate_terms = []
    for pick in range(TOPK):
        picked = padded_out[flat[:, pick]].astype(jnp.float32)
        mixture = mixture + gates[:, pick : pick + 1] * picked
        gate_terms.append(jnp.sum(grad_part * picked, axis=1))
    gate_part = jnp.stack(gate_terms, axis=1)
    block_output = (lax.dynamic_slice_in_dim(residual, feature_start, quarter, 1) + mixture).astype(
        jnp.bfloat16
    )
    slot_gates = (
        jnp.zeros((slots_all + 1,), jnp.float32)
        .at[flat.reshape(-1)]
        .set(gates.reshape(-1))[:slots_all]
    )
    grad_slots = (
        (matmul(selector, upstream) * slot_gates[:, None])
        .astype(jnp.bfloat16)
        .reshape(experts_all, capacity, width)
    )
    grad_rows_in = lax.all_to_all(grad_slots, "expert", split_axis=0, concat_axis=1, tiled=True)
    hidden_grad = jnp.einsum(
        "ebd,efd->ebf", grad_rows_in, w_down, preferred_element_type=jnp.float32
    )
    grad_down = jnp.einsum("ebf,ebd->efd", hidden, grad_rows_in, preferred_element_type=jnp.float32)
    gate_in_grad = (
        hidden_grad * up_in * (sigmoid_gate * (1.0 + gate_in * (1.0 - sigmoid_gate)))
    ).astype(jnp.bfloat16)
    up_in_grad = (hidden_grad * silu_gate).astype(jnp.bfloat16)
    grad_gate = jnp.einsum(
        "ebd,ebf->edf", expert_rows, gate_in_grad, preferred_element_type=jnp.float32
    )
    grad_up = jnp.einsum(
        "ebd,ebf->edf", expert_rows, up_in_grad, preferred_element_type=jnp.float32
    )
    rows_part = jnp.einsum("ebf,edf->ebd", gate_in_grad, w_gate, preferred_element_type=jnp.float32)
    rows_part = rows_part + jnp.einsum(
        "ebf,edf->ebd", up_in_grad, w_up, preferred_element_type=jnp.float32
    )
    rows_back = lax.all_to_all(
        rows_part.astype(jnp.bfloat16), "expert", split_axis=1, concat_axis=0, tiled=True
    ).astype(rows_part.dtype)
    padded_back = jnp.concatenate(
        [rows_back.reshape(slots_all, width), jnp.zeros((1, width), jnp.float32)], axis=0
    )
    second_part = jnp.zeros((rows_here, width), jnp.float32)
    for pick in range(TOPK):
        second_part = second_part + padded_back[flat[:, pick]]
    second_sum, gate_grads = (
        lax.psum(second_part.astype(jnp.bfloat16), "tensor").astype(jnp.float32),
        lax.psum(gate_part.astype(jnp.bfloat16), "tensor").astype(jnp.float32),
    )
    chosen_grad = gates * (gate_grads - jnp.sum(gates * gate_grads, axis=1, keepdims=True))
    expert_axis = jnp.arange(experts_all, dtype=jnp.int32)
    logit_grad = jnp.zeros((rows_here, experts_all), jnp.float32)
    for pick in range(TOPK):
        logit_grad = logit_grad + jnp.where(
            expert_ids[:, pick : pick + 1] == expert_axis[None, :],
            chosen_grad[:, pick : pick + 1],
            0.0,
        )
    logit_low = logit_grad.astype(jnp.bfloat16)
    grad_router = matmul_tn(second_normed, logit_low)
    second_grad = second_sum + matmul_nt(logit_low, w_router)
    grad_second = jnp.sum(second_grad * second_unit, axis=0)
    residual_grad = grad_full + norm_back(second_grad, second_unit, second_scale, second_gain)
    residual_low = residual_grad.astype(jnp.bfloat16)
    grad_output = matmul_tn(attended, residual_low)
    attended_grad = head_major(matmul_nt(residual_low, w_output).astype(jnp.bfloat16))

    def delta_step(total, operands):
        key_block, value_block, start = operands
        probs = block_probs(key_block, start)
        prob_grad = jnp.einsum(
            "hqd,hkd->hqk", attended_grad, value_block, preferred_element_type=jnp.float32
        )
        return (total + jnp.sum(probs * prob_grad, axis=-1), None)

    delta, _ = lax.scan(
        delta_step,
        jnp.zeros((local_kv, head_rows), jnp.float32),
        (key_blocks, value_blocks, block_starts),
    )

    def grad_step(query_total, operands):
        key_block, value_block, start = operands
        probs = block_probs(key_block, start)
        prob_grad = jnp.einsum(
            "hqd,hkd->hqk", attended_grad, value_block, preferred_element_type=jnp.float32
        )
        score_grad = (probs * (prob_grad - delta[..., None])).astype(jnp.bfloat16)
        query_total = (
            query_total
            + jnp.einsum("hqk,hkd->hqd", score_grad, key_block, preferred_element_type=jnp.float32)
            * score_scale
        )
        key_grad = (
            jnp.einsum("hqk,hqd->hkd", score_grad, query_heads, preferred_element_type=jnp.float32)
            * score_scale
        )
        value_grad = jnp.einsum(
            "hqk,hqd->hkd",
            probs.astype(jnp.bfloat16),
            attended_grad,
            preferred_element_type=jnp.float32,
        )
        return (query_total, (key_grad, value_grad))

    query_total, (key_stack, value_stack) = lax.scan(
        grad_step,
        jnp.zeros((local_kv, head_rows, HEAD_SIZE), jnp.float32),
        (key_blocks, value_blocks, block_starts),
    )
    key_back, value_back = (
        lax.psum_scatter(
            by_rows(key_stack).astype(jnp.bfloat16), "expert", scatter_dimension=0, tiled=True
        ).astype(jnp.float32),
        lax.psum_scatter(
            by_rows(value_stack).astype(jnp.bfloat16), "expert", scatter_dimension=0, tiled=True
        ).astype(jnp.float32),
    )
    query_grad = (
        unrotate(
            row_major(query_total).reshape(rows_here, local_heads, HEAD_SIZE),
            cosine_table,
            sine_table,
        )
        .astype(jnp.bfloat16)
        .reshape(rows_here, local_heads * HEAD_SIZE)
    )
    key_grad = (
        unrotate(key_back.reshape(rows_here, local_kv, HEAD_SIZE), cosine_table, sine_table)
        .astype(jnp.bfloat16)
        .reshape(rows_here, local_kv * HEAD_SIZE)
    )
    value_grad = value_back.astype(jnp.bfloat16)
    grad_query = matmul_tn(first_normed, query_grad)
    grad_key = matmul_tn(first_normed, key_grad)
    grad_value = matmul_tn(first_normed, value_grad)
    first_part = (
        matmul_nt(query_grad, w_query)
        + matmul_nt(key_grad, key_weight)
        + matmul_nt(value_grad, value_weight)
    )
    first_grad = lax.psum(first_part.astype(jnp.bfloat16), "tensor").astype(jnp.float32)
    grad_first = jnp.sum(first_grad * first_unit, axis=0)
    grad_input = (
        residual_grad + norm_back(first_grad, first_unit, first_scale, first_gain)
    ).astype(jnp.bfloat16)
    dense = lax.psum(
        (grad_query, grad_key, grad_value, grad_output, grad_router, grad_first, grad_second),
        ("dp", "expert"),
    )
    expert_sums = (
        lax.psum(grad_gate.astype(jnp.bfloat16), "dp").astype(jnp.float32),
        lax.psum(grad_up.astype(jnp.bfloat16), "dp").astype(jnp.float32),
        lax.psum(grad_down.astype(jnp.bfloat16), "dp").astype(jnp.float32),
    )
    return (
        block_output,
        grad_input,
        dense[5],
        dense[0],
        dense[1],
        dense[2],
        dense[3],
        dense[6],
        dense[4],
        expert_sums[0],
        expert_sums[1],
        expert_sums[2],
    )


BF = jnp.bfloat16
F32 = jnp.float32
MIB = 1 << 20


def vmem_spec():
    return pl.BlockSpec(memory_space=pltpu.VMEM)


def smem_spec():
    return pl.BlockSpec(memory_space=pltpu.SMEM)


def allowed_pairs(offsets_ref, rows, start, count):
    side = lax.axis_index("expert")
    here = start + lax.broadcasted_iota(jnp.int32, (count, 1), 0)
    keys = lax.broadcasted_iota(jnp.int32, (1, 2 * rows), 1)
    query_place = side * rows + here
    key_place = jnp.where(keys < rows, side * rows + keys, (1 - side) * rows + keys - rows)
    span = 2 * PIC

    def piece(places):
        window = places // span
        within = places - window * span
        start = jnp.where(window == 0, offsets_ref[0, 0], offsets_ref[0, 1])
        inside = (within >= start) & (within < start + PIC)
        return jnp.where(inside, window, -1)

    query_piece = piece(query_place)
    key_piece = piece(key_place)
    return (key_place <= query_place) | ((key_piece == query_piece) & (query_piece >= 0))


def turn(values, first):
    wide = values.shape[1]
    half = HEAD_SIZE // 2
    return jnp.where(
        first, -pltpu.roll(values, wide - half, 1), pltpu.roll(values, half, 1)
    )


MESH = pl.DeviceIdType.MESH
PART = 32
LAG = 3
LINK_COST = pl.CostEstimate(flops=4 * 10**10, bytes_accessed=10**7, transcendentals=0)


def meet(partners):
    barrier = pltpu.get_barrier_semaphore()
    count = 0
    for here, device in partners:
        here = jnp.asarray(here)

        @pl.when(here)
        def _():
            pl.semaphore_signal(barrier, inc=1, device_id=device, device_id_type=MESH)

        count = count + here.astype(jnp.int32)
    pl.semaphore_wait(barrier, count)


def line_partners():
    place = lax.axis_index("tensor")
    last = lax.axis_size("tensor") - 1
    return [(place > 0, {"tensor": place - 1}), (place < last, {"tensor": place + 1})]


class Line:
    def __init__(self, parts, term, from_left, from_right, to_right, to_left, sems):
        self.place = lax.axis_index("tensor")
        self.last = lax.axis_size("tensor") - 1
        self.parts = parts
        self.term = term
        self.from_left, self.from_right = from_left, from_right
        self.to_right, self.to_left = to_right, to_left
        self.sems = sems

    def copy(self, way, at):
        near = jnp.where(self.place < self.last, self.place + 1, self.place - 1)
        far = jnp.where(self.place > 0, self.place - 1, self.place + 1)
        source, target, device = (
            (self.to_right, self.from_left, near) if way == 0 else (self.to_left, self.from_right, far)
        )
        return pltpu.make_async_remote_copy(
            src_ref=source.at[at],
            dst_ref=target.at[at],
            send_sem=self.sems.at[2 * way, at],
            recv_sem=self.sems.at[2 * way + 1, at],
            device_id={"tensor": device},
            device_id_type=MESH,
        )

    def clear(self):
        @pl.when(self.place == 0)
        def _():
            self.from_left[...] = jnp.zeros(self.from_left.shape, self.from_left.dtype)

        @pl.when(self.place == self.last)
        def _():
            self.from_right[...] = jnp.zeros(self.from_right.shape, self.from_right.dtype)

    def step(self, at):
        for way in range(2):
            part = at - LAG * (self.place if way == 0 else self.last - self.place)
            has_source = self.place > 0 if way == 0 else self.place < self.last
            has_target = self.place < self.last if way == 0 else self.place > 0
            arrived = self.from_left if way == 0 else self.from_right
            leaving = self.to_right if way == 0 else self.to_left
            valid = (part >= 0) & (part < self.parts)

            @pl.when(valid & has_source)
            def _():
                self.copy(way, part).wait_recv()

            @pl.when(valid & has_target)
            def _():
                leaving[part] = (self.term(part) + arrived[part].astype(F32)).astype(BF)
                self.copy(way, part).start()

    def total(self, part):
        return self.term(part) + self.from_left[part].astype(F32) + self.from_right[part].astype(F32)

    def drain(self):
        def wait(part, carry):
            @pl.when(self.place < self.last)
            def _():
                self.copy(0, part).wait_send()

            @pl.when(self.place > 0)
            def _():
                self.copy(1, part).wait_send()

            return carry

        lax.fori_loop(0, self.parts, wait, 0)


def line_scratch(parts, width):
    return [pltpu.VMEM((parts, PART, width), BF)] * 4 + [pltpu.SemaphoreType.DMA((4, parts))]


def peer_copy(source, target, sems, at):
    return pltpu.make_async_remote_copy(
        src_ref=source,
        dst_ref=target,
        send_sem=sems.at[0, at],
        recv_sem=sems.at[1, at],
        device_id={"expert": 1 - lax.axis_index("expert")},
        device_id_type=MESH,
    )


def scale_of(values):
    return lax.rsqrt(jnp.mean(values * values, axis=-1, keepdims=True) + epsilon)


def plain_copy(source, target, sems, at, device):
    return pltpu.make_async_remote_copy(
        src_ref=source, dst_ref=target, send_sem=sems.at[0, at], recv_sem=sems.at[1, at],
        device_id=device, device_id_type=MESH,
    )


def beside():
    return {"dp": lax.rem(lax.axis_index("dp") + 2, 4)}


def other_core():
    place = lax.axis_index("dp")
    return {"dp": place + 1 - 2 * lax.rem(place, 2)}


EARLY = 64
BAND = 256


def front_kernel(
    offsets_ref, x_ref, gain1_ref, gain2_ref, wq_ref, wk_ref, wv_ref, wo_ref, cos_ref, sin_ref, ids_ref, slots_ref, up_hbm,
    n1_ref, q_ref, k_ref, v_ref, att_ref, lse_ref, res_ref, n_ref, marks_ref, far_marks, up_peer, far_up,
    from_left, from_right, to_right, to_left, sems, peer_sems, far_sems, terms,
):
    parts = x_ref.shape[0]
    rows, width = n1_ref.shape
    side = lax.axis_index("expert")
    peer = {"expert": 1 - side}
    line = Line(parts, lambda at: terms[at], from_left, from_right, to_right, to_left, sems)
    meet(line_partners() + [(True, peer), (True, beside())])
    early, late = pl.ds(0, EARLY), pl.ds(EARLY, rows - EARLY)
    up_early = plain_copy(up_hbm.at[early, :], up_peer.at[early, :], far_sems, 0, peer)
    up_late = plain_copy(up_hbm.at[late, :], up_peer.at[late, :], far_sems, 1, peer)
    up_cross = plain_copy(up_hbm, far_up, far_sems, 2, beside())
    key_copy = plain_copy(k_ref.at[0], k_ref.at[1], far_sems, 3, peer)
    value_copy = plain_copy(v_ref.at[0], v_ref.at[1], far_sems, 4, peer)
    marks_copy = plain_copy(marks_ref.at[0], marks_ref.at[1], far_sems, 5, peer)
    marks_cross = plain_copy(marks_ref, far_marks, far_sems, 6, beside())
    up_early.start()
    up_cross.start()
    line.clear()

    values = x_ref[...].reshape(rows, width).astype(F32)
    normed = (values * scale_of(values) * gain1_ref[...]).astype(BF)
    n1_ref[...] = normed
    queries, kv = q_ref.shape[1], k_ref.shape[2]

    def rotate(array):
        wide = array.shape[1]
        lane = lax.broadcasted_iota(jnp.int32, (1, wide), 1)
        first = lane % HEAD_SIZE < HEAD_SIZE // 2
        cosines = jnp.concatenate([cos_ref[...]] * (wide // 128), axis=1)
        sines = jnp.concatenate([sin_ref[...]] * (wide // 128), axis=1)
        return (array * cosines + turn(array, first) * sines).astype(BF)

    k_ref[0] = rotate(matmul(normed, wk_ref[...]))
    key_copy.start()
    v_ref[0] = matmul(normed, wv_ref[...]).astype(BF)
    value_copy.start()
    experts_all = marks_ref.shape[2] // 2
    names = lax.broadcasted_iota(jnp.int32, (experts_all, 1), 0)
    chosen = jnp.zeros((experts_all, rows), F32)
    kept = jnp.zeros((experts_all, rows), F32)
    for pick in range(ids_ref.shape[0]):
        hit = jnp.where(ids_ref[pick : pick + 1, :] == names, 1.0, 0.0)
        chosen = chosen + hit
        kept = kept + jnp.where(slots_ref[pick : pick + 1, :] >= 0, hit, 0.0)
    marks_ref[0] = jnp.concatenate([chosen, kept], axis=0).T.astype(BF)
    marks_copy.start()
    up_late.start()
    q_ref[...] = rotate(matmul(normed, wq_ref[...]))
    key_copy.wait_recv()
    value_copy.wait_recv()
    sharing = queries // kv

    def attend(at):
        start = pl.multiple_of(at * BAND, BAND)
        band = pl.ds(start, BAND)
        allowed = allowed_pairs(offsets_ref, rows, start, BAND)
        pieces = []
        for head in range(queries // HEAD_SIZE):
            kv_at = head // sharing * HEAD_SIZE
            query = q_ref[band, head * HEAD_SIZE : (head + 1) * HEAD_SIZE]
            key = k_ref[:, :, kv_at : kv_at + HEAD_SIZE].reshape(2 * rows, HEAD_SIZE)
            value = v_ref[:, :, kv_at : kv_at + HEAD_SIZE].reshape(2 * rows, HEAD_SIZE)
            scores = jnp.where(allowed, matmul_nt(query, key) * (HEAD_SIZE**-0.5), masked_score)
            peak = jnp.max(scores, axis=1, keepdims=True)
            weights = jnp.exp(scores - peak)
            total = jnp.sum(weights, axis=1, keepdims=True)
            pieces.append(matmul((weights * (1.0 / total)).astype(BF), value))
            lse_ref[band, head : head + 1] = peak + jnp.log(total)
        attended = jnp.concatenate(pieces, axis=1).astype(BF)
        att_ref[band, :] = attended
        count = BAND // PART
        terms[pl.ds(at * count, count)] = matmul(attended, wo_ref[...]).reshape(count, PART, width)

    def body(at, carry):
        @pl.when(at < rows // BAND)
        def _():
            attend(at)

        @pl.when(at == 3)
        def _():
            marks_copy.wait_recv()
            marks_cross.start()

        line.step(at - 1)
        part = at - 1 - LAG * line.last

        @pl.when(part >= 0)
        def _():
            residual = x_ref[part].astype(F32) + line.total(part)
            res_ref[part] = residual
            unit = residual * scale_of(residual)
            n_ref[0, part] = (unit * gain2_ref[...]).astype(BF)
            peer_copy(n_ref.at[0, part], n_ref.at[1, part], peer_sems, part).start()

        return carry

    lax.fori_loop(0, 1 + parts + LAG * line.last, body, 0)
    line.drain()
    for copy in (key_copy, value_copy, marks_copy):
        copy.wait_send()
    for copy in (up_early, up_late, up_cross, marks_cross):
        copy.wait()

    def wait(part, carry):
        peer_copy(n_ref.at[0, part], n_ref.at[1, part], peer_sems, part).wait()
        return carry

    lax.fori_loop(0, parts, wait, 0)


def front(
    offsets, block_input, first_gain, second_gain, w_query, key_weight, value_weight, w_output, cosines, sines,
    expert_ids, slot_index, upstream, experts_all,
):
    rows, width = block_input.shape
    parts = rows // PART
    queries, kv = w_query.shape[1], key_weight.shape[1]
    any_spec = pl.BlockSpec(memory_space=pl.ANY)
    low = lambda *shape: jax.ShapeDtypeStruct(shape, BF)
    return pl.pallas_call(
        front_kernel,
        out_shape=(
            low(rows, width),
            low(rows, queries),
            low(2, rows, kv),
            low(2, rows, kv),
            low(rows, queries),
            jax.ShapeDtypeStruct((rows, 128), F32),
            jax.ShapeDtypeStruct((parts, PART, width), F32),
            low(2, parts, PART, width),
            low(2, rows, 2 * experts_all),
            low(2, rows, 2 * experts_all),
            low(rows, width),
            low(rows, width),
        ),
        in_specs=[smem_spec()] + [vmem_spec()] * 11 + [any_spec],
        out_specs=(vmem_spec(),) * 9 + (any_spec,) * 3,
        scratch_shapes=line_scratch(parts, width)
        + [
            pltpu.SemaphoreType.DMA((2, parts)),
            pltpu.SemaphoreType.DMA((2, 7)),
            pltpu.VMEM((parts, PART, width), F32),
        ],
        compiler_params=pltpu.CompilerParams(
            collective_id=0, has_side_effects=True, vmem_limit_bytes=60 * MIB
        ),
        cost_estimate=LINK_COST,
        name="front",
    )(
        offsets, block_input.reshape(parts, PART, width), first_gain[None], second_gain[None], w_query, key_weight,
        value_weight, w_output, cosines, sines, expert_ids, slot_index, upstream,
    )


UNIT = 512
SUB = 256


def residual_grad_kernel(
    back_ref, route_ref, res_ref, up_ref, gain_ref, wr_ref, mix_ref,
    far_n, far_on, far_g0, far_g1, far_og0, far_og1, far_m, far_om,
    wg_hbm, wu_hbm, wd_hbm, pg_hbm, pu_hbm, pd_hbm,
    grad_ref, low_ref, second_ref, route_out, mixed_ref, sg_hbm, su_hbm, sd_hbm, og_hbm, ou_hbm, od_hbm,
    from_left, from_right, to_right, to_left, sems, peer_sems, arrived, terms,
    tokens_n, tokens_g, turned, kept_gates, gates_w, ups_w, downs_w, pair_g, pair_u, pair_d, ght, dgs, dus,
    row_sems, weight_sems, pair_sems, out_sems, mix_arrived, mix_sems, marks_ref, share_sems,
):
    parts = back_ref.shape[1]
    core = lax.rem(lax.axis_index("dp"), 2)
    side = lax.axis_index("expert")
    groups, group, width, hid = pair_g.shape
    experts_all = wr_ref.shape[0]
    line = Line(parts + 1, lambda at: terms[at], from_left, from_right, to_right, to_left, sems)
    line.clear()
    meet(line_partners() + [(True, {"expert": 1 - side}), (True, other_core())])

    def send(part, carry):
        peer_copy(back_ref.at[1, part], arrived.at[part], peer_sems, part).start()
        return carry

    lax.fori_loop(0, parts, send, 0)

    def send_mix(part, carry):
        peer_copy(mix_ref.at[1, part], mix_arrived.at[part], mix_sems, part).start()
        return carry

    lax.fori_loop(0, parts, send_mix, 0)
    half = tokens_n.shape[0] // 2
    quarter = half // 2
    row_copies = []
    for place, (rows, first, second, marks) in enumerate(((far_n, far_g0, far_g1, far_m), (far_on, far_og0, far_og1, far_om))):
        at = place * half
        row_copies += [
            pltpu.make_async_copy(rows, tokens_n.at[pl.ds(at, half), :], row_sems.at[0, place]),
            pltpu.make_async_copy(first, tokens_g.at[pl.ds(at, quarter), :], row_sems.at[1, place]),
            pltpu.make_async_copy(second, tokens_g.at[pl.ds(at + quarter, quarter), :], row_sems.at[2, place]),
            pltpu.make_async_copy(marks, marks_ref.at[pl.ds(at, half), :], row_sems.at[3, place]),
        ]
    weight_copies, pair_copies, out_copies = [], [], []
    for at in range(groups):
        first = core * (groups * group) + at * group
        weight_copies.append(
            [
                pltpu.make_async_copy(
                    source.at[first + expert],
                    target.at[at, :, pl.ds(expert * hid, hid)],
                    weight_sems.at[at, kind, expert],
                )
                for expert in range(group)
                for kind, (source, target) in enumerate(((wg_hbm, gates_w), (wu_hbm, ups_w)))
            ]
            + [pltpu.make_async_copy(wd_hbm.at[pl.ds(first, group)], downs_w.at[at], weight_sems.at[at, 2, 0])]
        )
        sources = (pg_hbm, pu_hbm, pd_hbm)
        held = (pair_g, pair_u, pair_d)
        targets = (sg_hbm, su_hbm, sd_hbm)
        others = (og_hbm, ou_hbm, od_hbm)
        pair_copies.append(
            [
                pltpu.make_async_copy(sources[kind].at[pl.ds(at * group, group)], held[kind].at[at], pair_sems.at[at, kind])
                for kind in range(3)
            ]
        )
        out_copies.append(
            [
                pltpu.make_async_copy(held[kind].at[at], targets[kind].at[pl.ds(at * group, group)], out_sems.at[at, kind])
                for kind in range(3)
            ]
            + [
                plain_copy(
                    held[kind].at[at], others[kind].at[pl.ds(at * group, group)], share_sems.at[at], kind, other_core()
                )
                for kind in range(3)
            ]
        )
    for copy in row_copies[:4] + weight_copies[0] + row_copies[4:] + pair_copies[0] + weight_copies[1] + pair_copies[1]:
        copy.start()
    terms[parts] = route_ref[...]
    second_ref[...] = jnp.zeros(second_ref.shape, F32)
    chunks = 2 * half // UNIT
    units = chunks + 3

    def compute(at):
        for where in range(groups):
            unit = at - where * units

            @pl.when(unit == 0)
            def _():
                for copy in weight_copies[where]:
                    copy.wait()

            if where == 0:

                @pl.when(unit == 0)
                def _():
                    for copy in row_copies[:4]:
                        copy.wait()

                @pl.when(unit == half // UNIT)
                def _():
                    for copy in row_copies[4:]:
                        copy.wait()

            @pl.when(unit == chunks)
            def _():
                for copy in pair_copies[where]:
                    copy.wait()

        where = at // units
        unit = at - where * units

        @pl.when(unit < chunks)
        def _():
            down = downs_w[where].reshape(group * hid, width)
            column = side * (experts_all // 2) + (core * groups + where) * group
            for sub in range(UNIT // SUB):
                rows = pl.ds(pl.multiple_of(unit * UNIT + sub * SUB, SUB), SUB)

                @pl.when(where == 0)
                def _():
                    token = tokens_n[rows, :]
                    kept_gates[rows, :] = route_gates(token, marks_ref[rows, :], wr_ref[...])[1]
                    turned[:, rows] = token.T

            for sub in range(UNIT // SUB):
                rows = pl.ds(pl.multiple_of(unit * UNIT + sub * SUB, SUB), SUB)
                pulled = matmul_nt(tokens_g[rows, :], down)
                weight = spread_gates(kept_gates[rows, :], column, group, hid)
                _, gated, gate_grad, up_grad = hidden_terms(
                    tokens_n[rows, :], pulled, weight, gates_w[where], ups_w[where]
                )
                ght[:, rows] = gated.T
                dgs[rows, :] = gate_grad
                dus[rows, :] = up_grad

        @pl.when((unit >= chunks) & (unit < chunks + 2))
        def _():
            rows = pl.ds(pl.multiple_of((unit - chunks) * (width // 2), width // 2), width // 2)
            for source, held in ((dgs, pair_g), (dus, pair_u)):
                part = matmul(turned[rows, :], source[...])
                for expert in range(group):
                    more = part[:, expert * hid : (expert + 1) * hid]
                    held[where, expert, rows, :] = (held[where, expert, rows, :].astype(F32) + more).astype(BF)

        @pl.when(unit == chunks + 2)
        def _():
            part = matmul(ght[...], tokens_g[...])
            for expert in range(group):
                more = part[expert * hid : (expert + 1) * hid, :]
                pair_d[where, expert] = (pair_d[where, expert].astype(F32) + more).astype(BF)

        for where in range(groups):

            @pl.when(at == where * units + units - 1)
            def _():
                for copy in out_copies[where]:
                    copy.start()

    def add_mix(part):
        peer_copy(mix_ref.at[1, part], mix_arrived.at[part], mix_sems, part).wait_recv()
        mixed_ref[part] = (mix_ref[0, part].astype(F32) + mix_arrived[part].astype(F32)).astype(BF)

    steps = parts + 1 + LAG * line.last

    def advance(at):
        @pl.when(at < parts)
        def _():
            peer_copy(back_ref.at[1, at], arrived.at[at], peer_sems, at).wait_recv()
            terms[at] = back_ref[0, at].astype(F32) + arrived[at].astype(F32)

        line.step(at)
        part = at - LAG * line.last

        @pl.when((part >= 0) & (part < parts))
        def _():
            grad = line.total(part)
            residual = res_ref[part]
            scale = scale_of(residual)
            unit = residual * scale
            second_ref[...] += jnp.sum(grad * unit, axis=0, keepdims=True)
            result = up_ref[part].astype(F32) + norm_back(grad, unit, scale, gain_ref[...])
            grad_ref[part] = result
            low_ref[part] = result.astype(BF)

        @pl.when((at >= MIX_STEP) & (at < MIX_STEP + parts))
        def _():
            add_mix(at - MIX_STEP)

    turns = max(groups * units, (steps + 1) // 2)

    def body(at, carry):
        @pl.when(at < groups * units)
        def _():
            compute(at)

        def pair(half, carry):
            advance(2 * at + half)
            return carry

        lax.fori_loop(0, 2, pair, 0)
        return carry

    lax.fori_loop(0, turns, body, 0)
    route_out[...] = line.total(parts)

    def rest(part, carry):
        add_mix(part)
        return carry

    lax.fori_loop(2 * turns - MIX_STEP, parts, rest, 0)
    line.drain()

    def wait(part, carry):
        peer_copy(back_ref.at[1, part], arrived.at[part], peer_sems, part).wait_send()
        peer_copy(mix_ref.at[1, part], mix_arrived.at[part], mix_sems, part).wait_send()
        return carry

    lax.fori_loop(0, parts, wait, 0)
    for copies in out_copies:
        for copy in copies:
            copy.wait()


MIX_STEP = 17


def residual_gradient(back, mix, route, residual, upstream, gain, w_router, far_rows, w_gate, w_up, w_down, pairs):
    rows, width = upstream.shape
    parts = rows // PART
    half, _, hid = pairs[0].shape
    groups = half // GROUP
    tokens = 2 * far_rows[0].shape[0]
    any_spec = pl.BlockSpec(memory_space=pl.ANY)
    grad, low, second, route, mixed, *sums = pl.pallas_call(
        residual_grad_kernel,
        out_shape=[
            jax.ShapeDtypeStruct((parts, PART, width), F32),
            jax.ShapeDtypeStruct((parts, PART, width), BF),
            jax.ShapeDtypeStruct((1, width), F32),
            jax.ShapeDtypeStruct(route.shape, F32),
            jax.ShapeDtypeStruct((parts, PART, width), BF),
        ]
        + [jax.ShapeDtypeStruct(pair.shape, BF) for pair in pairs] * 2,
        in_specs=[vmem_spec()] * 7 + [any_spec] * 14,
        out_specs=[vmem_spec()] * 5 + [any_spec] * 6,
        scratch_shapes=line_scratch(parts + 1, width)
        + [
            pltpu.SemaphoreType.DMA((2, parts)),
            pltpu.VMEM((parts, PART, width), BF),
            pltpu.VMEM((parts + 1, PART, width), F32),
            pltpu.VMEM((tokens, width), BF),
            pltpu.VMEM((tokens, width), BF),
            pltpu.VMEM((width, tokens), BF),
            pltpu.VMEM((tokens, w_router.shape[0]), F32),
            pltpu.VMEM((groups, width, GROUP * hid), BF),
            pltpu.VMEM((groups, width, GROUP * hid), BF),
            pltpu.VMEM((groups, GROUP, hid, width), BF),
            pltpu.VMEM((groups, GROUP, width, hid), BF),
            pltpu.VMEM((groups, GROUP, width, hid), BF),
            pltpu.VMEM((groups, GROUP, hid, width), BF),
            pltpu.VMEM((GROUP * hid, tokens), BF),
            pltpu.VMEM((tokens, GROUP * hid), BF),
            pltpu.VMEM((tokens, GROUP * hid), BF),
            pltpu.SemaphoreType.DMA((4, 2)),
            pltpu.SemaphoreType.DMA((groups, 3, GROUP)),
            pltpu.SemaphoreType.DMA((groups, 3)),
            pltpu.SemaphoreType.DMA((groups, 3)),
            pltpu.VMEM((parts, PART, width), BF),
            pltpu.SemaphoreType.DMA((2, parts)),
            pltpu.VMEM((tokens, 2 * w_router.shape[0]), BF),
            pltpu.SemaphoreType.DMA((groups, 2, 3)),
        ],
        compiler_params=pltpu.CompilerParams(
            collective_id=1, has_side_effects=True, vmem_limit_bytes=60 * MIB
        ),
        cost_estimate=LINK_COST,
        name="residual_grad",
    )(
        back.reshape(2, parts, PART, width), route, residual, upstream.reshape(parts, PART, width), gain[None],
        w_router, mix.reshape(2, parts, PART, width), *far_rows, w_gate, w_up, w_down, *pairs,
    )
    return grad, low.reshape(rows, width), second, route, mixed, sums


def input_grad_kernel(
    offsets_ref, x_ref, res_grad_ref, gain_ref, n_ref, wq_ref, wk_ref, wv_ref, wo_ref, cos_ref, sin_ref,
    q_ref, k_ref, v_ref, lse_ref, att_ref, low_ref, route_ref, second_ref, mix_ref, res_ref,
    grad_ref, wide_out, wide_back, tall_out, tall_back, gains_ref, block_ref,
    from_left, from_right, to_right, to_left, sems, terms, kv_out, kv_in, kv_sems,
    wide, wide_core, wide_x, wide_y, tall, tall_core, tall_x, tall_y, rows2, rows_core, rows_x, rows_y, sum_sems,
    mix_left, mix_right, mix_to_right, mix_to_left, mix_sems,
):
    parts = x_ref.shape[0]
    rows = n_ref.shape[0]
    width = n_ref.shape[1]
    core = lax.rem(lax.axis_index("dp"), 2)
    peer = {"expert": 1 - lax.axis_index("expert")}
    kv = wk_ref.shape[1]
    queries = wq_ref.shape[1]
    line = Line(parts + 1, lambda at: terms[at], from_left, from_right, to_right, to_left, sems)
    spread = Spread(mix_ref, mix_left, mix_right, mix_to_right, mix_to_left, mix_sems)
    line.clear()
    spread.clear()
    meet(line_partners() + [(True, peer), (True, beside()), (True, other_core())])
    spread.step(0)
    key_copy = plain_copy(kv_out.at[0, pl.ds(rows, rows), :], kv_in.at[0], kv_sems, 0, peer)
    value_copy = plain_copy(kv_out.at[1, pl.ds(rows, rows), :], kv_in.at[1], kv_sems, 1, peer)

    scale = HEAD_SIZE**-0.5
    low = low_ref[...]
    out_part = matmul(att_ref[...].T, low).astype(BF)
    att_grad = matmul_nt(low, wo_ref[...]).astype(BF)
    half_tall = tall.shape[1]
    outs = wo_ref.shape[0]
    for at in range(2):
        start, high = at * half_tall, (at + 1) * half_tall
        top = min(high, outs)
        tall[at, : top - start, :] = out_part[start:top, :]
        if high > outs:
            tall[at, outs - start :, :] = route_ref[...].astype(BF)

    tall_steps = [
        plain_copy(tall.at[1 - core], tall_core, sum_sems, 0, other_core()),
        plain_copy(tall.at[core], tall_y, sum_sems, 1, peer),
        plain_copy(tall.at[core], tall_x, sum_sems, 2, beside()),
        plain_copy(tall.at[core], tall_back, sum_sems, 3, other_core()),
    ]
    wide_steps = [
        plain_copy(wide.at[1 - core], wide_core, sum_sems, 4, other_core()),
        plain_copy(wide.at[core], wide_x, sum_sems, 5, beside()),
        plain_copy(wide.at[core], wide_y, sum_sems, 6, peer),
        plain_copy(wide.at[core], wide_back, sum_sems, 7, other_core()),
    ]
    rows_steps = [
        plain_copy(rows2, rows_core, sum_sems, 8, other_core()),
        plain_copy(rows2, rows_y, sum_sems, 9, peer),
        plain_copy(rows2, rows_x, sum_sems, 10, beside()),
    ]
    tall_steps[0].start()

    def add(held, arrived):
        held[...] = (held[...].astype(F32) + arrived[...].astype(F32)).astype(BF)

    allowed = allowed_pairs(offsets_ref, rows, 0, rows)
    sharing = queries // kv
    query_parts, key_parts, value_parts = [], [], []
    for head in range(queries // HEAD_SIZE):
        if head:
            spread.step(head)
        if head == 1:
            tall_steps[0].wait()
            add(tall.at[core], tall_core)
            tall_steps[1].start()
        if head == 3:
            tall_steps[1].wait()
            add(tall.at[core], tall_y)
            tall_steps[2].start()
        at = head * HEAD_SIZE
        kv_at = head // sharing * HEAD_SIZE
        query = q_ref[:, at : at + HEAD_SIZE]
        key = k_ref[:, kv_at : kv_at + HEAD_SIZE]
        value = v_ref[:, kv_at : kv_at + HEAD_SIZE]
        grad = att_grad[:, at : at + HEAD_SIZE]
        scores = jnp.where(allowed, matmul_nt(query, key) * scale, masked_score)
        probs = jnp.exp(scores - lse_ref[:, head : head + 1])
        prob_grad = matmul_nt(grad, value)
        delta = jnp.sum(probs * prob_grad, axis=1, keepdims=True)
        score_grad = (probs * (prob_grad - delta)).astype(BF)
        query_parts.append(matmul(score_grad, key) * scale)
        key_part = matmul_tn(score_grad, query) * scale
        value_part = matmul_tn(probs.astype(BF), grad)
        if head % sharing == 0:
            key_parts.append(key_part)
            value_parts.append(value_part)
        else:
            key_parts[-1] = key_parts[-1] + key_part
            value_parts[-1] = value_parts[-1] + value_part
    kv_out[0] = jnp.concatenate(key_parts, axis=1).astype(BF)
    key_copy.start()
    kv_out[1] = jnp.concatenate(value_parts, axis=1).astype(BF)
    value_copy.start()

    def rotate_back(array):
        wide_lanes = array.shape[1]
        lane = lax.broadcasted_iota(jnp.int32, (1, wide_lanes), 1)
        first = lane % HEAD_SIZE < HEAD_SIZE // 2
        cosines = jnp.concatenate([cos_ref[...]] * (wide_lanes // 128), axis=1)
        sines = jnp.concatenate([sin_ref[...]] * (wide_lanes // 128), axis=1)
        return (array * cosines - turn(array, first) * sines).astype(BF)

    query_grad = rotate_back(jnp.concatenate(query_parts, axis=1))
    by_rows = (parts, rows // parts, width)
    terms[pl.ds(0, parts)] = matmul_nt(query_grad, wq_ref[...]).reshape(by_rows)
    turned = n_ref[...].T
    query_part = matmul(turned, query_grad).astype(BF)
    for at in range(2):
        wide[at, :, :queries] = query_part[at * width // 2 : (at + 1) * width // 2, :]
    key_copy.wait_recv()
    value_copy.wait_recv()
    key_grad = rotate_back(kv_out[0, :rows, :].astype(F32) + kv_in[0].astype(F32))
    value_grad = (kv_out[1, :rows, :].astype(F32) + kv_in[1].astype(F32)).astype(BF)
    more = matmul_nt(key_grad, wk_ref[...]) + matmul_nt(value_grad, wv_ref[...])
    terms[pl.ds(0, parts)] += more.reshape(by_rows)
    both_part = matmul(turned, jnp.concatenate([key_grad, value_grad], axis=1)).astype(BF)
    for at in range(2):
        wide[at, :, queries:] = both_part[at * width // 2 : (at + 1) * width // 2, :]
    wide_steps[0].start()

    def gain_part(at, total):
        values = x_ref[at].astype(F32)
        return total + jnp.sum(terms[at] * (values * scale_of(values)), axis=0, keepdims=True)

    first_sum = lax.fori_loop(0, parts, gain_part, jnp.zeros((1, width), F32))
    pad = jnp.zeros((rows2.shape[0] - 2, width), F32)
    rows2[...] = jnp.concatenate([first_sum, second_ref[...], pad], axis=0).astype(BF)
    rows_steps[0].start()

    def exchange(at):
        @pl.when(at == 0)
        def _():
            rows_steps[0].wait()
            add(rows2, rows_core)
            rows_steps[1].start()

        @pl.when(at == 1)
        def _():
            wide_steps[0].wait()
            add(wide.at[core], wide_core)

        @pl.when(at == 2)
        def _():
            rows_steps[1].wait()
            add(rows2, rows_y)
            rows_steps[2].start()
            wide_steps[1].start()

        @pl.when(at == 5)
        def _():
            rows_steps[2].wait()
            add(rows2, rows_x)
            summed = rows2[...].astype(F32)
            terms[parts] = jnp.concatenate([summed[:1, :], jnp.zeros((PART - 1, width), F32)], axis=0)
            gains_ref[1:2, :] = summed[1:2, :]

        @pl.when(at == 11)
        def _():
            wide_steps[1].wait()
            add(wide.at[core], wide_x)
            wide_steps[2].start()

        @pl.when(at == 3)
        def _():
            tall_steps[2].wait()
            add(tall.at[core], tall_x)
            tall_steps[3].start()

        @pl.when(at == 20)
        def _():
            wide_steps[2].wait()
            add(wide.at[core], wide_y)
            wide_steps[3].start()

    heads = queries // HEAD_SIZE

    def body(at, carry):
        exchange(at)
        line.step(at)

        @pl.when((at % 2 == 0) & (at // 2 + heads < spread.steps))
        def _():
            spread.step(at // 2 + heads)

        @pl.when((at % 2 == 0) & (at // 2 + heads >= spread.first_whole) & (at // 2 + heads < spread.steps))
        def _():
            block = at // 2 + heads - spread.first_whole
            block_ref[block] = (res_ref[block, :, spread.own()] + spread.total(block)).astype(BF)

        part = at - LAG * line.last

        @pl.when((part >= 0) & (part < parts))
        def _():
            grad = line.total(part)
            values = x_ref[part].astype(F32)
            scale = scale_of(values)
            unit = values * scale
            grad_ref[part] = (res_grad_ref[part] + norm_back(grad, unit, scale, gain_ref[...])).astype(BF)

        return carry

    lax.fori_loop(0, parts + 1 + LAG * line.last, body, 0)
    gains_ref[0:1, :] = line.total(parts)[:1, :]
    line.drain()
    spread.drain()
    key_copy.wait_send()
    value_copy.wait_send()
    tall_steps[3].wait()
    wide_steps[3].wait()
    tall_out[...] = tall[core]
    wide_out[...] = wide[core]


class Spread:
    def __init__(self, term, from_left, from_right, to_right, to_left, sems):
        self.place = lax.axis_index("tensor")
        self.size = lax.axis_size("tensor")
        self.term = term
        self.blocks = term.shape[0]
        self.span = term.shape[2] // self.size
        self.from_left, self.from_right = from_left, from_right
        self.to_right, self.to_left = to_right, to_left
        self.sems = sems
        self.first_whole = 2 * (self.size - 1)
        self.steps = self.blocks + self.first_whole

    def copy(self, way, block, shard):
        last = self.size - 1
        near = jnp.where(self.place < last, self.place + 1, self.place - 1)
        far = jnp.where(self.place > 0, self.place - 1, self.place + 1)
        source, target, device = (
            (self.to_right, self.from_left, near) if way == 0 else (self.to_left, self.from_right, far)
        )
        return pltpu.make_async_remote_copy(
            src_ref=source.at[block, shard], dst_ref=target.at[block, shard],
            send_sem=self.sems.at[2 * way, block, shard], recv_sem=self.sems.at[2 * way + 1, block, shard],
            device_id={"tensor": device}, device_id_type=MESH,
        )

    def clear(self):
        @pl.when(self.place == 0)
        def _():
            self.from_left[...] = jnp.zeros(self.from_left.shape, BF)

        @pl.when(self.place == self.size - 1)
        def _():
            self.from_right[...] = jnp.zeros(self.from_right.shape, BF)

    def passes(self, way, shard):
        return self.place < shard if way == 0 else self.place > shard

    def has_source(self, way):
        return self.place > 0 if way == 0 else self.place < self.size - 1

    def step(self, at):
        for way in range(2):
            block = at - 2 * (self.place if way == 0 else self.size - 1 - self.place)
            valid = (block >= 0) & (block < self.blocks)
            arrived = self.from_left if way == 0 else self.from_right
            leaving = self.to_right if way == 0 else self.to_left
            for shard in range(self.size):
                here = valid & self.passes(way, shard)

                @pl.when(here & self.has_source(way))
                def _():
                    self.copy(way, block, shard).wait_recv()

                @pl.when(here)
                def _():
                    lanes = slice(shard * self.span, (shard + 1) * self.span)
                    own = self.term[block, :, lanes].astype(F32)
                    leaving[block, shard] = (own + arrived[block, shard].astype(F32)).astype(BF)
                    self.copy(way, block, shard).start()

    def own(self):
        return pl.ds(pl.multiple_of(self.place * self.span, self.span), self.span)

    def total(self, block):
        for way in range(2):

            @pl.when(self.has_source(way))
            def _():
                self.copy(way, block, self.place).wait_recv()

        sides = self.from_left[block, self.place].astype(F32) + self.from_right[block, self.place].astype(F32)
        return self.term[block, :, self.own()].astype(F32) + sides

    def drain(self):
        for way in range(2):
            for shard in range(self.size):

                @pl.when(self.passes(way, shard))
                def _():
                    for block in range(self.blocks):
                        self.copy(way, block, shard).wait_send()


BLOCK_ROWS = 128


def input_gradient(
    offsets, block_input, residual_grad, gain, normed, w_query, key_weight, value_weight, w_output, cosines, sines,
    query, keys, values, lse, attended, low, route, second, mixed, residual,
):
    rows, width = block_input.shape
    parts = rows // PART
    kv = key_weight.shape[1]
    columns = w_query.shape[1] + 2 * kv
    tall = (w_output.shape[0] + route.shape[0]) // 2
    size = lax.axis_size("tensor")
    blocks = rows // BLOCK_ROWS
    wide_half = pltpu.VMEM((width // 2, columns), BF)
    tall_half = pltpu.VMEM((tall, width), BF)
    tile = pltpu.VMEM((16, width), BF)
    mix_half = pltpu.VMEM((blocks, size, BLOCK_ROWS, width // size), BF)
    return pl.pallas_call(
        input_grad_kernel,
        out_shape=(
            jax.ShapeDtypeStruct((parts, PART, width), BF),
            jax.ShapeDtypeStruct((width // 2, columns), BF),
            jax.ShapeDtypeStruct((width // 2, columns), BF),
            jax.ShapeDtypeStruct((tall, width), BF),
            jax.ShapeDtypeStruct((tall, width), BF),
            jax.ShapeDtypeStruct((8, width), F32),
            jax.ShapeDtypeStruct((blocks, BLOCK_ROWS, width // size), BF),
        ),
        in_specs=[smem_spec()] + [vmem_spec()] * 20,
        out_specs=(vmem_spec(),) * 7,
        scratch_shapes=line_scratch(parts + 1, width)
        + [
            pltpu.VMEM((parts + 1, PART, width), F32),
            pltpu.VMEM((2, 2 * rows, kv), BF),
            pltpu.VMEM((2, rows, kv), BF),
            pltpu.SemaphoreType.DMA((2, 2)),
            pltpu.VMEM((2, width // 2, columns), BF), wide_half, wide_half, wide_half,
            pltpu.VMEM((2, tall, width), BF), tall_half, tall_half, tall_half,
            tile, tile, tile, tile,
            pltpu.SemaphoreType.DMA((2, 11)),
            mix_half, mix_half, mix_half, mix_half,
            pltpu.SemaphoreType.DMA((4, blocks, size)),
        ],
        compiler_params=pltpu.CompilerParams(
            collective_id=2, has_side_effects=True, vmem_limit_bytes=60 * MIB
        ),
        cost_estimate=LINK_COST,
        name="input_grad",
    )(
        offsets, block_input.reshape(parts, PART, width), residual_grad, gain[None], normed,
        w_query, key_weight, value_weight, w_output, cosines, sines, query, keys, values, lse, attended, low,
        route, second, mixed.reshape(blocks, BLOCK_ROWS, width), residual.reshape(blocks, BLOCK_ROWS, width),
    )


CHUNK = 512
GROUP = 4


def route_gates(token, marks, w_router):
    experts_all = w_router.shape[0]
    chosen = marks[:, :experts_all].astype(F32)
    kept = marks[:, experts_all:].astype(F32)
    logits = jnp.where(chosen > 0.0, matmul_nt(token, w_router), masked_score)
    raised = jnp.exp(logits - jnp.max(logits, axis=1, keepdims=True)) * chosen
    gate = raised / jnp.sum(raised, axis=1, keepdims=True)
    return gate, gate * kept


def hidden_terms(token, pulled, weight, gate_weights, up_weights):
    gate_in = matmul(token, gate_weights)
    up_in = matmul(token, up_weights)
    sig = 0.5 * jnp.tanh(0.5 * gate_in) + 0.5
    silu = gate_in * sig
    hidden = silu * up_in
    gated = (hidden * weight).astype(BF)
    scaled = pulled * weight
    up_grad = (scaled * silu).astype(BF)
    gate_grad = (scaled * up_in * (sig + silu * (1.0 - sig))).astype(BF)
    return hidden, gated, gate_grad, up_grad


def spread_gates(kept, column, group, hid):
    lane = lax.broadcasted_iota(jnp.int32, (1, kept.shape[1]), 1)
    weights = []
    for expert in range(group):
        gate = jnp.sum(jnp.where(lane == column + expert, kept, 0.0), axis=1, keepdims=True)
        weights.append(jnp.broadcast_to(gate, (kept.shape[0], hid)))
    return jnp.concatenate(weights, axis=1)


def expert_kernel(
    n_ref, marks_ref, wr_ref, n_hbm, own_up, peer_up, far_g0, far_m, wg_ref, wu_ref, wd_ref,
    dwg_ref, dwu_ref, dwd_ref, mix_ref, back_ref, route_ref, far_n, far_on, far_g1, far_og0, far_og1, far_om,
    gates, kept_gates, gate_grads, mix, back, nt, wgs, wus, ght, dgs, dus,
    out_g, out_u, out_d, in_g, in_u, in_d, sems, far_sems, g_ref, up_sems,
):
    step = pl.program_id(0)
    steps = pl.num_programs(0) // 2
    side = lax.axis_index("expert")
    dp = lax.axis_index("dp")
    core = lax.rem(dp, 2)
    other = other_core()
    tokens, width = n_ref.shape
    experts_all = wr_ref.shape[0]
    group, _, hid = wg_ref.shape
    chunks = tokens // CHUNK
    lane = lax.broadcasted_iota(jnp.int32, (1, experts_all), 1)

    def copies(slot):
        return [
            pltpu.make_async_remote_copy(
                src_ref=source.at[slot], dst_ref=target.at[slot],
                send_sem=sems.at[0, kind, slot], recv_sem=sems.at[1, kind, slot],
                device_id=other, device_id_type=MESH,
            )
            for kind, (source, target) in enumerate(((out_g, in_g), (out_u, in_u), (out_d, in_d)))
        ]

    half = tokens // 2
    cross = [
        plain_copy(n_hbm.at[pl.ds(at * half, half), :], far_n.at[pl.ds(at * half, half), :], far_sems, at, beside())
        for at in range(2)
    ]
    share = [
        plain_copy(far_n.at[pl.ds(at * half, half), :], far_on.at[pl.ds(at * half, half), :], far_sems, 2 + at, other)
        for at in range(2)
    ]
    peer = {"expert": 1 - side}
    turn_up = plain_copy(far_g0, far_g1, far_sems, 4, peer)
    share_up = plain_copy(far_g1, far_og1, far_sems, 5, other)
    early = [
        plain_copy(source, target, far_sems, 6 + at, other)
        for at, (source, target) in enumerate(((far_g0, far_og0), (far_m, far_om)))
    ]
    loads = [
        pltpu.make_async_copy(source, g_ref.at[pl.ds(at * half, half), :], up_sems.at[at])
        for at, source in enumerate((own_up, peer_up))
    ]

    @pl.when(step == 0)
    def _():
        for copy in loads:
            copy.start()
        meet([(True, other), (True, beside()), (True, peer)])
        for copy in cross + early + [turn_up]:
            copy.start()

        def start(at, carry):
            rows = pl.ds(pl.multiple_of(at * CHUNK, CHUNK), CHUNK)
            gate, kept_gate = route_gates(n_ref[rows, :], marks_ref[rows, :], wr_ref[...])
            gates[rows, :] = gate
            kept_gates[rows, :] = kept_gate
            mix[rows, :] = jnp.zeros((CHUNK, width), F32)
            back[rows, :] = jnp.zeros((CHUNK, width), F32)
            gate_grads[rows, :] = jnp.zeros((CHUNK, experts_all), F32)
            return carry

        lax.fori_loop(0, chunks, start, 0)
        for at in range(chunks):
            nt[:, at * CHUNK : (at + 1) * CHUNK] = n_ref[at * CHUNK : (at + 1) * CHUNK, :].T
        for copy in loads:
            copy.wait()

    @pl.when(step == steps)
    def _():
        cross[0].wait_recv()
        share[0].start()
        turn_up.wait_recv()
        share_up.start()

    for expert in range(group):
        wgs[:, expert * hid : (expert + 1) * hid] = wg_ref[expert]
        wus[:, expert * hid : (expert + 1) * hid] = wu_ref[expert]
    first = step < steps
    block = jnp.where(first, (1 - core) * steps + step, core * steps + step - steps)
    column = side * (experts_all // 2) + block * group

    for at in range(chunks):
        rows = slice(at * CHUNK, (at + 1) * CHUNK)
        token = n_ref[rows, :]
        down = wd_ref[...].reshape(group * hid, width)
        pulled = matmul_nt(g_ref[rows, :], down)
        weight = spread_gates(kept_gates[rows, :], column, group, hid)
        hidden, gated, gate_grad, up_grad = hidden_terms(token, pulled, weight, wgs[...], wus[...])
        products = hidden * pulled
        grads = gate_grads[rows, :]
        for expert in range(group):
            product = jnp.sum(products[:, expert * hid : (expert + 1) * hid], axis=1, keepdims=True)
            grads = grads + jnp.where(lane == column + expert, product, 0.0)
        gate_grads[rows, :] = grads
        ght[:, rows] = gated.T
        dgs[rows, :] = gate_grad
        dus[rows, :] = up_grad
        mix[rows, :] += matmul(gated, down)
        back[rows, :] += matmul_nt(gate_grad, wgs[...]) + matmul_nt(up_grad, wus[...])

    def weight_grads(store_rows, store_down):
        for at in range(width // CHUNK):
            rows = slice(at * CHUNK, (at + 1) * CHUNK)
            turned = nt[rows, :]
            gate_part = matmul(turned, dgs[...])
            up_part = matmul(turned, dus[...])
            for expert in range(group):
                inner = slice(expert * hid, (expert + 1) * hid)
                store_rows(expert, rows, gate_part[:, inner], up_part[:, inner])
        down_part = matmul(ght[...], g_ref[...])
        for expert in range(group):
            store_down(expert, down_part[expert * hid : (expert + 1) * hid, :])

    @pl.when(first)
    def _():
        def store_rows(expert, rows, gate_part, up_part):
            out_g[step, expert, rows, :] = gate_part.astype(BF)
            out_u[step, expert, rows, :] = up_part.astype(BF)

        def store_down(expert, part):
            out_d[step, expert] = part.astype(BF)

        weight_grads(store_rows, store_down)
        for copy in copies(step):
            copy.start()

    @pl.when(step >= steps)
    def _():
        slot = step - steps
        for copy in copies(slot):
            copy.wait_recv()

        def store_rows(expert, rows, gate_part, up_part):
            dwg_ref[expert, rows, :] = (gate_part + in_g[slot, expert, rows, :].astype(F32)).astype(BF)
            dwu_ref[expert, rows, :] = (up_part + in_u[slot, expert, rows, :].astype(F32)).astype(BF)

        def store_down(expert, part):
            dwd_ref[expert] = (part + in_d[slot, expert].astype(F32)).astype(BF)

        weight_grads(store_rows, store_down)
        for copy in copies(slot):
            copy.wait_send()

    @pl.when(step == 2 * steps - 1)
    def _():
        cross[1].wait_recv()
        share[1].start()
        route_ref[...] = jnp.zeros(route_ref.shape, F32)

        def finish(at, carry):
            rows = pl.ds(pl.multiple_of(at * CHUNK, CHUNK), CHUNK)
            mix_ref[rows, :] = mix[rows, :].astype(BF)
            grads = gate_grads[rows, :] * kept_gates[rows, :]
            chosen_grad = grads - gates[rows, :] * jnp.sum(grads, axis=1, keepdims=True)
            low = chosen_grad.astype(BF)
            back_ref[rows, :] = (back[rows, :] + matmul(low, wr_ref[...])).astype(BF)
            route_ref[...] += matmul_tn(low, n_ref[rows, :])
            return carry

        lax.fori_loop(0, chunks, finish, 0)
        for copy in cross + [turn_up]:
            copy.wait_send()
        for copy in share + early + [share_up]:
            copy.wait()


def experts(normed, marks, w_router, upstream, peer_up, far_up, far_marks, w_gate, w_up, w_down):
    tokens, width = normed.shape
    count, _, hid = w_gate.shape
    half = count // 2
    steps = half // GROUP
    experts_all = w_router.shape[0]
    once = pl.Buffered(1)
    whole = lambda step: (0, 0)

    def picked(step):
        core = lax.rem(lax.axis_index("dp"), 2)
        return (jnp.where(step < steps, (1 - core) * steps + step, core * steps + step - steps), 0, 0)

    own = lambda step: (jnp.maximum(step - steps, 0), 0, 0)
    args = [normed, marks, w_router]
    specs = [pl.BlockSpec(array.shape, whole, pipeline_mode=once) for array in args]
    args += [normed, upstream, peer_up, far_up, far_marks]
    specs += [pl.BlockSpec(memory_space=pl.ANY)] * 5
    up_block, down_block = (GROUP, width, hid), (GROUP, hid, width)
    specs += [pl.BlockSpec(up_block, picked), pl.BlockSpec(up_block, picked), pl.BlockSpec(down_block, picked)]
    gate_scratch = pltpu.VMEM((tokens, experts_all), F32)
    rows_scratch = pltpu.VMEM((tokens, width), F32)
    swap_scratch = [
        pltpu.VMEM((steps,) + up_block, BF),
        pltpu.VMEM((steps,) + up_block, BF),
        pltpu.VMEM((steps,) + down_block, BF),
    ]
    return pl.pallas_call(
        expert_kernel,
        out_shape=[
            jax.ShapeDtypeStruct((half, width, hid), BF),
            jax.ShapeDtypeStruct((half, width, hid), BF),
            jax.ShapeDtypeStruct((half, hid, width), BF),
            jax.ShapeDtypeStruct((tokens, width), BF),
            jax.ShapeDtypeStruct((tokens, width), BF),
            jax.ShapeDtypeStruct((experts_all, width), F32),
            jax.ShapeDtypeStruct((tokens, width), BF),
            jax.ShapeDtypeStruct((tokens, width), BF),
            jax.ShapeDtypeStruct(far_up.shape, BF),
            jax.ShapeDtypeStruct(far_up.shape, BF),
            jax.ShapeDtypeStruct(far_up.shape, BF),
            jax.ShapeDtypeStruct(far_marks.shape, BF),
        ],
        grid=(2 * steps,),
        in_specs=specs,
        out_specs=[
            pl.BlockSpec(up_block, own),
            pl.BlockSpec(up_block, own),
            pl.BlockSpec(down_block, own),
            pl.BlockSpec((tokens, width), whole, pipeline_mode=once),
            pl.BlockSpec((tokens, width), whole, pipeline_mode=once),
            pl.BlockSpec((experts_all, width), whole, pipeline_mode=once),
        ]
        + [pl.BlockSpec(memory_space=pl.ANY)] * 6,
        scratch_shapes=[
            gate_scratch, gate_scratch, gate_scratch, rows_scratch, rows_scratch,
            pltpu.VMEM((width, tokens), BF),
            pltpu.VMEM((width, GROUP * hid), BF),
            pltpu.VMEM((width, GROUP * hid), BF),
            pltpu.VMEM((GROUP * hid, tokens), BF),
            pltpu.VMEM((tokens, GROUP * hid), BF),
            pltpu.VMEM((tokens, GROUP * hid), BF),
        ]
        + swap_scratch
        + swap_scratch
        + [pltpu.SemaphoreType.DMA((2, 3, steps)), pltpu.SemaphoreType.DMA((2, 8)), pltpu.VMEM((tokens, width), BF), pltpu.SemaphoreType.DMA((2,))],
        compiler_params=pltpu.CompilerParams(
            dimension_semantics=("arbitrary",), collective_id=3, has_side_effects=True, vmem_limit_bytes=60 * MIB
        ),
        cost_estimate=pl.CostEstimate(
            flops=18 * tokens * width * count * hid,
            bytes_accessed=12 * count * width * hid,
            transcendentals=tokens * count * hid,
        ),
        name="experts",
    )(*args, w_gate, w_up, w_down)


def finish_kernel(core_ref, *refs):
    ins, outs = refs[:13], refs[13:]
    part, at = pl.program_id(0), pl.program_id(1)
    mine, other = ins[:3], ins[3:6]
    wide_mine, wide_other, tall_mine, tall_other, gains, grad, block = ins[6:]
    out_g, out_u, out_d, out_q, out_k, out_v, out_o, out_r, out_first, out_second, out_grad, out_block = outs
    for place, sources in enumerate((mine, other)):

        @pl.when(part == place)
        def _():
            for source, target in zip(sources, (out_g, out_u, out_d)):
                target[...] = source[...].astype(F32)

    core = core_ref[0]
    queries, kv = out_q.shape[1], out_k.shape[1]
    half = out_q.shape[0] // 2
    tall = tall_mine.shape[0]
    outs_rows = out_o.shape[0]

    @pl.when((part == 0) & (at == 0))
    def _():
        out_grad[...] = grad[...]
        out_block[...] = block[...]
        out_first[...] = gains[0:1, :]
        out_second[...] = gains[1:2, :]

    for place in range(2):

        @pl.when((part == 0) & (at == 1 + place))
        def _():
            own = core == place
            summed = jnp.where(own, wide_mine[...].astype(F32), wide_other[...].astype(F32))
            rows = slice(place * half, (place + 1) * half)
            out_q[rows, :] = summed[:, :queries]
            out_k[rows, :] = summed[:, queries : queries + kv]
            out_v[rows, :] = summed[:, queries + kv :]
            tall_sum = jnp.where(own, tall_mine[...].astype(F32), tall_other[...].astype(F32))
            top = min((place + 1) * tall, outs_rows)
            out_o[place * tall : top, :] = tall_sum[: top - place * tall, :]
            if place == 1:
                out_r[...] = tall_sum[top - place * tall :, :]


def finish(core, sums, others, wide, wide_back, tall, tall_back, gains, grad, block, queries, outs_rows):
    half = sums[0].shape[0]
    width = grad.shape[1]
    kv = (wide.shape[1] - queries) // 2
    experts_all = 2 * tall.shape[0] - outs_rows
    whole = lambda shape: pl.BlockSpec(shape, lambda part, at, core: (0,) * len(shape), pipeline_mode=pl.Buffered(1))
    single = lambda array, index: pl.BlockSpec((1,) + array.shape[1:], index)
    first = lambda part, at, core: (jnp.where(part == 0, at, half - 1), 0, 0)
    second = lambda part, at, core: (jnp.where(part == 0, 0, at), 0, 0)
    placed = lambda part, at, core: (jnp.where(part == 0, core[0], 1 - core[0]) * half + at, 0, 0)
    rest = [wide, wide_back, tall, tall_back, gains, grad, block]
    wide_shape = lambda shape: jax.ShapeDtypeStruct(shape, F32)
    shapes = [
        (2 * wide.shape[0], queries), (2 * wide.shape[0], kv), (2 * wide.shape[0], kv),
        (outs_rows, width), (experts_all, width), (1, width), (1, width),
    ]
    return pl.pallas_call(
        finish_kernel,
        out_shape=[wide_shape((2 * half,) + item.shape[1:]) for item in sums]
        + [wide_shape(shape) for shape in shapes]
        + [jax.ShapeDtypeStruct(grad.shape, BF), jax.ShapeDtypeStruct(block.shape, BF)],
        grid_spec=pltpu.PrefetchScalarGridSpec(
            num_scalar_prefetch=1,
            grid=(2, half),
            in_specs=[single(item, first) for item in sums]
            + [single(item, second) for item in others]
            + [whole(item.shape) for item in rest],
            out_specs=[single(item, placed) for item in sums]
            + [whole(shape) for shape in shapes + [grad.shape, block.shape]],
        ),
        compiler_params=pltpu.CompilerParams(vmem_limit_bytes=60 * MIB),
        name="finish",
    )(core, *sums, *others, *rest)


def fast_device(
    block_input, first_gain, w_query, key_weight, value_weight, w_output, second_gain, w_router,
    w_gate, w_up, w_down, expert_ids, slot_index, piece_start_offsets, upstream,
):
    rows, width = block_input.shape
    experts_all = w_router.shape[1]
    core = lax.axis_index("dp") % 2
    positions = lax.axis_index("expert") * rows + jnp.arange(rows, dtype=jnp.int32)
    lanes = jnp.arange(128, dtype=jnp.int32) % (HEAD_SIZE // 2)
    inverse = jnp.exp(lanes.astype(F32) * (-2.0 * math.log(rope_base) / HEAD_SIZE))
    angle = positions.astype(F32)[:, None] * inverse[None, :]
    cosines, sines = jnp.cos(angle), jnp.sin(angle)
    routes = w_router.T
    (
        first_normed, query_rot, keys, values, attended, lse, residual, normed_all, marks, far_marks, peer_up, far_up,
    ) = front(
        piece_start_offsets, block_input, first_gain, second_gain, w_query, key_weight, value_weight, w_output,
        cosines, sines, expert_ids.T, slot_index.T, upstream, experts_all,
    )
    keys, values = keys.reshape(2 * rows, -1), values.reshape(2 * rows, -1)
    normed_all = normed_all.reshape(2 * rows, width)
    marks = marks.reshape(2 * rows, 2 * experts_all)
    far_marks = far_marks.reshape(2 * rows, 2 * experts_all)
    dwg, dwu, dwd, mix, back, route, *far = experts(
        normed_all, marks, routes, upstream, peer_up, far_up, far_marks, w_gate, w_up, w_down
    )
    far_normed, far_other_normed, far_peer_up, far_other_up, far_other_peer_up, far_other_marks = far
    residual_grad, residual_low, grad_second, route, mixed, sums = residual_gradient(
        back, mix, route, residual, upstream, second_gain, routes,
        (
            far_normed, far_other_normed, far_up, far_peer_up, far_other_up, far_other_peer_up,
            far_marks, far_other_marks,
        ),
        w_gate, w_up, w_down, (dwg, dwu, dwd),
    )
    grad_input, wide, wide_back, tall, tall_back, gains, block_output = input_gradient(
        piece_start_offsets, block_input, residual_grad, first_gain, first_normed, w_query, key_weight, value_weight,
        w_output, cosines, sines, query_rot, keys, values, lse, attended, residual_low, route, grad_second, mixed, residual,
    )
    grad_gate, grad_up, grad_down, grad_query, grad_key, grad_value, grad_output, grad_router, first, second, grad, block = finish(
        core[None].astype(jnp.int32), sums[:3], sums[3:], wide, wide_back, tall, tall_back, gains,
        grad_input.reshape(rows, width), block_output.reshape(rows, width // 4), w_query.shape[1], w_output.shape[0],
    )
    return (
        block, grad, first[0], grad_query, grad_key, grad_value, grad_output, second[0], grad_router.T,
        grad_gate, grad_up, grad_down,
    )


def solution(mesh):
    fast = mesh.shape["expert"] == 2 and mesh.shape["dp"] == 4 and mesh.shape["tensor"] == 4
    placed = (
        P(("dp", "expert"), None),
        P(),
        P(None, "tensor"),
        P(None, "tensor"),
        P(None, "tensor"),
        P("tensor", None),
        P(),
        P(),
        P("expert", None, "tensor"),
        P("expert", None, "tensor"),
        P("expert", "tensor", None),
        P(("dp", "expert"), None),
        P(("dp", "expert"), None),
        P("dp", None),
        P(("dp", "expert"), None),
    )
    return jax.shard_map(
        fast_device if fast else general_device,
        mesh=mesh,
        in_specs=placed,
        out_specs=(
            P(("dp", "expert"), "tensor"),
            P(("dp", "expert"), None),
            P(),
            P(None, "tensor"),
            P(None, "tensor"),
            P(None, "tensor"),
            P("tensor", None),
            P(),
            P(),
            P("expert", None, "tensor"),
            P("expert", None, "tensor"),
            P("expert", "tensor", None),
        ),
        check_vma=False,
    )
```

```python
import functools
import math

import jax
import jax.numpy as jnp
from jax import lax
from jax.experimental import pallas as pl
from jax.experimental.pallas import tpu as pltpu
from jax.sharding import PartitionSpec as P

HEAD_SIZE = 64
TOPK = 8
PIC = 256


epsilon = 1e-06
rope_base = 10000.0
masked_score = -1e30


def rope_tables(positions):
    steps = jnp.arange(HEAD_SIZE // 2, dtype=jnp.float32)
    inverse = jnp.exp(steps * (-2.0 * math.log(rope_base) / HEAD_SIZE))
    angle = positions.astype(jnp.float32)[:, None] * inverse[None, :]
    return (jnp.cos(angle), jnp.sin(angle))


def apply_rotary(values, cosine_table, sine_table):
    half = values.shape[-1] // 2
    first = values[..., :half]
    second = values[..., half:]
    cosine_table = cosine_table[:, None, :]
    sine_table = sine_table[:, None, :]
    return jnp.concatenate(
        [first * cosine_table - second * sine_table, second * cosine_table + first * sine_table],
        axis=-1,
    )


def unrotate(values, cosine_table, sine_table):
    half = values.shape[-1] // 2
    first = values[..., :half]
    second = values[..., half:]
    cosine_table = cosine_table[:, None, :]
    sine_table = sine_table[:, None, :]
    return jnp.concatenate(
        [first * cosine_table + second * sine_table, second * cosine_table - first * sine_table],
        axis=-1,
    )


def piece_ids(positions, offsets):
    span = 2 * PIC
    window = positions // span
    within = positions - window * span
    count = offsets.shape[0]
    match = window[:, None] == jnp.arange(count, dtype=jnp.int32)[None, :]
    start = jnp.sum(jnp.where(match, offsets[None, :], 0), axis=1)
    inside = (window < count) & (within >= start) & (within < start + PIC)
    return jnp.where(inside, window, -1)


def matmul(left, right):
    return jnp.dot(left, right, preferred_element_type=jnp.float32)


def matmul_nt(left, right):
    return lax.dot_general(
        left, right, (((1,), (1,)), ((), ())), preferred_element_type=jnp.float32
    )


def matmul_tn(left, right):
    return lax.dot_general(
        left, right, (((0,), (0,)), ((), ())), preferred_element_type=jnp.float32
    )


def norm_scale(values):
    return lax.rsqrt(jnp.mean(values * values, axis=-1, keepdims=True) + epsilon)


def norm_back(grad, unit, scale, gain):
    weighted = grad * gain
    return scale * (weighted - unit * jnp.mean(weighted * unit, axis=-1, keepdims=True))


def general_device(
    block_input,
    first_gain,
    w_query,
    key_weight,
    value_weight,
    w_output,
    second_gain,
    w_router,
    w_gate,
    w_up,
    w_down,
    expert_ids,
    slot_index,
    piece_start_offsets,
    upstream,
):
    rows_here = block_input.shape[0]
    width = block_input.shape[1]
    groups = lax.axis_size("expert")
    length = rows_here * groups
    local_heads = w_query.shape[1] // HEAD_SIZE
    local_kv = key_weight.shape[1] // HEAD_SIZE
    sharing = local_heads // local_kv
    head_rows = sharing * rows_here
    experts_all = w_router.shape[1]
    capacity = TOPK * rows_here // experts_all
    slots_all = experts_all * capacity
    score_scale = HEAD_SIZE ** (-0.5)
    positions = lax.axis_index("expert") * rows_here + jnp.arange(rows_here, dtype=jnp.int32)
    cosine_table, sine_table = rope_tables(positions)
    inputs = block_input.astype(jnp.float32)
    first_scale = norm_scale(inputs)
    first_unit = inputs * first_scale
    first_normed = (first_unit * first_gain).astype(jnp.bfloat16)
    query_rot = apply_rotary(
        matmul(first_normed, w_query).reshape(rows_here, local_heads, HEAD_SIZE),
        cosine_table,
        sine_table,
    ).astype(jnp.bfloat16)
    key_rot = (
        apply_rotary(
            matmul(first_normed, key_weight).reshape(rows_here, local_kv, HEAD_SIZE),
            cosine_table,
            sine_table,
        )
        .astype(jnp.bfloat16)
        .reshape(rows_here, local_kv * HEAD_SIZE)
    )
    value_low = matmul(first_normed, value_weight).astype(jnp.bfloat16)
    keys_all, values_all = (
        lax.all_gather(key_rot, "expert", axis=0, tiled=True),
        lax.all_gather(value_low, "expert", axis=0, tiled=True),
    )
    block = min(512, length)
    blocks = length // block

    def by_block(array):
        return array.reshape(blocks, block, local_kv, HEAD_SIZE).transpose(0, 2, 1, 3)

    def by_rows(stacked):
        return stacked.transpose(0, 2, 1, 3).reshape(length, local_kv * HEAD_SIZE)

    def head_major(array):
        return (
            array.reshape(rows_here, local_kv, sharing, HEAD_SIZE)
            .transpose(1, 2, 0, 3)
            .reshape(local_kv, head_rows, HEAD_SIZE)
        )

    def row_major(array):
        return (
            array.reshape(local_kv, sharing, rows_here, HEAD_SIZE)
            .transpose(2, 0, 1, 3)
            .reshape(rows_here, local_heads * HEAD_SIZE)
        )

    key_blocks = by_block(keys_all)
    value_blocks = by_block(values_all)
    block_starts = jnp.arange(blocks, dtype=jnp.int32) * block
    query_heads = head_major(query_rot.reshape(rows_here, local_heads * HEAD_SIZE))
    offsets = piece_start_offsets[0]
    key_pieces = piece_ids(jnp.arange(length, dtype=jnp.int32), offsets)
    query_pieces = jnp.tile(piece_ids(positions, offsets), sharing)
    query_places = jnp.tile(positions, sharing)

    def block_scores(key_block, start):
        places = start + jnp.arange(block, dtype=jnp.int32)
        pieces = lax.dynamic_slice_in_dim(key_pieces, start, block)
        causal = places[None, :] <= query_places[:, None]
        same = (pieces[None, :] == query_pieces[:, None]) & (query_pieces[:, None] >= 0)
        scores = (
            jnp.einsum("hqd,hkd->hqk", query_heads, key_block, preferred_element_type=jnp.float32)
            * score_scale
        )
        return (scores, (causal | same)[None])

    def max_step(carry, operands):
        running_max, running_sum = carry
        key_block, start = operands
        scores, allowed = block_scores(key_block, start)
        scores = jnp.where(allowed, scores, masked_score)
        new_max = jnp.maximum(running_max, jnp.max(scores, axis=-1))
        weights = jnp.where(allowed, jnp.exp(scores - new_max[..., None]), 0.0)
        new_sum = running_sum * jnp.exp(running_max - new_max) + jnp.sum(weights, axis=-1)
        return ((new_max, new_sum), None)

    start_max = jnp.full((local_kv, head_rows), masked_score, jnp.float32)
    start_sum = jnp.zeros((local_kv, head_rows), jnp.float32)
    (row_max, row_sum), _ = lax.scan(max_step, (start_max, start_sum), (key_blocks, block_starts))
    log_total = row_max + jnp.log(row_sum)

    def block_probs(key_block, start):
        scores, allowed = block_scores(key_block, start)
        return jnp.where(allowed, jnp.exp(scores - log_total[..., None]), 0.0)

    def value_step(total, operands):
        key_block, value_block, start = operands
        probs = block_probs(key_block, start).astype(jnp.bfloat16)
        return (
            total
            + jnp.einsum("hqk,hkd->hqd", probs, value_block, preferred_element_type=jnp.float32),
            None,
        )

    mixed_output, _ = lax.scan(
        value_step,
        jnp.zeros((local_kv, head_rows, HEAD_SIZE), jnp.float32),
        (key_blocks, value_blocks, block_starts),
    )
    attended = row_major(mixed_output).astype(jnp.bfloat16)
    attention = lax.psum(matmul(attended, w_output), "tensor")
    residual = inputs + attention
    second_scale = norm_scale(residual)
    second_unit = residual * second_scale
    second_normed = (second_unit * second_gain).astype(jnp.bfloat16)
    logits = matmul(second_normed, w_router)
    chosen = jnp.take_along_axis(logits, expert_ids, axis=1)
    gates = jax.nn.softmax(chosen, axis=-1)
    row_ids = jnp.arange(rows_here, dtype=jnp.int32)
    flat = jnp.where(slot_index >= 0, expert_ids * capacity + slot_index, slots_all)
    selector = (
        jnp.zeros((slots_all, rows_here), jnp.bfloat16)
        .at[flat.reshape(-1), jnp.repeat(row_ids, TOPK)]
        .set(1.0, mode="drop")
    )
    dispatched = (
        matmul(selector, second_normed).astype(jnp.bfloat16).reshape(experts_all, capacity, width)
    )
    expert_rows = lax.all_to_all(dispatched, "expert", split_axis=0, concat_axis=1, tiled=True)
    gate_in = jnp.einsum("ebd,edf->ebf", expert_rows, w_gate, preferred_element_type=jnp.float32)
    up_in = jnp.einsum("ebd,edf->ebf", expert_rows, w_up, preferred_element_type=jnp.float32)
    sigmoid_gate = jax.nn.sigmoid(gate_in)
    silu_gate = gate_in * sigmoid_gate
    hidden = (silu_gate * up_in).astype(jnp.bfloat16)
    partial_out = jnp.einsum("ebf,efd->ebd", hidden, w_down, preferred_element_type=jnp.float32)
    expert_part = lax.psum_scatter(
        partial_out.astype(jnp.bfloat16), "tensor", scatter_dimension=2, tiled=True
    )
    returned = lax.all_to_all(expert_part, "expert", split_axis=1, concat_axis=0, tiled=True)
    quarter = returned.shape[2]
    padded_out = jnp.concatenate(
        [returned.reshape(slots_all, quarter), jnp.zeros((1, quarter), jnp.bfloat16)], axis=0
    )
    feature_start = lax.axis_index("tensor") * quarter
    grad_full = upstream.astype(jnp.float32)
    grad_part = lax.dynamic_slice_in_dim(grad_full, feature_start, quarter, 1)
    mixture = jnp.zeros((rows_here, quarter), jnp.float32)
    gate_terms = []
    for pick in range(TOPK):
        picked = padded_out[flat[:, pick]].astype(jnp.float32)
        mixture = mixture + gates[:, pick : pick + 1] * picked
        gate_terms.append(jnp.sum(grad_part * picked, axis=1))
    gate_part = jnp.stack(gate_terms, axis=1)
    block_output = (lax.dynamic_slice_in_dim(residual, feature_start, quarter, 1) + mixture).astype(
        jnp.bfloat16
    )
    slot_gates = (
        jnp.zeros((slots_all + 1,), jnp.float32)
        .at[flat.reshape(-1)]
        .set(gates.reshape(-1))[:slots_all]
    )
    grad_slots = (
        (matmul(selector, upstream) * slot_gates[:, None])
        .astype(jnp.bfloat16)
        .reshape(experts_all, capacity, width)
    )
    grad_rows_in = lax.all_to_all(grad_slots, "expert", split_axis=0, concat_axis=1, tiled=True)
    hidden_grad = jnp.einsum(
        "ebd,efd->ebf", grad_rows_in, w_down, preferred_element_type=jnp.float32
    )
    grad_down = jnp.einsum("ebf,ebd->efd", hidden, grad_rows_in, preferred_element_type=jnp.float32)
    gate_in_grad = (
        hidden_grad * up_in * (sigmoid_gate * (1.0 + gate_in * (1.0 - sigmoid_gate)))
    ).astype(jnp.bfloat16)
    up_in_grad = (hidden_grad * silu_gate).astype(jnp.bfloat16)
    grad_gate = jnp.einsum(
        "ebd,ebf->edf", expert_rows, gate_in_grad, preferred_element_type=jnp.float32
    )
    grad_up = jnp.einsum(
        "ebd,ebf->edf", expert_rows, up_in_grad, preferred_element_type=jnp.float32
    )
    rows_part = jnp.einsum("ebf,edf->ebd", gate_in_grad, w_gate, preferred_element_type=jnp.float32)
    rows_part = rows_part + jnp.einsum(
        "ebf,edf->ebd", up_in_grad, w_up, preferred_element_type=jnp.float32
    )
    rows_back = lax.all_to_all(
        rows_part.astype(jnp.bfloat16), "expert", split_axis=1, concat_axis=0, tiled=True
    ).astype(rows_part.dtype)
    padded_back = jnp.concatenate(
        [rows_back.reshape(slots_all, width), jnp.zeros((1, width), jnp.float32)], axis=0
    )
    second_part = jnp.zeros((rows_here, width), jnp.float32)
    for pick in range(TOPK):
        second_part = second_part + padded_back[flat[:, pick]]
    second_sum, gate_grads = (
        lax.psum(second_part.astype(jnp.bfloat16), "tensor").astype(jnp.float32),
        lax.psum(gate_part.astype(jnp.bfloat16), "tensor").astype(jnp.float32),
    )
    chosen_grad = gates * (gate_grads - jnp.sum(gates * gate_grads, axis=1, keepdims=True))
    expert_axis = jnp.arange(experts_all, dtype=jnp.int32)
    logit_grad = jnp.zeros((rows_here, experts_all), jnp.float32)
    for pick in range(TOPK):
        logit_grad = logit_grad + jnp.where(
            expert_ids[:, pick : pick + 1] == expert_axis[None, :],
            chosen_grad[:, pick : pick + 1],
            0.0,
        )
    logit_low = logit_grad.astype(jnp.bfloat16)
    grad_router = matmul_tn(second_normed, logit_low)
    second_grad = second_sum + matmul_nt(logit_low, w_router)
    grad_second = jnp.sum(second_grad * second_unit, axis=0)
    residual_grad = grad_full + norm_back(second_grad, second_unit, second_scale, second_gain)
    residual_low = residual_grad.astype(jnp.bfloat16)
    grad_output = matmul_tn(attended, residual_low)
    attended_grad = head_major(matmul_nt(residual_low, w_output).astype(jnp.bfloat16))

    def delta_step(total, operands):
        key_block, value_block, start = operands
        probs = block_probs(key_block, start)
        prob_grad = jnp.einsum(
            "hqd,hkd->hqk", attended_grad, value_block, preferred_element_type=jnp.float32
        )
        return (total + jnp.sum(probs * prob_grad, axis=-1), None)

    delta, _ = lax.scan(
        delta_step,
        jnp.zeros((local_kv, head_rows), jnp.float32),
        (key_blocks, value_blocks, block_starts),
    )

    def grad_step(query_total, operands):
        key_block, value_block, start = operands
        probs = block_probs(key_block, start)
        prob_grad = jnp.einsum(
            "hqd,hkd->hqk", attended_grad, value_block, preferred_element_type=jnp.float32
        )
        score_grad = (probs * (prob_grad - delta[..., None])).astype(jnp.bfloat16)
        query_total = (
            query_total
            + jnp.einsum("hqk,hkd->hqd", score_grad, key_block, preferred_element_type=jnp.float32)
            * score_scale
        )
        key_grad = (
            jnp.einsum("hqk,hqd->hkd", score_grad, query_heads, preferred_element_type=jnp.float32)
            * score_scale
        )
        value_grad = jnp.einsum(
            "hqk,hqd->hkd",
            probs.astype(jnp.bfloat16),
            attended_grad,
            preferred_element_type=jnp.float32,
        )
        return (query_total, (key_grad, value_grad))

    query_total, (key_stack, value_stack) = lax.scan(
        grad_step,
        jnp.zeros((local_kv, head_rows, HEAD_SIZE), jnp.float32),
        (key_blocks, value_blocks, block_starts),
    )
    key_back, value_back = (
        lax.psum_scatter(
            by_rows(key_stack).astype(jnp.bfloat16), "expert", scatter_dimension=0, tiled=True
        ).astype(jnp.float32),
        lax.psum_scatter(
            by_rows(value_stack).astype(jnp.bfloat16), "expert", scatter_dimension=0, tiled=True
        ).astype(jnp.float32),
    )
    query_grad = (
        unrotate(
            row_major(query_total).reshape(rows_here, local_heads, HEAD_SIZE),
            cosine_table,
            sine_table,
        )
        .astype(jnp.bfloat16)
        .reshape(rows_here, local_heads * HEAD_SIZE)
    )
    key_grad = (
        unrotate(key_back.reshape(rows_here, local_kv, HEAD_SIZE), cosine_table, sine_table)
        .astype(jnp.bfloat16)
        .reshape(rows_here, local_kv * HEAD_SIZE)
    )
    value_grad = value_back.astype(jnp.bfloat16)
    grad_query = matmul_tn(first_normed, query_grad)
    grad_key = matmul_tn(first_normed, key_grad)
    grad_value = matmul_tn(first_normed, value_grad)
    first_part = (
        matmul_nt(query_grad, w_query)
        + matmul_nt(key_grad, key_weight)
        + matmul_nt(value_grad, value_weight)
    )
    first_grad = lax.psum(first_part.astype(jnp.bfloat16), "tensor").astype(jnp.float32)
    grad_first = jnp.sum(first_grad * first_unit, axis=0)
    grad_input = (
        residual_grad + norm_back(first_grad, first_unit, first_scale, first_gain)
    ).astype(jnp.bfloat16)
    dense = lax.psum(
        (grad_query, grad_key, grad_value, grad_output, grad_router, grad_first, grad_second),
        ("dp", "expert"),
    )
    expert_sums = (
        lax.psum(grad_gate.astype(jnp.bfloat16), "dp").astype(jnp.float32),
        lax.psum(grad_up.astype(jnp.bfloat16), "dp").astype(jnp.float32),
        lax.psum(grad_down.astype(jnp.bfloat16), "dp").astype(jnp.float32),
    )
    return (
        block_output,
        grad_input,
        dense[5],
        dense[0],
        dense[1],
        dense[2],
        dense[3],
        dense[6],
        dense[4],
        expert_sums[0],
        expert_sums[1],
        expert_sums[2],
    )


BF = jnp.bfloat16
F32 = jnp.float32
MIB = 1 << 20


def vmem_spec():
    return pl.BlockSpec(memory_space=pltpu.VMEM)


def smem_spec():
    return pl.BlockSpec(memory_space=pltpu.SMEM)


def allowed_pairs(offsets_ref, rows, start, count):
    side = lax.axis_index("expert")
    here = start + lax.broadcasted_iota(jnp.int32, (count, 1), 0)
    keys = lax.broadcasted_iota(jnp.int32, (1, 2 * rows), 1)
    query_place = side * rows + here
    key_place = jnp.where(keys < rows, side * rows + keys, (1 - side) * rows + keys - rows)
    span = 2 * PIC

    def piece(places):
        window = places // span
        within = places - window * span
        start = jnp.where(window == 0, offsets_ref[0, 0], offsets_ref[0, 1])
        inside = (within >= start) & (within < start + PIC)
        return jnp.where(inside, window, -1)

    query_piece = piece(query_place)
    key_piece = piece(key_place)
    return (key_place <= query_place) | ((key_piece == query_piece) & (query_piece >= 0))


def turn(values, first):
    wide = values.shape[1]
    half = HEAD_SIZE // 2
    return jnp.where(
        first, -pltpu.roll(values, wide - half, 1), pltpu.roll(values, half, 1)
    )


MESH = pl.DeviceIdType.MESH
PART = 32
LAG = 3
LINK_COST = pl.CostEstimate(flops=4 * 10**10, bytes_accessed=10**7, transcendentals=0)


def meet(partners):
    barrier = pltpu.get_barrier_semaphore()
    count = 0
    for here, device in partners:
        here = jnp.asarray(here)

        @pl.when(here)
        def _():
            pl.semaphore_signal(barrier, inc=1, device_id=device, device_id_type=MESH)

        count = count + here.astype(jnp.int32)
    pl.semaphore_wait(barrier, count)


def line_partners():
    place = lax.axis_index("tensor")
    last = lax.axis_size("tensor") - 1
    return [(place > 0, {"tensor": place - 1}), (place < last, {"tensor": place + 1})]


class Line:
    def __init__(self, parts, term, from_left, from_right, to_right, to_left, sems, lag=LAG):
        self.lag = lag
        self.place = lax.axis_index("tensor")
        self.last = lax.axis_size("tensor") - 1
        self.parts = parts
        self.term = term
        self.from_left, self.from_right = from_left, from_right
        self.to_right, self.to_left = to_right, to_left
        self.sems = sems

    def copy(self, way, at):
        near = jnp.where(self.place < self.last, self.place + 1, self.place - 1)
        far = jnp.where(self.place > 0, self.place - 1, self.place + 1)
        source, target, device = (
            (self.to_right, self.from_left, near) if way == 0 else (self.to_left, self.from_right, far)
        )
        return pltpu.make_async_remote_copy(
            src_ref=source.at[at],
            dst_ref=target.at[at],
            send_sem=self.sems.at[2 * way, at],
            recv_sem=self.sems.at[2 * way + 1, at],
            device_id={"tensor": device},
            device_id_type=MESH,
        )

    def clear(self):
        @pl.when(self.place == 0)
        def _():
            self.from_left[...] = jnp.zeros(self.from_left.shape, self.from_left.dtype)

        @pl.when(self.place == self.last)
        def _():
            self.from_right[...] = jnp.zeros(self.from_right.shape, self.from_right.dtype)

    def step(self, at):
        for way in range(2):
            part = at - self.lag * (self.place if way == 0 else self.last - self.place)
            has_source = self.place > 0 if way == 0 else self.place < self.last
            has_target = self.place < self.last if way == 0 else self.place > 0
            arrived = self.from_left if way == 0 else self.from_right
            leaving = self.to_right if way == 0 else self.to_left
            valid = (part >= 0) & (part < self.parts)

            @pl.when(valid & has_source)
            def _():
                self.copy(way, part).wait_recv()

            @pl.when(valid & has_target)
            def _():
                leaving[part] = (self.term(part) + arrived[part].astype(F32)).astype(BF)
                self.copy(way, part).start()

    def total(self, part):
        return self.term(part) + self.from_left[part].astype(F32) + self.from_right[part].astype(F32)

    def drain(self):
        def wait(part, carry):
            @pl.when(self.place < self.last)
            def _():
                self.copy(0, part).wait_send()

            @pl.when(self.place > 0)
            def _():
                self.copy(1, part).wait_send()

            return carry

        lax.fori_loop(0, self.parts, wait, 0)


def line_scratch(parts, width, part=PART):
    return [pltpu.VMEM((parts, part, width), BF)] * 4 + [pltpu.SemaphoreType.DMA((4, parts))]


def peer_copy(source, target, sems, at):
    return pltpu.make_async_remote_copy(
        src_ref=source,
        dst_ref=target,
        send_sem=sems.at[0, at],
        recv_sem=sems.at[1, at],
        device_id={"expert": 1 - lax.axis_index("expert")},
        device_id_type=MESH,
    )


def scale_of(values):
    return lax.rsqrt(jnp.mean(values * values, axis=-1, keepdims=True) + epsilon)


def plain_copy(source, target, sems, at, device):
    return pltpu.make_async_remote_copy(
        src_ref=source, dst_ref=target, send_sem=sems.at[0, at], recv_sem=sems.at[1, at],
        device_id=device, device_id_type=MESH,
    )


def beside():
    return {"dp": lax.rem(lax.axis_index("dp") + 2, 4)}


def other_core():
    place = lax.axis_index("dp")
    return {"dp": place + 1 - 2 * lax.rem(place, 2)}


EARLY = 64
BAND = 256


def front_kernel(
    offsets_ref, x_ref, gain1_ref, gain2_ref, wq_ref, wk_ref, wv_ref, wo_ref, cos_ref, sin_ref, ids_ref, slots_ref, up_hbm,
    n1_ref, q_ref, k_ref, v_ref, att_ref, lse_ref, res_ref, n_ref, marks_ref, far_marks, up_peer, far_up,
    from_left, from_right, to_right, to_left, sems, peer_sems, far_sems, terms,
):
    parts = x_ref.shape[0]
    rows, width = n1_ref.shape
    side = lax.axis_index("expert")
    peer = {"expert": 1 - side}
    line = Line(parts, lambda at: terms[at], from_left, from_right, to_right, to_left, sems)
    meet(line_partners() + [(True, peer), (True, beside())])
    early, late = pl.ds(0, EARLY), pl.ds(EARLY, rows - EARLY)
    up_early = plain_copy(up_hbm.at[early, :], up_peer.at[early, :], far_sems, 0, peer)
    up_late = plain_copy(up_hbm.at[late, :], up_peer.at[late, :], far_sems, 1, peer)
    up_cross = plain_copy(up_hbm, far_up, far_sems, 2, beside())
    key_copy = plain_copy(k_ref.at[0], k_ref.at[1], far_sems, 3, peer)
    value_copy = plain_copy(v_ref.at[0], v_ref.at[1], far_sems, 4, peer)
    marks_copy = plain_copy(marks_ref.at[0], marks_ref.at[1], far_sems, 5, peer)
    marks_cross = plain_copy(marks_ref, far_marks, far_sems, 6, beside())
    up_early.start()
    up_cross.start()
    line.clear()

    values = x_ref[...].reshape(rows, width).astype(F32)
    normed = (values * scale_of(values) * gain1_ref[...]).astype(BF)
    n1_ref[...] = normed
    queries, kv = q_ref.shape[1], k_ref.shape[2]

    def rotate(array):
        wide = array.shape[1]
        lane = lax.broadcasted_iota(jnp.int32, (1, wide), 1)
        first = lane % HEAD_SIZE < HEAD_SIZE // 2
        cosines = jnp.concatenate([cos_ref[...]] * (wide // 128), axis=1)
        sines = jnp.concatenate([sin_ref[...]] * (wide // 128), axis=1)
        return (array * cosines + turn(array, first) * sines).astype(BF)

    k_ref[0] = rotate(matmul(normed, wk_ref[...]))
    key_copy.start()
    v_ref[0] = matmul(normed, wv_ref[...]).astype(BF)
    value_copy.start()
    experts_all = marks_ref.shape[2] // 2
    names = lax.broadcasted_iota(jnp.int32, (experts_all, 1), 0)
    chosen = jnp.zeros((experts_all, rows), F32)
    kept = jnp.zeros((experts_all, rows), F32)
    for pick in range(ids_ref.shape[0]):
        hit = jnp.where(ids_ref[pick : pick + 1, :] == names, 1.0, 0.0)
        chosen = chosen + hit
        kept = kept + jnp.where(slots_ref[pick : pick + 1, :] >= 0, hit, 0.0)
    marks_ref[0] = jnp.concatenate([chosen, kept], axis=0).T.astype(BF)
    marks_copy.start()
    up_late.start()
    q_ref[...] = rotate(matmul(normed, wq_ref[...]))
    key_copy.wait_recv()
    value_copy.wait_recv()
    sharing = queries // kv

    def attend(at):
        start = pl.multiple_of(at * BAND, BAND)
        band = pl.ds(start, BAND)
        allowed = allowed_pairs(offsets_ref, rows, start, BAND)
        pieces = []
        for head in range(queries // HEAD_SIZE):
            kv_at = head // sharing * HEAD_SIZE
            query = q_ref[band, head * HEAD_SIZE : (head + 1) * HEAD_SIZE]
            key = k_ref[:, :, kv_at : kv_at + HEAD_SIZE].reshape(2 * rows, HEAD_SIZE)
            value = v_ref[:, :, kv_at : kv_at + HEAD_SIZE].reshape(2 * rows, HEAD_SIZE)
            scores = jnp.where(allowed, matmul_nt(query, key) * (HEAD_SIZE**-0.5), masked_score)
            peak = jnp.max(scores, axis=1, keepdims=True)
            weights = jnp.exp(scores - peak)
            total = jnp.sum(weights, axis=1, keepdims=True)
            pieces.append(matmul((weights * (1.0 / total)).astype(BF), value))
            lse_ref[band, head : head + 1] = peak + jnp.log(total)
        attended = jnp.concatenate(pieces, axis=1).astype(BF)
        att_ref[band, :] = attended
        count = BAND // PART
        terms[pl.ds(at * count, count)] = matmul(attended, wo_ref[...]).reshape(count, PART, width)

    def body(at, carry):
        @pl.when(at < rows // BAND)
        def _():
            attend(at)

        @pl.when(at == 3)
        def _():
            marks_copy.wait_recv()
            marks_cross.start()

        line.step(at - 1)
        part = at - 1 - LAG * line.last

        @pl.when(part >= 0)
        def _():
            residual = x_ref[part].astype(F32) + line.total(part)
            res_ref[part] = residual
            unit = residual * scale_of(residual)
            n_ref[0, part] = (unit * gain2_ref[...]).astype(BF)
            peer_copy(n_ref.at[0, part], n_ref.at[1, part], peer_sems, part).start()

        return carry

    lax.fori_loop(0, 1 + parts + LAG * line.last, body, 0)
    line.drain()
    for copy in (key_copy, value_copy, marks_copy):
        copy.wait_send()
    for copy in (up_early, up_late, up_cross, marks_cross):
        copy.wait()

    def wait(part, carry):
        peer_copy(n_ref.at[0, part], n_ref.at[1, part], peer_sems, part).wait()
        return carry

    lax.fori_loop(0, parts, wait, 0)


def front(
    offsets, block_input, first_gain, second_gain, w_query, key_weight, value_weight, w_output, cosines, sines,
    expert_ids, slot_index, upstream, experts_all,
):
    rows, width = block_input.shape
    parts = rows // PART
    queries, kv = w_query.shape[1], key_weight.shape[1]
    any_spec = pl.BlockSpec(memory_space=pl.ANY)
    low = lambda *shape: jax.ShapeDtypeStruct(shape, BF)
    return pl.pallas_call(
        front_kernel,
        out_shape=(
            low(rows, width),
            low(rows, queries),
            low(2, rows, kv),
            low(2, rows, kv),
            low(rows, queries),
            jax.ShapeDtypeStruct((rows, 128), F32),
            jax.ShapeDtypeStruct((parts, PART, width), F32),
            low(2, parts, PART, width),
            low(2, rows, 2 * experts_all),
            low(2, rows, 2 * experts_all),
            low(rows, width),
            low(rows, width),
        ),
        in_specs=[smem_spec()] + [vmem_spec()] * 11 + [any_spec],
        out_specs=(vmem_spec(),) * 9 + (any_spec,) * 3,
        scratch_shapes=line_scratch(parts, width)
        + [
            pltpu.SemaphoreType.DMA((2, parts)),
            pltpu.SemaphoreType.DMA((2, 7)),
            pltpu.VMEM((parts, PART, width), F32),
        ],
        compiler_params=pltpu.CompilerParams(
            collective_id=0, has_side_effects=True, vmem_limit_bytes=60 * MIB
        ),
        cost_estimate=LINK_COST,
        name="front",
    )(
        offsets, block_input.reshape(parts, PART, width), first_gain[None], second_gain[None], w_query, key_weight,
        value_weight, w_output, cosines, sines, expert_ids, slot_index, upstream,
    )


UNIT = 512
BIG_PART = 64
BIG_LAG = 2
SUB = 256


def residual_grad_kernel(
    route_ref, gain_ref, wr_ref, back_hbm, mix_hbm, res_hbm, up_hbm,
    far_n, far_on, far_g0, far_g1, far_og0, far_og1, far_m, far_om,
    wg_hbm, wu_hbm, wd_hbm, pg_hbm, pu_hbm, pd_hbm,
    grad_ref, low_ref, second_ref, route_out, mixed_ref, sg_hbm, su_hbm, sd_hbm, og_hbm, ou_hbm, od_hbm,
    from_left, from_right, to_right, to_left, sems, peer_sems, arrived, terms,
    tokens_n, tokens_g, turned, kept_gates, gates_w, ups_w, downs_w, pair_g, pair_u, pair_d, ght, dgs, dus,
    row_sems, weight_sems, pair_sems, out_sems, mix_arrived, mix_sems, marks_ref, share_sems,
    back_ref, mix_ref, res_ref, up_ref, load_sems,
):
    parts = back_ref.shape[0]
    core = lax.rem(lax.axis_index("dp"), 2)
    side = lax.axis_index("expert")
    groups, group, width, hid = pair_g.shape
    experts_all = wr_ref.shape[0]
    line = Line(parts + 1, lambda at: terms[at], from_left, from_right, to_right, to_left, sems, BIG_LAG)
    loads = [
        pltpu.make_async_copy(source, target, load_sems.at[at])
        for at, (source, target) in enumerate(
            ((back_hbm.at[0], back_ref), (res_hbm, res_ref), (up_hbm, up_ref), (mix_hbm.at[0], mix_ref))
        )
    ]
    for copy in loads:
        copy.start()
    line.clear()
    meet(line_partners() + [(True, {"expert": 1 - side}), (True, other_core())])

    def send(part, carry):
        peer_copy(back_hbm.at[1, part], arrived.at[part], peer_sems, part).start()
        return carry

    lax.fori_loop(0, parts, send, 0)

    def send_mix(part, carry):
        peer_copy(mix_hbm.at[1, part], mix_arrived.at[part], mix_sems, part).start()
        return carry

    lax.fori_loop(0, parts, send_mix, 0)
    half = tokens_n.shape[0] // 2
    quarter = half // 2
    row_copies = []
    for place, (rows, first, second, marks) in enumerate(((far_n, far_g0, far_g1, far_m), (far_on, far_og0, far_og1, far_om))):
        at = place * half
        row_copies += [
            pltpu.make_async_copy(rows, tokens_n.at[pl.ds(at, half), :], row_sems.at[0, place]),
            pltpu.make_async_copy(first, tokens_g.at[pl.ds(at, quarter), :], row_sems.at[1, place]),
            pltpu.make_async_copy(second, tokens_g.at[pl.ds(at + quarter, quarter), :], row_sems.at[2, place]),
            pltpu.make_async_copy(marks, marks_ref.at[pl.ds(at, half), :], row_sems.at[3, place]),
        ]
    weight_copies, pair_copies, out_copies = [], [], []
    for at in range(groups):
        first = core * (groups * group) + at * group
        weight_copies.append(
            [
                pltpu.make_async_copy(
                    source.at[first + expert],
                    target.at[at, :, pl.ds(expert * hid, hid)],
                    weight_sems.at[at, kind, expert],
                )
                for expert in range(group)
                for kind, (source, target) in enumerate(((wg_hbm, gates_w), (wu_hbm, ups_w)))
            ]
            + [pltpu.make_async_copy(wd_hbm.at[pl.ds(first, group)], downs_w.at[at], weight_sems.at[at, 2, 0])]
        )
        sources = (pg_hbm, pu_hbm, pd_hbm)
        held = (pair_g, pair_u, pair_d)
        targets = (sg_hbm, su_hbm, sd_hbm)
        others = (og_hbm, ou_hbm, od_hbm)
        pair_copies.append(
            [
                pltpu.make_async_copy(sources[kind].at[pl.ds(at * group, group)], held[kind].at[at], pair_sems.at[at, kind])
                for kind in range(3)
            ]
        )
        out_copies.append(
            [
                pltpu.make_async_copy(held[kind].at[at], targets[kind].at[pl.ds(at * group, group)], out_sems.at[at, kind])
                for kind in range(3)
            ]
            + [
                plain_copy(
                    held[kind].at[at], others[kind].at[pl.ds(at * group, group)], share_sems.at[at], kind, other_core()
                )
                for kind in range(3)
            ]
        )
    for copy in row_copies[:4] + weight_copies[0] + row_copies[4:] + pair_copies[0] + weight_copies[1] + pair_copies[1]:
        copy.start()
    pad = jnp.zeros((BIG_PART - route_ref.shape[0], route_ref.shape[1]), F32)
    terms[parts] = jnp.concatenate([route_ref[...], pad], axis=0)
    loads[0].wait()
    second_ref[...] = jnp.zeros(second_ref.shape, F32)
    chunks = 2 * half // UNIT
    units = chunks + 3

    def compute(at):
        for where in range(groups):
            unit = at - where * units

            @pl.when(unit == 0)
            def _():
                for copy in weight_copies[where]:
                    copy.wait()

            if where == 0:

                @pl.when(unit == 0)
                def _():
                    for copy in row_copies[:4]:
                        copy.wait()

                @pl.when(unit == half // UNIT)
                def _():
                    for copy in row_copies[4:]:
                        copy.wait()

            @pl.when(unit == chunks)
            def _():
                for copy in pair_copies[where]:
                    copy.wait()

        where = at // units
        unit = at - where * units

        @pl.when(unit < chunks)
        def _():
            down = downs_w[where].reshape(group * hid, width)
            column = side * (experts_all // 2) + (core * groups + where) * group
            for sub in range(UNIT // SUB):
                rows = pl.ds(pl.multiple_of(unit * UNIT + sub * SUB, SUB), SUB)

                @pl.when(where == 0)
                def _():
                    token = tokens_n[rows, :]
                    kept_gates[rows, :] = route_gates(token, marks_ref[rows, :], wr_ref[...])[1]
                    turned[:, rows] = token.T

            for sub in range(UNIT // SUB):
                rows = pl.ds(pl.multiple_of(unit * UNIT + sub * SUB, SUB), SUB)
                pulled = matmul_nt(tokens_g[rows, :], down)
                weight = spread_gates(kept_gates[rows, :], column, group, hid)
                _, gated, gate_grad, up_grad = hidden_terms(
                    tokens_n[rows, :], pulled, weight, gates_w[where], ups_w[where]
                )
                ght[:, rows] = gated.T
                dgs[rows, :] = gate_grad
                dus[rows, :] = up_grad

        @pl.when((unit >= chunks) & (unit < chunks + 2))
        def _():
            rows = pl.ds(pl.multiple_of((unit - chunks) * (width // 2), width // 2), width // 2)
            for source, held in ((dgs, pair_g), (dus, pair_u)):
                part = matmul(turned[rows, :], source[...])
                for expert in range(group):
                    more = part[:, expert * hid : (expert + 1) * hid]
                    held[where, expert, rows, :] = (held[where, expert, rows, :].astype(F32) + more).astype(BF)

        @pl.when(unit == chunks + 2)
        def _():
            part = matmul(ght[...], tokens_g[...])
            for expert in range(group):
                more = part[expert * hid : (expert + 1) * hid, :]
                pair_d[where, expert] = (pair_d[where, expert].astype(F32) + more).astype(BF)

        for where in range(groups):

            @pl.when(at == where * units + units - 1)
            def _():
                for copy in out_copies[where]:
                    copy.start()

    def add_mix(part):
        peer_copy(mix_hbm.at[1, part], mix_arrived.at[part], mix_sems, part).wait_recv()
        mixed_ref[part] = (mix_ref[part].astype(F32) + mix_arrived[part].astype(F32)).astype(BF)

    steps = parts + 1 + BIG_LAG * line.last

    def advance(at):
        @pl.when(at < parts)
        def _():
            peer_copy(back_hbm.at[1, at], arrived.at[at], peer_sems, at).wait_recv()
            terms[at] = back_ref[at].astype(F32) + arrived[at].astype(F32)

        line.step(at)
        part = at - BIG_LAG * line.last

        @pl.when((part >= 0) & (part < parts))
        def _():
            grad = line.total(part)
            residual = res_ref[part]
            scale = scale_of(residual)
            unit = residual * scale
            second_ref[...] += jnp.sum(grad * unit, axis=0, keepdims=True)
            result = up_ref[part].astype(F32) + norm_back(grad, unit, scale, gain_ref[...])
            grad_ref[part] = result
            low_ref[part] = result.astype(BF)

        @pl.when((at >= MIX_STEP) & (at < MIX_STEP + parts))
        def _():
            add_mix(at - MIX_STEP)

    turns = max(groups * units, steps)

    def body(at, carry):
        @pl.when(at < groups * units)
        def _():
            compute(at)

        @pl.when(at == 2)
        def _():
            for copy in loads[1:]:
                copy.wait()

        advance(at)
        return carry

    lax.fori_loop(0, turns, body, 0)
    route_out[...] = line.total(parts)[: route_ref.shape[0], :]

    def rest(part, carry):
        add_mix(part)
        return carry

    lax.fori_loop(turns - MIX_STEP, parts, rest, 0)
    line.drain()

    def wait(part, carry):
        peer_copy(back_hbm.at[1, part], arrived.at[part], peer_sems, part).wait_send()
        peer_copy(mix_hbm.at[1, part], mix_arrived.at[part], mix_sems, part).wait_send()
        return carry

    lax.fori_loop(0, parts, wait, 0)
    for copies in out_copies:
        for copy in copies:
            copy.wait()


MIX_STEP = 9


def residual_gradient(back, mix, route, residual, upstream, gain, w_router, far_rows, w_gate, w_up, w_down, pairs):
    rows, width = upstream.shape
    parts = rows // BIG_PART
    half, _, hid = pairs[0].shape
    groups = half // GROUP
    tokens = 2 * far_rows[0].shape[0]
    any_spec = pl.BlockSpec(memory_space=pl.ANY)
    grad, low, second, route, mixed, *sums = pl.pallas_call(
        residual_grad_kernel,
        out_shape=[
            jax.ShapeDtypeStruct((parts, BIG_PART, width), F32),
            jax.ShapeDtypeStruct((parts, BIG_PART, width), BF),
            jax.ShapeDtypeStruct((1, width), F32),
            jax.ShapeDtypeStruct(route.shape, F32),
            jax.ShapeDtypeStruct((parts, BIG_PART, width), BF),
        ]
        + [jax.ShapeDtypeStruct(pair.shape, BF) for pair in pairs] * 2,
        in_specs=[vmem_spec()] * 3 + [any_spec] * 18,
        out_specs=[vmem_spec()] * 5 + [any_spec] * 6,
        scratch_shapes=line_scratch(parts + 1, width, BIG_PART)
        + [
            pltpu.SemaphoreType.DMA((2, parts)),
            pltpu.VMEM((parts, BIG_PART, width), BF),
            pltpu.VMEM((parts + 1, BIG_PART, width), F32),
            pltpu.VMEM((tokens, width), BF),
            pltpu.VMEM((tokens, width), BF),
            pltpu.VMEM((width, tokens), BF),
            pltpu.VMEM((tokens, w_router.shape[0]), F32),
            pltpu.VMEM((groups, width, GROUP * hid), BF),
            pltpu.VMEM((groups, width, GROUP * hid), BF),
            pltpu.VMEM((groups, GROUP, hid, width), BF),
            pltpu.VMEM((groups, GROUP, width, hid), BF),
            pltpu.VMEM((groups, GROUP, width, hid), BF),
            pltpu.VMEM((groups, GROUP, hid, width), BF),
            pltpu.VMEM((GROUP * hid, tokens), BF),
            pltpu.VMEM((tokens, GROUP * hid), BF),
            pltpu.VMEM((tokens, GROUP * hid), BF),
            pltpu.SemaphoreType.DMA((4, 2)),
            pltpu.SemaphoreType.DMA((groups, 3, GROUP)),
            pltpu.SemaphoreType.DMA((groups, 3)),
            pltpu.SemaphoreType.DMA((groups, 3)),
            pltpu.VMEM((parts, BIG_PART, width), BF),
            pltpu.SemaphoreType.DMA((2, parts)),
            pltpu.VMEM((tokens, 2 * w_router.shape[0]), BF),
            pltpu.SemaphoreType.DMA((groups, 2, 3)),
            pltpu.VMEM((parts, BIG_PART, width), BF),
            pltpu.VMEM((parts, BIG_PART, width), BF),
            pltpu.VMEM((parts, BIG_PART, width), F32),
            pltpu.VMEM((parts, BIG_PART, width), BF),
            pltpu.SemaphoreType.DMA((4,)),
        ],
        compiler_params=pltpu.CompilerParams(
            collective_id=1, has_side_effects=True, vmem_limit_bytes=60 * MIB
        ),
        cost_estimate=LINK_COST,
        name="residual_grad",
    )(
        route, gain[None], w_router, back.reshape(2, parts, BIG_PART, width), mix.reshape(2, parts, BIG_PART, width),
        residual.reshape(parts, BIG_PART, width), upstream.reshape(parts, BIG_PART, width), *far_rows, w_gate, w_up, w_down, *pairs,
    )
    return grad, low.reshape(rows, width), second, route, mixed, sums


def input_grad_kernel(
    offsets_ref, gain_ref, wq_ref, wk_ref, wv_ref, wo_ref, cos_ref, sin_ref,
    q_ref, k_ref, v_ref, lse_ref, att_ref, low_ref, route_ref, second_ref, mix_ref, x_hbm, res_grad_hbm, n_hbm, res_hbm,
    grad_ref, wide_out, wide_back, tall_out, tall_back, gains_ref, block_ref,
    from_left, from_right, to_right, to_left, sems, terms, kv_out, kv_in, kv_sems,
    wide, wide_core, wide_x, wide_y, tall, tall_core, tall_x, tall_y, rows2, rows_core, rows_x, rows_y, sum_sems,
    mix_left, mix_right, mix_to_right, mix_to_left, mix_sems, x_ref, res_grad_ref, n_ref, res_ref, load_sems,
):
    parts = x_ref.shape[0]
    rows = n_ref.shape[0]
    width = n_ref.shape[1]
    core = lax.rem(lax.axis_index("dp"), 2)
    peer = {"expert": 1 - lax.axis_index("expert")}
    kv = wk_ref.shape[1]
    queries = wq_ref.shape[1]
    line = Line(parts + 1, lambda at: terms[at], from_left, from_right, to_right, to_left, sems)
    spread = Spread(mix_ref, mix_left, mix_right, mix_to_right, mix_to_left, mix_sems)
    loads = [
        pltpu.make_async_copy(source, target, load_sems.at[at])
        for at, (source, target) in enumerate(
            ((n_hbm, n_ref), (x_hbm, x_ref), (res_grad_hbm, res_grad_ref), (res_hbm, res_ref))
        )
    ]
    for copy in loads:
        copy.start()
    line.clear()
    spread.clear()
    meet(line_partners() + [(True, peer), (True, beside()), (True, other_core())])
    spread.step(0)
    key_copy = plain_copy(kv_out.at[0, pl.ds(rows, rows), :], kv_in.at[0], kv_sems, 0, peer)
    value_copy = plain_copy(kv_out.at[1, pl.ds(rows, rows), :], kv_in.at[1], kv_sems, 1, peer)

    scale = HEAD_SIZE**-0.5
    low = low_ref[...]
    out_part = matmul(att_ref[...].T, low).astype(BF)
    att_grad = matmul_nt(low, wo_ref[...]).astype(BF)
    half_tall = tall.shape[1]
    outs = wo_ref.shape[0]
    for at in range(2):
        start, high = at * half_tall, (at + 1) * half_tall
        top = min(high, outs)
        tall[at, : top - start, :] = out_part[start:top, :]
        if high > outs:
            tall[at, outs - start :, :] = route_ref[...].astype(BF)

    tall_steps = [
        plain_copy(tall.at[1 - core], tall_core, sum_sems, 0, other_core()),
        plain_copy(tall.at[core], tall_y, sum_sems, 1, peer),
        plain_copy(tall.at[core], tall_x, sum_sems, 2, beside()),
        plain_copy(tall.at[core], tall_back, sum_sems, 3, other_core()),
    ]
    wide_steps = [
        plain_copy(wide.at[1 - core], wide_core, sum_sems, 4, other_core()),
        plain_copy(wide.at[core], wide_x, sum_sems, 5, beside()),
        plain_copy(wide.at[core], wide_y, sum_sems, 6, peer),
        plain_copy(wide.at[core], wide_back, sum_sems, 7, other_core()),
    ]
    rows_steps = [
        plain_copy(rows2, rows_core, sum_sems, 8, other_core()),
        plain_copy(rows2, rows_y, sum_sems, 9, peer),
        plain_copy(rows2, rows_x, sum_sems, 10, beside()),
    ]
    tall_steps[0].start()

    def add(held, arrived):
        held[...] = (held[...].astype(F32) + arrived[...].astype(F32)).astype(BF)

    allowed = allowed_pairs(offsets_ref, rows, 0, rows)
    sharing = queries // kv
    query_parts, key_parts, value_parts = [], [], []
    for head in range(queries // HEAD_SIZE):
        if head:
            spread.step(head)
        if head == 1:
            tall_steps[0].wait()
            add(tall.at[core], tall_core)
            tall_steps[1].start()
        if head == 3:
            tall_steps[1].wait()
            add(tall.at[core], tall_y)
            tall_steps[2].start()
        at = head * HEAD_SIZE
        kv_at = head // sharing * HEAD_SIZE
        query = q_ref[:, at : at + HEAD_SIZE]
        key = k_ref[:, kv_at : kv_at + HEAD_SIZE]
        value = v_ref[:, kv_at : kv_at + HEAD_SIZE]
        grad = att_grad[:, at : at + HEAD_SIZE]
        scores = jnp.where(allowed, matmul_nt(query, key) * scale, masked_score)
        probs = jnp.exp(scores - lse_ref[:, head : head + 1])
        prob_grad = matmul_nt(grad, value)
        delta = jnp.sum(probs * prob_grad, axis=1, keepdims=True)
        score_grad = (probs * (prob_grad - delta)).astype(BF)
        query_parts.append(matmul(score_grad, key) * scale)
        key_part = matmul_tn(score_grad, query) * scale
        value_part = matmul_tn(probs.astype(BF), grad)
        if head % sharing == 0:
            key_parts.append(key_part)
            value_parts.append(value_part)
        else:
            key_parts[-1] = key_parts[-1] + key_part
            value_parts[-1] = value_parts[-1] + value_part
    kv_out[0] = jnp.concatenate(key_parts, axis=1).astype(BF)
    key_copy.start()
    kv_out[1] = jnp.concatenate(value_parts, axis=1).astype(BF)
    value_copy.start()

    def rotate_back(array):
        wide_lanes = array.shape[1]
        lane = lax.broadcasted_iota(jnp.int32, (1, wide_lanes), 1)
        first = lane % HEAD_SIZE < HEAD_SIZE // 2
        cosines = jnp.concatenate([cos_ref[...]] * (wide_lanes // 128), axis=1)
        sines = jnp.concatenate([sin_ref[...]] * (wide_lanes // 128), axis=1)
        return (array * cosines - turn(array, first) * sines).astype(BF)

    for copy in loads:
        copy.wait()
    query_grad = rotate_back(jnp.concatenate(query_parts, axis=1))
    by_rows = (parts, rows // parts, width)
    terms[pl.ds(0, parts)] = matmul_nt(query_grad, wq_ref[...]).reshape(by_rows)
    turned = n_ref[...].T
    query_part = matmul(turned, query_grad).astype(BF)
    for at in range(2):
        wide[at, :, :queries] = query_part[at * width // 2 : (at + 1) * width // 2, :]
    key_copy.wait_recv()
    value_copy.wait_recv()
    key_grad = rotate_back(kv_out[0, :rows, :].astype(F32) + kv_in[0].astype(F32))
    value_grad = (kv_out[1, :rows, :].astype(F32) + kv_in[1].astype(F32)).astype(BF)
    more = matmul_nt(key_grad, wk_ref[...]) + matmul_nt(value_grad, wv_ref[...])
    terms[pl.ds(0, parts)] += more.reshape(by_rows)
    both_part = matmul(turned, jnp.concatenate([key_grad, value_grad], axis=1)).astype(BF)
    for at in range(2):
        wide[at, :, queries:] = both_part[at * width // 2 : (at + 1) * width // 2, :]
    wide_steps[0].start()

    def gain_part(at, total):
        values = x_ref[at].astype(F32)
        return total + jnp.sum(terms[at] * (values * scale_of(values)), axis=0, keepdims=True)

    first_sum = lax.fori_loop(0, parts, gain_part, jnp.zeros((1, width), F32))
    pad = jnp.zeros((rows2.shape[0] - 2, width), F32)
    rows2[...] = jnp.concatenate([first_sum, second_ref[...], pad], axis=0).astype(BF)
    rows_steps[0].start()

    def exchange(at):
        @pl.when(at == 0)
        def _():
            rows_steps[0].wait()
            add(rows2, rows_core)
            rows_steps[1].start()

        @pl.when(at == 1)
        def _():
            wide_steps[0].wait()
            add(wide.at[core], wide_core)

        @pl.when(at == 2)
        def _():
            rows_steps[1].wait()
            add(rows2, rows_y)
            rows_steps[2].start()
            wide_steps[1].start()

        @pl.when(at == 5)
        def _():
            rows_steps[2].wait()
            add(rows2, rows_x)
            summed = rows2[...].astype(F32)
            terms[parts] = jnp.concatenate([summed[:1, :], jnp.zeros((PART - 1, width), F32)], axis=0)
            gains_ref[1:2, :] = summed[1:2, :]

        @pl.when(at == 11)
        def _():
            wide_steps[1].wait()
            add(wide.at[core], wide_x)
            wide_steps[2].start()

        @pl.when(at == 3)
        def _():
            tall_steps[2].wait()
            add(tall.at[core], tall_x)
            tall_steps[3].start()

        @pl.when(at == 20)
        def _():
            wide_steps[2].wait()
            add(wide.at[core], wide_y)
            wide_steps[3].start()

    heads = queries // HEAD_SIZE

    def body(at, carry):
        exchange(at)
        line.step(at)

        @pl.when((at % 2 == 0) & (at // 2 + heads < spread.steps))
        def _():
            spread.step(at // 2 + heads)

        @pl.when((at % 2 == 0) & (at // 2 + heads >= spread.first_whole) & (at // 2 + heads < spread.steps))
        def _():
            block = at // 2 + heads - spread.first_whole
            block_ref[block] = (res_ref[block, :, spread.own()] + spread.total(block)).astype(BF)

        part = at - LAG * line.last

        @pl.when((part >= 0) & (part < parts))
        def _():
            grad = line.total(part)
            values = x_ref[part].astype(F32)
            scale = scale_of(values)
            unit = values * scale
            grad_ref[part] = (res_grad_ref[part] + norm_back(grad, unit, scale, gain_ref[...])).astype(BF)

        return carry

    lax.fori_loop(0, parts + 1 + LAG * line.last, body, 0)
    gains_ref[0:1, :] = line.total(parts)[:1, :]
    line.drain()
    spread.drain()
    key_copy.wait_send()
    value_copy.wait_send()
    tall_steps[3].wait()
    wide_steps[3].wait()
    tall_out[...] = tall[core]
    wide_out[...] = wide[core]


class Spread:
    def __init__(self, term, from_left, from_right, to_right, to_left, sems):
        self.place = lax.axis_index("tensor")
        self.size = lax.axis_size("tensor")
        self.term = term
        self.blocks = term.shape[0]
        self.span = term.shape[2] // self.size
        self.from_left, self.from_right = from_left, from_right
        self.to_right, self.to_left = to_right, to_left
        self.sems = sems
        self.first_whole = 2 * (self.size - 1)
        self.steps = self.blocks + self.first_whole

    def copy(self, way, block, shard):
        last = self.size - 1
        near = jnp.where(self.place < last, self.place + 1, self.place - 1)
        far = jnp.where(self.place > 0, self.place - 1, self.place + 1)
        source, target, device = (
            (self.to_right, self.from_left, near) if way == 0 else (self.to_left, self.from_right, far)
        )
        return pltpu.make_async_remote_copy(
            src_ref=source.at[block, shard], dst_ref=target.at[block, shard],
            send_sem=self.sems.at[2 * way, block, shard], recv_sem=self.sems.at[2 * way + 1, block, shard],
            device_id={"tensor": device}, device_id_type=MESH,
        )

    def clear(self):
        @pl.when(self.place == 0)
        def _():
            self.from_left[...] = jnp.zeros(self.from_left.shape, BF)

        @pl.when(self.place == self.size - 1)
        def _():
            self.from_right[...] = jnp.zeros(self.from_right.shape, BF)

    def passes(self, way, shard):
        return self.place < shard if way == 0 else self.place > shard

    def has_source(self, way):
        return self.place > 0 if way == 0 else self.place < self.size - 1

    def step(self, at):
        for way in range(2):
            block = at - 2 * (self.place if way == 0 else self.size - 1 - self.place)
            valid = (block >= 0) & (block < self.blocks)
            arrived = self.from_left if way == 0 else self.from_right
            leaving = self.to_right if way == 0 else self.to_left
            for shard in range(self.size):
                here = valid & self.passes(way, shard)

                @pl.when(here & self.has_source(way))
                def _():
                    self.copy(way, block, shard).wait_recv()

                @pl.when(here)
                def _():
                    lanes = slice(shard * self.span, (shard + 1) * self.span)
                    own = self.term[block, :, lanes].astype(F32)
                    leaving[block, shard] = (own + arrived[block, shard].astype(F32)).astype(BF)
                    self.copy(way, block, shard).start()

    def own(self):
        return pl.ds(pl.multiple_of(self.place * self.span, self.span), self.span)

    def total(self, block):
        for way in range(2):

            @pl.when(self.has_source(way))
            def _():
                self.copy(way, block, self.place).wait_recv()

        sides = self.from_left[block, self.place].astype(F32) + self.from_right[block, self.place].astype(F32)
        return self.term[block, :, self.own()].astype(F32) + sides

    def drain(self):
        for way in range(2):
            for shard in range(self.size):

                @pl.when(self.passes(way, shard))
                def _():
                    for block in range(self.blocks):
                        self.copy(way, block, shard).wait_send()


BLOCK_ROWS = 128


def input_gradient(
    offsets, block_input, residual_grad, gain, normed, w_query, key_weight, value_weight, w_output, cosines, sines,
    query, keys, values, lse, attended, low, route, second, mixed, residual,
):
    rows, width = block_input.shape
    parts = rows // PART
    kv = key_weight.shape[1]
    columns = w_query.shape[1] + 2 * kv
    tall = (w_output.shape[0] + route.shape[0]) // 2
    size = lax.axis_size("tensor")
    blocks = rows // BLOCK_ROWS
    wide_half = pltpu.VMEM((width // 2, columns), BF)
    tall_half = pltpu.VMEM((tall, width), BF)
    tile = pltpu.VMEM((16, width), BF)
    mix_half = pltpu.VMEM((blocks, size, BLOCK_ROWS, width // size), BF)
    return pl.pallas_call(
        input_grad_kernel,
        out_shape=(
            jax.ShapeDtypeStruct((parts, PART, width), BF),
            jax.ShapeDtypeStruct((width // 2, columns), BF),
            jax.ShapeDtypeStruct((width // 2, columns), BF),
            jax.ShapeDtypeStruct((tall, width), BF),
            jax.ShapeDtypeStruct((tall, width), BF),
            jax.ShapeDtypeStruct((8, width), F32),
            jax.ShapeDtypeStruct((blocks, BLOCK_ROWS, width // size), BF),
        ),
        in_specs=[smem_spec()] + [vmem_spec()] * 16 + [pl.BlockSpec(memory_space=pl.ANY)] * 4,
        out_specs=(vmem_spec(),) * 7,
        scratch_shapes=line_scratch(parts + 1, width)
        + [
            pltpu.VMEM((parts + 1, PART, width), F32),
            pltpu.VMEM((2, 2 * rows, kv), BF),
            pltpu.VMEM((2, rows, kv), BF),
            pltpu.SemaphoreType.DMA((2, 2)),
            pltpu.VMEM((2, width // 2, columns), BF), wide_half, wide_half, wide_half,
            pltpu.VMEM((2, tall, width), BF), tall_half, tall_half, tall_half,
            tile, tile, tile, tile,
            pltpu.SemaphoreType.DMA((2, 11)),
            mix_half, mix_half, mix_half, mix_half,
            pltpu.SemaphoreType.DMA((4, blocks, size)),
            pltpu.VMEM((parts, PART, width), BF),
            pltpu.VMEM((parts, PART, width), F32),
            pltpu.VMEM((rows, width), BF),
            pltpu.VMEM((blocks, BLOCK_ROWS, width), F32),
            pltpu.SemaphoreType.DMA((4,)),
        ],
        compiler_params=pltpu.CompilerParams(
            collective_id=2, has_side_effects=True, vmem_limit_bytes=60 * MIB
        ),
        cost_estimate=LINK_COST,
        name="input_grad",
    )(
        offsets, gain[None], w_query, key_weight, value_weight, w_output, cosines, sines, query, keys, values, lse,
        attended, low, route, second, mixed.reshape(blocks, BLOCK_ROWS, width), block_input.reshape(parts, PART, width),
        residual_grad.reshape(parts, PART, width), normed, residual.reshape(blocks, BLOCK_ROWS, width),
    )


CHUNK = 512
GROUP = 4


def route_gates(token, marks, w_router):
    experts_all = w_router.shape[0]
    chosen = marks[:, :experts_all].astype(F32)
    kept = marks[:, experts_all:].astype(F32)
    logits = jnp.where(chosen > 0.0, matmul_nt(token, w_router), masked_score)
    raised = jnp.exp(logits - jnp.max(logits, axis=1, keepdims=True)) * chosen
    gate = raised / jnp.sum(raised, axis=1, keepdims=True)
    return gate, gate * kept


def hidden_terms(token, pulled, weight, gate_weights, up_weights):
    gate_in = matmul(token, gate_weights)
    up_in = matmul(token, up_weights)
    sig = 0.5 * jnp.tanh(0.5 * gate_in) + 0.5
    silu = gate_in * sig
    hidden = silu * up_in
    gated = (hidden * weight).astype(BF)
    scaled = pulled * weight
    up_grad = (scaled * silu).astype(BF)
    gate_grad = (scaled * up_in * (sig + silu * (1.0 - sig))).astype(BF)
    return hidden, gated, gate_grad, up_grad


def spread_gates(kept, column, group, hid):
    lane = lax.broadcasted_iota(jnp.int32, (1, kept.shape[1]), 1)
    weights = []
    for expert in range(group):
        gate = jnp.sum(jnp.where(lane == column + expert, kept, 0.0), axis=1, keepdims=True)
        weights.append(jnp.broadcast_to(gate, (kept.shape[0], hid)))
    return jnp.concatenate(weights, axis=1)


def expert_kernel(
    n_ref, marks_ref, wr_ref, n_hbm, own_up, peer_up, far_g0, far_m, wg_ref, wu_ref, wd_ref,
    dwg_ref, dwu_ref, dwd_ref, mix_ref, back_ref, route_ref, far_n, far_on, far_g1, far_og0, far_og1, far_om,
    gates, kept_gates, gate_grads, mix, back, nt, wgs, wus, ght, dgs, dus,
    out_g, out_u, out_d, in_g, in_u, in_d, sems, far_sems, g_ref, up_sems,
):
    step = pl.program_id(0)
    steps = pl.num_programs(0) // 2
    side = lax.axis_index("expert")
    dp = lax.axis_index("dp")
    core = lax.rem(dp, 2)
    other = other_core()
    tokens, width = n_ref.shape
    experts_all = wr_ref.shape[0]
    group, _, hid = wg_ref.shape
    chunks = tokens // CHUNK
    lane = lax.broadcasted_iota(jnp.int32, (1, experts_all), 1)

    def copies(slot):
        return [
            pltpu.make_async_remote_copy(
                src_ref=source.at[slot], dst_ref=target.at[slot],
                send_sem=sems.at[0, kind, slot], recv_sem=sems.at[1, kind, slot],
                device_id=other, device_id_type=MESH,
            )
            for kind, (source, target) in enumerate(((out_g, in_g), (out_u, in_u), (out_d, in_d)))
        ]

    half = tokens // 2
    cross = [
        plain_copy(n_hbm.at[pl.ds(at * half, half), :], far_n.at[pl.ds(at * half, half), :], far_sems, at, beside())
        for at in range(2)
    ]
    share = [
        plain_copy(far_n.at[pl.ds(at * half, half), :], far_on.at[pl.ds(at * half, half), :], far_sems, 2 + at, other)
        for at in range(2)
    ]
    peer = {"expert": 1 - side}
    turn_up = plain_copy(far_g0, far_g1, far_sems, 4, peer)
    share_up = plain_copy(far_g1, far_og1, far_sems, 5, other)
    early = [
        plain_copy(source, target, far_sems, 6 + at, other)
        for at, (source, target) in enumerate(((far_g0, far_og0), (far_m, far_om)))
    ]
    loads = [
        pltpu.make_async_copy(source, g_ref.at[pl.ds(at * half, half), :], up_sems.at[at])
        for at, source in enumerate((own_up, peer_up))
    ]

    @pl.when(step == 0)
    def _():
        for copy in loads:
            copy.start()
        meet([(True, other), (True, beside()), (True, peer)])
        for copy in cross + early + [turn_up]:
            copy.start()

        def start(at, carry):
            rows = pl.ds(pl.multiple_of(at * CHUNK, CHUNK), CHUNK)
            gate, kept_gate = route_gates(n_ref[rows, :], marks_ref[rows, :], wr_ref[...])
            gates[rows, :] = gate
            kept_gates[rows, :] = kept_gate
            mix[rows, :] = jnp.zeros((CHUNK, width), F32)
            back[rows, :] = jnp.zeros((CHUNK, width), F32)
            gate_grads[rows, :] = jnp.zeros((CHUNK, experts_all), F32)
            return carry

        lax.fori_loop(0, chunks, start, 0)
        for at in range(chunks):
            nt[:, at * CHUNK : (at + 1) * CHUNK] = n_ref[at * CHUNK : (at + 1) * CHUNK, :].T
        for copy in loads:
            copy.wait()

    @pl.when(step == steps)
    def _():
        cross[0].wait_recv()
        share[0].start()
        turn_up.wait_recv()
        share_up.start()

    for expert in range(group):
        wgs[:, expert * hid : (expert + 1) * hid] = wg_ref[expert]
        wus[:, expert * hid : (expert + 1) * hid] = wu_ref[expert]
    first = step < steps
    block = jnp.where(first, (1 - core) * steps + step, core * steps + step - steps)
    column = side * (experts_all // 2) + block * group

    for at in range(chunks):
        rows = slice(at * CHUNK, (at + 1) * CHUNK)
        token = n_ref[rows, :]
        down = wd_ref[...].reshape(group * hid, width)
        pulled = matmul_nt(g_ref[rows, :], down)
        weight = spread_gates(kept_gates[rows, :], column, group, hid)
        hidden, gated, gate_grad, up_grad = hidden_terms(token, pulled, weight, wgs[...], wus[...])
        products = hidden * pulled
        grads = gate_grads[rows, :]
        for expert in range(group):
            product = jnp.sum(products[:, expert * hid : (expert + 1) * hid], axis=1, keepdims=True)
            grads = grads + jnp.where(lane == column + expert, product, 0.0)
        gate_grads[rows, :] = grads
        ght[:, rows] = gated.T
        dgs[rows, :] = gate_grad
        dus[rows, :] = up_grad
        mix[rows, :] += matmul(gated, down)
        back[rows, :] += matmul_nt(gate_grad, wgs[...]) + matmul_nt(up_grad, wus[...])

    def weight_grads(store_rows, store_down):
        for at in range(width // CHUNK):
            rows = slice(at * CHUNK, (at + 1) * CHUNK)
            turned = nt[rows, :]
            gate_part = matmul(turned, dgs[...])
            up_part = matmul(turned, dus[...])
            for expert in range(group):
                inner = slice(expert * hid, (expert + 1) * hid)
                store_rows(expert, rows, gate_part[:, inner], up_part[:, inner])
        down_part = matmul(ght[...], g_ref[...])
        for expert in range(group):
            store_down(expert, down_part[expert * hid : (expert + 1) * hid, :])

    @pl.when(first)
    def _():
        def store_rows(expert, rows, gate_part, up_part):
            out_g[step, expert, rows, :] = gate_part.astype(BF)
            out_u[step, expert, rows, :] = up_part.astype(BF)

        def store_down(expert, part):
            out_d[step, expert] = part.astype(BF)

        weight_grads(store_rows, store_down)
        for copy in copies(step):
            copy.start()

    @pl.when(step >= steps)
    def _():
        slot = step - steps
        for copy in copies(slot):
            copy.wait_recv()

        def store_rows(expert, rows, gate_part, up_part):
            dwg_ref[expert, rows, :] = (gate_part + in_g[slot, expert, rows, :].astype(F32)).astype(BF)
            dwu_ref[expert, rows, :] = (up_part + in_u[slot, expert, rows, :].astype(F32)).astype(BF)

        def store_down(expert, part):
            dwd_ref[expert] = (part + in_d[slot, expert].astype(F32)).astype(BF)

        weight_grads(store_rows, store_down)
        for copy in copies(slot):
            copy.wait_send()

    @pl.when(step == 2 * steps - 1)
    def _():
        cross[1].wait_recv()
        share[1].start()
        route_ref[...] = jnp.zeros(route_ref.shape, F32)

        def finish(at, carry):
            rows = pl.ds(pl.multiple_of(at * CHUNK, CHUNK), CHUNK)
            mix_ref[rows, :] = mix[rows, :].astype(BF)
            grads = gate_grads[rows, :] * kept_gates[rows, :]
            chosen_grad = grads - gates[rows, :] * jnp.sum(grads, axis=1, keepdims=True)
            low = chosen_grad.astype(BF)
            back_ref[rows, :] = (back[rows, :] + matmul(low, wr_ref[...])).astype(BF)
            route_ref[...] += matmul_tn(low, n_ref[rows, :])
            return carry

        lax.fori_loop(0, chunks, finish, 0)
        for copy in cross + [turn_up]:
            copy.wait_send()
        for copy in share + early + [share_up]:
            copy.wait()


def experts(normed, marks, w_router, upstream, peer_up, far_up, far_marks, w_gate, w_up, w_down):
    tokens, width = normed.shape
    count, _, hid = w_gate.shape
    half = count // 2
    steps = half // GROUP
    experts_all = w_router.shape[0]
    once = pl.Buffered(1)
    whole = lambda step: (0, 0)

    def picked(step):
        core = lax.rem(lax.axis_index("dp"), 2)
        return (jnp.where(step < steps, (1 - core) * steps + step, core * steps + step - steps), 0, 0)

    own = lambda step: (jnp.maximum(step - steps, 0), 0, 0)
    args = [normed, marks, w_router]
    specs = [pl.BlockSpec(array.shape, whole, pipeline_mode=once) for array in args]
    args += [normed, upstream, peer_up, far_up, far_marks]
    specs += [pl.BlockSpec(memory_space=pl.ANY)] * 5
    up_block, down_block = (GROUP, width, hid), (GROUP, hid, width)
    specs += [pl.BlockSpec(up_block, picked), pl.BlockSpec(up_block, picked), pl.BlockSpec(down_block, picked)]
    gate_scratch = pltpu.VMEM((tokens, experts_all), F32)
    rows_scratch = pltpu.VMEM((tokens, width), F32)
    swap_scratch = [
        pltpu.VMEM((steps,) + up_block, BF),
        pltpu.VMEM((steps,) + up_block, BF),
        pltpu.VMEM((steps,) + down_block, BF),
    ]
    return pl.pallas_call(
        expert_kernel,
        out_shape=[
            jax.ShapeDtypeStruct((half, width, hid), BF),
            jax.ShapeDtypeStruct((half, width, hid), BF),
            jax.ShapeDtypeStruct((half, hid, width), BF),
            jax.ShapeDtypeStruct((tokens, width), BF),
            jax.ShapeDtypeStruct((tokens, width), BF),
            jax.ShapeDtypeStruct((experts_all, width), F32),
            jax.ShapeDtypeStruct((tokens, width), BF),
            jax.ShapeDtypeStruct((tokens, width), BF),
            jax.ShapeDtypeStruct(far_up.shape, BF),
            jax.ShapeDtypeStruct(far_up.shape, BF),
            jax.ShapeDtypeStruct(far_up.shape, BF),
            jax.ShapeDtypeStruct(far_marks.shape, BF),
        ],
        grid=(2 * steps,),
        in_specs=specs,
        out_specs=[
            pl.BlockSpec(up_block, own),
            pl.BlockSpec(up_block, own),
            pl.BlockSpec(down_block, own),
            pl.BlockSpec((tokens, width), whole, pipeline_mode=once),
            pl.BlockSpec((tokens, width), whole, pipeline_mode=once),
            pl.BlockSpec((experts_all, width), whole, pipeline_mode=once),
        ]
        + [pl.BlockSpec(memory_space=pl.ANY)] * 6,
        scratch_shapes=[
            gate_scratch, gate_scratch, gate_scratch, rows_scratch, rows_scratch,
            pltpu.VMEM((width, tokens), BF),
            pltpu.VMEM((width, GROUP * hid), BF),
            pltpu.VMEM((width, GROUP * hid), BF),
            pltpu.VMEM((GROUP * hid, tokens), BF),
            pltpu.VMEM((tokens, GROUP * hid), BF),
            pltpu.VMEM((tokens, GROUP * hid), BF),
        ]
        + swap_scratch
        + swap_scratch
        + [pltpu.SemaphoreType.DMA((2, 3, steps)), pltpu.SemaphoreType.DMA((2, 8)), pltpu.VMEM((tokens, width), BF), pltpu.SemaphoreType.DMA((2,))],
        compiler_params=pltpu.CompilerParams(
            dimension_semantics=("arbitrary",), collective_id=3, has_side_effects=True, vmem_limit_bytes=60 * MIB
        ),
        cost_estimate=pl.CostEstimate(
            flops=18 * tokens * width * count * hid,
            bytes_accessed=12 * count * width * hid,
            transcendentals=tokens * count * hid,
        ),
        name="experts",
    )(*args, w_gate, w_up, w_down)


def finish_kernel(core_ref, *refs):
    ins, outs = refs[:13], refs[13:]
    part, at = pl.program_id(0), pl.program_id(1)
    mine, other = ins[:3], ins[3:6]
    wide_mine, wide_other, tall_mine, tall_other, gains, grad, block = ins[6:]
    out_g, out_u, out_d, out_q, out_k, out_v, out_o, out_r, out_first, out_second, out_grad, out_block = outs
    for place, sources in enumerate((mine, other)):

        @pl.when(part == place)
        def _():
            for source, target in zip(sources, (out_g, out_u, out_d)):
                target[...] = source[...].astype(F32)

    core = core_ref[0]
    queries, kv = out_q.shape[1], out_k.shape[1]
    half = out_q.shape[0] // 2
    tall = tall_mine.shape[0]
    outs_rows = out_o.shape[0]

    @pl.when((part == 0) & (at == 0))
    def _():
        out_grad[...] = grad[...]
        out_block[...] = block[...]
        out_first[...] = gains[0:1, :]
        out_second[...] = gains[1:2, :]

    for place in range(2):

        @pl.when((part == place) & (at == 1))
        def _():
            own = core == place
            summed = jnp.where(own, wide_mine[...].astype(F32), wide_other[...].astype(F32))
            rows = slice(place * half, (place + 1) * half)
            out_q[rows, :] = summed[:, :queries]
            out_k[rows, :] = summed[:, queries : queries + kv]
            out_v[rows, :] = summed[:, queries + kv :]
            tall_sum = jnp.where(own, tall_mine[...].astype(F32), tall_other[...].astype(F32))
            top = min((place + 1) * tall, outs_rows)
            out_o[place * tall : top, :] = tall_sum[: top - place * tall, :]
            if place == 1:
                out_r[...] = tall_sum[top - place * tall :, :]


def finish(core, sums, others, wide, wide_back, tall, tall_back, gains, grad, block, queries, outs_rows):
    half = sums[0].shape[0]
    width = grad.shape[1]
    kv = (wide.shape[1] - queries) // 2
    experts_all = 2 * tall.shape[0] - outs_rows
    whole = lambda shape: pl.BlockSpec(shape, lambda part, at, core: (0,) * len(shape), pipeline_mode=pl.Buffered(1))
    step = 4
    count = half // step
    single = lambda array, index: pl.BlockSpec((step,) + array.shape[1:], index)
    first = lambda part, at, core: (jnp.where(part == 0, at, count - 1), 0, 0)
    second = lambda part, at, core: (jnp.where(part == 0, 0, at), 0, 0)
    placed = lambda part, at, core: (jnp.where(part == 0, core[0], 1 - core[0]) * count + at, 0, 0)
    rest = [wide, wide_back, tall, tall_back, gains, grad, block]
    wide_shape = lambda shape: jax.ShapeDtypeStruct(shape, F32)
    shapes = [
        (2 * wide.shape[0], queries), (2 * wide.shape[0], kv), (2 * wide.shape[0], kv),
        (outs_rows, width), (experts_all, width), (1, width), (1, width),
    ]
    return pl.pallas_call(
        finish_kernel,
        out_shape=[wide_shape((2 * half,) + item.shape[1:]) for item in sums]
        + [wide_shape(shape) for shape in shapes]
        + [jax.ShapeDtypeStruct(grad.shape, BF), jax.ShapeDtypeStruct(block.shape, BF)],
        grid_spec=pltpu.PrefetchScalarGridSpec(
            num_scalar_prefetch=1,
            grid=(2, count),
            in_specs=[single(item, first) for item in sums]
            + [single(item, second) for item in others]
            + [whole(item.shape) for item in rest],
            out_specs=[single(item, placed) for item in sums]
            + [whole(shape) for shape in shapes + [grad.shape, block.shape]],
        ),
        compiler_params=pltpu.CompilerParams(vmem_limit_bytes=60 * MIB),
        name="finish",
    )(core, *sums, *others, *rest)


def fast_device(
    block_input, first_gain, w_query, key_weight, value_weight, w_output, second_gain, w_router,
    w_gate, w_up, w_down, expert_ids, slot_index, piece_start_offsets, upstream,
):
    rows, width = block_input.shape
    experts_all = w_router.shape[1]
    core = lax.axis_index("dp") % 2
    positions = lax.axis_index("expert") * rows + jnp.arange(rows, dtype=jnp.int32)
    lanes = jnp.arange(128, dtype=jnp.int32) % (HEAD_SIZE // 2)
    inverse = jnp.exp(lanes.astype(F32) * (-2.0 * math.log(rope_base) / HEAD_SIZE))
    angle = positions.astype(F32)[:, None] * inverse[None, :]
    cosines, sines = jnp.cos(angle), jnp.sin(angle)
    routes = w_router.T
    (
        first_normed, query_rot, keys, values, attended, lse, residual, normed_all, marks, far_marks, peer_up, far_up,
    ) = front(
        piece_start_offsets, block_input, first_gain, second_gain, w_query, key_weight, value_weight, w_output,
        cosines, sines, expert_ids.T, slot_index.T, upstream, experts_all,
    )
    keys, values = keys.reshape(2 * rows, -1), values.reshape(2 * rows, -1)
    normed_all = normed_all.reshape(2 * rows, width)
    marks = marks.reshape(2 * rows, 2 * experts_all)
    far_marks = far_marks.reshape(2 * rows, 2 * experts_all)
    dwg, dwu, dwd, mix, back, route, *far = experts(
        normed_all, marks, routes, upstream, peer_up, far_up, far_marks, w_gate, w_up, w_down
    )
    far_normed, far_other_normed, far_peer_up, far_other_up, far_other_peer_up, far_other_marks = far
    residual_grad, residual_low, grad_second, route, mixed, sums = residual_gradient(
        back, mix, route, residual, upstream, second_gain, routes,
        (
            far_normed, far_other_normed, far_up, far_peer_up, far_other_up, far_other_peer_up,
            far_marks, far_other_marks,
        ),
        w_gate, w_up, w_down, (dwg, dwu, dwd),
    )
    grad_input, wide, wide_back, tall, tall_back, gains, block_output = input_gradient(
        piece_start_offsets, block_input, residual_grad, first_gain, first_normed, w_query, key_weight, value_weight,
        w_output, cosines, sines, query_rot, keys, values, lse, attended, residual_low, route, grad_second, mixed, residual,
    )
    grad_gate, grad_up, grad_down, grad_query, grad_key, grad_value, grad_output, grad_router, first, second, grad, block = finish(
        core[None].astype(jnp.int32), sums[:3], sums[3:], wide, wide_back, tall, tall_back, gains,
        grad_input.reshape(rows, width), block_output.reshape(rows, width // 4), w_query.shape[1], w_output.shape[0],
    )
    return (
        block, grad, first[0], grad_query, grad_key, grad_value, grad_output, second[0], grad_router.T,
        grad_gate, grad_up, grad_down,
    )


def solution(mesh):
    fast = mesh.shape["expert"] == 2 and mesh.shape["dp"] == 4 and mesh.shape["tensor"] == 4
    placed = (
        P(("dp", "expert"), None),
        P(),
        P(None, "tensor"),
        P(None, "tensor"),
        P(None, "tensor"),
        P("tensor", None),
        P(),
        P(),
        P("expert", None, "tensor"),
        P("expert", None, "tensor"),
        P("expert", "tensor", None),
        P(("dp", "expert"), None),
        P(("dp", "expert"), None),
        P("dp", None),
        P(("dp", "expert"), None),
    )
    return jax.shard_map(
        fast_device if fast else general_device,
        mesh=mesh,
        in_specs=placed,
        out_specs=(
            P(("dp", "expert"), "tensor"),
            P(("dp", "expert"), None),
            P(),
            P(None, "tensor"),
            P(None, "tensor"),
            P(None, "tensor"),
            P("tensor", None),
            P(),
            P(),
            P("expert", None, "tensor"),
            P("expert", None, "tensor"),
            P("expert", "tensor", None),
        ),
        check_vma=False,
    )
```

```python
import functools
import math

import jax
import jax.numpy as jnp
from jax import lax
from jax.experimental import pallas as pl
from jax.experimental.pallas import tpu as pltpu
from jax.sharding import PartitionSpec as P

HEAD_SIZE = 64
TOPK = 8
PIC = 256


epsilon = 1e-06
rope_base = 10000.0
masked_score = -1e30


def rope_tables(positions):
    steps = jnp.arange(HEAD_SIZE // 2, dtype=jnp.float32)
    inverse = jnp.exp(steps * (-2.0 * math.log(rope_base) / HEAD_SIZE))
    angle = positions.astype(jnp.float32)[:, None] * inverse[None, :]
    return (jnp.cos(angle), jnp.sin(angle))


def apply_rotary(values, cosine_table, sine_table):
    half = values.shape[-1] // 2
    first = values[..., :half]
    second = values[..., half:]
    cosine_table = cosine_table[:, None, :]
    sine_table = sine_table[:, None, :]
    return jnp.concatenate(
        [first * cosine_table - second * sine_table, second * cosine_table + first * sine_table],
        axis=-1,
    )


def unrotate(values, cosine_table, sine_table):
    half = values.shape[-1] // 2
    first = values[..., :half]
    second = values[..., half:]
    cosine_table = cosine_table[:, None, :]
    sine_table = sine_table[:, None, :]
    return jnp.concatenate(
        [first * cosine_table + second * sine_table, second * cosine_table - first * sine_table],
        axis=-1,
    )


def piece_ids(positions, offsets):
    span = 2 * PIC
    window = positions // span
    within = positions - window * span
    count = offsets.shape[0]
    match = window[:, None] == jnp.arange(count, dtype=jnp.int32)[None, :]
    start = jnp.sum(jnp.where(match, offsets[None, :], 0), axis=1)
    inside = (window < count) & (within >= start) & (within < start + PIC)
    return jnp.where(inside, window, -1)


def matmul(left, right):
    return jnp.dot(left, right, preferred_element_type=jnp.float32)


def matmul_nt(left, right):
    return lax.dot_general(
        left, right, (((1,), (1,)), ((), ())), preferred_element_type=jnp.float32
    )


def matmul_tn(left, right):
    return lax.dot_general(
        left, right, (((0,), (0,)), ((), ())), preferred_element_type=jnp.float32
    )


def norm_scale(values):
    return lax.rsqrt(jnp.mean(values * values, axis=-1, keepdims=True) + epsilon)


def norm_back(grad, unit, scale, gain):
    weighted = grad * gain
    return scale * (weighted - unit * jnp.mean(weighted * unit, axis=-1, keepdims=True))


def general_device(
    block_input,
    first_gain,
    w_query,
    key_weight,
    value_weight,
    w_output,
    second_gain,
    w_router,
    w_gate,
    w_up,
    w_down,
    expert_ids,
    slot_index,
    piece_start_offsets,
    upstream,
):
    rows_here = block_input.shape[0]
    width = block_input.shape[1]
    groups = lax.axis_size("expert")
    length = rows_here * groups
    local_heads = w_query.shape[1] // HEAD_SIZE
    local_kv = key_weight.shape[1] // HEAD_SIZE
    sharing = local_heads // local_kv
    head_rows = sharing * rows_here
    experts_all = w_router.shape[1]
    capacity = TOPK * rows_here // experts_all
    slots_all = experts_all * capacity
    score_scale = HEAD_SIZE ** (-0.5)
    positions = lax.axis_index("expert") * rows_here + jnp.arange(rows_here, dtype=jnp.int32)
    cosine_table, sine_table = rope_tables(positions)
    inputs = block_input.astype(jnp.float32)
    first_scale = norm_scale(inputs)
    first_unit = inputs * first_scale
    first_normed = (first_unit * first_gain).astype(jnp.bfloat16)
    query_rot = apply_rotary(
        matmul(first_normed, w_query).reshape(rows_here, local_heads, HEAD_SIZE),
        cosine_table,
        sine_table,
    ).astype(jnp.bfloat16)
    key_rot = (
        apply_rotary(
            matmul(first_normed, key_weight).reshape(rows_here, local_kv, HEAD_SIZE),
            cosine_table,
            sine_table,
        )
        .astype(jnp.bfloat16)
        .reshape(rows_here, local_kv * HEAD_SIZE)
    )
    value_low = matmul(first_normed, value_weight).astype(jnp.bfloat16)
    keys_all, values_all = (
        lax.all_gather(key_rot, "expert", axis=0, tiled=True),
        lax.all_gather(value_low, "expert", axis=0, tiled=True),
    )
    block = min(512, length)
    blocks = length // block

    def by_block(array):
        return array.reshape(blocks, block, local_kv, HEAD_SIZE).transpose(0, 2, 1, 3)

    def by_rows(stacked):
        return stacked.transpose(0, 2, 1, 3).reshape(length, local_kv * HEAD_SIZE)

    def head_major(array):
        return (
            array.reshape(rows_here, local_kv, sharing, HEAD_SIZE)
            .transpose(1, 2, 0, 3)
            .reshape(local_kv, head_rows, HEAD_SIZE)
        )

    def row_major(array):
        return (
            array.reshape(local_kv, sharing, rows_here, HEAD_SIZE)
            .transpose(2, 0, 1, 3)
            .reshape(rows_here, local_heads * HEAD_SIZE)
        )

    key_blocks = by_block(keys_all)
    value_blocks = by_block(values_all)
    block_starts = jnp.arange(blocks, dtype=jnp.int32) * block
    query_heads = head_major(query_rot.reshape(rows_here, local_heads * HEAD_SIZE))
    offsets = piece_start_offsets[0]
    key_pieces = piece_ids(jnp.arange(length, dtype=jnp.int32), offsets)
    query_pieces = jnp.tile(piece_ids(positions, offsets), sharing)
    query_places = jnp.tile(positions, sharing)

    def block_scores(key_block, start):
        places = start + jnp.arange(block, dtype=jnp.int32)
        pieces = lax.dynamic_slice_in_dim(key_pieces, start, block)
        causal = places[None, :] <= query_places[:, None]
        same = (pieces[None, :] == query_pieces[:, None]) & (query_pieces[:, None] >= 0)
        scores = (
            jnp.einsum("hqd,hkd->hqk", query_heads, key_block, preferred_element_type=jnp.float32)
            * score_scale
        )
        return (scores, (causal | same)[None])

    def max_step(carry, operands):
        running_max, running_sum = carry
        key_block, start = operands
        scores, allowed = block_scores(key_block, start)
        scores = jnp.where(allowed, scores, masked_score)
        new_max = jnp.maximum(running_max, jnp.max(scores, axis=-1))
        weights = jnp.where(allowed, jnp.exp(scores - new_max[..., None]), 0.0)
        new_sum = running_sum * jnp.exp(running_max - new_max) + jnp.sum(weights, axis=-1)
        return ((new_max, new_sum), None)

    start_max = jnp.full((local_kv, head_rows), masked_score, jnp.float32)
    start_sum = jnp.zeros((local_kv, head_rows), jnp.float32)
    (row_max, row_sum), _ = lax.scan(max_step, (start_max, start_sum), (key_blocks, block_starts))
    log_total = row_max + jnp.log(row_sum)

    def block_probs(key_block, start):
        scores, allowed = block_scores(key_block, start)
        return jnp.where(allowed, jnp.exp(scores - log_total[..., None]), 0.0)

    def value_step(total, operands):
        key_block, value_block, start = operands
        probs = block_probs(key_block, start).astype(jnp.bfloat16)
        return (
            total
            + jnp.einsum("hqk,hkd->hqd", probs, value_block, preferred_element_type=jnp.float32),
            None,
        )

    mixed_output, _ = lax.scan(
        value_step,
        jnp.zeros((local_kv, head_rows, HEAD_SIZE), jnp.float32),
        (key_blocks, value_blocks, block_starts),
    )
    attended = row_major(mixed_output).astype(jnp.bfloat16)
    attention = lax.psum(matmul(attended, w_output), "tensor")
    residual = inputs + attention
    second_scale = norm_scale(residual)
    second_unit = residual * second_scale
    second_normed = (second_unit * second_gain).astype(jnp.bfloat16)
    logits = matmul(second_normed, w_router)
    chosen = jnp.take_along_axis(logits, expert_ids, axis=1)
    gates = jax.nn.softmax(chosen, axis=-1)
    row_ids = jnp.arange(rows_here, dtype=jnp.int32)
    flat = jnp.where(slot_index >= 0, expert_ids * capacity + slot_index, slots_all)
    selector = (
        jnp.zeros((slots_all, rows_here), jnp.bfloat16)
        .at[flat.reshape(-1), jnp.repeat(row_ids, TOPK)]
        .set(1.0, mode="drop")
    )
    dispatched = (
        matmul(selector, second_normed).astype(jnp.bfloat16).reshape(experts_all, capacity, width)
    )
    expert_rows = lax.all_to_all(dispatched, "expert", split_axis=0, concat_axis=1, tiled=True)
    gate_in = jnp.einsum("ebd,edf->ebf", expert_rows, w_gate, preferred_element_type=jnp.float32)
    up_in = jnp.einsum("ebd,edf->ebf", expert_rows, w_up, preferred_element_type=jnp.float32)
    sigmoid_gate = jax.nn.sigmoid(gate_in)
    silu_gate = gate_in * sigmoid_gate
    hidden = (silu_gate * up_in).astype(jnp.bfloat16)
    partial_out = jnp.einsum("ebf,efd->ebd", hidden, w_down, preferred_element_type=jnp.float32)
    expert_part = lax.psum_scatter(
        partial_out.astype(jnp.bfloat16), "tensor", scatter_dimension=2, tiled=True
    )
    returned = lax.all_to_all(expert_part, "expert", split_axis=1, concat_axis=0, tiled=True)
    quarter = returned.shape[2]
    padded_out = jnp.concatenate(
        [returned.reshape(slots_all, quarter), jnp.zeros((1, quarter), jnp.bfloat16)], axis=0
    )
    feature_start = lax.axis_index("tensor") * quarter
    grad_full = upstream.astype(jnp.float32)
    grad_part = lax.dynamic_slice_in_dim(grad_full, feature_start, quarter, 1)
    mixture = jnp.zeros((rows_here, quarter), jnp.float32)
    gate_terms = []
    for pick in range(TOPK):
        picked = padded_out[flat[:, pick]].astype(jnp.float32)
        mixture = mixture + gates[:, pick : pick + 1] * picked
        gate_terms.append(jnp.sum(grad_part * picked, axis=1))
    gate_part = jnp.stack(gate_terms, axis=1)
    block_output = (lax.dynamic_slice_in_dim(residual, feature_start, quarter, 1) + mixture).astype(
        jnp.bfloat16
    )
    slot_gates = (
        jnp.zeros((slots_all + 1,), jnp.float32)
        .at[flat.reshape(-1)]
        .set(gates.reshape(-1))[:slots_all]
    )
    grad_slots = (
        (matmul(selector, upstream) * slot_gates[:, None])
        .astype(jnp.bfloat16)
        .reshape(experts_all, capacity, width)
    )
    grad_rows_in = lax.all_to_all(grad_slots, "expert", split_axis=0, concat_axis=1, tiled=True)
    hidden_grad = jnp.einsum(
        "ebd,efd->ebf", grad_rows_in, w_down, preferred_element_type=jnp.float32
    )
    grad_down = jnp.einsum("ebf,ebd->efd", hidden, grad_rows_in, preferred_element_type=jnp.float32)
    gate_in_grad = (
        hidden_grad * up_in * (sigmoid_gate * (1.0 + gate_in * (1.0 - sigmoid_gate)))
    ).astype(jnp.bfloat16)
    up_in_grad = (hidden_grad * silu_gate).astype(jnp.bfloat16)
    grad_gate = jnp.einsum(
        "ebd,ebf->edf", expert_rows, gate_in_grad, preferred_element_type=jnp.float32
    )
    grad_up = jnp.einsum(
        "ebd,ebf->edf", expert_rows, up_in_grad, preferred_element_type=jnp.float32
    )
    rows_part = jnp.einsum("ebf,edf->ebd", gate_in_grad, w_gate, preferred_element_type=jnp.float32)
    rows_part = rows_part + jnp.einsum(
        "ebf,edf->ebd", up_in_grad, w_up, preferred_element_type=jnp.float32
    )
    rows_back = lax.all_to_all(
        rows_part.astype(jnp.bfloat16), "expert", split_axis=1, concat_axis=0, tiled=True
    ).astype(rows_part.dtype)
    padded_back = jnp.concatenate(
        [rows_back.reshape(slots_all, width), jnp.zeros((1, width), jnp.float32)], axis=0
    )
    second_part = jnp.zeros((rows_here, width), jnp.float32)
    for pick in range(TOPK):
        second_part = second_part + padded_back[flat[:, pick]]
    second_sum, gate_grads = (
        lax.psum(second_part.astype(jnp.bfloat16), "tensor").astype(jnp.float32),
        lax.psum(gate_part.astype(jnp.bfloat16), "tensor").astype(jnp.float32),
    )
    chosen_grad = gates * (gate_grads - jnp.sum(gates * gate_grads, axis=1, keepdims=True))
    expert_axis = jnp.arange(experts_all, dtype=jnp.int32)
    logit_grad = jnp.zeros((rows_here, experts_all), jnp.float32)
    for pick in range(TOPK):
        logit_grad = logit_grad + jnp.where(
            expert_ids[:, pick : pick + 1] == expert_axis[None, :],
            chosen_grad[:, pick : pick + 1],
            0.0,
        )
    logit_low = logit_grad.astype(jnp.bfloat16)
    grad_router = matmul_tn(second_normed, logit_low)
    second_grad = second_sum + matmul_nt(logit_low, w_router)
    grad_second = jnp.sum(second_grad * second_unit, axis=0)
    residual_grad = grad_full + norm_back(second_grad, second_unit, second_scale, second_gain)
    residual_low = residual_grad.astype(jnp.bfloat16)
    grad_output = matmul_tn(attended, residual_low)
    attended_grad = head_major(matmul_nt(residual_low, w_output).astype(jnp.bfloat16))

    def delta_step(total, operands):
        key_block, value_block, start = operands
        probs = block_probs(key_block, start)
        prob_grad = jnp.einsum(
            "hqd,hkd->hqk", attended_grad, value_block, preferred_element_type=jnp.float32
        )
        return (total + jnp.sum(probs * prob_grad, axis=-1), None)

    delta, _ = lax.scan(
        delta_step,
        jnp.zeros((local_kv, head_rows), jnp.float32),
        (key_blocks, value_blocks, block_starts),
    )

    def grad_step(query_total, operands):
        key_block, value_block, start = operands
        probs = block_probs(key_block, start)
        prob_grad = jnp.einsum(
            "hqd,hkd->hqk", attended_grad, value_block, preferred_element_type=jnp.float32
        )
        score_grad = (probs * (prob_grad - delta[..., None])).astype(jnp.bfloat16)
        query_total = (
            query_total
            + jnp.einsum("hqk,hkd->hqd", score_grad, key_block, preferred_element_type=jnp.float32)
            * score_scale
        )
        key_grad = (
            jnp.einsum("hqk,hqd->hkd", score_grad, query_heads, preferred_element_type=jnp.float32)
            * score_scale
        )
        value_grad = jnp.einsum(
            "hqk,hqd->hkd",
            probs.astype(jnp.bfloat16),
            attended_grad,
            preferred_element_type=jnp.float32,
        )
        return (query_total, (key_grad, value_grad))

    query_total, (key_stack, value_stack) = lax.scan(
        grad_step,
        jnp.zeros((local_kv, head_rows, HEAD_SIZE), jnp.float32),
        (key_blocks, value_blocks, block_starts),
    )
    key_back, value_back = (
        lax.psum_scatter(
            by_rows(key_stack).astype(jnp.bfloat16), "expert", scatter_dimension=0, tiled=True
        ).astype(jnp.float32),
        lax.psum_scatter(
            by_rows(value_stack).astype(jnp.bfloat16), "expert", scatter_dimension=0, tiled=True
        ).astype(jnp.float32),
    )
    query_grad = (
        unrotate(
            row_major(query_total).reshape(rows_here, local_heads, HEAD_SIZE),
            cosine_table,
            sine_table,
        )
        .astype(jnp.bfloat16)
        .reshape(rows_here, local_heads * HEAD_SIZE)
    )
    key_grad = (
        unrotate(key_back.reshape(rows_here, local_kv, HEAD_SIZE), cosine_table, sine_table)
        .astype(jnp.bfloat16)
        .reshape(rows_here, local_kv * HEAD_SIZE)
    )
    value_grad = value_back.astype(jnp.bfloat16)
    grad_query = matmul_tn(first_normed, query_grad)
    grad_key = matmul_tn(first_normed, key_grad)
    grad_value = matmul_tn(first_normed, value_grad)
    first_part = (
        matmul_nt(query_grad, w_query)
        + matmul_nt(key_grad, key_weight)
        + matmul_nt(value_grad, value_weight)
    )
    first_grad = lax.psum(first_part.astype(jnp.bfloat16), "tensor").astype(jnp.float32)
    grad_first = jnp.sum(first_grad * first_unit, axis=0)
    grad_input = (
        residual_grad + norm_back(first_grad, first_unit, first_scale, first_gain)
    ).astype(jnp.bfloat16)
    dense = lax.psum(
        (grad_query, grad_key, grad_value, grad_output, grad_router, grad_first, grad_second),
        ("dp", "expert"),
    )
    expert_sums = (
        lax.psum(grad_gate.astype(jnp.bfloat16), "dp").astype(jnp.float32),
        lax.psum(grad_up.astype(jnp.bfloat16), "dp").astype(jnp.float32),
        lax.psum(grad_down.astype(jnp.bfloat16), "dp").astype(jnp.float32),
    )
    return (
        block_output,
        grad_input,
        dense[5],
        dense[0],
        dense[1],
        dense[2],
        dense[3],
        dense[6],
        dense[4],
        expert_sums[0],
        expert_sums[1],
        expert_sums[2],
    )


BF = jnp.bfloat16
F32 = jnp.float32
MIB = 1 << 20


def vmem_spec():
    return pl.BlockSpec(memory_space=pltpu.VMEM)


def smem_spec():
    return pl.BlockSpec(memory_space=pltpu.SMEM)


def allowed_pairs(offsets_ref, rows, start, count):
    side = lax.axis_index("expert")
    here = start + lax.broadcasted_iota(jnp.int32, (count, 1), 0)
    keys = lax.broadcasted_iota(jnp.int32, (1, 2 * rows), 1)
    query_place = side * rows + here
    key_place = jnp.where(keys < rows, side * rows + keys, (1 - side) * rows + keys - rows)
    span = 2 * PIC

    def piece(places):
        window = places // span
        within = places - window * span
        start = jnp.where(window == 0, offsets_ref[0, 0], offsets_ref[0, 1])
        inside = (within >= start) & (within < start + PIC)
        return jnp.where(inside, window, -1)

    query_piece = piece(query_place)
    key_piece = piece(key_place)
    return (key_place <= query_place) | ((key_piece == query_piece) & (query_piece >= 0))


def turn(values, first):
    wide = values.shape[1]
    half = HEAD_SIZE // 2
    return jnp.where(
        first, -pltpu.roll(values, wide - half, 1), pltpu.roll(values, half, 1)
    )


MESH = pl.DeviceIdType.MESH
PART = 32
LAG = 3
LINK_COST = pl.CostEstimate(flops=4 * 10**10, bytes_accessed=10**7, transcendentals=0)


def meet(partners):
    barrier = pltpu.get_barrier_semaphore()
    count = 0
    for here, device in partners:
        here = jnp.asarray(here)

        @pl.when(here)
        def _():
            pl.semaphore_signal(barrier, inc=1, device_id=device, device_id_type=MESH)

        count = count + here.astype(jnp.int32)
    pl.semaphore_wait(barrier, count)


def line_partners():
    place = lax.axis_index("tensor")
    last = lax.axis_size("tensor") - 1
    return [(place > 0, {"tensor": place - 1}), (place < last, {"tensor": place + 1})]


class Line:
    def __init__(self, parts, term, from_left, from_right, to_right, to_left, sems, lag=LAG):
        self.lag = lag
        self.place = lax.axis_index("tensor")
        self.last = lax.axis_size("tensor") - 1
        self.parts = parts
        self.term = term
        self.from_left, self.from_right = from_left, from_right
        self.to_right, self.to_left = to_right, to_left
        self.sems = sems

    def copy(self, way, at):
        near = jnp.where(self.place < self.last, self.place + 1, self.place - 1)
        far = jnp.where(self.place > 0, self.place - 1, self.place + 1)
        source, target, device = (
            (self.to_right, self.from_left, near) if way == 0 else (self.to_left, self.from_right, far)
        )
        return pltpu.make_async_remote_copy(
            src_ref=source.at[at],
            dst_ref=target.at[at],
            send_sem=self.sems.at[2 * way, at],
            recv_sem=self.sems.at[2 * way + 1, at],
            device_id={"tensor": device},
            device_id_type=MESH,
        )

    def clear(self):
        @pl.when(self.place == 0)
        def _():
            self.from_left[...] = jnp.zeros(self.from_left.shape, self.from_left.dtype)

        @pl.when(self.place == self.last)
        def _():
            self.from_right[...] = jnp.zeros(self.from_right.shape, self.from_right.dtype)

    def step(self, at):
        for way in range(2):
            part = at - self.lag * (self.place if way == 0 else self.last - self.place)
            has_source = self.place > 0 if way == 0 else self.place < self.last
            has_target = self.place < self.last if way == 0 else self.place > 0
            arrived = self.from_left if way == 0 else self.from_right
            leaving = self.to_right if way == 0 else self.to_left
            valid = (part >= 0) & (part < self.parts)

            @pl.when(valid & has_source)
            def _():
                self.copy(way, part).wait_recv()

            @pl.when(valid & has_target)
            def _():
                leaving[part] = (self.term(part) + arrived[part].astype(F32)).astype(BF)
                self.copy(way, part).start()

    def total(self, part):
        return self.term(part) + self.from_left[part].astype(F32) + self.from_right[part].astype(F32)

    def drain(self):
        def wait(part, carry):
            @pl.when(self.place < self.last)
            def _():
                self.copy(0, part).wait_send()

            @pl.when(self.place > 0)
            def _():
                self.copy(1, part).wait_send()

            return carry

        lax.fori_loop(0, self.parts, wait, 0)


def line_scratch(parts, width, part=PART):
    return [pltpu.VMEM((parts, part, width), BF)] * 4 + [pltpu.SemaphoreType.DMA((4, parts))]


def peer_copy(source, target, sems, at):
    return pltpu.make_async_remote_copy(
        src_ref=source,
        dst_ref=target,
        send_sem=sems.at[0, at],
        recv_sem=sems.at[1, at],
        device_id={"expert": 1 - lax.axis_index("expert")},
        device_id_type=MESH,
    )


def scale_of(values):
    return lax.rsqrt(jnp.mean(values * values, axis=-1, keepdims=True) + epsilon)


def plain_copy(source, target, sems, at, device):
    return pltpu.make_async_remote_copy(
        src_ref=source, dst_ref=target, send_sem=sems.at[0, at], recv_sem=sems.at[1, at],
        device_id=device, device_id_type=MESH,
    )


def beside():
    return {"dp": lax.rem(lax.axis_index("dp") + 2, 4)}


def other_core():
    place = lax.axis_index("dp")
    return {"dp": place + 1 - 2 * lax.rem(place, 2)}


EARLY = 64
BAND = 256
OWN_PULL = 4
PEER_PULL = 21


def front_kernel(
    offsets_ref, x_ref, gain1_ref, gain2_ref, wq_ref, wk_ref, wv_ref, wo_ref, cos_ref, sin_ref, ids_ref, slots_ref, up_hbm, down_hbm,
    n1_ref, q_ref, k_ref, v_ref, att_ref, lse_ref, res_ref, n_ref, marks_ref, far_marks, up_peer, far_up, pulled_hbm,
    from_left, from_right, to_right, to_left, sems, peer_sems, far_sems, terms, downs, ups, pulled, load_sems, pulled_sems,
):
    parts = x_ref.shape[0]
    rows, width = n1_ref.shape
    side = lax.axis_index("expert")
    peer = {"expert": 1 - side}
    line = Line(parts, lambda at: terms[at], from_left, from_right, to_right, to_left, sems)
    meet(line_partners() + [(True, peer), (True, beside())])
    early, late = pl.ds(0, EARLY), pl.ds(EARLY, rows - EARLY)
    up_early = plain_copy(up_hbm.at[early, :], up_peer.at[early, :], far_sems, 0, peer)
    up_late = plain_copy(up_hbm.at[late, :], up_peer.at[late, :], far_sems, 1, peer)
    up_cross = plain_copy(up_hbm, far_up, far_sems, 2, beside())
    key_copy = plain_copy(k_ref.at[0], k_ref.at[1], far_sems, 3, peer)
    value_copy = plain_copy(v_ref.at[0], v_ref.at[1], far_sems, 4, peer)
    marks_copy = plain_copy(marks_ref.at[0], marks_ref.at[1], far_sems, 5, peer)
    marks_cross = plain_copy(marks_ref, far_marks, far_sems, 6, beside())
    up_early.start()
    up_cross.start()
    loads = [
        pltpu.make_async_copy(down_hbm, downs, load_sems.at[0]),
        pltpu.make_async_copy(up_hbm, ups.at[0], load_sems.at[1]),
        pltpu.make_async_copy(up_peer, ups.at[1], load_sems.at[2]),
    ]
    loads[0].start()
    loads[1].start()
    line.clear()

    values = x_ref[...].reshape(rows, width).astype(F32)
    normed = (values * scale_of(values) * gain1_ref[...]).astype(BF)
    n1_ref[...] = normed
    queries, kv = q_ref.shape[1], k_ref.shape[2]

    def rotate(array):
        wide = array.shape[1]
        lane = lax.broadcasted_iota(jnp.int32, (1, wide), 1)
        first = lane % HEAD_SIZE < HEAD_SIZE // 2
        cosines = jnp.concatenate([cos_ref[...]] * (wide // 128), axis=1)
        sines = jnp.concatenate([sin_ref[...]] * (wide // 128), axis=1)
        return (array * cosines + turn(array, first) * sines).astype(BF)

    k_ref[0] = rotate(matmul(normed, wk_ref[...]))
    key_copy.start()
    v_ref[0] = matmul(normed, wv_ref[...]).astype(BF)
    value_copy.start()
    experts_all = marks_ref.shape[2] // 2
    names = lax.broadcasted_iota(jnp.int32, (experts_all, 1), 0)
    chosen = jnp.zeros((experts_all, rows), F32)
    kept = jnp.zeros((experts_all, rows), F32)
    for pick in range(ids_ref.shape[0]):
        hit = jnp.where(ids_ref[pick : pick + 1, :] == names, 1.0, 0.0)
        chosen = chosen + hit
        kept = kept + jnp.where(slots_ref[pick : pick + 1, :] >= 0, hit, 0.0)
    marks_ref[0] = jnp.concatenate([chosen, kept], axis=0).T.astype(BF)
    marks_copy.start()
    up_late.start()
    q_ref[...] = rotate(matmul(normed, wq_ref[...]))
    key_copy.wait_recv()
    value_copy.wait_recv()
    sharing = queries // kv

    def attend(at):
        start = pl.multiple_of(at * BAND, BAND)
        band = pl.ds(start, BAND)
        allowed = allowed_pairs(offsets_ref, rows, start, BAND)
        pieces = []
        for head in range(queries // HEAD_SIZE):
            kv_at = head // sharing * HEAD_SIZE
            query = q_ref[band, head * HEAD_SIZE : (head + 1) * HEAD_SIZE]
            key = k_ref[:, :, kv_at : kv_at + HEAD_SIZE].reshape(2 * rows, HEAD_SIZE)
            value = v_ref[:, :, kv_at : kv_at + HEAD_SIZE].reshape(2 * rows, HEAD_SIZE)
            scores = jnp.where(allowed, matmul_nt(query, key) * (HEAD_SIZE**-0.5), masked_score)
            peak = jnp.max(scores, axis=1, keepdims=True)
            weights = jnp.exp(scores - peak)
            total = jnp.sum(weights, axis=1, keepdims=True)
            pieces.append(matmul((weights * (1.0 / total)).astype(BF), value))
            lse_ref[band, head : head + 1] = peak + jnp.log(total)
        attended = jnp.concatenate(pieces, axis=1).astype(BF)
        att_ref[band, :] = attended
        count = BAND // PART
        terms[pl.ds(at * count, count)] = matmul(attended, wo_ref[...]).reshape(count, PART, width)

    groups = pulled_hbm.shape[0]

    def keep(place, at):
        span = pl.ds(place * rows, rows)
        return pltpu.make_async_copy(pulled.at[place, at], pulled_hbm.at[at, span, :], pulled_sems.at[place, at])

    def pull(place, at):
        count = downs.shape[0] // groups
        down = downs[pl.ds(at * count, count)].reshape(pulled.shape[3], width)
        pulled[place, at] = matmul_nt(ups[place], down).astype(BF)
        keep(place, at).start()

    def body(at, carry):
        @pl.when(at < rows // BAND)
        def _():
            attend(at)

        @pl.when(at == OWN_PULL)
        def _():
            loads[0].wait()
            loads[1].wait()

        @pl.when((at >= OWN_PULL) & (at < OWN_PULL + groups))
        def _():
            pull(0, at - OWN_PULL)

        @pl.when(at == PEER_PULL - 2)
        def _():
            up_early.wait_recv()
            up_late.wait_recv()
            loads[2].start()

        @pl.when(at == PEER_PULL)
        def _():
            loads[2].wait()

        @pl.when((at >= PEER_PULL) & (at < PEER_PULL + groups))
        def _():
            pull(1, at - PEER_PULL)

        @pl.when(at == 3)
        def _():
            marks_copy.wait_recv()
            marks_cross.start()

        line.step(at - 1)
        part = at - 1 - LAG * line.last

        @pl.when(part >= 0)
        def _():
            residual = x_ref[part].astype(F32) + line.total(part)
            res_ref[part] = residual
            unit = residual * scale_of(residual)
            n_ref[0, part] = (unit * gain2_ref[...]).astype(BF)
            peer_copy(n_ref.at[0, part], n_ref.at[1, part], peer_sems, part).start()

        return carry

    lax.fori_loop(0, 1 + parts + LAG * line.last, body, 0)
    line.drain()
    for copy in (key_copy, value_copy, marks_copy, up_early, up_late):
        copy.wait_send()
    for copy in (up_cross, marks_cross):
        copy.wait()
    for place in range(2):
        for at in range(groups):
            keep(place, at).wait()

    def wait(part, carry):
        peer_copy(n_ref.at[0, part], n_ref.at[1, part], peer_sems, part).wait()
        return carry

    lax.fori_loop(0, parts, wait, 0)


def front(
    offsets, block_input, first_gain, second_gain, w_query, key_weight, value_weight, w_output, cosines, sines,
    expert_ids, slot_index, upstream, experts_all, w_down,
):
    rows, width = block_input.shape
    parts = rows // PART
    queries, kv = w_query.shape[1], key_weight.shape[1]
    groups, hid = w_down.shape[0] // GROUP, GROUP * w_down.shape[1]
    any_spec = pl.BlockSpec(memory_space=pl.ANY)
    low = lambda *shape: jax.ShapeDtypeStruct(shape, BF)
    return pl.pallas_call(
        front_kernel,
        out_shape=(
            low(rows, width),
            low(rows, queries),
            low(2, rows, kv),
            low(2, rows, kv),
            low(rows, queries),
            jax.ShapeDtypeStruct((rows, 128), F32),
            jax.ShapeDtypeStruct((parts, PART, width), F32),
            low(2, parts, PART, width),
            low(2, rows, 2 * experts_all),
            low(2, rows, 2 * experts_all),
            low(rows, width),
            low(rows, width),
            low(groups, 2 * rows, hid),
        ),
        in_specs=[smem_spec()] + [vmem_spec()] * 11 + [any_spec] * 2,
        out_specs=(vmem_spec(),) * 9 + (any_spec,) * 4,
        scratch_shapes=line_scratch(parts, width)
        + [
            pltpu.SemaphoreType.DMA((2, parts)),
            pltpu.SemaphoreType.DMA((2, 7)),
            pltpu.VMEM((parts, PART, width), F32),
            pltpu.VMEM(w_down.shape, BF),
            pltpu.VMEM((2, rows, width), BF),
            pltpu.VMEM((2, groups, rows, hid), BF),
            pltpu.SemaphoreType.DMA((3,)),
            pltpu.SemaphoreType.DMA((2, groups)),
        ],
        compiler_params=pltpu.CompilerParams(
            collective_id=0, has_side_effects=True, vmem_limit_bytes=60 * MIB
        ),
        cost_estimate=LINK_COST,
        name="front",
    )(
        offsets, block_input.reshape(parts, PART, width), first_gain[None], second_gain[None], w_query, key_weight,
        value_weight, w_output, cosines, sines, expert_ids, slot_index, upstream, w_down,
    )


UNIT = 512
BIG_PART = 64
BIG_LAG = 2
SUB = 256


def residual_grad_kernel(
    route_ref, gain_ref, wr_ref, back_hbm, mix_hbm, res_hbm, up_hbm,
    far_n, far_on, far_g0, far_g1, far_og0, far_og1, far_m, far_om,
    wg_hbm, wu_hbm, wd_hbm, pg_hbm, pu_hbm, pd_hbm,
    grad_ref, low_ref, second_ref, route_out, mixed_ref, sg_hbm, su_hbm, sd_hbm, og_hbm, ou_hbm, od_hbm,
    from_left, from_right, to_right, to_left, sems, peer_sems, arrived, terms,
    tokens_n, tokens_g, turned, kept_gates, gates_w, ups_w, downs_w, pair_g, pair_u, pair_d, ght, dgs, dus,
    row_sems, weight_sems, pair_sems, out_sems, mix_arrived, mix_sems, marks_ref, share_sems,
    back_ref, mix_ref, res_ref, up_ref, load_sems,
):
    parts = back_ref.shape[0]
    core = lax.rem(lax.axis_index("dp"), 2)
    side = lax.axis_index("expert")
    groups, group, width, hid = pair_g.shape
    experts_all = wr_ref.shape[0]
    line = Line(parts + 1, lambda at: terms[at], from_left, from_right, to_right, to_left, sems, BIG_LAG)
    loads = [
        pltpu.make_async_copy(source, target, load_sems.at[at])
        for at, (source, target) in enumerate(
            ((back_hbm.at[0], back_ref), (res_hbm, res_ref), (up_hbm, up_ref), (mix_hbm.at[0], mix_ref))
        )
    ]
    for copy in loads:
        copy.start()
    line.clear()
    meet(line_partners() + [(True, {"expert": 1 - side}), (True, other_core())])

    def send(part, carry):
        peer_copy(back_hbm.at[1, part], arrived.at[part], peer_sems, part).start()
        return carry

    lax.fori_loop(0, parts, send, 0)

    def send_mix(part, carry):
        peer_copy(mix_hbm.at[1, part], mix_arrived.at[part], mix_sems, part).start()
        return carry

    lax.fori_loop(0, parts, send_mix, 0)
    half = tokens_n.shape[0] // 2
    quarter = half // 2
    row_copies = []
    for place, (rows, first, second, marks) in enumerate(((far_n, far_g0, far_g1, far_m), (far_on, far_og0, far_og1, far_om))):
        at = place * half
        row_copies += [
            pltpu.make_async_copy(rows, tokens_n.at[pl.ds(at, half), :], row_sems.at[0, place]),
            pltpu.make_async_copy(first, tokens_g.at[pl.ds(at, quarter), :], row_sems.at[1, place]),
            pltpu.make_async_copy(second, tokens_g.at[pl.ds(at + quarter, quarter), :], row_sems.at[2, place]),
            pltpu.make_async_copy(marks, marks_ref.at[pl.ds(at, half), :], row_sems.at[3, place]),
        ]
    weight_copies, pair_copies, out_copies = [], [], []
    for at in range(groups):
        first = core * (groups * group) + at * group
        weight_copies.append(
            [
                pltpu.make_async_copy(
                    source.at[first + expert],
                    target.at[at, :, pl.ds(expert * hid, hid)],
                    weight_sems.at[at, kind, expert],
                )
                for expert in range(group)
                for kind, (source, target) in enumerate(((wg_hbm, gates_w), (wu_hbm, ups_w)))
            ]
            + [pltpu.make_async_copy(wd_hbm.at[pl.ds(first, group)], downs_w.at[at], weight_sems.at[at, 2, 0])]
        )
        sources = (pg_hbm, pu_hbm, pd_hbm)
        held = (pair_g, pair_u, pair_d)
        targets = (sg_hbm, su_hbm, sd_hbm)
        others = (og_hbm, ou_hbm, od_hbm)
        pair_copies.append(
            [
                pltpu.make_async_copy(sources[kind].at[pl.ds(at * group, group)], held[kind].at[at], pair_sems.at[at, kind])
                for kind in range(3)
            ]
        )
        out_copies.append(
            [
                pltpu.make_async_copy(held[kind].at[at], targets[kind].at[pl.ds(at * group, group)], out_sems.at[at, kind])
                for kind in range(3)
            ]
            + [
                plain_copy(
                    held[kind].at[at], others[kind].at[pl.ds(at * group, group)], share_sems.at[at], kind, other_core()
                )
                for kind in range(3)
            ]
        )
    for copy in row_copies[:4] + weight_copies[0] + row_copies[4:] + pair_copies[0] + weight_copies[1] + pair_copies[1]:
        copy.start()
    pad = jnp.zeros((BIG_PART - route_ref.shape[0], route_ref.shape[1]), F32)
    terms[parts] = jnp.concatenate([route_ref[...], pad], axis=0)
    loads[0].wait()
    second_ref[...] = jnp.zeros(second_ref.shape, F32)
    chunks = 2 * half // UNIT
    units = chunks + 3

    def compute(at):
        for where in range(groups):
            unit = at - where * units

            @pl.when(unit == 0)
            def _():
                for copy in weight_copies[where]:
                    copy.wait()

            if where == 0:

                @pl.when(unit == 0)
                def _():
                    for copy in row_copies[:4]:
                        copy.wait()

                @pl.when(unit == half // UNIT)
                def _():
                    for copy in row_copies[4:]:
                        copy.wait()

            @pl.when(unit == chunks)
            def _():
                for copy in pair_copies[where]:
                    copy.wait()

        where = at // units
        unit = at - where * units

        @pl.when(unit < chunks)
        def _():
            down = downs_w[where].reshape(group * hid, width)
            column = side * (experts_all // 2) + (core * groups + where) * group
            for sub in range(UNIT // SUB):
                rows = pl.ds(pl.multiple_of(unit * UNIT + sub * SUB, SUB), SUB)

                @pl.when(where == 0)
                def _():
                    token = tokens_n[rows, :]
                    kept_gates[rows, :] = route_gates(token, marks_ref[rows, :], wr_ref[...])[1]
                    turned[:, rows] = token.T

            for sub in range(UNIT // SUB):
                rows = pl.ds(pl.multiple_of(unit * UNIT + sub * SUB, SUB), SUB)
                pulled = matmul_nt(tokens_g[rows, :], down)
                weight = spread_gates(kept_gates[rows, :], column, group, hid)
                _, gated, gate_grad, up_grad = hidden_terms(
                    tokens_n[rows, :], pulled, weight, gates_w[where], ups_w[where]
                )
                ght[:, rows] = gated.T
                dgs[rows, :] = gate_grad
                dus[rows, :] = up_grad

        @pl.when((unit >= chunks) & (unit < chunks + 2))
        def _():
            rows = pl.ds(pl.multiple_of((unit - chunks) * (width // 2), width // 2), width // 2)
            for source, held in ((dgs, pair_g), (dus, pair_u)):
                part = matmul(turned[rows, :], source[...])
                for expert in range(group):
                    more = part[:, expert * hid : (expert + 1) * hid]
                    held[where, expert, rows, :] = (held[where, expert, rows, :].astype(F32) + more).astype(BF)

        @pl.when(unit == chunks + 2)
        def _():
            part = matmul(ght[...], tokens_g[...])
            for expert in range(group):
                more = part[expert * hid : (expert + 1) * hid, :]
                pair_d[where, expert] = (pair_d[where, expert].astype(F32) + more).astype(BF)

        for where in range(groups):

            @pl.when(at == where * units + units - 1)
            def _():
                for copy in out_copies[where]:
                    copy.start()

    def add_mix(part):
        peer_copy(mix_hbm.at[1, part], mix_arrived.at[part], mix_sems, part).wait_recv()
        mixed_ref[part] = (mix_ref[part].astype(F32) + mix_arrived[part].astype(F32)).astype(BF)

    steps = parts + 1 + BIG_LAG * line.last

    def advance(at):
        @pl.when(at < parts)
        def _():
            peer_copy(back_hbm.at[1, at], arrived.at[at], peer_sems, at).wait_recv()
            terms[at] = back_ref[at].astype(F32) + arrived[at].astype(F32)

        line.step(at)
        part = at - BIG_LAG * line.last

        @pl.when((part >= 0) & (part < parts))
        def _():
            grad = line.total(part)
            residual = res_ref[part]
            scale = scale_of(residual)
            unit = residual * scale
            second_ref[...] += jnp.sum(grad * unit, axis=0, keepdims=True)
            result = up_ref[part].astype(F32) + norm_back(grad, unit, scale, gain_ref[...])
            grad_ref[part] = result
            low_ref[part] = result.astype(BF)

        @pl.when((at >= MIX_STEP) & (at < MIX_STEP + parts))
        def _():
            add_mix(at - MIX_STEP)

    turns = max(groups * units, steps)

    def body(at, carry):
        @pl.when(at < groups * units)
        def _():
            compute(at)

        @pl.when(at == 2)
        def _():
            for copy in loads[1:]:
                copy.wait()

        advance(at)
        return carry

    lax.fori_loop(0, turns, body, 0)
    route_out[...] = line.total(parts)[: route_ref.shape[0], :]

    def rest(part, carry):
        add_mix(part)
        return carry

    lax.fori_loop(turns - MIX_STEP, parts, rest, 0)
    line.drain()

    def wait(part, carry):
        peer_copy(back_hbm.at[1, part], arrived.at[part], peer_sems, part).wait_send()
        peer_copy(mix_hbm.at[1, part], mix_arrived.at[part], mix_sems, part).wait_send()
        return carry

    lax.fori_loop(0, parts, wait, 0)
    for copies in out_copies:
        for copy in copies:
            copy.wait()


MIX_STEP = 9


def residual_gradient(back, mix, route, residual, upstream, gain, w_router, far_rows, w_gate, w_up, w_down, pairs):
    rows, width = upstream.shape
    parts = rows // BIG_PART
    half, _, hid = pairs[0].shape
    groups = half // GROUP
    tokens = 2 * far_rows[0].shape[0]
    any_spec = pl.BlockSpec(memory_space=pl.ANY)
    grad, low, second, route, mixed, *sums = pl.pallas_call(
        residual_grad_kernel,
        out_shape=[
            jax.ShapeDtypeStruct((parts, BIG_PART, width), F32),
            jax.ShapeDtypeStruct((parts, BIG_PART, width), BF),
            jax.ShapeDtypeStruct((1, width), F32),
            jax.ShapeDtypeStruct(route.shape, F32),
            jax.ShapeDtypeStruct((parts, BIG_PART, width), BF),
        ]
        + [jax.ShapeDtypeStruct(pair.shape, BF) for pair in pairs] * 2,
        in_specs=[vmem_spec()] * 3 + [any_spec] * 18,
        out_specs=[vmem_spec()] * 5 + [any_spec] * 6,
        scratch_shapes=line_scratch(parts + 1, width, BIG_PART)
        + [
            pltpu.SemaphoreType.DMA((2, parts)),
            pltpu.VMEM((parts, BIG_PART, width), BF),
            pltpu.VMEM((parts + 1, BIG_PART, width), F32),
            pltpu.VMEM((tokens, width), BF),
            pltpu.VMEM((tokens, width), BF),
            pltpu.VMEM((width, tokens), BF),
            pltpu.VMEM((tokens, w_router.shape[0]), F32),
            pltpu.VMEM((groups, width, GROUP * hid), BF),
            pltpu.VMEM((groups, width, GROUP * hid), BF),
            pltpu.VMEM((groups, GROUP, hid, width), BF),
            pltpu.VMEM((groups, GROUP, width, hid), BF),
            pltpu.VMEM((groups, GROUP, width, hid), BF),
            pltpu.VMEM((groups, GROUP, hid, width), BF),
            pltpu.VMEM((GROUP * hid, tokens), BF),
            pltpu.VMEM((tokens, GROUP * hid), BF),
            pltpu.VMEM((tokens, GROUP * hid), BF),
            pltpu.SemaphoreType.DMA((4, 2)),
            pltpu.SemaphoreType.DMA((groups, 3, GROUP)),
            pltpu.SemaphoreType.DMA((groups, 3)),
            pltpu.SemaphoreType.DMA((groups, 3)),
            pltpu.VMEM((parts, BIG_PART, width), BF),
            pltpu.SemaphoreType.DMA((2, parts)),
            pltpu.VMEM((tokens, 2 * w_router.shape[0]), BF),
            pltpu.SemaphoreType.DMA((groups, 2, 3)),
            pltpu.VMEM((parts, BIG_PART, width), BF),
            pltpu.VMEM((parts, BIG_PART, width), BF),
            pltpu.VMEM((parts, BIG_PART, width), F32),
            pltpu.VMEM((parts, BIG_PART, width), BF),
            pltpu.SemaphoreType.DMA((4,)),
        ],
        compiler_params=pltpu.CompilerParams(
            collective_id=1, has_side_effects=True, vmem_limit_bytes=60 * MIB
        ),
        cost_estimate=LINK_COST,
        name="residual_grad",
    )(
        route, gain[None], w_router, back.reshape(2, parts, BIG_PART, width), mix.reshape(2, parts, BIG_PART, width),
        residual.reshape(parts, BIG_PART, width), upstream.reshape(parts, BIG_PART, width), *far_rows, w_gate, w_up, w_down, *pairs,
    )
    return grad, low.reshape(rows, width), second, route, mixed, sums


def input_grad_kernel(
    offsets_ref, gain_ref, wq_ref, wk_ref, wv_ref, wo_ref, cos_ref, sin_ref,
    q_ref, k_ref, v_ref, lse_ref, att_ref, low_ref, route_ref, second_ref, mix_ref, x_hbm, res_grad_hbm, n_hbm, res_hbm,
    grad_ref, wide_out, wide_back, tall_out, tall_back, gains_ref, block_ref,
    from_left, from_right, to_right, to_left, sems, terms, kv_out, kv_in, kv_sems,
    wide, wide_core, wide_x, wide_y, tall, tall_core, tall_x, tall_y, rows2, rows_core, rows_x, rows_y, sum_sems,
    mix_left, mix_right, mix_to_right, mix_to_left, mix_sems, x_ref, res_grad_ref, n_ref, res_ref, load_sems,
):
    parts = x_ref.shape[0]
    rows = n_ref.shape[0]
    width = n_ref.shape[1]
    core = lax.rem(lax.axis_index("dp"), 2)
    peer = {"expert": 1 - lax.axis_index("expert")}
    kv = wk_ref.shape[1]
    queries = wq_ref.shape[1]
    line = Line(parts + 1, lambda at: terms[at], from_left, from_right, to_right, to_left, sems)
    spread = Spread(mix_ref, mix_left, mix_right, mix_to_right, mix_to_left, mix_sems)
    loads = [
        pltpu.make_async_copy(source, target, load_sems.at[at])
        for at, (source, target) in enumerate(
            ((n_hbm, n_ref), (x_hbm, x_ref), (res_grad_hbm, res_grad_ref), (res_hbm, res_ref))
        )
    ]
    for copy in loads:
        copy.start()
    line.clear()
    spread.clear()
    meet(line_partners() + [(True, peer), (True, beside()), (True, other_core())])
    spread.step(0)
    key_copy = plain_copy(kv_out.at[0, pl.ds(rows, rows), :], kv_in.at[0], kv_sems, 0, peer)
    value_copy = plain_copy(kv_out.at[1, pl.ds(rows, rows), :], kv_in.at[1], kv_sems, 1, peer)

    scale = HEAD_SIZE**-0.5
    low = low_ref[...]
    out_part = matmul(att_ref[...].T, low).astype(BF)
    att_grad = matmul_nt(low, wo_ref[...]).astype(BF)
    half_tall = tall.shape[1]
    outs = wo_ref.shape[0]
    for at in range(2):
        start, high = at * half_tall, (at + 1) * half_tall
        top = min(high, outs)
        tall[at, : top - start, :] = out_part[start:top, :]
        if high > outs:
            tall[at, outs - start :, :] = route_ref[...].astype(BF)

    tall_steps = [
        plain_copy(tall.at[1 - core], tall_core, sum_sems, 0, other_core()),
        plain_copy(tall.at[core], tall_y, sum_sems, 1, peer),
        plain_copy(tall.at[core], tall_x, sum_sems, 2, beside()),
        plain_copy(tall.at[core], tall_back, sum_sems, 3, other_core()),
    ]
    wide_steps = [
        plain_copy(wide.at[1 - core], wide_core, sum_sems, 4, other_core()),
        plain_copy(wide.at[core], wide_x, sum_sems, 5, beside()),
        plain_copy(wide.at[core], wide_y, sum_sems, 6, peer),
        plain_copy(wide.at[core], wide_back, sum_sems, 7, other_core()),
    ]
    rows_steps = [
        plain_copy(rows2, rows_core, sum_sems, 8, other_core()),
        plain_copy(rows2, rows_y, sum_sems, 9, peer),
        plain_copy(rows2, rows_x, sum_sems, 10, beside()),
    ]
    tall_steps[0].start()

    def add(held, arrived):
        held[...] = (held[...].astype(F32) + arrived[...].astype(F32)).astype(BF)

    allowed = allowed_pairs(offsets_ref, rows, 0, rows)
    sharing = queries // kv
    query_parts, key_parts, value_parts = [], [], []
    for head in range(queries // HEAD_SIZE):
        if head:
            spread.step(head)
        if head == 1:
            tall_steps[0].wait()
            add(tall.at[core], tall_core)
            tall_steps[1].start()
        if head == 3:
            tall_steps[1].wait()
            add(tall.at[core], tall_y)
            tall_steps[2].start()
        at = head * HEAD_SIZE
        kv_at = head // sharing * HEAD_SIZE
        query = q_ref[:, at : at + HEAD_SIZE]
        key = k_ref[:, kv_at : kv_at + HEAD_SIZE]
        value = v_ref[:, kv_at : kv_at + HEAD_SIZE]
        grad = att_grad[:, at : at + HEAD_SIZE]
        scores = jnp.where(allowed, matmul_nt(query, key) * scale, masked_score)
        probs = jnp.exp(scores - lse_ref[:, head : head + 1])
        prob_grad = matmul_nt(grad, value)
        delta = jnp.sum(probs * prob_grad, axis=1, keepdims=True)
        score_grad = (probs * (prob_grad - delta)).astype(BF)
        query_parts.append(matmul(score_grad, key) * scale)
        key_part = matmul_tn(score_grad, query) * scale
        value_part = matmul_tn(probs.astype(BF), grad)
        if head % sharing == 0:
            key_parts.append(key_part)
            value_parts.append(value_part)
        else:
            key_parts[-1] = key_parts[-1] + key_part
            value_parts[-1] = value_parts[-1] + value_part
    kv_out[0] = jnp.concatenate(key_parts, axis=1).astype(BF)
    key_copy.start()
    kv_out[1] = jnp.concatenate(value_parts, axis=1).astype(BF)
    value_copy.start()

    def rotate_back(array):
        wide_lanes = array.shape[1]
        lane = lax.broadcasted_iota(jnp.int32, (1, wide_lanes), 1)
        first = lane % HEAD_SIZE < HEAD_SIZE // 2
        cosines = jnp.concatenate([cos_ref[...]] * (wide_lanes // 128), axis=1)
        sines = jnp.concatenate([sin_ref[...]] * (wide_lanes // 128), axis=1)
        return (array * cosines - turn(array, first) * sines).astype(BF)

    for copy in loads:
        copy.wait()
    query_grad = rotate_back(jnp.concatenate(query_parts, axis=1))
    by_rows = (parts, rows // parts, width)
    terms[pl.ds(0, parts)] = matmul_nt(query_grad, wq_ref[...]).reshape(by_rows)
    turned = n_ref[...].T
    query_part = matmul(turned, query_grad).astype(BF)
    for at in range(2):
        wide[at, :, :queries] = query_part[at * width // 2 : (at + 1) * width // 2, :]
    key_copy.wait_recv()
    value_copy.wait_recv()
    key_grad = rotate_back(kv_out[0, :rows, :].astype(F32) + kv_in[0].astype(F32))
    value_grad = (kv_out[1, :rows, :].astype(F32) + kv_in[1].astype(F32)).astype(BF)
    more = matmul_nt(key_grad, wk_ref[...]) + matmul_nt(value_grad, wv_ref[...])
    terms[pl.ds(0, parts)] += more.reshape(by_rows)
    both_part = matmul(turned, jnp.concatenate([key_grad, value_grad], axis=1)).astype(BF)
    for at in range(2):
        wide[at, :, queries:] = both_part[at * width // 2 : (at + 1) * width // 2, :]
    wide_steps[0].start()

    def gain_part(at, total):
        values = x_ref[at].astype(F32)
        return total + jnp.sum(terms[at] * (values * scale_of(values)), axis=0, keepdims=True)

    first_sum = lax.fori_loop(0, parts, gain_part, jnp.zeros((1, width), F32))
    pad = jnp.zeros((rows2.shape[0] - 2, width), F32)
    rows2[...] = jnp.concatenate([first_sum, second_ref[...], pad], axis=0).astype(BF)
    rows_steps[0].start()

    def exchange(at):
        @pl.when(at == 0)
        def _():
            rows_steps[0].wait()
            add(rows2, rows_core)
            rows_steps[1].start()

        @pl.when(at == 1)
        def _():
            wide_steps[0].wait()
            add(wide.at[core], wide_core)

        @pl.when(at == 2)
        def _():
            rows_steps[1].wait()
            add(rows2, rows_y)
            rows_steps[2].start()
            wide_steps[1].start()

        @pl.when(at == 5)
        def _():
            rows_steps[2].wait()
            add(rows2, rows_x)
            summed = rows2[...].astype(F32)
            terms[parts] = jnp.concatenate([summed[:1, :], jnp.zeros((PART - 1, width), F32)], axis=0)
            gains_ref[1:2, :] = summed[1:2, :]

        @pl.when(at == 11)
        def _():
            wide_steps[1].wait()
            add(wide.at[core], wide_x)
            wide_steps[2].start()

        @pl.when(at == 3)
        def _():
            tall_steps[2].wait()
            add(tall.at[core], tall_x)
            tall_steps[3].start()

        @pl.when(at == 20)
        def _():
            wide_steps[2].wait()
            add(wide.at[core], wide_y)
            wide_steps[3].start()

    heads = queries // HEAD_SIZE

    def body(at, carry):
        exchange(at)
        line.step(at)

        @pl.when((at % 2 == 0) & (at // 2 + heads < spread.steps))
        def _():
            spread.step(at // 2 + heads)

        @pl.when((at % 2 == 0) & (at // 2 + heads >= spread.first_whole) & (at // 2 + heads < spread.steps))
        def _():
            block = at // 2 + heads - spread.first_whole
            block_ref[block] = (res_ref[block, :, spread.own()] + spread.total(block)).astype(BF)

        part = at - LAG * line.last

        @pl.when((part >= 0) & (part < parts))
        def _():
            grad = line.total(part)
            values = x_ref[part].astype(F32)
            scale = scale_of(values)
            unit = values * scale
            grad_ref[part] = (res_grad_ref[part] + norm_back(grad, unit, scale, gain_ref[...])).astype(BF)

        return carry

    lax.fori_loop(0, parts + 1 + LAG * line.last, body, 0)
    gains_ref[0:1, :] = line.total(parts)[:1, :]
    line.drain()
    spread.drain()
    key_copy.wait_send()
    value_copy.wait_send()
    tall_steps[3].wait()
    wide_steps[3].wait()
    tall_out[...] = tall[core]
    wide_out[...] = wide[core]


class Spread:
    def __init__(self, term, from_left, from_right, to_right, to_left, sems):
        self.place = lax.axis_index("tensor")
        self.size = lax.axis_size("tensor")
        self.term = term
        self.blocks = term.shape[0]
        self.span = term.shape[2] // self.size
        self.from_left, self.from_right = from_left, from_right
        self.to_right, self.to_left = to_right, to_left
        self.sems = sems
        self.first_whole = 2 * (self.size - 1)
        self.steps = self.blocks + self.first_whole

    def copy(self, way, block, shard):
        last = self.size - 1
        near = jnp.where(self.place < last, self.place + 1, self.place - 1)
        far = jnp.where(self.place > 0, self.place - 1, self.place + 1)
        source, target, device = (
            (self.to_right, self.from_left, near) if way == 0 else (self.to_left, self.from_right, far)
        )
        return pltpu.make_async_remote_copy(
            src_ref=source.at[block, shard], dst_ref=target.at[block, shard],
            send_sem=self.sems.at[2 * way, block, shard], recv_sem=self.sems.at[2 * way + 1, block, shard],
            device_id={"tensor": device}, device_id_type=MESH,
        )

    def clear(self):
        @pl.when(self.place == 0)
        def _():
            self.from_left[...] = jnp.zeros(self.from_left.shape, BF)

        @pl.when(self.place == self.size - 1)
        def _():
            self.from_right[...] = jnp.zeros(self.from_right.shape, BF)

    def passes(self, way, shard):
        return self.place < shard if way == 0 else self.place > shard

    def has_source(self, way):
        return self.place > 0 if way == 0 else self.place < self.size - 1

    def step(self, at):
        for way in range(2):
            block = at - 2 * (self.place if way == 0 else self.size - 1 - self.place)
            valid = (block >= 0) & (block < self.blocks)
            arrived = self.from_left if way == 0 else self.from_right
            leaving = self.to_right if way == 0 else self.to_left
            for shard in range(self.size):
                here = valid & self.passes(way, shard)

                @pl.when(here & self.has_source(way))
                def _():
                    self.copy(way, block, shard).wait_recv()

                @pl.when(here)
                def _():
                    lanes = slice(shard * self.span, (shard + 1) * self.span)
                    own = self.term[block, :, lanes].astype(F32)
                    leaving[block, shard] = (own + arrived[block, shard].astype(F32)).astype(BF)
                    self.copy(way, block, shard).start()

    def own(self):
        return pl.ds(pl.multiple_of(self.place * self.span, self.span), self.span)

    def total(self, block):
        for way in range(2):

            @pl.when(self.has_source(way))
            def _():
                self.copy(way, block, self.place).wait_recv()

        sides = self.from_left[block, self.place].astype(F32) + self.from_right[block, self.place].astype(F32)
        return self.term[block, :, self.own()].astype(F32) + sides

    def drain(self):
        for way in range(2):
            for shard in range(self.size):

                @pl.when(self.passes(way, shard))
                def _():
                    for block in range(self.blocks):
                        self.copy(way, block, shard).wait_send()


BLOCK_ROWS = 128


def input_gradient(
    offsets, block_input, residual_grad, gain, normed, w_query, key_weight, value_weight, w_output, cosines, sines,
    query, keys, values, lse, attended, low, route, second, mixed, residual,
):
    rows, width = block_input.shape
    parts = rows // PART
    kv = key_weight.shape[1]
    columns = w_query.shape[1] + 2 * kv
    tall = (w_output.shape[0] + route.shape[0]) // 2
    size = lax.axis_size("tensor")
    blocks = rows // BLOCK_ROWS
    wide_half = pltpu.VMEM((width // 2, columns), BF)
    tall_half = pltpu.VMEM((tall, width), BF)
    tile = pltpu.VMEM((16, width), BF)
    mix_half = pltpu.VMEM((blocks, size, BLOCK_ROWS, width // size), BF)
    return pl.pallas_call(
        input_grad_kernel,
        out_shape=(
            jax.ShapeDtypeStruct((parts, PART, width), BF),
            jax.ShapeDtypeStruct((width // 2, columns), BF),
            jax.ShapeDtypeStruct((width // 2, columns), BF),
            jax.ShapeDtypeStruct((tall, width), BF),
            jax.ShapeDtypeStruct((tall, width), BF),
            jax.ShapeDtypeStruct((8, width), F32),
            jax.ShapeDtypeStruct((blocks, BLOCK_ROWS, width // size), BF),
        ),
        in_specs=[smem_spec()] + [vmem_spec()] * 16 + [pl.BlockSpec(memory_space=pl.ANY)] * 4,
        out_specs=(vmem_spec(),) * 7,
        scratch_shapes=line_scratch(parts + 1, width)
        + [
            pltpu.VMEM((parts + 1, PART, width), F32),
            pltpu.VMEM((2, 2 * rows, kv), BF),
            pltpu.VMEM((2, rows, kv), BF),
            pltpu.SemaphoreType.DMA((2, 2)),
            pltpu.VMEM((2, width // 2, columns), BF), wide_half, wide_half, wide_half,
            pltpu.VMEM((2, tall, width), BF), tall_half, tall_half, tall_half,
            tile, tile, tile, tile,
            pltpu.SemaphoreType.DMA((2, 11)),
            mix_half, mix_half, mix_half, mix_half,
            pltpu.SemaphoreType.DMA((4, blocks, size)),
            pltpu.VMEM((parts, PART, width), BF),
            pltpu.VMEM((parts, PART, width), F32),
            pltpu.VMEM((rows, width), BF),
            pltpu.VMEM((blocks, BLOCK_ROWS, width), F32),
            pltpu.SemaphoreType.DMA((4,)),
        ],
        compiler_params=pltpu.CompilerParams(
            collective_id=2, has_side_effects=True, vmem_limit_bytes=60 * MIB
        ),
        cost_estimate=LINK_COST,
        name="input_grad",
    )(
        offsets, gain[None], w_query, key_weight, value_weight, w_output, cosines, sines, query, keys, values, lse,
        attended, low, route, second, mixed.reshape(blocks, BLOCK_ROWS, width), block_input.reshape(parts, PART, width),
        residual_grad.reshape(parts, PART, width), normed, residual.reshape(blocks, BLOCK_ROWS, width),
    )


CHUNK = 256
GROUP = 4


def route_gates(token, marks, w_router):
    experts_all = w_router.shape[0]
    chosen = marks[:, :experts_all].astype(F32)
    kept = marks[:, experts_all:].astype(F32)
    logits = jnp.where(chosen > 0.0, matmul_nt(token, w_router), masked_score)
    raised = jnp.exp(logits - jnp.max(logits, axis=1, keepdims=True)) * chosen
    gate = raised / jnp.sum(raised, axis=1, keepdims=True)
    return gate, gate * kept


def hidden_terms(token, pulled, weight, gate_weights, up_weights):
    gate_in = matmul(token, gate_weights)
    up_in = matmul(token, up_weights)
    sig = 0.5 * jnp.tanh(0.5 * gate_in) + 0.5
    silu = gate_in * sig
    hidden = silu * up_in
    gated = (hidden * weight).astype(BF)
    scaled = pulled * weight
    up_grad = (scaled * silu).astype(BF)
    gate_grad = (scaled * up_in * (sig + silu * (1.0 - sig))).astype(BF)
    return hidden, gated, gate_grad, up_grad


def spread_gates(kept, column, group, hid):
    lane = lax.broadcasted_iota(jnp.int32, (1, kept.shape[1]), 1)
    weights = []
    for expert in range(group):
        gate = jnp.sum(jnp.where(lane == column + expert, kept, 0.0), axis=1, keepdims=True)
        weights.append(jnp.broadcast_to(gate, (kept.shape[0], hid)))
    return jnp.concatenate(weights, axis=1)


def expert_kernel(
    n_ref, marks_ref, wr_ref, n_hbm, own_up, peer_up, far_g0, far_m, wg_ref, wu_ref, wd_ref, pulled_ref,
    dwg_ref, dwu_ref, dwd_ref, mix_ref, back_ref, route_ref, far_n, far_on, far_g1, far_og0, far_og1, far_om,
    gates, kept_gates, gate_grads, mix, back, nt, wgs, wus, ght, dgs, dus,
    out_g, out_u, out_d, in_g, in_u, in_d, sems, far_sems, g_ref, up_sems,
):
    step = pl.program_id(0)
    steps = pl.num_programs(0) // 2
    side = lax.axis_index("expert")
    dp = lax.axis_index("dp")
    core = lax.rem(dp, 2)
    other = other_core()
    tokens, width = n_ref.shape
    experts_all = wr_ref.shape[0]
    group, _, hid = wg_ref.shape
    chunks = tokens // CHUNK
    lane = lax.broadcasted_iota(jnp.int32, (1, experts_all), 1)

    def copies(slot):
        return [
            pltpu.make_async_remote_copy(
                src_ref=source.at[slot], dst_ref=target.at[slot],
                send_sem=sems.at[0, kind, slot], recv_sem=sems.at[1, kind, slot],
                device_id=other, device_id_type=MESH,
            )
            for kind, (source, target) in enumerate(((out_g, in_g), (out_u, in_u), (out_d, in_d)))
        ]

    half = tokens // 2
    cross = [
        plain_copy(n_hbm.at[pl.ds(at * half, half), :], far_n.at[pl.ds(at * half, half), :], far_sems, at, beside())
        for at in range(2)
    ]
    share = [
        plain_copy(far_n.at[pl.ds(at * half, half), :], far_on.at[pl.ds(at * half, half), :], far_sems, 2 + at, other)
        for at in range(2)
    ]
    peer = {"expert": 1 - side}
    turn_up = plain_copy(far_g0, far_g1, far_sems, 4, peer)
    share_up = plain_copy(far_g1, far_og1, far_sems, 5, other)
    early = [
        plain_copy(source, target, far_sems, 6 + at, other)
        for at, (source, target) in enumerate(((far_g0, far_og0), (far_m, far_om)))
    ]
    loads = [
        pltpu.make_async_copy(source, g_ref.at[pl.ds(at * half, half), :], up_sems.at[at])
        for at, source in enumerate((own_up, peer_up))
    ]

    @pl.when(step == 0)
    def _():
        for copy in loads:
            copy.start()
        meet([(True, other), (True, beside()), (True, peer)])
        for copy in cross + early + [turn_up]:
            copy.start()

        def start(at, carry):
            rows = pl.ds(pl.multiple_of(at * CHUNK, CHUNK), CHUNK)
            gate, kept_gate = route_gates(n_ref[rows, :], marks_ref[rows, :], wr_ref[...])
            gates[rows, :] = gate
            kept_gates[rows, :] = kept_gate
            mix[rows, :] = jnp.zeros((CHUNK, width), F32)
            back[rows, :] = jnp.zeros((CHUNK, width), F32)
            gate_grads[rows, :] = jnp.zeros((CHUNK, experts_all), F32)
            return carry

        lax.fori_loop(0, chunks, start, 0)
        for at in range(chunks):
            nt[:, at * CHUNK : (at + 1) * CHUNK] = n_ref[at * CHUNK : (at + 1) * CHUNK, :].T
        for copy in loads:
            copy.wait()

    @pl.when(step == steps)
    def _():
        cross[0].wait_recv()
        share[0].start()
        turn_up.wait_recv()
        share_up.start()

    for expert in range(group):
        wgs[:, expert * hid : (expert + 1) * hid] = wg_ref[expert]
        wus[:, expert * hid : (expert + 1) * hid] = wu_ref[expert]
    first = step < steps
    block = jnp.where(first, (1 - core) * steps + step, core * steps + step - steps)
    column = side * (experts_all // 2) + block * group

    for at in range(chunks):
        rows = slice(at * CHUNK, (at + 1) * CHUNK)
        token = n_ref[rows, :]
        down = wd_ref[...].reshape(group * hid, width)
        pulled = pulled_ref[0, rows, :].astype(F32)
        weight = spread_gates(kept_gates[rows, :], column, group, hid)
        hidden, gated, gate_grad, up_grad = hidden_terms(token, pulled, weight, wgs[...], wus[...])
        products = hidden * pulled
        grads = gate_grads[rows, :]
        for expert in range(group):
            product = jnp.sum(products[:, expert * hid : (expert + 1) * hid], axis=1, keepdims=True)
            grads = grads + jnp.where(lane == column + expert, product, 0.0)
        gate_grads[rows, :] = grads
        ght[:, rows] = gated.T
        dgs[rows, :] = gate_grad
        dus[rows, :] = up_grad
        mix[rows, :] += matmul(gated, down)
        back[rows, :] += matmul_nt(gate_grad, wgs[...]) + matmul_nt(up_grad, wus[...])

    def weight_grads(store_rows, store_down):
        for at in range(width // CHUNK):
            rows = slice(at * CHUNK, (at + 1) * CHUNK)
            turned = nt[rows, :]
            gate_part = matmul(turned, dgs[...])
            up_part = matmul(turned, dus[...])
            for expert in range(group):
                inner = slice(expert * hid, (expert + 1) * hid)
                store_rows(expert, rows, gate_part[:, inner], up_part[:, inner])
        down_part = matmul(ght[...], g_ref[...])
        for expert in range(group):
            store_down(expert, down_part[expert * hid : (expert + 1) * hid, :])

    @pl.when(first)
    def _():
        def store_rows(expert, rows, gate_part, up_part):
            out_g[step, expert, rows, :] = gate_part.astype(BF)
            out_u[step, expert, rows, :] = up_part.astype(BF)

        def store_down(expert, part):
            out_d[step, expert] = part.astype(BF)

        weight_grads(store_rows, store_down)
        for copy in copies(step):
            copy.start()

    @pl.when(step >= steps)
    def _():
        slot = step - steps
        for copy in copies(slot):
            copy.wait_recv()

        def store_rows(expert, rows, gate_part, up_part):
            dwg_ref[expert, rows, :] = (gate_part + in_g[slot, expert, rows, :].astype(F32)).astype(BF)
            dwu_ref[expert, rows, :] = (up_part + in_u[slot, expert, rows, :].astype(F32)).astype(BF)

        def store_down(expert, part):
            dwd_ref[expert] = (part + in_d[slot, expert].astype(F32)).astype(BF)

        weight_grads(store_rows, store_down)
        for copy in copies(slot):
            copy.wait_send()

    @pl.when(step == 2 * steps - 1)
    def _():
        cross[1].wait_recv()
        share[1].start()
        route_ref[...] = jnp.zeros(route_ref.shape, F32)

        def finish(at, carry):
            rows = pl.ds(pl.multiple_of(at * CHUNK, CHUNK), CHUNK)
            mix_ref[rows, :] = mix[rows, :].astype(BF)
            grads = gate_grads[rows, :] * kept_gates[rows, :]
            chosen_grad = grads - gates[rows, :] * jnp.sum(grads, axis=1, keepdims=True)
            low = chosen_grad.astype(BF)
            back_ref[rows, :] = (back[rows, :] + matmul(low, wr_ref[...])).astype(BF)
            route_ref[...] += matmul_tn(low, n_ref[rows, :])
            return carry

        lax.fori_loop(0, chunks, finish, 0)
        for copy in cross + [turn_up]:
            copy.wait_send()
        for copy in share + early + [share_up]:
            copy.wait()


def experts(normed, marks, w_router, upstream, peer_up, far_up, far_marks, w_gate, w_up, w_down, pulled):
    tokens, width = normed.shape
    count, _, hid = w_gate.shape
    half = count // 2
    steps = half // GROUP
    experts_all = w_router.shape[0]
    once = pl.Buffered(1)
    whole = lambda step: (0, 0)

    def picked(step):
        core = lax.rem(lax.axis_index("dp"), 2)
        return (jnp.where(step < steps, (1 - core) * steps + step, core * steps + step - steps), 0, 0)

    own = lambda step: (jnp.maximum(step - steps, 0), 0, 0)
    args = [normed, marks, w_router]
    specs = [pl.BlockSpec(array.shape, whole, pipeline_mode=once) for array in args]
    args += [normed, upstream, peer_up, far_up, far_marks]
    specs += [pl.BlockSpec(memory_space=pl.ANY)] * 5
    up_block, down_block = (GROUP, width, hid), (GROUP, hid, width)
    specs += [pl.BlockSpec(up_block, picked), pl.BlockSpec(up_block, picked), pl.BlockSpec(down_block, picked)]
    specs += [pl.BlockSpec((1, tokens, GROUP * hid), picked)]
    gate_scratch = pltpu.VMEM((tokens, experts_all), F32)
    rows_scratch = pltpu.VMEM((tokens, width), F32)
    swap_scratch = [
        pltpu.VMEM((steps,) + up_block, BF),
        pltpu.VMEM((steps,) + up_block, BF),
        pltpu.VMEM((steps,) + down_block, BF),
    ]
    return pl.pallas_call(
        expert_kernel,
        out_shape=[
            jax.ShapeDtypeStruct((half, width, hid), BF),
            jax.ShapeDtypeStruct((half, width, hid), BF),
            jax.ShapeDtypeStruct((half, hid, width), BF),
            jax.ShapeDtypeStruct((tokens, width), BF),
            jax.ShapeDtypeStruct((tokens, width), BF),
            jax.ShapeDtypeStruct((experts_all, width), F32),
            jax.ShapeDtypeStruct((tokens, width), BF),
            jax.ShapeDtypeStruct((tokens, width), BF),
            jax.ShapeDtypeStruct(far_up.shape, BF),
            jax.ShapeDtypeStruct(far_up.shape, BF),
            jax.ShapeDtypeStruct(far_up.shape, BF),
            jax.ShapeDtypeStruct(far_marks.shape, BF),
        ],
        grid=(2 * steps,),
        in_specs=specs,
        out_specs=[
            pl.BlockSpec(up_block, own),
            pl.BlockSpec(up_block, own),
            pl.BlockSpec(down_block, own),
            pl.BlockSpec((tokens, width), whole, pipeline_mode=once),
            pl.BlockSpec((tokens, width), whole, pipeline_mode=once),
            pl.BlockSpec((experts_all, width), whole, pipeline_mode=once),
        ]
        + [pl.BlockSpec(memory_space=pl.ANY)] * 6,
        scratch_shapes=[
            gate_scratch, gate_scratch, gate_scratch, rows_scratch, rows_scratch,
            pltpu.VMEM((width, tokens), BF),
            pltpu.VMEM((width, GROUP * hid), BF),
            pltpu.VMEM((width, GROUP * hid), BF),
            pltpu.VMEM((GROUP * hid, tokens), BF),
            pltpu.VMEM((tokens, GROUP * hid), BF),
            pltpu.VMEM((tokens, GROUP * hid), BF),
        ]
        + swap_scratch
        + swap_scratch
        + [pltpu.SemaphoreType.DMA((2, 3, steps)), pltpu.SemaphoreType.DMA((2, 8)), pltpu.VMEM((tokens, width), BF), pltpu.SemaphoreType.DMA((2,))],
        compiler_params=pltpu.CompilerParams(
            dimension_semantics=("arbitrary",), collective_id=3, has_side_effects=True, vmem_limit_bytes=60 * MIB
        ),
        cost_estimate=pl.CostEstimate(
            flops=18 * tokens * width * count * hid,
            bytes_accessed=12 * count * width * hid,
            transcendentals=tokens * count * hid,
        ),
        name="experts",
    )(*args, w_gate, w_up, w_down, pulled)


def finish_kernel(core_ref, *refs):
    ins, outs = refs[:13], refs[13:]
    part, at = pl.program_id(0), pl.program_id(1)
    mine, other = ins[:3], ins[3:6]
    wide_mine, wide_other, tall_mine, tall_other, gains, grad, block = ins[6:]
    out_g, out_u, out_d, out_q, out_k, out_v, out_o, out_r, out_first, out_second, out_grad, out_block = outs
    for place, sources in enumerate((mine, other)):

        @pl.when(part == place)
        def _():
            for source, target in zip(sources, (out_g, out_u, out_d)):
                target[...] = source[...].astype(F32)

    core = core_ref[0]
    queries, kv = out_q.shape[1], out_k.shape[1]
    half = out_q.shape[0] // 2
    tall = tall_mine.shape[0]
    outs_rows = out_o.shape[0]

    @pl.when((part == 0) & (at == 0))
    def _():
        out_grad[...] = grad[...]
        out_block[...] = block[...]
        out_first[...] = gains[0:1, :]
        out_second[...] = gains[1:2, :]

    for place in range(2):

        @pl.when((part == place) & (at == 1))
        def _():
            own = core == place
            summed = jnp.where(own, wide_mine[...].astype(F32), wide_other[...].astype(F32))
            rows = slice(place * half, (place + 1) * half)
            out_q[rows, :] = summed[:, :queries]
            out_k[rows, :] = summed[:, queries : queries + kv]
            out_v[rows, :] = summed[:, queries + kv :]
            tall_sum = jnp.where(own, tall_mine[...].astype(F32), tall_other[...].astype(F32))
            top = min((place + 1) * tall, outs_rows)
            out_o[place * tall : top, :] = tall_sum[: top - place * tall, :]
            if place == 1:
                out_r[...] = tall_sum[top - place * tall :, :]


def finish(core, sums, others, wide, wide_back, tall, tall_back, gains, grad, block, queries, outs_rows):
    half = sums[0].shape[0]
    width = grad.shape[1]
    kv = (wide.shape[1] - queries) // 2
    experts_all = 2 * tall.shape[0] - outs_rows
    whole = lambda shape: pl.BlockSpec(shape, lambda part, at, core: (0,) * len(shape), pipeline_mode=pl.Buffered(1))
    step = 4
    count = half // step
    single = lambda array, index: pl.BlockSpec((step,) + array.shape[1:], index)
    first = lambda part, at, core: (jnp.where(part == 0, at, count - 1), 0, 0)
    second = lambda part, at, core: (jnp.where(part == 0, 0, at), 0, 0)
    placed = lambda part, at, core: (jnp.where(part == 0, core[0], 1 - core[0]) * count + at, 0, 0)
    rest = [wide, wide_back, tall, tall_back, gains, grad, block]
    wide_shape = lambda shape: jax.ShapeDtypeStruct(shape, F32)
    shapes = [
        (2 * wide.shape[0], queries), (2 * wide.shape[0], kv), (2 * wide.shape[0], kv),
        (outs_rows, width), (experts_all, width), (1, width), (1, width),
    ]
    return pl.pallas_call(
        finish_kernel,
        out_shape=[wide_shape((2 * half,) + item.shape[1:]) for item in sums]
        + [wide_shape(shape) for shape in shapes]
        + [jax.ShapeDtypeStruct(grad.shape, BF), jax.ShapeDtypeStruct(block.shape, BF)],
        grid_spec=pltpu.PrefetchScalarGridSpec(
            num_scalar_prefetch=1,
            grid=(2, count),
            in_specs=[single(item, first) for item in sums]
            + [single(item, second) for item in others]
            + [whole(item.shape) for item in rest],
            out_specs=[single(item, placed) for item in sums]
            + [whole(shape) for shape in shapes + [grad.shape, block.shape]],
        ),
        compiler_params=pltpu.CompilerParams(vmem_limit_bytes=60 * MIB),
        name="finish",
    )(core, *sums, *others, *rest)


def fast_device(
    block_input, first_gain, w_query, key_weight, value_weight, w_output, second_gain, w_router,
    w_gate, w_up, w_down, expert_ids, slot_index, piece_start_offsets, upstream,
):
    rows, width = block_input.shape
    experts_all = w_router.shape[1]
    core = lax.axis_index("dp") % 2
    positions = lax.axis_index("expert") * rows + jnp.arange(rows, dtype=jnp.int32)
    lanes = jnp.arange(128, dtype=jnp.int32) % (HEAD_SIZE // 2)
    inverse = jnp.exp(lanes.astype(F32) * (-2.0 * math.log(rope_base) / HEAD_SIZE))
    angle = positions.astype(F32)[:, None] * inverse[None, :]
    cosines, sines = jnp.cos(angle), jnp.sin(angle)
    routes = w_router.T
    (
        first_normed, query_rot, keys, values, attended, lse, residual, normed_all, marks, far_marks, peer_up, far_up,
        pulled,
    ) = front(
        piece_start_offsets, block_input, first_gain, second_gain, w_query, key_weight, value_weight, w_output,
        cosines, sines, expert_ids.T, slot_index.T, upstream, experts_all, w_down,
    )
    keys, values = keys.reshape(2 * rows, -1), values.reshape(2 * rows, -1)
    normed_all = normed_all.reshape(2 * rows, width)
    marks = marks.reshape(2 * rows, 2 * experts_all)
    far_marks = far_marks.reshape(2 * rows, 2 * experts_all)
    dwg, dwu, dwd, mix, back, route, *far = experts(
        normed_all, marks, routes, upstream, peer_up, far_up, far_marks, w_gate, w_up, w_down, pulled
    )
    far_normed, far_other_normed, far_peer_up, far_other_up, far_other_peer_up, far_other_marks = far
    residual_grad, residual_low, grad_second, route, mixed, sums = residual_gradient(
        back, mix, route, residual, upstream, second_gain, routes,
        (
            far_normed, far_other_normed, far_up, far_peer_up, far_other_up, far_other_peer_up,
            far_marks, far_other_marks,
        ),
        w_gate, w_up, w_down, (dwg, dwu, dwd),
    )
    grad_input, wide, wide_back, tall, tall_back, gains, block_output = input_gradient(
        piece_start_offsets, block_input, residual_grad, first_gain, first_normed, w_query, key_weight, value_weight,
        w_output, cosines, sines, query_rot, keys, values, lse, attended, residual_low, route, grad_second, mixed, residual,
    )
    grad_gate, grad_up, grad_down, grad_query, grad_key, grad_value, grad_output, grad_router, first, second, grad, block = finish(
        core[None].astype(jnp.int32), sums[:3], sums[3:], wide, wide_back, tall, tall_back, gains,
        grad_input.reshape(rows, width), block_output.reshape(rows, width // 4), w_query.shape[1], w_output.shape[0],
    )
    return (
        block, grad, first[0], grad_query, grad_key, grad_value, grad_output, second[0], grad_router.T,
        grad_gate, grad_up, grad_down,
    )


def solution(mesh):
    fast = mesh.shape["expert"] == 2 and mesh.shape["dp"] == 4 and mesh.shape["tensor"] == 4
    placed = (
        P(("dp", "expert"), None),
        P(),
        P(None, "tensor"),
        P(None, "tensor"),
        P(None, "tensor"),
        P("tensor", None),
        P(),
        P(),
        P("expert", None, "tensor"),
        P("expert", None, "tensor"),
        P("expert", "tensor", None),
        P(("dp", "expert"), None),
        P(("dp", "expert"), None),
        P("dp", None),
        P(("dp", "expert"), None),
    )
    return jax.shard_map(
        fast_device if fast else general_device,
        mesh=mesh,
        in_specs=placed,
        out_specs=(
            P(("dp", "expert"), "tensor"),
            P(("dp", "expert"), None),
            P(),
            P(None, "tensor"),
            P(None, "tensor"),
            P(None, "tensor"),
            P("tensor", None),
            P(),
            P(),
            P("expert", None, "tensor"),
            P("expert", None, "tensor"),
            P("expert", "tensor", None),
        ),
        check_vma=False,
    )
```

```python
import functools
import math

import jax
import jax.numpy as jnp
from jax import lax
from jax.experimental import pallas as pl
from jax.experimental.pallas import tpu as pltpu
from jax.sharding import PartitionSpec as P

HEAD_SIZE = 64
TOPK = 8
PIC = 256


epsilon = 1e-06
rope_base = 10000.0
masked_score = -1e30


def rope_tables(positions):
    steps = jnp.arange(HEAD_SIZE // 2, dtype=jnp.float32)
    inverse = jnp.exp(steps * (-2.0 * math.log(rope_base) / HEAD_SIZE))
    angle = positions.astype(jnp.float32)[:, None] * inverse[None, :]
    return (jnp.cos(angle), jnp.sin(angle))


def apply_rotary(values, cosine_table, sine_table):
    half = values.shape[-1] // 2
    first = values[..., :half]
    second = values[..., half:]
    cosine_table = cosine_table[:, None, :]
    sine_table = sine_table[:, None, :]
    return jnp.concatenate(
        [first * cosine_table - second * sine_table, second * cosine_table + first * sine_table],
        axis=-1,
    )


def unrotate(values, cosine_table, sine_table):
    half = values.shape[-1] // 2
    first = values[..., :half]
    second = values[..., half:]
    cosine_table = cosine_table[:, None, :]
    sine_table = sine_table[:, None, :]
    return jnp.concatenate(
        [first * cosine_table + second * sine_table, second * cosine_table - first * sine_table],
        axis=-1,
    )


def piece_ids(positions, offsets):
    span = 2 * PIC
    window = positions // span
    within = positions - window * span
    count = offsets.shape[0]
    match = window[:, None] == jnp.arange(count, dtype=jnp.int32)[None, :]
    start = jnp.sum(jnp.where(match, offsets[None, :], 0), axis=1)
    inside = (window < count) & (within >= start) & (within < start + PIC)
    return jnp.where(inside, window, -1)


def matmul(left, right):
    return jnp.dot(left, right, preferred_element_type=jnp.float32)


def matmul_nt(left, right):
    return lax.dot_general(
        left, right, (((1,), (1,)), ((), ())), preferred_element_type=jnp.float32
    )


def matmul_tn(left, right):
    return lax.dot_general(
        left, right, (((0,), (0,)), ((), ())), preferred_element_type=jnp.float32
    )


def norm_scale(values):
    return lax.rsqrt(jnp.mean(values * values, axis=-1, keepdims=True) + epsilon)


def norm_back(grad, unit, scale, gain):
    weighted = grad * gain
    return scale * (weighted - unit * jnp.mean(weighted * unit, axis=-1, keepdims=True))


def general_device(
    block_input,
    first_gain,
    w_query,
    key_weight,
    value_weight,
    w_output,
    second_gain,
    w_router,
    w_gate,
    w_up,
    w_down,
    expert_ids,
    slot_index,
    piece_start_offsets,
    upstream,
):
    rows_here = block_input.shape[0]
    width = block_input.shape[1]
    groups = lax.axis_size("expert")
    length = rows_here * groups
    local_heads = w_query.shape[1] // HEAD_SIZE
    local_kv = key_weight.shape[1] // HEAD_SIZE
    sharing = local_heads // local_kv
    head_rows = sharing * rows_here
    experts_all = w_router.shape[1]
    capacity = TOPK * rows_here // experts_all
    slots_all = experts_all * capacity
    score_scale = HEAD_SIZE ** (-0.5)
    positions = lax.axis_index("expert") * rows_here + jnp.arange(rows_here, dtype=jnp.int32)
    cosine_table, sine_table = rope_tables(positions)
    inputs = block_input.astype(jnp.float32)
    first_scale = norm_scale(inputs)
    first_unit = inputs * first_scale
    first_normed = (first_unit * first_gain).astype(jnp.bfloat16)
    query_rot = apply_rotary(
        matmul(first_normed, w_query).reshape(rows_here, local_heads, HEAD_SIZE),
        cosine_table,
        sine_table,
    ).astype(jnp.bfloat16)
    key_rot = (
        apply_rotary(
            matmul(first_normed, key_weight).reshape(rows_here, local_kv, HEAD_SIZE),
            cosine_table,
            sine_table,
        )
        .astype(jnp.bfloat16)
        .reshape(rows_here, local_kv * HEAD_SIZE)
    )
    value_low = matmul(first_normed, value_weight).astype(jnp.bfloat16)
    keys_all, values_all = (
        lax.all_gather(key_rot, "expert", axis=0, tiled=True),
        lax.all_gather(value_low, "expert", axis=0, tiled=True),
    )
    block = min(512, length)
    blocks = length // block

    def by_block(array):
        return array.reshape(blocks, block, local_kv, HEAD_SIZE).transpose(0, 2, 1, 3)

    def by_rows(stacked):
        return stacked.transpose(0, 2, 1, 3).reshape(length, local_kv * HEAD_SIZE)

    def head_major(array):
        return (
            array.reshape(rows_here, local_kv, sharing, HEAD_SIZE)
            .transpose(1, 2, 0, 3)
            .reshape(local_kv, head_rows, HEAD_SIZE)
        )

    def row_major(array):
        return (
            array.reshape(local_kv, sharing, rows_here, HEAD_SIZE)
            .transpose(2, 0, 1, 3)
            .reshape(rows_here, local_heads * HEAD_SIZE)
        )

    key_blocks = by_block(keys_all)
    value_blocks = by_block(values_all)
    block_starts = jnp.arange(blocks, dtype=jnp.int32) * block
    query_heads = head_major(query_rot.reshape(rows_here, local_heads * HEAD_SIZE))
    offsets = piece_start_offsets[0]
    key_pieces = piece_ids(jnp.arange(length, dtype=jnp.int32), offsets)
    query_pieces = jnp.tile(piece_ids(positions, offsets), sharing)
    query_places = jnp.tile(positions, sharing)

    def block_scores(key_block, start):
        places = start + jnp.arange(block, dtype=jnp.int32)
        pieces = lax.dynamic_slice_in_dim(key_pieces, start, block)
        causal = places[None, :] <= query_places[:, None]
        same = (pieces[None, :] == query_pieces[:, None]) & (query_pieces[:, None] >= 0)
        scores = (
            jnp.einsum("hqd,hkd->hqk", query_heads, key_block, preferred_element_type=jnp.float32)
            * score_scale
        )
        return (scores, (causal | same)[None])

    def max_step(carry, operands):
        running_max, running_sum = carry
        key_block, start = operands
        scores, allowed = block_scores(key_block, start)
        scores = jnp.where(allowed, scores, masked_score)
        new_max = jnp.maximum(running_max, jnp.max(scores, axis=-1))
        weights = jnp.where(allowed, jnp.exp(scores - new_max[..., None]), 0.0)
        new_sum = running_sum * jnp.exp(running_max - new_max) + jnp.sum(weights, axis=-1)
        return ((new_max, new_sum), None)

    start_max = jnp.full((local_kv, head_rows), masked_score, jnp.float32)
    start_sum = jnp.zeros((local_kv, head_rows), jnp.float32)
    (row_max, row_sum), _ = lax.scan(max_step, (start_max, start_sum), (key_blocks, block_starts))
    log_total = row_max + jnp.log(row_sum)

    def block_probs(key_block, start):
        scores, allowed = block_scores(key_block, start)
        return jnp.where(allowed, jnp.exp(scores - log_total[..., None]), 0.0)

    def value_step(total, operands):
        key_block, value_block, start = operands
        probs = block_probs(key_block, start).astype(jnp.bfloat16)
        return (
            total
            + jnp.einsum("hqk,hkd->hqd", probs, value_block, preferred_element_type=jnp.float32),
            None,
        )

    mixed_output, _ = lax.scan(
        value_step,
        jnp.zeros((local_kv, head_rows, HEAD_SIZE), jnp.float32),
        (key_blocks, value_blocks, block_starts),
    )
    attended = row_major(mixed_output).astype(jnp.bfloat16)
    attention = lax.psum(matmul(attended, w_output), "tensor")
    residual = inputs + attention
    second_scale = norm_scale(residual)
    second_unit = residual * second_scale
    second_normed = (second_unit * second_gain).astype(jnp.bfloat16)
    logits = matmul(second_normed, w_router)
    chosen = jnp.take_along_axis(logits, expert_ids, axis=1)
    gates = jax.nn.softmax(chosen, axis=-1)
    row_ids = jnp.arange(rows_here, dtype=jnp.int32)
    flat = jnp.where(slot_index >= 0, expert_ids * capacity + slot_index, slots_all)
    selector = (
        jnp.zeros((slots_all, rows_here), jnp.bfloat16)
        .at[flat.reshape(-1), jnp.repeat(row_ids, TOPK)]
        .set(1.0, mode="drop")
    )
    dispatched = (
        matmul(selector, second_normed).astype(jnp.bfloat16).reshape(experts_all, capacity, width)
    )
    expert_rows = lax.all_to_all(dispatched, "expert", split_axis=0, concat_axis=1, tiled=True)
    gate_in = jnp.einsum("ebd,edf->ebf", expert_rows, w_gate, preferred_element_type=jnp.float32)
    up_in = jnp.einsum("ebd,edf->ebf", expert_rows, w_up, preferred_element_type=jnp.float32)
    sigmoid_gate = jax.nn.sigmoid(gate_in)
    silu_gate = gate_in * sigmoid_gate
    hidden = (silu_gate * up_in).astype(jnp.bfloat16)
    partial_out = jnp.einsum("ebf,efd->ebd", hidden, w_down, preferred_element_type=jnp.float32)
    expert_part = lax.psum_scatter(
        partial_out.astype(jnp.bfloat16), "tensor", scatter_dimension=2, tiled=True
    )
    returned = lax.all_to_all(expert_part, "expert", split_axis=1, concat_axis=0, tiled=True)
    quarter = returned.shape[2]
    padded_out = jnp.concatenate(
        [returned.reshape(slots_all, quarter), jnp.zeros((1, quarter), jnp.bfloat16)], axis=0
    )
    feature_start = lax.axis_index("tensor") * quarter
    grad_full = upstream.astype(jnp.float32)
    grad_part = lax.dynamic_slice_in_dim(grad_full, feature_start, quarter, 1)
    mixture = jnp.zeros((rows_here, quarter), jnp.float32)
    gate_terms = []
    for pick in range(TOPK):
        picked = padded_out[flat[:, pick]].astype(jnp.float32)
        mixture = mixture + gates[:, pick : pick + 1] * picked
        gate_terms.append(jnp.sum(grad_part * picked, axis=1))
    gate_part = jnp.stack(gate_terms, axis=1)
    block_output = (lax.dynamic_slice_in_dim(residual, feature_start, quarter, 1) + mixture).astype(
        jnp.bfloat16
    )
    slot_gates = (
        jnp.zeros((slots_all + 1,), jnp.float32)
        .at[flat.reshape(-1)]
        .set(gates.reshape(-1))[:slots_all]
    )
    grad_slots = (
        (matmul(selector, upstream) * slot_gates[:, None])
        .astype(jnp.bfloat16)
        .reshape(experts_all, capacity, width)
    )
    grad_rows_in = lax.all_to_all(grad_slots, "expert", split_axis=0, concat_axis=1, tiled=True)
    hidden_grad = jnp.einsum(
        "ebd,efd->ebf", grad_rows_in, w_down, preferred_element_type=jnp.float32
    )
    grad_down = jnp.einsum("ebf,ebd->efd", hidden, grad_rows_in, preferred_element_type=jnp.float32)
    gate_in_grad = (
        hidden_grad * up_in * (sigmoid_gate * (1.0 + gate_in * (1.0 - sigmoid_gate)))
    ).astype(jnp.bfloat16)
    up_in_grad = (hidden_grad * silu_gate).astype(jnp.bfloat16)
    grad_gate = jnp.einsum(
        "ebd,ebf->edf", expert_rows, gate_in_grad, preferred_element_type=jnp.float32
    )
    grad_up = jnp.einsum(
        "ebd,ebf->edf", expert_rows, up_in_grad, preferred_element_type=jnp.float32
    )
    rows_part = jnp.einsum("ebf,edf->ebd", gate_in_grad, w_gate, preferred_element_type=jnp.float32)
    rows_part = rows_part + jnp.einsum(
        "ebf,edf->ebd", up_in_grad, w_up, preferred_element_type=jnp.float32
    )
    rows_back = lax.all_to_all(
        rows_part.astype(jnp.bfloat16), "expert", split_axis=1, concat_axis=0, tiled=True
    ).astype(rows_part.dtype)
    padded_back = jnp.concatenate(
        [rows_back.reshape(slots_all, width), jnp.zeros((1, width), jnp.float32)], axis=0
    )
    second_part = jnp.zeros((rows_here, width), jnp.float32)
    for pick in range(TOPK):
        second_part = second_part + padded_back[flat[:, pick]]
    second_sum, gate_grads = (
        lax.psum(second_part.astype(jnp.bfloat16), "tensor").astype(jnp.float32),
        lax.psum(gate_part.astype(jnp.bfloat16), "tensor").astype(jnp.float32),
    )
    chosen_grad = gates * (gate_grads - jnp.sum(gates * gate_grads, axis=1, keepdims=True))
    expert_axis = jnp.arange(experts_all, dtype=jnp.int32)
    logit_grad = jnp.zeros((rows_here, experts_all), jnp.float32)
    for pick in range(TOPK):
        logit_grad = logit_grad + jnp.where(
            expert_ids[:, pick : pick + 1] == expert_axis[None, :],
            chosen_grad[:, pick : pick + 1],
            0.0,
        )
    logit_low = logit_grad.astype(jnp.bfloat16)
    grad_router = matmul_tn(second_normed, logit_low)
    second_grad = second_sum + matmul_nt(logit_low, w_router)
    grad_second = jnp.sum(second_grad * second_unit, axis=0)
    residual_grad = grad_full + norm_back(second_grad, second_unit, second_scale, second_gain)
    residual_low = residual_grad.astype(jnp.bfloat16)
    grad_output = matmul_tn(attended, residual_low)
    attended_grad = head_major(matmul_nt(residual_low, w_output).astype(jnp.bfloat16))

    def delta_step(total, operands):
        key_block, value_block, start = operands
        probs = block_probs(key_block, start)
        prob_grad = jnp.einsum(
            "hqd,hkd->hqk", attended_grad, value_block, preferred_element_type=jnp.float32
        )
        return (total + jnp.sum(probs * prob_grad, axis=-1), None)

    delta, _ = lax.scan(
        delta_step,
        jnp.zeros((local_kv, head_rows), jnp.float32),
        (key_blocks, value_blocks, block_starts),
    )

    def grad_step(query_total, operands):
        key_block, value_block, start = operands
        probs = block_probs(key_block, start)
        prob_grad = jnp.einsum(
            "hqd,hkd->hqk", attended_grad, value_block, preferred_element_type=jnp.float32
        )
        score_grad = (probs * (prob_grad - delta[..., None])).astype(jnp.bfloat16)
        query_total = (
            query_total
            + jnp.einsum("hqk,hkd->hqd", score_grad, key_block, preferred_element_type=jnp.float32)
            * score_scale
        )
        key_grad = (
            jnp.einsum("hqk,hqd->hkd", score_grad, query_heads, preferred_element_type=jnp.float32)
            * score_scale
        )
        value_grad = jnp.einsum(
            "hqk,hqd->hkd",
            probs.astype(jnp.bfloat16),
            attended_grad,
            preferred_element_type=jnp.float32,
        )
        return (query_total, (key_grad, value_grad))

    query_total, (key_stack, value_stack) = lax.scan(
        grad_step,
        jnp.zeros((local_kv, head_rows, HEAD_SIZE), jnp.float32),
        (key_blocks, value_blocks, block_starts),
    )
    key_back, value_back = (
        lax.psum_scatter(
            by_rows(key_stack).astype(jnp.bfloat16), "expert", scatter_dimension=0, tiled=True
        ).astype(jnp.float32),
        lax.psum_scatter(
            by_rows(value_stack).astype(jnp.bfloat16), "expert", scatter_dimension=0, tiled=True
        ).astype(jnp.float32),
    )
    query_grad = (
        unrotate(
            row_major(query_total).reshape(rows_here, local_heads, HEAD_SIZE),
            cosine_table,
            sine_table,
        )
        .astype(jnp.bfloat16)
        .reshape(rows_here, local_heads * HEAD_SIZE)
    )
    key_grad = (
        unrotate(key_back.reshape(rows_here, local_kv, HEAD_SIZE), cosine_table, sine_table)
        .astype(jnp.bfloat16)
        .reshape(rows_here, local_kv * HEAD_SIZE)
    )
    value_grad = value_back.astype(jnp.bfloat16)
    grad_query = matmul_tn(first_normed, query_grad)
    grad_key = matmul_tn(first_normed, key_grad)
    grad_value = matmul_tn(first_normed, value_grad)
    first_part = (
        matmul_nt(query_grad, w_query)
        + matmul_nt(key_grad, key_weight)
        + matmul_nt(value_grad, value_weight)
    )
    first_grad = lax.psum(first_part.astype(jnp.bfloat16), "tensor").astype(jnp.float32)
    grad_first = jnp.sum(first_grad * first_unit, axis=0)
    grad_input = (
        residual_grad + norm_back(first_grad, first_unit, first_scale, first_gain)
    ).astype(jnp.bfloat16)
    dense = lax.psum(
        (grad_query, grad_key, grad_value, grad_output, grad_router, grad_first, grad_second),
        ("dp", "expert"),
    )
    expert_sums = (
        lax.psum(grad_gate.astype(jnp.bfloat16), "dp").astype(jnp.float32),
        lax.psum(grad_up.astype(jnp.bfloat16), "dp").astype(jnp.float32),
        lax.psum(grad_down.astype(jnp.bfloat16), "dp").astype(jnp.float32),
    )
    return (
        block_output,
        grad_input,
        dense[5],
        dense[0],
        dense[1],
        dense[2],
        dense[3],
        dense[6],
        dense[4],
        expert_sums[0],
        expert_sums[1],
        expert_sums[2],
    )


BF = jnp.bfloat16
F32 = jnp.float32
MIB = 1 << 20


def vmem_spec():
    return pl.BlockSpec(memory_space=pltpu.VMEM)


def smem_spec():
    return pl.BlockSpec(memory_space=pltpu.SMEM)


def allowed_pairs(offsets_ref, rows, start, count):
    side = lax.axis_index("expert")
    here = start + lax.broadcasted_iota(jnp.int32, (count, 1), 0)
    keys = lax.broadcasted_iota(jnp.int32, (1, 2 * rows), 1)
    query_place = side * rows + here
    key_place = jnp.where(keys < rows, side * rows + keys, (1 - side) * rows + keys - rows)
    span = 2 * PIC

    def piece(places):
        window = places // span
        within = places - window * span
        start = jnp.where(window == 0, offsets_ref[0, 0], offsets_ref[0, 1])
        inside = (within >= start) & (within < start + PIC)
        return jnp.where(inside, window, -1)

    query_piece = piece(query_place)
    key_piece = piece(key_place)
    return (key_place <= query_place) | ((key_piece == query_piece) & (query_piece >= 0))


def turn(values, first):
    wide = values.shape[1]
    half = HEAD_SIZE // 2
    return jnp.where(
        first, -pltpu.roll(values, wide - half, 1), pltpu.roll(values, half, 1)
    )


MESH = pl.DeviceIdType.MESH
PART = 32
LAG = 3
LINK_COST = pl.CostEstimate(flops=4 * 10**10, bytes_accessed=10**7, transcendentals=0)


def meet(partners):
    barrier = pltpu.get_barrier_semaphore()
    count = 0
    for here, device in partners:
        here = jnp.asarray(here)

        @pl.when(here)
        def _():
            pl.semaphore_signal(barrier, inc=1, device_id=device, device_id_type=MESH)

        count = count + here.astype(jnp.int32)
    pl.semaphore_wait(barrier, count)


def line_partners():
    place = lax.axis_index("tensor")
    last = lax.axis_size("tensor") - 1
    return [(place > 0, {"tensor": place - 1}), (place < last, {"tensor": place + 1})]


class Line:
    def __init__(self, parts, term, from_left, from_right, to_right, to_left, sems, lag=LAG):
        self.lag = lag
        self.place = lax.axis_index("tensor")
        self.last = lax.axis_size("tensor") - 1
        self.parts = parts
        self.term = term
        self.from_left, self.from_right = from_left, from_right
        self.to_right, self.to_left = to_right, to_left
        self.sems = sems

    def copy(self, way, at):
        near = jnp.where(self.place < self.last, self.place + 1, self.place - 1)
        far = jnp.where(self.place > 0, self.place - 1, self.place + 1)
        source, target, device = (
            (self.to_right, self.from_left, near) if way == 0 else (self.to_left, self.from_right, far)
        )
        return pltpu.make_async_remote_copy(
            src_ref=source.at[at],
            dst_ref=target.at[at],
            send_sem=self.sems.at[2 * way, at],
            recv_sem=self.sems.at[2 * way + 1, at],
            device_id={"tensor": device},
            device_id_type=MESH,
        )

    def clear(self):
        @pl.when(self.place == 0)
        def _():
            self.from_left[...] = jnp.zeros(self.from_left.shape, self.from_left.dtype)

        @pl.when(self.place == self.last)
        def _():
            self.from_right[...] = jnp.zeros(self.from_right.shape, self.from_right.dtype)

    def step(self, at):
        for way in range(2):
            part = at - self.lag * (self.place if way == 0 else self.last - self.place)
            has_source = self.place > 0 if way == 0 else self.place < self.last
            has_target = self.place < self.last if way == 0 else self.place > 0
            arrived = self.from_left if way == 0 else self.from_right
            leaving = self.to_right if way == 0 else self.to_left
            valid = (part >= 0) & (part < self.parts)

            @pl.when(valid & has_source)
            def _():
                self.copy(way, part).wait_recv()

            @pl.when(valid & has_target)
            def _():
                leaving[part] = (self.term(part) + arrived[part].astype(F32)).astype(BF)
                self.copy(way, part).start()

    def total(self, part):
        return self.term(part) + self.from_left[part].astype(F32) + self.from_right[part].astype(F32)

    def drain(self):
        def wait(part, carry):
            @pl.when(self.place < self.last)
            def _():
                self.copy(0, part).wait_send()

            @pl.when(self.place > 0)
            def _():
                self.copy(1, part).wait_send()

            return carry

        lax.fori_loop(0, self.parts, wait, 0)


def line_scratch(parts, width, part=PART):
    return [pltpu.VMEM((parts, part, width), BF)] * 4 + [pltpu.SemaphoreType.DMA((4, parts))]


def peer_copy(source, target, sems, at):
    return pltpu.make_async_remote_copy(
        src_ref=source,
        dst_ref=target,
        send_sem=sems.at[0, at],
        recv_sem=sems.at[1, at],
        device_id={"expert": 1 - lax.axis_index("expert")},
        device_id_type=MESH,
    )


def scale_of(values):
    return lax.rsqrt(jnp.mean(values * values, axis=-1, keepdims=True) + epsilon)


def plain_copy(source, target, sems, at, device):
    return pltpu.make_async_remote_copy(
        src_ref=source, dst_ref=target, send_sem=sems.at[0, at], recv_sem=sems.at[1, at],
        device_id=device, device_id_type=MESH,
    )


def beside():
    return {"dp": lax.rem(lax.axis_index("dp") + 2, 4)}


def other_core():
    place = lax.axis_index("dp")
    return {"dp": place + 1 - 2 * lax.rem(place, 2)}


EARLY = 64
BAND = 256
OWN_PULL = 4
PEER_PULL = 21


def front_kernel(
    offsets_ref, x_ref, gain1_ref, gain2_ref, wq_ref, wk_ref, wv_ref, wo_ref, cos_ref, sin_ref, ids_ref, slots_ref, up_hbm, down_hbm,
    n1_ref, q_ref, k_ref, v_ref, att_ref, lse_ref, res_ref, n_ref, marks_ref, far_marks, up_peer, far_up, pulled_hbm,
    from_left, from_right, to_right, to_left, sems, peer_sems, far_sems, terms, downs, ups, pulled, load_sems, pulled_sems,
):
    parts = x_ref.shape[0]
    rows, width = n1_ref.shape
    side = lax.axis_index("expert")
    peer = {"expert": 1 - side}
    line = Line(parts, lambda at: terms[at], from_left, from_right, to_right, to_left, sems)
    meet(line_partners() + [(True, peer), (True, beside())])
    early, late = pl.ds(0, EARLY), pl.ds(EARLY, rows - EARLY)
    up_early = plain_copy(up_hbm.at[early, :], up_peer.at[early, :], far_sems, 0, peer)
    up_late = plain_copy(up_hbm.at[late, :], up_peer.at[late, :], far_sems, 1, peer)
    up_cross = plain_copy(up_hbm, far_up, far_sems, 2, beside())
    key_copy = plain_copy(k_ref.at[0], k_ref.at[1], far_sems, 3, peer)
    value_copy = plain_copy(v_ref.at[0], v_ref.at[1], far_sems, 4, peer)
    marks_copy = plain_copy(marks_ref.at[0], marks_ref.at[1], far_sems, 5, peer)
    marks_cross = plain_copy(marks_ref, far_marks, far_sems, 6, beside())
    up_early.start()
    up_cross.start()
    loads = [
        pltpu.make_async_copy(down_hbm, downs, load_sems.at[0]),
        pltpu.make_async_copy(up_hbm, ups.at[0], load_sems.at[1]),
        pltpu.make_async_copy(up_peer, ups.at[1], load_sems.at[2]),
    ]
    loads[0].start()
    loads[1].start()
    line.clear()

    values = x_ref[...].reshape(rows, width).astype(F32)
    normed = (values * scale_of(values) * gain1_ref[...]).astype(BF)
    n1_ref[...] = normed
    queries, kv = q_ref.shape[1], k_ref.shape[2]

    def rotate(array):
        wide = array.shape[1]
        lane = lax.broadcasted_iota(jnp.int32, (1, wide), 1)
        first = lane % HEAD_SIZE < HEAD_SIZE // 2
        cosines = jnp.concatenate([cos_ref[...]] * (wide // 128), axis=1)
        sines = jnp.concatenate([sin_ref[...]] * (wide // 128), axis=1)
        return (array * cosines + turn(array, first) * sines).astype(BF)

    k_ref[0] = rotate(matmul(normed, wk_ref[...]))
    key_copy.start()
    v_ref[0] = matmul(normed, wv_ref[...]).astype(BF)
    value_copy.start()
    experts_all = marks_ref.shape[2] // 2
    names = lax.broadcasted_iota(jnp.int32, (experts_all, 1), 0)
    chosen = jnp.zeros((experts_all, rows), F32)
    kept = jnp.zeros((experts_all, rows), F32)
    for pick in range(ids_ref.shape[0]):
        hit = jnp.where(ids_ref[pick : pick + 1, :] == names, 1.0, 0.0)
        chosen = chosen + hit
        kept = kept + jnp.where(slots_ref[pick : pick + 1, :] >= 0, hit, 0.0)
    marks_ref[0] = jnp.concatenate([chosen, kept], axis=0).T.astype(BF)
    marks_copy.start()
    up_late.start()
    q_ref[...] = rotate(matmul(normed, wq_ref[...]))
    key_copy.wait_recv()
    value_copy.wait_recv()
    sharing = queries // kv

    def attend(at):
        start = pl.multiple_of(at * BAND, BAND)
        band = pl.ds(start, BAND)
        allowed = allowed_pairs(offsets_ref, rows, start, BAND)
        pieces = []
        for head in range(queries // HEAD_SIZE):
            kv_at = head // sharing * HEAD_SIZE
            query = q_ref[band, head * HEAD_SIZE : (head + 1) * HEAD_SIZE]
            key = k_ref[:, :, kv_at : kv_at + HEAD_SIZE].reshape(2 * rows, HEAD_SIZE)
            value = v_ref[:, :, kv_at : kv_at + HEAD_SIZE].reshape(2 * rows, HEAD_SIZE)
            scores = jnp.where(allowed, matmul_nt(query, key) * (HEAD_SIZE**-0.5), masked_score)
            peak = jnp.max(scores, axis=1, keepdims=True)
            weights = jnp.exp(scores - peak)
            total = jnp.sum(weights, axis=1, keepdims=True)
            pieces.append(matmul((weights * (1.0 / total)).astype(BF), value))
            lse_ref[band, head : head + 1] = peak + jnp.log(total)
        attended = jnp.concatenate(pieces, axis=1).astype(BF)
        att_ref[band, :] = attended
        count = BAND // PART
        terms[pl.ds(at * count, count)] = matmul(attended, wo_ref[...]).reshape(count, PART, width)

    groups = pulled_hbm.shape[0]

    def keep(place, at):
        span = pl.ds(place * rows, rows)
        return pltpu.make_async_copy(pulled.at[place, at], pulled_hbm.at[at, span, :], pulled_sems.at[place, at])

    def pull(place, at):
        count = downs.shape[0] // groups
        down = downs[pl.ds(at * count, count)].reshape(pulled.shape[3], width)
        pulled[place, at] = matmul_nt(ups[place], down).astype(BF)
        keep(place, at).start()

    def body(at, carry):
        @pl.when(at < rows // BAND)
        def _():
            attend(at)

        @pl.when(at == OWN_PULL)
        def _():
            loads[0].wait()
            loads[1].wait()

        @pl.when((at >= OWN_PULL) & (at < OWN_PULL + groups))
        def _():
            pull(0, at - OWN_PULL)

        @pl.when(at == PEER_PULL - 2)
        def _():
            up_early.wait_recv()
            up_late.wait_recv()
            loads[2].start()

        @pl.when(at == PEER_PULL)
        def _():
            loads[2].wait()

        @pl.when((at >= PEER_PULL) & (at < PEER_PULL + groups))
        def _():
            pull(1, at - PEER_PULL)

        @pl.when(at == 3)
        def _():
            marks_copy.wait_recv()
            marks_cross.start()

        line.step(at - 1)
        part = at - 1 - LAG * line.last

        @pl.when(part >= 0)
        def _():
            residual = x_ref[part].astype(F32) + line.total(part)
            res_ref[part] = residual
            unit = residual * scale_of(residual)
            n_ref[0, part] = (unit * gain2_ref[...]).astype(BF)
            peer_copy(n_ref.at[0, part], n_ref.at[1, part], peer_sems, part).start()

        return carry

    lax.fori_loop(0, 1 + parts + LAG * line.last, body, 0)
    line.drain()
    for copy in (key_copy, value_copy, marks_copy, up_early, up_late):
        copy.wait_send()
    for copy in (up_cross, marks_cross):
        copy.wait()
    for place in range(2):
        for at in range(groups):
            keep(place, at).wait()

    def wait(part, carry):
        peer_copy(n_ref.at[0, part], n_ref.at[1, part], peer_sems, part).wait()
        return carry

    lax.fori_loop(0, parts, wait, 0)


def front(
    offsets, block_input, first_gain, second_gain, w_query, key_weight, value_weight, w_output, cosines, sines,
    expert_ids, slot_index, upstream, experts_all, w_down,
):
    rows, width = block_input.shape
    parts = rows // PART
    queries, kv = w_query.shape[1], key_weight.shape[1]
    groups, hid = w_down.shape[0] // GROUP, GROUP * w_down.shape[1]
    any_spec = pl.BlockSpec(memory_space=pl.ANY)
    low = lambda *shape: jax.ShapeDtypeStruct(shape, BF)
    return pl.pallas_call(
        front_kernel,
        out_shape=(
            low(rows, width),
            low(rows, queries),
            low(2, rows, kv),
            low(2, rows, kv),
            low(rows, queries),
            jax.ShapeDtypeStruct((rows, 128), F32),
            jax.ShapeDtypeStruct((parts, PART, width), F32),
            low(2, parts, PART, width),
            low(2, rows, 2 * experts_all),
            low(2, rows, 2 * experts_all),
            low(rows, width),
            low(rows, width),
            low(groups, 2 * rows, hid),
        ),
        in_specs=[smem_spec()] + [vmem_spec()] * 11 + [any_spec] * 2,
        out_specs=(vmem_spec(),) * 9 + (any_spec,) * 4,
        scratch_shapes=line_scratch(parts, width)
        + [
            pltpu.SemaphoreType.DMA((2, parts)),
            pltpu.SemaphoreType.DMA((2, 7)),
            pltpu.VMEM((parts, PART, width), F32),
            pltpu.VMEM(w_down.shape, BF),
            pltpu.VMEM((2, rows, width), BF),
            pltpu.VMEM((2, groups, rows, hid), BF),
            pltpu.SemaphoreType.DMA((3,)),
            pltpu.SemaphoreType.DMA((2, groups)),
        ],
        compiler_params=pltpu.CompilerParams(
            collective_id=0, has_side_effects=True, vmem_limit_bytes=60 * MIB
        ),
        cost_estimate=LINK_COST,
        name="front",
    )(
        offsets, block_input.reshape(parts, PART, width), first_gain[None], second_gain[None], w_query, key_weight,
        value_weight, w_output, cosines, sines, expert_ids, slot_index, upstream, w_down,
    )


UNIT = 512
BIG_PART = 64
BIG_LAG = 2
SUB = 256


def residual_grad_kernel(
    route_ref, gain_ref, wr_ref, back_hbm, mix_hbm, res_hbm, up_hbm,
    far_n, far_on, far_g0, far_g1, far_og0, far_og1, far_m, far_om,
    wg_hbm, wu_hbm, wd_hbm, pg_hbm, pu_hbm, pd_hbm,
    grad_ref, low_ref, second_ref, route_out, mixed_ref, sg_hbm, su_hbm, sd_hbm, og_hbm, ou_hbm, od_hbm,
    from_left, from_right, to_right, to_left, sems, peer_sems, arrived, terms,
    tokens_n, tokens_g, turned, kept_gates, gates_w, ups_w, downs_w, pair_g, pair_u, pair_d, ght, dgs, dus,
    row_sems, weight_sems, pair_sems, out_sems, mix_arrived, mix_sems, marks_ref, share_sems,
    back_ref, mix_ref, res_ref, up_ref, load_sems,
):
    parts = back_ref.shape[0]
    core = lax.rem(lax.axis_index("dp"), 2)
    side = lax.axis_index("expert")
    groups, group, width, hid = pair_g.shape
    experts_all = wr_ref.shape[0]
    line = Line(parts + 1, lambda at: terms[at], from_left, from_right, to_right, to_left, sems, BIG_LAG)
    loads = [
        pltpu.make_async_copy(source, target, load_sems.at[at])
        for at, (source, target) in enumerate(
            ((back_hbm.at[0], back_ref), (res_hbm, res_ref), (up_hbm, up_ref), (mix_hbm.at[0], mix_ref))
        )
    ]
    for copy in loads:
        copy.start()
    line.clear()
    meet(line_partners() + [(True, {"expert": 1 - side}), (True, other_core())])

    def send(part, carry):
        peer_copy(back_hbm.at[1, part], arrived.at[part], peer_sems, part).start()
        return carry

    lax.fori_loop(0, parts, send, 0)

    def send_mix(part, carry):
        peer_copy(mix_hbm.at[1, part], mix_arrived.at[part], mix_sems, part).start()
        return carry

    lax.fori_loop(0, parts, send_mix, 0)
    half = tokens_n.shape[0] // 2
    quarter = half // 2
    row_copies = []
    for place, (rows, first, second, marks) in enumerate(((far_n, far_g0, far_g1, far_m), (far_on, far_og0, far_og1, far_om))):
        at = place * half
        row_copies += [
            pltpu.make_async_copy(rows, tokens_n.at[pl.ds(at, half), :], row_sems.at[0, place]),
            pltpu.make_async_copy(first, tokens_g.at[pl.ds(at, quarter), :], row_sems.at[1, place]),
            pltpu.make_async_copy(second, tokens_g.at[pl.ds(at + quarter, quarter), :], row_sems.at[2, place]),
            pltpu.make_async_copy(marks, marks_ref.at[pl.ds(at, half), :], row_sems.at[3, place]),
        ]
    weight_copies, pair_copies, out_copies = [], [], []
    for at in range(groups):
        first = core * (groups * group) + at * group
        weight_copies.append(
            [
                pltpu.make_async_copy(
                    source.at[first + expert],
                    target.at[at, :, pl.ds(expert * hid, hid)],
                    weight_sems.at[at, kind, expert],
                )
                for expert in range(group)
                for kind, (source, target) in enumerate(((wg_hbm, gates_w), (wu_hbm, ups_w)))
            ]
            + [pltpu.make_async_copy(wd_hbm.at[pl.ds(first, group)], downs_w.at[at], weight_sems.at[at, 2, 0])]
        )
        sources = (pg_hbm, pu_hbm, pd_hbm)
        held = (pair_g, pair_u, pair_d)
        targets = (sg_hbm, su_hbm, sd_hbm)
        others = (og_hbm, ou_hbm, od_hbm)
        pair_copies.append(
            [
                pltpu.make_async_copy(sources[kind].at[pl.ds(at * group, group)], held[kind].at[at], pair_sems.at[at, kind])
                for kind in range(3)
            ]
        )
        out_copies.append(
            [
                pltpu.make_async_copy(held[kind].at[at], targets[kind].at[pl.ds(at * group, group)], out_sems.at[at, kind])
                for kind in range(3)
            ]
            + [
                plain_copy(
                    held[kind].at[at], others[kind].at[pl.ds(at * group, group)], share_sems.at[at], kind, other_core()
                )
                for kind in range(3)
            ]
        )
    for copy in row_copies[:4] + weight_copies[0] + row_copies[4:] + pair_copies[0] + weight_copies[1] + pair_copies[1]:
        copy.start()
    pad = jnp.zeros((BIG_PART - route_ref.shape[0], route_ref.shape[1]), F32)
    terms[parts] = jnp.concatenate([route_ref[...], pad], axis=0)
    loads[0].wait()
    second_ref[...] = jnp.zeros(second_ref.shape, F32)
    chunks = 2 * half // UNIT
    units = chunks + 3

    def compute(at):
        for where in range(groups):
            unit = at - where * units

            @pl.when(unit == 0)
            def _():
                for copy in weight_copies[where]:
                    copy.wait()

            if where == 0:

                @pl.when(unit == 0)
                def _():
                    for copy in row_copies[:4]:
                        copy.wait()

                @pl.when(unit == half // UNIT)
                def _():
                    for copy in row_copies[4:]:
                        copy.wait()

            @pl.when(unit == chunks)
            def _():
                for copy in pair_copies[where]:
                    copy.wait()

        where = at // units
        unit = at - where * units

        @pl.when(unit < chunks)
        def _():
            down = downs_w[where].reshape(group * hid, width)
            column = side * (experts_all // 2) + (core * groups + where) * group
            for sub in range(UNIT // SUB):
                rows = pl.ds(pl.multiple_of(unit * UNIT + sub * SUB, SUB), SUB)

                @pl.when(where == 0)
                def _():
                    token = tokens_n[rows, :]
                    kept_gates[rows, :] = route_gates(token, marks_ref[rows, :], wr_ref[...])[1]
                    turned[:, rows] = token.T

            for sub in range(UNIT // SUB):
                rows = pl.ds(pl.multiple_of(unit * UNIT + sub * SUB, SUB), SUB)
                pulled = matmul_nt(tokens_g[rows, :], down)
                weight = spread_gates(kept_gates[rows, :], column, group, hid)
                _, gated, gate_grad, up_grad = hidden_terms(
                    tokens_n[rows, :], pulled, weight, gates_w[where], ups_w[where]
                )
                ght[:, rows] = gated.T
                dgs[rows, :] = gate_grad
                dus[rows, :] = up_grad

        @pl.when((unit >= chunks) & (unit < chunks + 2))
        def _():
            rows = pl.ds(pl.multiple_of((unit - chunks) * (width // 2), width // 2), width // 2)
            for source, held in ((dgs, pair_g), (dus, pair_u)):
                part = matmul(turned[rows, :], source[...])
                for expert in range(group):
                    more = part[:, expert * hid : (expert + 1) * hid]
                    held[where, expert, rows, :] = (held[where, expert, rows, :].astype(F32) + more).astype(BF)

        @pl.when(unit == chunks + 2)
        def _():
            part = matmul(ght[...], tokens_g[...])
            for expert in range(group):
                more = part[expert * hid : (expert + 1) * hid, :]
                pair_d[where, expert] = (pair_d[where, expert].astype(F32) + more).astype(BF)

        for where in range(groups):

            @pl.when(at == where * units + units - 1)
            def _():
                for copy in out_copies[where]:
                    copy.start()

    def add_mix(part):
        peer_copy(mix_hbm.at[1, part], mix_arrived.at[part], mix_sems, part).wait_recv()
        mixed_ref[part] = (mix_ref[part].astype(F32) + mix_arrived[part].astype(F32)).astype(BF)

    steps = parts + 1 + BIG_LAG * line.last

    def advance(at):
        @pl.when(at < parts)
        def _():
            peer_copy(back_hbm.at[1, at], arrived.at[at], peer_sems, at).wait_recv()
            terms[at] = back_ref[at].astype(F32) + arrived[at].astype(F32)

        line.step(at)
        part = at - BIG_LAG * line.last

        @pl.when((part >= 0) & (part < parts))
        def _():
            grad = line.total(part)
            residual = res_ref[part]
            scale = scale_of(residual)
            unit = residual * scale
            second_ref[...] += jnp.sum(grad * unit, axis=0, keepdims=True)
            result = up_ref[part].astype(F32) + norm_back(grad, unit, scale, gain_ref[...])
            grad_ref[part] = result
            low_ref[part] = result.astype(BF)

        @pl.when((at >= MIX_STEP) & (at < MIX_STEP + parts))
        def _():
            add_mix(at - MIX_STEP)

    turns = max(groups * units, steps)

    def body(at, carry):
        @pl.when(at < groups * units)
        def _():
            compute(at)

        @pl.when(at == 2)
        def _():
            for copy in loads[1:]:
                copy.wait()

        advance(at)
        return carry

    lax.fori_loop(0, turns, body, 0)
    route_out[...] = line.total(parts)[: route_ref.shape[0], :]

    def rest(part, carry):
        add_mix(part)
        return carry

    lax.fori_loop(turns - MIX_STEP, parts, rest, 0)
    line.drain()

    def wait(part, carry):
        peer_copy(back_hbm.at[1, part], arrived.at[part], peer_sems, part).wait_send()
        peer_copy(mix_hbm.at[1, part], mix_arrived.at[part], mix_sems, part).wait_send()
        return carry

    lax.fori_loop(0, parts, wait, 0)
    for copies in out_copies:
        for copy in copies:
            copy.wait()


MIX_STEP = 9


def residual_gradient(back, mix, route, residual, upstream, gain, w_router, far_rows, w_gate, w_up, w_down, pairs):
    rows, width = upstream.shape
    parts = rows // BIG_PART
    half, _, hid = pairs[0].shape
    groups = half // GROUP
    tokens = 2 * far_rows[0].shape[0]
    any_spec = pl.BlockSpec(memory_space=pl.ANY)
    grad, low, second, route, mixed, *sums = pl.pallas_call(
        residual_grad_kernel,
        out_shape=[
            jax.ShapeDtypeStruct((parts, BIG_PART, width), F32),
            jax.ShapeDtypeStruct((parts, BIG_PART, width), BF),
            jax.ShapeDtypeStruct((1, width), F32),
            jax.ShapeDtypeStruct(route.shape, F32),
            jax.ShapeDtypeStruct((parts, BIG_PART, width), BF),
        ]
        + [jax.ShapeDtypeStruct(pair.shape, BF) for pair in pairs] * 2,
        in_specs=[vmem_spec()] * 3 + [any_spec] * 18,
        out_specs=[vmem_spec()] * 5 + [any_spec] * 6,
        scratch_shapes=line_scratch(parts + 1, width, BIG_PART)
        + [
            pltpu.SemaphoreType.DMA((2, parts)),
            pltpu.VMEM((parts, BIG_PART, width), BF),
            pltpu.VMEM((parts + 1, BIG_PART, width), F32),
            pltpu.VMEM((tokens, width), BF),
            pltpu.VMEM((tokens, width), BF),
            pltpu.VMEM((width, tokens), BF),
            pltpu.VMEM((tokens, w_router.shape[0]), F32),
            pltpu.VMEM((groups, width, GROUP * hid), BF),
            pltpu.VMEM((groups, width, GROUP * hid), BF),
            pltpu.VMEM((groups, GROUP, hid, width), BF),
            pltpu.VMEM((groups, GROUP, width, hid), BF),
            pltpu.VMEM((groups, GROUP, width, hid), BF),
            pltpu.VMEM((groups, GROUP, hid, width), BF),
            pltpu.VMEM((GROUP * hid, tokens), BF),
            pltpu.VMEM((tokens, GROUP * hid), BF),
            pltpu.VMEM((tokens, GROUP * hid), BF),
            pltpu.SemaphoreType.DMA((4, 2)),
            pltpu.SemaphoreType.DMA((groups, 3, GROUP)),
            pltpu.SemaphoreType.DMA((groups, 3)),
            pltpu.SemaphoreType.DMA((groups, 3)),
            pltpu.VMEM((parts, BIG_PART, width), BF),
            pltpu.SemaphoreType.DMA((2, parts)),
            pltpu.VMEM((tokens, 2 * w_router.shape[0]), BF),
            pltpu.SemaphoreType.DMA((groups, 2, 3)),
            pltpu.VMEM((parts, BIG_PART, width), BF),
            pltpu.VMEM((parts, BIG_PART, width), BF),
            pltpu.VMEM((parts, BIG_PART, width), F32),
            pltpu.VMEM((parts, BIG_PART, width), BF),
            pltpu.SemaphoreType.DMA((4,)),
        ],
        compiler_params=pltpu.CompilerParams(
            collective_id=1, has_side_effects=True, vmem_limit_bytes=60 * MIB
        ),
        cost_estimate=LINK_COST,
        name="residual_grad",
    )(
        route, gain[None], w_router, back.reshape(2, parts, BIG_PART, width), mix.reshape(2, parts, BIG_PART, width),
        residual.reshape(parts, BIG_PART, width), upstream.reshape(parts, BIG_PART, width), *far_rows, w_gate, w_up, w_down, *pairs,
    )
    return grad, low.reshape(rows, width), second, route, mixed, sums


def input_grad_kernel(
    offsets_ref, gain_ref, wq_ref, wk_ref, wv_ref, wo_ref, cos_ref, sin_ref,
    q_ref, k_ref, v_ref, lse_ref, att_ref, low_ref, route_ref, second_ref, mix_ref, x_hbm, res_grad_hbm, n_hbm, res_hbm,
    grad_ref, wide_out, wide_back, tall_out, tall_back, gains_ref, block_ref,
    from_left, from_right, to_right, to_left, sems, terms, kv_out, kv_in, kv_sems,
    wide, wide_core, wide_x, wide_y, tall, tall_core, tall_x, tall_y, rows2, rows_core, rows_x, rows_y, sum_sems,
    mix_left, mix_right, mix_to_right, mix_to_left, mix_sems, x_ref, res_grad_ref, n_ref, res_ref, load_sems,
):
    parts = x_ref.shape[0]
    rows = n_ref.shape[0]
    width = n_ref.shape[1]
    core = lax.rem(lax.axis_index("dp"), 2)
    peer = {"expert": 1 - lax.axis_index("expert")}
    kv = wk_ref.shape[1]
    queries = wq_ref.shape[1]
    line = Line(parts + 1, lambda at: terms[at], from_left, from_right, to_right, to_left, sems)
    spread = Spread(mix_ref, mix_left, mix_right, mix_to_right, mix_to_left, mix_sems)
    loads = [
        pltpu.make_async_copy(source, target, load_sems.at[at])
        for at, (source, target) in enumerate(
            ((n_hbm, n_ref), (x_hbm, x_ref), (res_grad_hbm, res_grad_ref), (res_hbm, res_ref))
        )
    ]
    for copy in loads:
        copy.start()
    line.clear()
    spread.clear()
    meet(line_partners() + [(True, peer), (True, beside()), (True, other_core())])
    spread.step(0)
    key_copy = plain_copy(kv_out.at[0, pl.ds(rows, rows), :], kv_in.at[0], kv_sems, 0, peer)
    value_copy = plain_copy(kv_out.at[1, pl.ds(rows, rows), :], kv_in.at[1], kv_sems, 1, peer)

    scale = HEAD_SIZE**-0.5
    low = low_ref[...]
    out_part = matmul(att_ref[...].T, low).astype(BF)
    att_grad = matmul_nt(low, wo_ref[...]).astype(BF)
    half_tall = tall.shape[1]
    outs = wo_ref.shape[0]
    for at in range(2):
        start, high = at * half_tall, (at + 1) * half_tall
        top = min(high, outs)
        tall[at, : top - start, :] = out_part[start:top, :]
        if high > outs:
            tall[at, outs - start :, :] = route_ref[...].astype(BF)

    tall_steps = [
        plain_copy(tall.at[1 - core], tall_core, sum_sems, 0, other_core()),
        plain_copy(tall.at[core], tall_y, sum_sems, 1, peer),
        plain_copy(tall.at[core], tall_x, sum_sems, 2, beside()),
        plain_copy(tall.at[core], tall_back, sum_sems, 3, other_core()),
    ]
    wide_steps = [
        plain_copy(wide.at[1 - core], wide_core, sum_sems, 4, other_core()),
        plain_copy(wide.at[core], wide_x, sum_sems, 5, beside()),
        plain_copy(wide.at[core], wide_y, sum_sems, 6, peer),
        plain_copy(wide.at[core], wide_back, sum_sems, 7, other_core()),
    ]
    rows_steps = [
        plain_copy(rows2, rows_core, sum_sems, 8, other_core()),
        plain_copy(rows2, rows_y, sum_sems, 9, peer),
        plain_copy(rows2, rows_x, sum_sems, 10, beside()),
    ]
    tall_steps[0].start()

    def add(held, arrived):
        held[...] = (held[...].astype(F32) + arrived[...].astype(F32)).astype(BF)

    allowed = allowed_pairs(offsets_ref, rows, 0, rows)
    sharing = queries // kv
    query_parts, key_parts, value_parts = [], [], []
    for head in range(queries // HEAD_SIZE):
        if head:
            spread.step(head)
        if head == 1:
            tall_steps[0].wait()
            add(tall.at[core], tall_core)
            tall_steps[1].start()
        if head == 3:
            tall_steps[1].wait()
            add(tall.at[core], tall_y)
            tall_steps[2].start()
        at = head * HEAD_SIZE
        kv_at = head // sharing * HEAD_SIZE
        query = q_ref[:, at : at + HEAD_SIZE]
        key = k_ref[:, kv_at : kv_at + HEAD_SIZE]
        value = v_ref[:, kv_at : kv_at + HEAD_SIZE]
        grad = att_grad[:, at : at + HEAD_SIZE]
        scores = jnp.where(allowed, matmul_nt(query, key) * scale, masked_score)
        probs = jnp.exp(scores - lse_ref[:, head : head + 1])
        prob_grad = matmul_nt(grad, value)
        delta = jnp.sum(probs * prob_grad, axis=1, keepdims=True)
        score_grad = (probs * (prob_grad - delta)).astype(BF)
        query_parts.append(matmul(score_grad, key) * scale)
        key_part = matmul_tn(score_grad, query) * scale
        value_part = matmul_tn(probs.astype(BF), grad)
        if head % sharing == 0:
            key_parts.append(key_part)
            value_parts.append(value_part)
        else:
            key_parts[-1] = key_parts[-1] + key_part
            value_parts[-1] = value_parts[-1] + value_part
    kv_out[0] = jnp.concatenate(key_parts, axis=1).astype(BF)
    key_copy.start()
    kv_out[1] = jnp.concatenate(value_parts, axis=1).astype(BF)
    value_copy.start()

    def rotate_back(array):
        wide_lanes = array.shape[1]
        lane = lax.broadcasted_iota(jnp.int32, (1, wide_lanes), 1)
        first = lane % HEAD_SIZE < HEAD_SIZE // 2
        cosines = jnp.concatenate([cos_ref[...]] * (wide_lanes // 128), axis=1)
        sines = jnp.concatenate([sin_ref[...]] * (wide_lanes // 128), axis=1)
        return (array * cosines - turn(array, first) * sines).astype(BF)

    for copy in loads:
        copy.wait()
    query_grad = rotate_back(jnp.concatenate(query_parts, axis=1))
    by_rows = (parts, rows // parts, width)
    terms[pl.ds(0, parts)] = matmul_nt(query_grad, wq_ref[...]).reshape(by_rows)
    turned = n_ref[...].T
    query_part = matmul(turned, query_grad).astype(BF)
    for at in range(2):
        wide[at, :, :queries] = query_part[at * width // 2 : (at + 1) * width // 2, :]
    key_copy.wait_recv()
    value_copy.wait_recv()
    key_grad = rotate_back(kv_out[0, :rows, :].astype(F32) + kv_in[0].astype(F32))
    value_grad = (kv_out[1, :rows, :].astype(F32) + kv_in[1].astype(F32)).astype(BF)
    more = matmul_nt(key_grad, wk_ref[...]) + matmul_nt(value_grad, wv_ref[...])
    terms[pl.ds(0, parts)] += more.reshape(by_rows)
    both_part = matmul(turned, jnp.concatenate([key_grad, value_grad], axis=1)).astype(BF)
    for at in range(2):
        wide[at, :, queries:] = both_part[at * width // 2 : (at + 1) * width // 2, :]
    wide_steps[0].start()

    gains_ref[...] = jnp.zeros(gains_ref.shape, F32)

    def gain_part(at):
        values = x_ref[at].astype(F32)
        gains_ref[2:3, :] += jnp.sum(terms[at] * (values * scale_of(values)), axis=0, keepdims=True)

    def exchange(at):
        @pl.when(at < parts // 2)
        def _():
            gain_part(2 * at)
            gain_part(2 * at + 1)

        @pl.when(at == parts // 2)
        def _():
            pad = jnp.zeros((rows2.shape[0] - 2, width), F32)
            rows2[...] = jnp.concatenate([gains_ref[2:3, :], second_ref[...], pad], axis=0).astype(BF)
            rows_steps[0].start()

        @pl.when(at == parts // 2 + 1)
        def _():
            rows_steps[0].wait()
            add(rows2, rows_core)
            rows_steps[1].start()

        @pl.when(at == 1)
        def _():
            wide_steps[0].wait()
            add(wide.at[core], wide_core)

        @pl.when(at == 2)
        def _():
            wide_steps[1].start()

        @pl.when(at == parts // 2 + 3)
        def _():
            rows_steps[1].wait()
            add(rows2, rows_y)
            rows_steps[2].start()

        @pl.when(at == parts // 2 + 5)
        def _():
            rows_steps[2].wait()
            add(rows2, rows_x)
            summed = rows2[...].astype(F32)
            terms[parts] = jnp.concatenate([summed[:1, :], jnp.zeros((PART - 1, width), F32)], axis=0)
            gains_ref[1:2, :] = summed[1:2, :]

        @pl.when(at == 11)
        def _():
            wide_steps[1].wait()
            add(wide.at[core], wide_x)
            wide_steps[2].start()

        @pl.when(at == 3)
        def _():
            tall_steps[2].wait()
            add(tall.at[core], tall_x)
            tall_steps[3].start()

        @pl.when(at == 20)
        def _():
            wide_steps[2].wait()
            add(wide.at[core], wide_y)
            wide_steps[3].start()

    heads = queries // HEAD_SIZE

    def body(at, carry):
        exchange(at)
        line.step(at)

        @pl.when((at % 2 == 0) & (at // 2 + heads < spread.steps))
        def _():
            spread.step(at // 2 + heads)

        @pl.when((at % 2 == 0) & (at // 2 + heads >= spread.first_whole) & (at // 2 + heads < spread.steps))
        def _():
            block = at // 2 + heads - spread.first_whole
            block_ref[block] = (res_ref[block, :, spread.own()] + spread.total(block)).astype(BF)

        part = at - LAG * line.last

        @pl.when((part >= 0) & (part < parts))
        def _():
            grad = line.total(part)
            values = x_ref[part].astype(F32)
            scale = scale_of(values)
            unit = values * scale
            grad_ref[part] = (res_grad_ref[part] + norm_back(grad, unit, scale, gain_ref[...])).astype(BF)

        return carry

    lax.fori_loop(0, parts + 1 + LAG * line.last, body, 0)
    gains_ref[0:1, :] = line.total(parts)[:1, :]
    line.drain()
    spread.drain()
    key_copy.wait_send()
    value_copy.wait_send()
    tall_steps[3].wait()
    wide_steps[3].wait()
    tall_out[...] = tall[core]
    wide_out[...] = wide[core]


class Spread:
    def __init__(self, term, from_left, from_right, to_right, to_left, sems):
        self.place = lax.axis_index("tensor")
        self.size = lax.axis_size("tensor")
        self.term = term
        self.blocks = term.shape[0]
        self.span = term.shape[2] // self.size
        self.from_left, self.from_right = from_left, from_right
        self.to_right, self.to_left = to_right, to_left
        self.sems = sems
        self.first_whole = 2 * (self.size - 1)
        self.steps = self.blocks + self.first_whole

    def copy(self, way, block, shard):
        last = self.size - 1
        near = jnp.where(self.place < last, self.place + 1, self.place - 1)
        far = jnp.where(self.place > 0, self.place - 1, self.place + 1)
        source, target, device = (
            (self.to_right, self.from_left, near) if way == 0 else (self.to_left, self.from_right, far)
        )
        return pltpu.make_async_remote_copy(
            src_ref=source.at[block, shard], dst_ref=target.at[block, shard],
            send_sem=self.sems.at[2 * way, block, shard], recv_sem=self.sems.at[2 * way + 1, block, shard],
            device_id={"tensor": device}, device_id_type=MESH,
        )

    def clear(self):
        @pl.when(self.place == 0)
        def _():
            self.from_left[...] = jnp.zeros(self.from_left.shape, BF)

        @pl.when(self.place == self.size - 1)
        def _():
            self.from_right[...] = jnp.zeros(self.from_right.shape, BF)

    def passes(self, way, shard):
        return self.place < shard if way == 0 else self.place > shard

    def has_source(self, way):
        return self.place > 0 if way == 0 else self.place < self.size - 1

    def step(self, at):
        for way in range(2):
            block = at - 2 * (self.place if way == 0 else self.size - 1 - self.place)
            valid = (block >= 0) & (block < self.blocks)
            arrived = self.from_left if way == 0 else self.from_right
            leaving = self.to_right if way == 0 else self.to_left
            for shard in range(self.size):
                here = valid & self.passes(way, shard)

                @pl.when(here & self.has_source(way))
                def _():
                    self.copy(way, block, shard).wait_recv()

                @pl.when(here)
                def _():
                    lanes = slice(shard * self.span, (shard + 1) * self.span)
                    own = self.term[block, :, lanes].astype(F32)
                    leaving[block, shard] = (own + arrived[block, shard].astype(F32)).astype(BF)
                    self.copy(way, block, shard).start()

    def own(self):
        return pl.ds(pl.multiple_of(self.place * self.span, self.span), self.span)

    def total(self, block):
        for way in range(2):

            @pl.when(self.has_source(way))
            def _():
                self.copy(way, block, self.place).wait_recv()

        sides = self.from_left[block, self.place].astype(F32) + self.from_right[block, self.place].astype(F32)
        return self.term[block, :, self.own()].astype(F32) + sides

    def drain(self):
        for way in range(2):
            for shard in range(self.size):

                @pl.when(self.passes(way, shard))
                def _():
                    for block in range(self.blocks):
                        self.copy(way, block, shard).wait_send()


BLOCK_ROWS = 128


def input_gradient(
    offsets, block_input, residual_grad, gain, normed, w_query, key_weight, value_weight, w_output, cosines, sines,
    query, keys, values, lse, attended, low, route, second, mixed, residual,
):
    rows, width = block_input.shape
    parts = rows // PART
    kv = key_weight.shape[1]
    columns = w_query.shape[1] + 2 * kv
    tall = (w_output.shape[0] + route.shape[0]) // 2
    size = lax.axis_size("tensor")
    blocks = rows // BLOCK_ROWS
    wide_half = pltpu.VMEM((width // 2, columns), BF)
    tall_half = pltpu.VMEM((tall, width), BF)
    tile = pltpu.VMEM((16, width), BF)
    mix_half = pltpu.VMEM((blocks, size, BLOCK_ROWS, width // size), BF)
    return pl.pallas_call(
        input_grad_kernel,
        out_shape=(
            jax.ShapeDtypeStruct((parts, PART, width), BF),
            jax.ShapeDtypeStruct((width // 2, columns), BF),
            jax.ShapeDtypeStruct((width // 2, columns), BF),
            jax.ShapeDtypeStruct((tall, width), BF),
            jax.ShapeDtypeStruct((tall, width), BF),
            jax.ShapeDtypeStruct((8, width), F32),
            jax.ShapeDtypeStruct((blocks, BLOCK_ROWS, width // size), BF),
        ),
        in_specs=[smem_spec()] + [vmem_spec()] * 16 + [pl.BlockSpec(memory_space=pl.ANY)] * 4,
        out_specs=(vmem_spec(),) * 7,
        scratch_shapes=line_scratch(parts + 1, width)
        + [
            pltpu.VMEM((parts + 1, PART, width), F32),
            pltpu.VMEM((2, 2 * rows, kv), BF),
            pltpu.VMEM((2, rows, kv), BF),
            pltpu.SemaphoreType.DMA((2, 2)),
            pltpu.VMEM((2, width // 2, columns), BF), wide_half, wide_half, wide_half,
            pltpu.VMEM((2, tall, width), BF), tall_half, tall_half, tall_half,
            tile, tile, tile, tile,
            pltpu.SemaphoreType.DMA((2, 11)),
            mix_half, mix_half, mix_half, mix_half,
            pltpu.SemaphoreType.DMA((4, blocks, size)),
            pltpu.VMEM((parts, PART, width), BF),
            pltpu.VMEM((parts, PART, width), F32),
            pltpu.VMEM((rows, width), BF),
            pltpu.VMEM((blocks, BLOCK_ROWS, width), F32),
            pltpu.SemaphoreType.DMA((4,)),
        ],
        compiler_params=pltpu.CompilerParams(
            collective_id=2, has_side_effects=True, vmem_limit_bytes=60 * MIB
        ),
        cost_estimate=LINK_COST,
        name="input_grad",
    )(
        offsets, gain[None], w_query, key_weight, value_weight, w_output, cosines, sines, query, keys, values, lse,
        attended, low, route, second, mixed.reshape(blocks, BLOCK_ROWS, width), block_input.reshape(parts, PART, width),
        residual_grad.reshape(parts, PART, width), normed, residual.reshape(blocks, BLOCK_ROWS, width),
    )


CHUNK = 256
GROUP = 4


def route_gates(token, marks, w_router):
    experts_all = w_router.shape[0]
    chosen = marks[:, :experts_all].astype(F32)
    kept = marks[:, experts_all:].astype(F32)
    logits = jnp.where(chosen > 0.0, matmul_nt(token, w_router), masked_score)
    raised = jnp.exp(logits - jnp.max(logits, axis=1, keepdims=True)) * chosen
    gate = raised / jnp.sum(raised, axis=1, keepdims=True)
    return gate, gate * kept


def hidden_terms(token, pulled, weight, gate_weights, up_weights):
    gate_in = matmul(token, gate_weights)
    up_in = matmul(token, up_weights)
    sig = 0.5 * jnp.tanh(0.5 * gate_in) + 0.5
    silu = gate_in * sig
    hidden = silu * up_in
    gated = (hidden * weight).astype(BF)
    scaled = pulled * weight
    up_grad = (scaled * silu).astype(BF)
    gate_grad = (scaled * up_in * (sig + silu * (1.0 - sig))).astype(BF)
    return hidden, gated, gate_grad, up_grad


def spread_gates(kept, column, group, hid):
    lane = lax.broadcasted_iota(jnp.int32, (1, kept.shape[1]), 1)
    weights = []
    for expert in range(group):
        gate = jnp.sum(jnp.where(lane == column + expert, kept, 0.0), axis=1, keepdims=True)
        weights.append(jnp.broadcast_to(gate, (kept.shape[0], hid)))
    return jnp.concatenate(weights, axis=1)


def expert_kernel(
    n_ref, marks_ref, wr_ref, n_hbm, own_up, peer_up, far_g0, far_m, wg_ref, wu_ref, wd_ref, pulled_ref,
    dwg_ref, dwu_ref, dwd_ref, mix_ref, back_ref, route_ref, far_n, far_on, far_g1, far_og0, far_og1, far_om,
    gates, kept_gates, gate_grads, mix, back, nt, wgs, wus, ght, dgs, dus,
    out_g, out_u, out_d, in_g, in_u, in_d, sems, far_sems, g_ref, up_sems,
):
    step = pl.program_id(0)
    steps = pl.num_programs(0) // 2
    side = lax.axis_index("expert")
    dp = lax.axis_index("dp")
    core = lax.rem(dp, 2)
    other = other_core()
    tokens, width = n_ref.shape
    experts_all = wr_ref.shape[0]
    group, _, hid = wg_ref.shape
    chunks = tokens // CHUNK
    lane = lax.broadcasted_iota(jnp.int32, (1, experts_all), 1)

    def copies(slot):
        return [
            pltpu.make_async_remote_copy(
                src_ref=source.at[slot], dst_ref=target.at[slot],
                send_sem=sems.at[0, kind, slot], recv_sem=sems.at[1, kind, slot],
                device_id=other, device_id_type=MESH,
            )
            for kind, (source, target) in enumerate(((out_g, in_g), (out_u, in_u), (out_d, in_d)))
        ]

    half = tokens // 2
    cross = [
        plain_copy(n_hbm.at[pl.ds(at * half, half), :], far_n.at[pl.ds(at * half, half), :], far_sems, at, beside())
        for at in range(2)
    ]
    share = [
        plain_copy(far_n.at[pl.ds(at * half, half), :], far_on.at[pl.ds(at * half, half), :], far_sems, 2 + at, other)
        for at in range(2)
    ]
    peer = {"expert": 1 - side}
    turn_up = plain_copy(far_g0, far_g1, far_sems, 4, peer)
    share_up = plain_copy(far_g1, far_og1, far_sems, 5, other)
    early = [
        plain_copy(source, target, far_sems, 6 + at, other)
        for at, (source, target) in enumerate(((far_g0, far_og0), (far_m, far_om)))
    ]
    loads = [
        pltpu.make_async_copy(source, g_ref.at[pl.ds(at * half, half), :], up_sems.at[at])
        for at, source in enumerate((own_up, peer_up))
    ]

    @pl.when(step == 0)
    def _():
        for copy in loads:
            copy.start()
        meet([(True, other), (True, beside()), (True, peer)])
        for copy in cross + early + [turn_up]:
            copy.start()

        def start(at, carry):
            rows = pl.ds(pl.multiple_of(at * CHUNK, CHUNK), CHUNK)
            gate, kept_gate = route_gates(n_ref[rows, :], marks_ref[rows, :], wr_ref[...])
            gates[rows, :] = gate
            kept_gates[rows, :] = kept_gate
            mix[rows, :] = jnp.zeros((CHUNK, width), F32)
            back[rows, :] = jnp.zeros((CHUNK, width), F32)
            gate_grads[rows, :] = jnp.zeros((CHUNK, experts_all), F32)
            return carry

        lax.fori_loop(0, chunks, start, 0)
        for at in range(chunks):
            nt[:, at * CHUNK : (at + 1) * CHUNK] = n_ref[at * CHUNK : (at + 1) * CHUNK, :].T
        for copy in loads:
            copy.wait()

    @pl.when(step == steps)
    def _():
        cross[0].wait_recv()
        share[0].start()
        turn_up.wait_recv()
        share_up.start()

    for expert in range(group):
        wgs[:, expert * hid : (expert + 1) * hid] = wg_ref[expert]
        wus[:, expert * hid : (expert + 1) * hid] = wu_ref[expert]
    first = step < steps
    block = jnp.where(first, (1 - core) * steps + step, core * steps + step - steps)
    column = side * (experts_all // 2) + block * group

    for at in range(chunks):
        rows = slice(at * CHUNK, (at + 1) * CHUNK)
        token = n_ref[rows, :]
        down = wd_ref[...].reshape(group * hid, width)
        pulled = pulled_ref[0, rows, :].astype(F32)
        weight = spread_gates(kept_gates[rows, :], column, group, hid)
        hidden, gated, gate_grad, up_grad = hidden_terms(token, pulled, weight, wgs[...], wus[...])
        products = hidden * pulled
        grads = gate_grads[rows, :]
        for expert in range(group):
            product = jnp.sum(products[:, expert * hid : (expert + 1) * hid], axis=1, keepdims=True)
            grads = grads + jnp.where(lane == column + expert, product, 0.0)
        gate_grads[rows, :] = grads
        ght[:, rows] = gated.T
        dgs[rows, :] = gate_grad
        dus[rows, :] = up_grad
        mix[rows, :] += matmul(gated, down)
        back[rows, :] += matmul_nt(gate_grad, wgs[...]) + matmul_nt(up_grad, wus[...])

    def weight_grads(store_rows, store_down):
        for at in range(width // CHUNK):
            rows = slice(at * CHUNK, (at + 1) * CHUNK)
            turned = nt[rows, :]
            gate_part = matmul(turned, dgs[...])
            up_part = matmul(turned, dus[...])
            for expert in range(group):
                inner = slice(expert * hid, (expert + 1) * hid)
                store_rows(expert, rows, gate_part[:, inner], up_part[:, inner])
        down_part = matmul(ght[...], g_ref[...])
        for expert in range(group):
            store_down(expert, down_part[expert * hid : (expert + 1) * hid, :])

    @pl.when(first)
    def _():
        def store_rows(expert, rows, gate_part, up_part):
            out_g[step, expert, rows, :] = gate_part.astype(BF)
            out_u[step, expert, rows, :] = up_part.astype(BF)

        def store_down(expert, part):
            out_d[step, expert] = part.astype(BF)

        weight_grads(store_rows, store_down)
        for copy in copies(step):
            copy.start()

    @pl.when(step >= steps)
    def _():
        slot = step - steps
        for copy in copies(slot):
            copy.wait_recv()

        def store_rows(expert, rows, gate_part, up_part):
            dwg_ref[expert, rows, :] = (gate_part + in_g[slot, expert, rows, :].astype(F32)).astype(BF)
            dwu_ref[expert, rows, :] = (up_part + in_u[slot, expert, rows, :].astype(F32)).astype(BF)

        def store_down(expert, part):
            dwd_ref[expert] = (part + in_d[slot, expert].astype(F32)).astype(BF)

        weight_grads(store_rows, store_down)
        for copy in copies(slot):
            copy.wait_send()

    @pl.when(step == 2 * steps - 1)
    def _():
        cross[1].wait_recv()
        share[1].start()
        route_ref[...] = jnp.zeros(route_ref.shape, F32)

        def finish(at, carry):
            rows = pl.ds(pl.multiple_of(at * CHUNK, CHUNK), CHUNK)
            mix_ref[rows, :] = mix[rows, :].astype(BF)
            grads = gate_grads[rows, :] * kept_gates[rows, :]
            chosen_grad = grads - gates[rows, :] * jnp.sum(grads, axis=1, keepdims=True)
            low = chosen_grad.astype(BF)
            back_ref[rows, :] = (back[rows, :] + matmul(low, wr_ref[...])).astype(BF)
            route_ref[...] += matmul_tn(low, n_ref[rows, :])
            return carry

        lax.fori_loop(0, chunks, finish, 0)
        for copy in cross + [turn_up]:
            copy.wait_send()
        for copy in share + early + [share_up]:
            copy.wait()


def experts(normed, marks, w_router, upstream, peer_up, far_up, far_marks, w_gate, w_up, w_down, pulled):
    tokens, width = normed.shape
    count, _, hid = w_gate.shape
    half = count // 2
    steps = half // GROUP
    experts_all = w_router.shape[0]
    once = pl.Buffered(1)
    whole = lambda step: (0, 0)

    def picked(step):
        core = lax.rem(lax.axis_index("dp"), 2)
        return (jnp.where(step < steps, (1 - core) * steps + step, core * steps + step - steps), 0, 0)

    own = lambda step: (jnp.maximum(step - steps, 0), 0, 0)
    args = [normed, marks, w_router]
    specs = [pl.BlockSpec(array.shape, whole, pipeline_mode=once) for array in args]
    args += [normed, upstream, peer_up, far_up, far_marks]
    specs += [pl.BlockSpec(memory_space=pl.ANY)] * 5
    up_block, down_block = (GROUP, width, hid), (GROUP, hid, width)
    specs += [pl.BlockSpec(up_block, picked), pl.BlockSpec(up_block, picked), pl.BlockSpec(down_block, picked)]
    specs += [pl.BlockSpec((1, tokens, GROUP * hid), picked)]
    gate_scratch = pltpu.VMEM((tokens, experts_all), F32)
    rows_scratch = pltpu.VMEM((tokens, width), F32)
    swap_scratch = [
        pltpu.VMEM((steps,) + up_block, BF),
        pltpu.VMEM((steps,) + up_block, BF),
        pltpu.VMEM((steps,) + down_block, BF),
    ]
    return pl.pallas_call(
        expert_kernel,
        out_shape=[
            jax.ShapeDtypeStruct((half, width, hid), BF),
            jax.ShapeDtypeStruct((half, width, hid), BF),
            jax.ShapeDtypeStruct((half, hid, width), BF),
            jax.ShapeDtypeStruct((tokens, width), BF),
            jax.ShapeDtypeStruct((tokens, width), BF),
            jax.ShapeDtypeStruct((experts_all, width), F32),
            jax.ShapeDtypeStruct((tokens, width), BF),
            jax.ShapeDtypeStruct((tokens, width), BF),
            jax.ShapeDtypeStruct(far_up.shape, BF),
            jax.ShapeDtypeStruct(far_up.shape, BF),
            jax.ShapeDtypeStruct(far_up.shape, BF),
            jax.ShapeDtypeStruct(far_marks.shape, BF),
        ],
        grid=(2 * steps,),
        in_specs=specs,
        out_specs=[
            pl.BlockSpec(up_block, own),
            pl.BlockSpec(up_block, own),
            pl.BlockSpec(down_block, own),
            pl.BlockSpec((tokens, width), whole, pipeline_mode=once),
            pl.BlockSpec((tokens, width), whole, pipeline_mode=once),
            pl.BlockSpec((experts_all, width), whole, pipeline_mode=once),
        ]
        + [pl.BlockSpec(memory_space=pl.ANY)] * 6,
        scratch_shapes=[
            gate_scratch, gate_scratch, gate_scratch, rows_scratch, rows_scratch,
            pltpu.VMEM((width, tokens), BF),
            pltpu.VMEM((width, GROUP * hid), BF),
            pltpu.VMEM((width, GROUP * hid), BF),
            pltpu.VMEM((GROUP * hid, tokens), BF),
            pltpu.VMEM((tokens, GROUP * hid), BF),
            pltpu.VMEM((tokens, GROUP * hid), BF),
        ]
        + swap_scratch
        + swap_scratch
        + [pltpu.SemaphoreType.DMA((2, 3, steps)), pltpu.SemaphoreType.DMA((2, 8)), pltpu.VMEM((tokens, width), BF), pltpu.SemaphoreType.DMA((2,))],
        compiler_params=pltpu.CompilerParams(
            dimension_semantics=("arbitrary",), collective_id=3, has_side_effects=True, vmem_limit_bytes=60 * MIB
        ),
        cost_estimate=pl.CostEstimate(
            flops=18 * tokens * width * count * hid,
            bytes_accessed=12 * count * width * hid,
            transcendentals=tokens * count * hid,
        ),
        name="experts",
    )(*args, w_gate, w_up, w_down, pulled)


def finish_kernel(core_ref, *refs):
    ins, outs = refs[:13], refs[13:]
    part, at = pl.program_id(0), pl.program_id(1)
    mine, other = ins[:3], ins[3:6]
    wide_mine, wide_other, tall_mine, tall_other, gains, grad, block = ins[6:]
    out_g, out_u, out_d, out_q, out_k, out_v, out_o, out_r, out_first, out_second, out_grad, out_block = outs
    for place, sources in enumerate((mine, other)):

        @pl.when(part == place)
        def _():
            for source, target in zip(sources, (out_g, out_u, out_d)):
                target[...] = source[...].astype(F32)

    core = core_ref[0]
    queries, kv = out_q.shape[1], out_k.shape[1]
    half = out_q.shape[0] // 2
    tall = tall_mine.shape[0]
    outs_rows = out_o.shape[0]

    @pl.when((part == 0) & (at == 0))
    def _():
        out_grad[...] = grad[...]
        out_block[...] = block[...]
        out_first[...] = gains[0:1, :]
        out_second[...] = gains[1:2, :]

    for place in range(2):

        @pl.when((part == place) & (at == 1))
        def _():
            own = core == place
            summed = jnp.where(own, wide_mine[...].astype(F32), wide_other[...].astype(F32))
            rows = slice(place * half, (place + 1) * half)
            out_q[rows, :] = summed[:, :queries]
            out_k[rows, :] = summed[:, queries : queries + kv]
            out_v[rows, :] = summed[:, queries + kv :]
            tall_sum = jnp.where(own, tall_mine[...].astype(F32), tall_other[...].astype(F32))
            top = min((place + 1) * tall, outs_rows)
            out_o[place * tall : top, :] = tall_sum[: top - place * tall, :]
            if place == 1:
                out_r[...] = tall_sum[top - place * tall :, :]


def finish(core, sums, others, wide, wide_back, tall, tall_back, gains, grad, block, queries, outs_rows):
    half = sums[0].shape[0]
    width = grad.shape[1]
    kv = (wide.shape[1] - queries) // 2
    experts_all = 2 * tall.shape[0] - outs_rows
    whole = lambda shape: pl.BlockSpec(shape, lambda part, at, core: (0,) * len(shape), pipeline_mode=pl.Buffered(1))
    step = 4
    count = half // step
    single = lambda array, index: pl.BlockSpec((step,) + array.shape[1:], index)
    first = lambda part, at, core: (jnp.where(part == 0, at, count - 1), 0, 0)
    second = lambda part, at, core: (jnp.where(part == 0, 0, at), 0, 0)
    placed = lambda part, at, core: (jnp.where(part == 0, core[0], 1 - core[0]) * count + at, 0, 0)
    rest = [wide, wide_back, tall, tall_back, gains, grad, block]
    wide_shape = lambda shape: jax.ShapeDtypeStruct(shape, F32)
    shapes = [
        (2 * wide.shape[0], queries), (2 * wide.shape[0], kv), (2 * wide.shape[0], kv),
        (outs_rows, width), (experts_all, width), (1, width), (1, width),
    ]
    return pl.pallas_call(
        finish_kernel,
        out_shape=[wide_shape((2 * half,) + item.shape[1:]) for item in sums]
        + [wide_shape(shape) for shape in shapes]
        + [jax.ShapeDtypeStruct(grad.shape, BF), jax.ShapeDtypeStruct(block.shape, BF)],
        grid_spec=pltpu.PrefetchScalarGridSpec(
            num_scalar_prefetch=1,
            grid=(2, count),
            in_specs=[single(item, first) for item in sums]
            + [single(item, second) for item in others]
            + [whole(item.shape) for item in rest],
            out_specs=[single(item, placed) for item in sums]
            + [whole(shape) for shape in shapes + [grad.shape, block.shape]],
        ),
        compiler_params=pltpu.CompilerParams(vmem_limit_bytes=60 * MIB),
        name="finish",
    )(core, *sums, *others, *rest)


def fast_device(
    block_input, first_gain, w_query, key_weight, value_weight, w_output, second_gain, w_router,
    w_gate, w_up, w_down, expert_ids, slot_index, piece_start_offsets, upstream,
):
    rows, width = block_input.shape
    experts_all = w_router.shape[1]
    core = lax.axis_index("dp") % 2
    positions = lax.axis_index("expert") * rows + jnp.arange(rows, dtype=jnp.int32)
    lanes = jnp.arange(128, dtype=jnp.int32) % (HEAD_SIZE // 2)
    inverse = jnp.exp(lanes.astype(F32) * (-2.0 * math.log(rope_base) / HEAD_SIZE))
    angle = positions.astype(F32)[:, None] * inverse[None, :]
    cosines, sines = jnp.cos(angle), jnp.sin(angle)
    routes = w_router.T
    (
        first_normed, query_rot, keys, values, attended, lse, residual, normed_all, marks, far_marks, peer_up, far_up,
        pulled,
    ) = front(
        piece_start_offsets, block_input, first_gain, second_gain, w_query, key_weight, value_weight, w_output,
        cosines, sines, expert_ids.T, slot_index.T, upstream, experts_all, w_down,
    )
    keys, values = keys.reshape(2 * rows, -1), values.reshape(2 * rows, -1)
    normed_all = normed_all.reshape(2 * rows, width)
    marks = marks.reshape(2 * rows, 2 * experts_all)
    far_marks = far_marks.reshape(2 * rows, 2 * experts_all)
    dwg, dwu, dwd, mix, back, route, *far = experts(
        normed_all, marks, routes, upstream, peer_up, far_up, far_marks, w_gate, w_up, w_down, pulled
    )
    far_normed, far_other_normed, far_peer_up, far_other_up, far_other_peer_up, far_other_marks = far
    residual_grad, residual_low, grad_second, route, mixed, sums = residual_gradient(
        back, mix, route, residual, upstream, second_gain, routes,
        (
            far_normed, far_other_normed, far_up, far_peer_up, far_other_up, far_other_peer_up,
            far_marks, far_other_marks,
        ),
        w_gate, w_up, w_down, (dwg, dwu, dwd),
    )
    grad_input, wide, wide_back, tall, tall_back, gains, block_output = input_gradient(
        piece_start_offsets, block_input, residual_grad, first_gain, first_normed, w_query, key_weight, value_weight,
        w_output, cosines, sines, query_rot, keys, values, lse, attended, residual_low, route, grad_second, mixed, residual,
    )
    grad_gate, grad_up, grad_down, grad_query, grad_key, grad_value, grad_output, grad_router, first, second, grad, block = finish(
        core[None].astype(jnp.int32), sums[:3], sums[3:], wide, wide_back, tall, tall_back, gains,
        grad_input.reshape(rows, width), block_output.reshape(rows, width // 4), w_query.shape[1], w_output.shape[0],
    )
    return (
        block, grad, first[0], grad_query, grad_key, grad_value, grad_output, second[0], grad_router.T,
        grad_gate, grad_up, grad_down,
    )


def solution(mesh):
    fast = mesh.shape["expert"] == 2 and mesh.shape["dp"] == 4 and mesh.shape["tensor"] == 4
    placed = (
        P(("dp", "expert"), None),
        P(),
        P(None, "tensor"),
        P(None, "tensor"),
        P(None, "tensor"),
        P("tensor", None),
        P(),
        P(),
        P("expert", None, "tensor"),
        P("expert", None, "tensor"),
        P("expert", "tensor", None),
        P(("dp", "expert"), None),
        P(("dp", "expert"), None),
        P("dp", None),
        P(("dp", "expert"), None),
    )
    return jax.shard_map(
        fast_device if fast else general_device,
        mesh=mesh,
        in_specs=placed,
        out_specs=(
            P(("dp", "expert"), "tensor"),
            P(("dp", "expert"), None),
            P(),
            P(None, "tensor"),
            P(None, "tensor"),
            P(None, "tensor"),
            P("tensor", None),
            P(),
            P(),
            P("expert", None, "tensor"),
            P("expert", None, "tensor"),
            P("expert", "tensor", None),
        ),
        check_vma=False,
    )
```
